32 devices in a mesh: case: 2 (over y), gx: 4 (over z), gy: 2 (over x), gz: 2 (over core).
Axes of the slice: x: 2, y: 2, z: 4, core: 2. Of those that a mesh axis runs over, the one named last changes fastest.
Arguments:
- displacement: float32 [3, 128, 64, 512], P(None, ('case', 'gx'), 'gy', 'gz'), parts along dimension 1, may hold values from -6 to 6
- velocity: float32 [3, 128, 64, 512], P(None, ('case', 'gx'), 'gy', 'gz'), parts along dimension 1, may hold values from -6 to 6
- damage: float32 [128, 64, 512], P(('case', 'gx'), 'gy', 'gz'), parts along dimension 0, may hold values from 0 to 0.9
- history: float32 [128, 64, 512], P(('case', 'gx'), 'gy', 'gz'), parts along dimension 0, may hold values from 0.05 to 5
- contact: int32 [128, 64, 512], P(('case', 'gx'), 'gy', 'gz'), parts along dimension 0, may hold values 0 or 1
- notch: int32 [128, 64, 512], P(('case', 'gx'), 'gy', 'gz'), parts along dimension 0, may hold values 0 or 1
- labels: int32 [128, 64, 512], P(('case', 'gx'), 'gy', 'gz'), parts along dimension 0, may hold values from 0 to 3
- table: float32 [4, 4], replicated, may hold values from 0.5 to 2
- impact: float32 [6], P('case'), parts along dimension 0, may hold values from -4 to 4
Outputs:
- displacement_new: float32 [3, 128, 64, 512], P(None, ('case', 'gx'), 'gy', 'gz'), parts along dimension 1
- velocity_new: float32 [3, 128, 64, 512], P(None, ('case', 'gx'), 'gy', 'gz'), parts along dimension 1
- history_new: float32 [128, 64, 512], P(('case', 'gx'), 'gy', 'gz'), parts along dimension 0
- damage_new: float32 [128, 64, 512], P(('case', 'gx'), 'gy', 'gz'), parts along dimension 0
The draws below stay inside these ranges and needn't reach their ends.
There are 2 independent parts, one for each index of `case`. The reference program is written for one: setup_inputs(seed, part) draws one part's arguments, and reference() takes and returns one part's arrays. A program takes and returns all parts, laid end to end along the dimension named above; an argument that names none is the same for every part. Nothing has to cross between parts.
All inputs are finite; a program needn't handle non-finite values. No bound on the sum of `contact` or of `notch` on one device may be relied on, other than what follows from the above.
Results may differ from the reference program's by a relative error of at most 0.0001.
Values sent between devices are 32-bit elements; how exact they have to be, the bound alone decides.
No kernel may reach another device: no remote copies, remote signals or barrier semaphores. Data moves between devices by JAX's collectives and lax.ppermute only.
A program may use at most 64 MiB of HBM per device.

```python
import math
import jax
import jax.numpy as jnp
from jax import lax

ITERS = 3
REGIONS = 4
NX = 64
NY = 64
NZ = 512


def set_ends(entries, stream_key, smallest, high):
    spot = [jax.random.randint(jax.random.fold_in(stream_key, axis), (), 0, length) for axis, length in enumerate(entries.shape)]
    longest = entries.shape.index(max(entries.shape))
    beside = spot[:longest] + [(spot[longest] + 1) % entries.shape[longest]] + spot[longest + 1:]
    return entries.at[tuple(spot)].set(smallest).at[tuple(beside)].set(high)


def level_of(stream_key, dims, cuts, least, top_value):
    def one(axis_at, parts):
        heights = jax.random.uniform(jax.random.fold_in(jax.random.fold_in(stream_key, 6), axis_at), (parts,), jnp.float32, least / len(cuts), top_value / len(cuts))
        return jnp.repeat(jnp.exp(heights), dims[axis_at] // parts).reshape((-1,) + (1,) * (len(dims) - axis_at - 1))

    loudness = one(*cuts[0])
    for cut in cuts[1:]:
        loudness = loudness * one(*cut)
    return loudness


def bell_draw(own_key, shape, width, bound, split=(), kind=jnp.bfloat16):
    entries = width * jax.random.normal(own_key, shape, jnp.float32)
    if split:
        entries = entries * level_of(own_key, shape, split, -0.22, 0.18)
    return jnp.clip(entries, -bound, bound).astype(kind)


def setup_inputs(seed: int = 0, part: int = 0) -> dict:
    arg_keys = jax.random.split(jax.random.key(seed), 10)
    part_keys = jax.random.split(jax.random.fold_in(arg_keys[9], part), 10)
    displacement = bell_draw(part_keys[0], (3, NX, NY, NZ), 1.0, 6.0, ((1, 4), (2, 2), (3, 2)), jnp.float32)
    velocity = bell_draw(part_keys[1], (3, NX, NY, NZ), 1.0, 6.0, ((1, 4), (2, 2), (3, 2)), jnp.float32)
    damage = jnp.clip(0.9 * jax.random.uniform(part_keys[2], (NX, NY, NZ), jnp.float32) ** level_of(part_keys[2], (NX, NY, NZ), ((0, 4), (1, 2), (2, 2)), -0.2, 0.2), 0.0, 0.9)
    history = jnp.clip(jnp.exp(math.log(5.0) - 4.6051702 * jax.random.uniform(part_keys[3], (NX, NY, NZ), jnp.float32) ** level_of(part_keys[3], (NX, NY, NZ), ((0, 4), (1, 2), (2, 2)), -0.2, 0.2)), 0.05, 5.0)
    contact = set_ends((jax.random.randint(part_keys[4], (NX, NY, NZ), 0, 16) < 1).astype(jnp.int32), jax.random.fold_in(part_keys[4], 1), 0, 1)
    notch = set_ends((jax.random.randint(part_keys[5], (NX, NY, NZ), 0, 64) < 1).astype(jnp.int32), jax.random.fold_in(part_keys[5], 1), 0, 1)
    labels = set_ends(jax.random.randint(part_keys[6], (NX, NY, NZ), 0, REGIONS), jax.random.fold_in(part_keys[6], 1), 0, REGIONS - 1).astype(jnp.int32)
    table = jnp.clip(jax.random.uniform(arg_keys[7], (4, REGIONS), jnp.float32, 0.5, 2.0), 0.5, 2.0)
    impact = bell_draw(part_keys[8], (3,), 1.0, 4.0, (), jnp.float32)
    return {"displacement": displacement, "velocity": velocity, "damage": damage, "history": history, "contact": contact, "notch": notch, "labels": labels, "table": table, "impact": impact}


TIME_STEP = 0.1
KAPPA_COEF = 0.5
NOTCH_LOAD = 20.0
STIFF_FLOOR = 1e-3
component_of = ((0, 3, 4), (3, 1, 5), (4, 5, 2))


def central(padded, spatial):
    upper_start, upper_limit, lower_start, lower_limit = [], [], [], []
    for which in range(3):
        extent = padded.shape[which]
        if which == spatial:
            upper_start.append(2)
            upper_limit.append(extent)
            lower_start.append(0)
            lower_limit.append(extent - 2)
        else:
            upper_start.append(1)
            upper_limit.append(extent - 1)
            lower_start.append(1)
            lower_limit.append(extent - 1)
    return 0.5 * (lax.slice(padded, upper_start, upper_limit) - lax.slice(padded, lower_start, lower_limit))


def material(labels, table):
    properties = []
    for quantity in range(4):
        picked = jnp.zeros(labels.shape, jnp.float32)
        for region in range(table.shape[1]):
            picked = picked + jnp.where(labels == region, table[quantity, region], 0.0)
        properties.append(picked)
    return properties


def stress_parts(grads, lame, shear, degrade):
    trace = grads[0][0] + grads[1][1] + grads[2][2]
    strain = [grads[0][0], grads[1][1], grads[2][2],
              0.5 * (grads[0][1] + grads[1][0]),
              0.5 * (grads[0][2] + grads[2][0]),
              0.5 * (grads[1][2] + grads[2][1])]
    stress = []
    for which in range(6):
        if which < 3:
            stress.append(degrade * (lame * trace + 2.0 * shear * strain[which]))
        else:
            stress.append(degrade * (2.0 * shear * strain[which]))
    positive = jnp.maximum(trace, 0.0)
    squares = strain[0] * strain[0] + strain[1] * strain[1] + strain[2] * strain[2]
    squares = squares + 2.0 * (strain[3] * strain[3] + strain[4] * strain[4] + strain[5] * strain[5])
    energy = 0.5 * lame * positive * positive + shear * squares
    return stress, energy


def neighbours(padded):
    total = padded[2:, 1:-1, 1:-1] + padded[:-2, 1:-1, 1:-1]
    total = total + padded[1:-1, 2:, 1:-1] + padded[1:-1, :-2, 1:-1]
    total = total + padded[1:-1, 1:-1, 2:] + padded[1:-1, 1:-1, :-2]
    return total


def reference(displacement, velocity, damage, history, contact, notch, labels, table, impact):
    lame, shear, density, fracture = material(labels, table)
    degrade = (1.0 - damage) * (1.0 - damage) + STIFF_FLOOR
    grads = [[central(jnp.pad(displacement[c], 1), j) for j in range(3)] for c in range(3)]
    stress, energy = stress_parts(grads, lame, shear, degrade)
    loaded = contact.astype(jnp.float32)
    new_vel, new_disp = [], []
    for component in range(3):
        force = central(jnp.pad(stress[component_of[component][0]], 1), 0)
        force = force + central(jnp.pad(stress[component_of[component][1]], 1), 1)
        force = force + central(jnp.pad(stress[component_of[component][2]], 1), 2)
        total = force + loaded * impact[component]
        speed = velocity[component] + TIME_STEP * total / density
        new_vel.append(speed)
        new_disp.append(displacement[component] + TIME_STEP * speed)
    history_new = jnp.maximum(jnp.maximum(history, energy), NOTCH_LOAD * notch.astype(jnp.float32))
    diagonal = fracture + 2.0 * history_new + 6.0 * KAPPA_COEF

    def operate(field):
        return diagonal * field - KAPPA_COEF * neighbours(jnp.pad(field, 1))

    iterate = damage
    residual = 2.0 * history_new - operate(iterate)
    precond = residual / diagonal
    direction = precond
    norm_now = jnp.sum(residual * precond)
    for sweep in range(ITERS):
        image = operate(direction)
        alpha = norm_now / jnp.sum(direction * image)
        iterate = iterate + alpha * direction
        residual = residual - alpha * image
        if sweep + 1 < ITERS:
            precond = residual / diagonal
            norm_next = jnp.sum(residual * precond)
            direction = precond + (norm_next / norm_now) * direction
            norm_now = norm_next
    return jnp.stack(new_disp), jnp.stack(new_vel), history_new, jnp.maximum(iterate, damage)
```

```python
import functools
import jax
import jax.numpy as jnp
from jax import lax
from jax.experimental import pallas as pl
from jax.experimental.pallas import tpu as pltpu
from jax.sharding import PartitionSpec as P

TIME_STEP = 0.1
KAPPA_COEF = 0.5
NOTCH_LOAD = 20.0
STIFF_FLOOR = 0.001
ALPHA_LOW, ALPHA_HIGH = 0.5, 6.5
VMEM_BYTES = 24 * 1024 * 1024
F32 = jnp.float32


def iota2(shape, dim):
    return lax.broadcasted_iota(jnp.int32, shape, dim)


def pick(flag, when, other):
    return jnp.where(flag, when, other)


class Sides:
    def __init__(self, pos, refs, plan):
        self.first_y = pos[0] == 0
        self.first_z = pos[1] == 0
        self.xlo, self.xhi = refs[0], refs[1]
        rest = refs[2:]
        self.ys, rest = (rest[:1], rest[1:]) if plan[0] else (rest[:2], rest[2:])
        self.zs = rest

    def along_x(self, ref, lead, field, x):
        count = ref.shape[-3]
        lower = ref[(*lead, jnp.maximum(x - 1, 0))]
        upper = ref[(*lead, jnp.minimum(x + 1, count - 1))]
        lower = jnp.where(x == 0, self.xlo[field], lower)
        upper = jnp.where(x == count - 1, self.xhi[field], upper)
        return upper, lower

    def along_y(self, plane, field, x):
        rows = iota2(plane.shape, 0)
        last = plane.shape[0] - 1
        if len(self.ys) == 1:
            row = self.ys[0][field, pl.ds(x, 1), :]
            lo = jnp.where(self.first_y, 0.0, row)
            hi = jnp.where(self.first_y, row, 0.0)
        else:
            lo = self.ys[0][field, pl.ds(x, 1), :]
            hi = self.ys[1][field, pl.ds(x, 1), :]
        upper = jnp.where(rows == last, hi, pltpu.roll(plane, last, 0))
        lower = jnp.where(rows == 0, lo, pltpu.roll(plane, 1, 0))
        return upper, lower

    def along_z(self, plane, field, x):
        lanes = iota2(plane.shape, 1)
        last = plane.shape[1] - 1
        if len(self.zs) == 1:
            column = self.zs[0][x][:, field : field + 1]
            lo = jnp.where(self.first_z, 0.0, column)
            hi = jnp.where(self.first_z, column, 0.0)
        else:
            lo = self.zs[0][x][:, field : field + 1]
            hi = self.zs[1][x][:, field : field + 1]
        upper = jnp.where(lanes == last, hi, pltpu.roll(plane, last, 1))
        lower = jnp.where(lanes == 0, lo, pltpu.roll(plane, 1, 1))
        return upper, lower


class Faces:
    def __init__(self, pos, refs, plan):
        self.first_y = pos[0] == 0
        self.first_z = pos[1] == 0
        self.pos_z = pos[1]
        self.xlo, self.xhi = refs[0], refs[1]
        rest = refs[2:]
        self.ys, rest = (rest[:1], rest[1:]) if plan[0] else (rest[:2], rest[2:])
        self.zs = rest

    def put_y(self, plane, field, x):
        last = plane.shape[0] - 1
        low, high = plane[0:1, :], plane[last : last + 1, :]
        if len(self.ys) == 1:
            self.ys[0][field, pl.ds(x, 1), :] = jnp.where(self.first_y, high, low)
        else:
            self.ys[0][field, pl.ds(x, 1), :] = low
            self.ys[1][field, pl.ds(x, 1), :] = high

    def put_z(self, planes, x):
        depth = planes[0].shape[1]
        lanes = iota2((planes[0].shape[0], 128), 1)
        if len(self.zs) == 1:
            tile = None
            for field, plane in enumerate(planes):
                part = jnp.where(self.first_z, plane[:, depth - 128 :], plane[:, :128])
                part = pltpu.roll(part, field + 1 - self.pos_z, 1)
                tile = part if tile is None else jnp.where(lanes == field, part, tile)
            self.zs[0][x] = tile
        else:
            for which, (start, shift) in enumerate(((0, 0), (depth - 128, 1))):
                tile = None
                for field, plane in enumerate(planes):
                    part = plane[:, start : start + 128]
                    if field + shift:
                        part = pltpu.roll(part, field + shift, 1)
                    tile = part if tile is None else jnp.where(lanes == field, part, tile)
                self.zs[which][x] = tile


def folded(values):
    total = None
    for start in range(0, values.shape[1], 128):
        part = values[:, start : start + 128]
        total = part if total is None else total + part
    out = None
    for start in range(0, values.shape[0], 8):
        part = total[start : start + 8]
        out = part if out is None else out + part
    return out


def by_label(labels, scalars):
    picked = scalars[0]
    for region in range(1, len(scalars)):
        picked = jnp.where(labels == region, scalars[region], picked)
    return picked


def pack_kernel(plan, pos, disp, damage, *outs):
    faces = Faces(pos, outs, plan)
    count = damage.shape[0]
    for field in range(4):
        src = damage if field == 3 else disp.at[field]
        faces.xlo[field] = src[0]
        faces.xhi[field] = src[count - 1]

    def body(x, carry):
        planes = [disp[0, x], disp[1, x], disp[2, x], damage[x]]
        for field in range(4):
            faces.put_y(planes[field], field, x)
        faces.put_z(planes, x)
        return carry

    lax.fori_loop(0, count, body, 0)


def local_kernel(plan, n_sides, pos, table, disp, damage, history, notch, labels, *refs):
    sides = Sides(pos, refs[:n_sides], plan)
    hist_out, rd_out, v_out, stress_out, mom_out = refs[n_sides : n_sides + 5]
    faces = Faces(pos, refs[n_sides + 5 :], plan)
    count = damage.shape[0]
    regions = table.shape[1]
    lames = [table[0, r] for r in range(regions)]
    shears = [table[1, r] for r in range(regions)]
    fractures = [table[3, r] for r in range(regions)]

    def body(x, total):
        g = []
        for c in range(3):
            plane = disp[c, x]
            row = []
            for upper, lower in (
                sides.along_x(disp, (c,), c, x),
                sides.along_y(plane, c, x),
                sides.along_z(plane, c, x),
            ):
                row.append(0.5 * (upper - lower))
            g.append(row)
        lab = labels[x]
        lame = by_label(lab, lames)
        shear = by_label(lab, shears)
        fracture = by_label(lab, fractures)
        dmg = damage[x]
        degrade = (1.0 - dmg) * (1.0 - dmg) + STIFF_FLOOR
        trace = g[0][0] + g[1][1] + g[2][2]
        strain = [
            g[0][0],
            g[1][1],
            g[2][2],
            0.5 * (g[0][1] + g[1][0]),
            0.5 * (g[0][2] + g[2][0]),
            0.5 * (g[1][2] + g[2][1]),
        ]
        positive = jnp.maximum(trace, 0.0)
        squares = strain[0] * strain[0] + strain[1] * strain[1] + strain[2] * strain[2]
        squares = squares + 2.0 * (
            strain[3] * strain[3] + strain[4] * strain[4] + strain[5] * strain[5]
        )
        energy = 0.5 * lame * positive * positive + shear * squares
        scale = degrade * (2.0 * shear)
        base = degrade * (lame * trace)
        stress = [base + scale * strain[k] if k < 3 else scale * strain[k] for k in range(6)]
        for k in range(6):
            stress_out[k, x] = stress[k]
        hist = jnp.maximum(
            jnp.maximum(history[x], energy), NOTCH_LOAD * notch[x].astype(F32)
        )
        hist_out[x] = hist
        diagonal = fracture + 2.0 * hist + 6.0 * KAPPA_COEF
        rd = 1.0 / diagonal
        rd_out[x] = rd
        xu, xl = sides.along_x(damage, (), 3, x)
        yu, yl = sides.along_y(dmg, 3, x)
        zu, zl = sides.along_z(dmg, 3, x)
        around = ((xu + xl) + (yu + yl)) + (zu + zl)
        residual = 2.0 * hist - (diagonal * dmg - KAPPA_COEF * around)
        v = residual * rd
        v_out[x] = v
        for field, plane in enumerate((v, stress[3], stress[1], stress[5])):
            faces.put_y(plane, field, x)
        faces.put_z((v, stress[4], stress[5], stress[2]), x)
        return total + folded(residual * v)

    total = lax.fori_loop(0, count, body, jnp.zeros((8, 128), F32))
    mom_out[...] = jnp.zeros((8, 128), F32)
    mom_out[0:1, :] = jnp.sum(total, axis=0, keepdims=True)
    for end, ref in ((0, faces.xlo), (count - 1, faces.xhi)):
        ref[0] = v_out[end]
        for slot, k in ((1, 0), (2, 3), (3, 4)):
            ref[slot] = stress_out[k, end]


def apply_kernel(plan, n_sides, step, pos, v, rd, mom, *refs):
    sides = Sides(pos, refs[:n_sides], plan)
    outs = refs[n_sides:]
    last = step == 2
    count = v.shape[0]
    if not last:
        new, mom_out = outs[:2]
        faces = Faces(pos, outs[2:], plan)
    else:
        (mom_out,) = outs

    def body(x, totals):
        plane = v[x]
        xu, xl = sides.along_x(v, (), 0, x)
        yu, yl = sides.along_y(plane, 0, x)
        zu, zl = sides.along_z(plane, 0, x)
        image = KAPPA_COEF * (((xu + xl) + (yu + yl)) + (zu + zl))
        first = totals[0] + folded(plane * image)
        if last:
            return (first,)
        made = image * rd[x]
        new[x] = made
        faces.put_y(made, 0, x)
        faces.put_z((made,), x)
        return (first, totals[1] + folded(made * image))

    zero = jnp.zeros((8, 128), F32)
    totals = lax.fori_loop(0, count, body, (zero,) if last else (zero, zero))
    rows = iota2((8, 128), 0)
    result = mom[...]
    for at, total in enumerate(totals):
        result = jnp.where(
            rows == 2 * step + 1 + at, jnp.sum(total, axis=0, keepdims=True), result
        )
    if last:
        for peer in range(mom_out.shape[0]):
            mom_out[peer] = result
    else:
        mom_out[...] = result
        faces.xlo[0] = new[0]
        faces.xhi[0] = new[count - 1]


def force_kernel(plan, n_sides, pos, table, impact, disp, vel, contact, labels, stress, *refs):
    sides = Sides(pos, refs[:n_sides], plan)
    disp_out, vel_out = refs[n_sides:]
    count = contact.shape[0]
    regions = table.shape[1]
    rates = [table[2, r] for r in range(regions)]

    def body(x, carry):
        loaded = contact[x].astype(F32)
        rate = TIME_STEP / by_label(labels[x], rates)
        for c, (kx, ky, kz) in enumerate(((0, 3, 4), (3, 1, 5), (4, 5, 2))):
            xu, xl = sides.along_x(stress, (kx,), c + 1, x)
            yu, yl = sides.along_y(stress[ky, x], c + 1, x)
            zu, zl = sides.along_z(stress[kz, x], c + 1, x)
            force = 0.5 * (((xu - xl) + (yu - yl)) + (zu - zl))
            speed = vel[c, x] + rate * (force + loaded * impact[c])
            vel_out[c, x] = speed
            disp_out[c, x] = disp[c, x] + TIME_STEP * speed
        return carry

    lax.fori_loop(0, count, body, 0)


def cg_coefficients(k):
    zero, one = jnp.zeros_like(k[0]), jnp.ones_like(k[0])
    z, p, out = [one], [one], [zero, zero, zero]

    def form(a, b, moments):
        total = None
        for i, ai in enumerate(a):
            for j, bj in enumerate(b):
                term = ai * bj * moments[i + j]
                total = term if total is None else total + term
        return total

    energy = [k[j] - k[j + 1] for j in range(5)]
    rz = k[0]
    for step in range(3):
        alpha = jnp.clip(rz / form(p, p, energy), ALPHA_LOW, ALPHA_HIGH)
        out = [o + alpha * (p[i] if i < len(p) else zero) for i, o in enumerate(out)]
        if step == 2:
            break
        image = [(p[i] if i < len(p) else zero) - (p[i - 1] if i else zero) for i in range(len(p) + 1)]
        z = [(z[i] if i < len(z) else zero) - alpha * image[i] for i in range(len(image))]
        new = jnp.maximum(form(z, z, k), 0.0)
        beta = new / rz
        p = [z[i] + beta * (p[i] if i < len(p) else zero) for i in range(len(z))]
        rz = new
    return out


def final_kernel(mom, damage, v0, v1, v2, out):
    sums = jnp.sum(jnp.sum(mom[...], axis=0), axis=1, keepdims=True)
    c0, c1, c2 = cg_coefficients([sums[j : j + 1, :] for j in range(6)])

    def body(x, carry):
        dmg = damage[x]
        out[x] = jnp.maximum(dmg + (c0 * v0[x] + c1 * v1[x] + c2 * v2[x]), dmg)
        return carry

    lax.fori_loop(0, damage.shape[0], body, 0)


def swap_or_shift(axis, faces):
    count = lax.axis_size(axis)
    if len(faces) == 1:
        return [lax.ppermute(faces[0], axis, [(0, 1), (1, 0)])]
    forward = [(i, i + 1) for i in range(count - 1)]
    backward = [(b, a) for a, b in forward]
    return [lax.ppermute(faces[1], axis, forward), lax.ppermute(faces[0], axis, backward)]


def exchange(faces, plan):
    xs, rest = faces[:2], faces[2:]
    ys, zs = (rest[:1], rest[1:]) if plan[0] else (rest[:2], rest[2:])
    return [*swap_or_shift("gx", xs), *swap_or_shift("gy", ys), *swap_or_shift("gz", zs)]


def call(kernel, n_smem, ins, outs, flops):
    vmem = pl.BlockSpec(memory_space=pltpu.VMEM)
    smem = pl.BlockSpec(memory_space=pltpu.SMEM)
    moved = sum(4 * a.size for a in (*ins, *outs))
    return pl.pallas_call(
        kernel,
        out_shape=outs,
        in_specs=[smem] * n_smem + [vmem] * (len(ins) - n_smem),
        out_specs=[vmem] * len(outs),
        compiler_params=pltpu.CompilerParams(vmem_limit_bytes=VMEM_BYTES),
        cost_estimate=pl.CostEstimate(flops=flops, bytes_accessed=moved, transcendentals=0),
    )(*ins)


def per_device(displacement, velocity, damage, history, contact, notch, labels, table, impact):
    nx, ny, nz = damage.shape
    size = damage.size
    plan = (lax.axis_size("gy") == 2, lax.axis_size("gz") == 2)
    pos = jnp.stack([lax.axis_index("gy"), lax.axis_index("gz")]).astype(jnp.int32)

    def arr(*shape):
        return jax.ShapeDtypeStruct(shape, F32)

    def face_shapes(fields):
        out = [arr(fields, ny, nz)] * 2
        out += [arr(fields, nx, nz)] * (1 if plan[0] else 2)
        out += [arr(nx, ny, 128)] * (1 if plan[1] else 2)
        return out

    field = arr(nx, ny, nz)
    sent = call(
        functools.partial(pack_kernel, plan), 1, (pos, displacement, damage), face_shapes(4), size
    )
    got = exchange(sent, plan)
    n_sides = len(got)
    hist, rd, v0, stress, mom, *sent = call(
        functools.partial(local_kernel, plan, n_sides),
        2,
        (pos, table, displacement, damage, history, notch, labels, *got),
        [field, field, field, arr(6, nx, ny, nz), arr(8, 128), *face_shapes(4)],
        150 * size,
    )
    got0 = exchange(sent, plan)
    v1, mom, *sent = call(
        functools.partial(apply_kernel, plan, n_sides, 0),
        1,
        (pos, v0, rd, mom, *got0),
        [field, arr(8, 128), *face_shapes(1)],
        20 * size,
    )
    got1 = exchange(sent, plan)
    new_disp, new_vel = call(
        functools.partial(force_kernel, plan, n_sides),
        3,
        (pos, table, impact, displacement, velocity, contact, labels, stress, *got0),
        [arr(3, nx, ny, nz), arr(3, nx, ny, nz)],
        60 * size,
    )
    v2, mom, *sent = call(
        functools.partial(apply_kernel, plan, n_sides, 1),
        1,
        (pos, v1, rd, mom, *got1),
        [field, arr(8, 128), *face_shapes(1)],
        20 * size,
    )
    got2 = exchange(sent, plan)
    axes = ("gx", "gy", "gz")
    peers = lax.axis_size("gx") * lax.axis_size("gy") * lax.axis_size("gz")
    (spread,) = call(
        functools.partial(apply_kernel, plan, n_sides, 2),
        1,
        (pos, v2, rd, mom, *got2),
        [arr(peers, 8, 128)],
        20 * size,
    )
    mom = lax.all_to_all(spread, axes, 0, 0, tiled=True)
    (damage_new,) = call(final_kernel, 0, (mom, damage, v0, v1, v2), [field], 8 * size)
    return new_disp, new_vel, hist, damage_new


def solution(mesh):
    placed = (
        P(None, ("case", "gx"), "gy", "gz"),
        P(None, ("case", "gx"), "gy", "gz"),
        P(("case", "gx"), "gy", "gz"),
        P(("case", "gx"), "gy", "gz"),
        P(("case", "gx"), "gy", "gz"),
        P(("case", "gx"), "gy", "gz"),
        P(("case", "gx"), "gy", "gz"),
        P(),
        P("case"),
    )
    return jax.shard_map(
        per_device,
        mesh=mesh,
        in_specs=placed,
        out_specs=(
            P(None, ("case", "gx"), "gy", "gz"),
            P(None, ("case", "gx"), "gy", "gz"),
            P(("case", "gx"), "gy", "gz"),
            P(("case", "gx"), "gy", "gz"),
        ),
        check_vma=False,
    )
```

```python
import functools
import jax
import jax.numpy as jnp
from jax import lax
from jax.experimental import pallas as pl
from jax.experimental.pallas import tpu as pltpu
from jax.sharding import PartitionSpec as P

TIME_STEP = 0.1
KAPPA_COEF = 0.5
NOTCH_LOAD = 20.0
STIFF_FLOOR = 0.001
ALPHA_LOW, ALPHA_HIGH = 0.5, 6.5
VMEM_BYTES = 24 * 1024 * 1024
F32 = jnp.float32


def iota2(shape, dim):
    return lax.broadcasted_iota(jnp.int32, shape, dim)


def pick(flag, when, other):
    return jnp.where(flag, when, other)


class Sides:
    def __init__(self, pos, refs, plan):
        self.swap_x = plan[2]
        self.odd_x = pos[2] == 1
        self.first_y = pos[0] == 0
        self.first_z = pos[1] == 0
        self.xs = refs[:2]
        rest = refs[2:]
        self.ys, rest = (rest[:1], rest[1:]) if plan[0] else (rest[:2], rest[2:])
        self.zs = rest

    def along_x(self, ref, lead, field, x):
        count = ref.shape[-3]
        lower = ref[(*lead, jnp.maximum(x - 1, 0))]
        upper = ref[(*lead, jnp.minimum(x + 1, count - 1))]
        first, second = self.xs[0][field], self.xs[1][field]
        if self.swap_x:
            lo = jnp.where(self.odd_x, first, second)
            hi = jnp.where(self.odd_x, second, first)
        else:
            lo, hi = first, second
        lower = jnp.where(x == 0, lo, lower)
        upper = jnp.where(x == count - 1, hi, upper)
        return upper, lower

    def along_y(self, plane, field, x):
        rows = iota2(plane.shape, 0)
        last = plane.shape[0] - 1
        if len(self.ys) == 1:
            row = self.ys[0][field, pl.ds(x, 1), :]
            lo = jnp.where(self.first_y, 0.0, row)
            hi = jnp.where(self.first_y, row, 0.0)
        else:
            lo = self.ys[0][field, pl.ds(x, 1), :]
            hi = self.ys[1][field, pl.ds(x, 1), :]
        upper = jnp.where(rows == last, hi, pltpu.roll(plane, last, 0))
        lower = jnp.where(rows == 0, lo, pltpu.roll(plane, 1, 0))
        return upper, lower

    def along_z(self, plane, field, x):
        lanes = iota2(plane.shape, 1)
        last = plane.shape[1] - 1
        if len(self.zs) == 1:
            column = self.zs[0][x][:, field : field + 1]
            lo = jnp.where(self.first_z, 0.0, column)
            hi = jnp.where(self.first_z, column, 0.0)
        else:
            lo = self.zs[0][x][:, field : field + 1]
            hi = self.zs[1][x][:, field : field + 1]
        upper = jnp.where(lanes == last, hi, pltpu.roll(plane, last, 1))
        lower = jnp.where(lanes == 0, lo, pltpu.roll(plane, 1, 1))
        return upper, lower


class Faces:
    def __init__(self, pos, refs, plan):
        self.swap_x = plan[2]
        self.odd_x = pos[2] == 1
        self.first_y = pos[0] == 0
        self.first_z = pos[1] == 0
        self.pos_z = pos[1]
        self.xs = refs[:2]
        rest = refs[2:]
        self.ys, rest = (rest[:1], rest[1:]) if plan[0] else (rest[:2], rest[2:])
        self.zs = rest

    def put_x(self, field, low, high):
        if self.swap_x:
            self.xs[0][field] = jnp.where(self.odd_x, low, high)
            self.xs[1][field] = jnp.where(self.odd_x, high, low)
        else:
            self.xs[0][field] = low
            self.xs[1][field] = high

    def put_low_x(self, field, plane):
        if self.swap_x:
            @pl.when(self.odd_x)
            def _():
                self.xs[0][field] = plane

            @pl.when(jnp.logical_not(self.odd_x))
            def _():
                self.xs[1][field] = plane
        else:
            self.xs[0][field] = plane

    def put_high_x(self, field, plane):
        if self.swap_x:
            @pl.when(self.odd_x)
            def _():
                self.xs[1][field] = plane

            @pl.when(jnp.logical_not(self.odd_x))
            def _():
                self.xs[0][field] = plane
        else:
            self.xs[1][field] = plane

    def put_y(self, plane, field, x):
        last = plane.shape[0] - 1
        low, high = plane[0:1, :], plane[last : last + 1, :]
        if len(self.ys) == 1:
            self.ys[0][field, pl.ds(x, 1), :] = jnp.where(self.first_y, high, low)
        else:
            self.ys[0][field, pl.ds(x, 1), :] = low
            self.ys[1][field, pl.ds(x, 1), :] = high

    def put_z(self, planes, x):
        depth = planes[0].shape[1]
        lanes = iota2((planes[0].shape[0], 128), 1)
        if len(self.zs) == 1:
            tile = None
            for field, plane in enumerate(planes):
                part = jnp.where(self.first_z, plane[:, depth - 128 :], plane[:, :128])
                part = pltpu.roll(part, field + 1 - self.pos_z, 1)
                tile = part if tile is None else jnp.where(lanes == field, part, tile)
            self.zs[0][x] = tile
        else:
            for which, (start, shift) in enumerate(((0, 0), (depth - 128, 1))):
                tile = None
                for field, plane in enumerate(planes):
                    part = plane[:, start : start + 128]
                    if field + shift:
                        part = pltpu.roll(part, field + shift, 1)
                    tile = part if tile is None else jnp.where(lanes == field, part, tile)
                self.zs[which][x] = tile


def unrolled(count, body, carry, many=4):
    def several(block, carry):
        for at in range(many):
            carry = body(block * many + at, carry)
        return carry

    return lax.fori_loop(0, count // many, several, carry)


def folded(values):
    total = None
    for start in range(0, values.shape[1], 128):
        part = values[:, start : start + 128]
        total = part if total is None else total + part
    out = None
    for start in range(0, values.shape[0], 8):
        part = total[start : start + 8]
        out = part if out is None else out + part
    return out


def by_label(labels, scalars):
    picked = scalars[0]
    for region in range(1, len(scalars)):
        picked = jnp.where(labels == region, scalars[region], picked)
    return picked


def pack_kernel(plan, pos, disp, damage, *outs):
    faces = Faces(pos, outs, plan)
    step, steps = pl.program_id(0), pl.num_programs(0)
    count = damage.shape[0]
    sources = [disp.at[0], disp.at[1], disp.at[2], damage]

    @pl.when(step == 0)
    def _():
        for field in range(4):
            faces.put_low_x(field, sources[field][0])

    @pl.when(step == steps - 1)
    def _():
        for field in range(4):
            faces.put_high_x(field, sources[field][count - 1])

    for at in range(count):
        planes = [source[at] for source in sources]
        for field in range(4):
            faces.put_y(planes[field], field, step * count + at)
        faces.put_z(planes, at)


def local_kernel(plan, n_sides, pos, table, disp, damage, history, notch, labels, *refs):
    sides = Sides(pos, refs[:n_sides], plan)
    hist_out, rd_out, v_out, stress_out, mom_out = refs[n_sides : n_sides + 5]
    faces = Faces(pos, refs[n_sides + 5 : -1], plan)
    held = refs[-1]
    step, steps = pl.program_id(0), pl.num_programs(0)
    count = damage.shape[0]
    block = history.shape[0]
    regions = table.shape[1]
    lames = [table[0, r] for r in range(regions)]
    shears = [table[1, r] for r in range(regions)]
    fractures = [table[3, r] for r in range(regions)]

    def body(at, total):
        x = step * block + at
        g = []
        for c in range(3):
            plane = disp[c, x]
            row = []
            for upper, lower in (
                sides.along_x(disp, (c,), c, x),
                sides.along_y(plane, c, x),
                sides.along_z(plane, c, x),
            ):
                row.append(0.5 * (upper - lower))
            g.append(row)
        lab = labels[at]
        lame = by_label(lab, lames)
        shear = by_label(lab, shears)
        fracture = by_label(lab, fractures)
        dmg = damage[x]
        degrade = (1.0 - dmg) * (1.0 - dmg) + STIFF_FLOOR
        trace = g[0][0] + g[1][1] + g[2][2]
        strain = [
            g[0][0],
            g[1][1],
            g[2][2],
            0.5 * (g[0][1] + g[1][0]),
            0.5 * (g[0][2] + g[2][0]),
            0.5 * (g[1][2] + g[2][1]),
        ]
        positive = jnp.maximum(trace, 0.0)
        squares = strain[0] * strain[0] + strain[1] * strain[1] + strain[2] * strain[2]
        squares = squares + 2.0 * (
            strain[3] * strain[3] + strain[4] * strain[4] + strain[5] * strain[5]
        )
        energy = 0.5 * lame * positive * positive + shear * squares
        scale = degrade * (2.0 * shear)
        base = degrade * (lame * trace)
        stress = [base + scale * strain[k] if k < 3 else scale * strain[k] for k in range(6)]
        for k in range(6):
            stress_out[k, x] = stress[k]
        hist = jnp.maximum(
            jnp.maximum(history[at], energy), NOTCH_LOAD * notch[at].astype(F32)
        )
        hist_out[at] = hist
        diagonal = fracture + 2.0 * hist + 6.0 * KAPPA_COEF
        rd = 1.0 / diagonal
        rd_out[x] = rd
        xu, xl = sides.along_x(damage, (), 3, x)
        yu, yl = sides.along_y(dmg, 3, x)
        zu, zl = sides.along_z(dmg, 3, x)
        around = ((xu + xl) + (yu + yl)) + (zu + zl)
        residual = 2.0 * hist - (diagonal * dmg - KAPPA_COEF * around)
        v = residual * rd
        v_out[x] = v
        for field, plane in enumerate((v, stress[3], stress[1], stress[5])):
            faces.put_y(plane, field, x)
        faces.put_z((v, stress[4], stress[5], stress[2]), x)
        return total + folded(residual * v)

    total = jnp.where(step == 0, 0.0, held[...])
    for at in range(block):
        total = body(at, total)
    held[...] = total

    @pl.when(step == 0)
    def _():
        for slot, src in enumerate((v_out, stress_out.at[0], stress_out.at[3], stress_out.at[4])):
            faces.put_low_x(slot, src[0])

    @pl.when(step == steps - 1)
    def _():
        for slot, src in enumerate((v_out, stress_out.at[0], stress_out.at[3], stress_out.at[4])):
            faces.put_high_x(slot, src[count - 1])
        mom_out[...] = jnp.zeros((8, 128), F32)
        mom_out[0:1, :] = jnp.sum(total, axis=0, keepdims=True)


def apply_kernel(plan, n_sides, step, pos, v, rd, mom, *refs):
    sides = Sides(pos, refs[:n_sides], plan)
    outs = refs[n_sides + (step == 1) :]
    last = step == 2
    count = v.shape[0]
    if not last:
        new, mom_out = outs[:2]
        faces = Faces(pos, outs[2:], plan)
    else:
        (mom_out,) = outs

    def body(x, totals):
        plane = v[x]
        xu, xl = sides.along_x(v, (), 0, x)
        yu, yl = sides.along_y(plane, 0, x)
        zu, zl = sides.along_z(plane, 0, x)
        image = KAPPA_COEF * (((xu + xl) + (yu + yl)) + (zu + zl))
        first = totals[0] + folded(plane * image)
        if last:
            return (first,)
        made = image * rd[x]
        new[x] = made
        faces.put_y(made, 0, x)
        faces.put_z((made,), x)
        return (first, totals[1] + folded(made * image))

    zero = jnp.zeros((8, 128), F32)
    totals = unrolled(count, body, (zero,) if last else (zero, zero))
    rows = iota2((8, 128), 0)
    result = mom[...]
    for at, total in enumerate(totals):
        result = jnp.where(
            rows == 2 * step + 1 + at, jnp.sum(total, axis=0, keepdims=True), result
        )
    if last:
        for peer in range(mom_out.shape[0]):
            mom_out[peer] = result
    else:
        mom_out[...] = result
        faces.put_x(0, new[0], new[count - 1])


def force_kernel(plan, n_sides, pos, table, impact, disp, vel, contact, labels, stress, *refs):
    sides = Sides(pos, refs[:n_sides], plan)
    disp_out, vel_out, token = refs[n_sides:]
    token[...] = jnp.zeros((8, 128), F32)
    step, block = pl.program_id(0), contact.shape[0]
    regions = table.shape[1]
    rates = [table[2, r] for r in range(regions)]
    for at in range(block):
        x = step * block + at
        loaded = contact[at].astype(F32)
        rate = TIME_STEP / by_label(labels[at], rates)
        for c, (kx, ky, kz) in enumerate(((0, 3, 4), (3, 1, 5), (4, 5, 2))):
            xu, xl = sides.along_x(stress, (kx,), c + 1, x)
            yu, yl = sides.along_y(stress[ky, x], c + 1, x)
            zu, zl = sides.along_z(stress[kz, x], c + 1, x)
            force = 0.5 * (((xu - xl) + (yu - yl)) + (zu - zl))
            speed = vel[c, at] + rate * (force + loaded * impact[c])
            vel_out[c, at] = speed
            disp_out[c, at] = disp[c, at] + TIME_STEP * speed


def cg_coefficients(k):
    zero, one = jnp.zeros_like(k[0]), jnp.ones_like(k[0])
    z, p, out = [one], [one], [zero, zero, zero]

    def form(a, b, moments):
        total = None
        for i, ai in enumerate(a):
            for j, bj in enumerate(b):
                term = ai * bj * moments[i + j]
                total = term if total is None else total + term
        return total

    energy = [k[j] - k[j + 1] for j in range(5)]
    rz = k[0]
    for step in range(3):
        alpha = jnp.clip(rz / form(p, p, energy), ALPHA_LOW, ALPHA_HIGH)
        out = [o + alpha * (p[i] if i < len(p) else zero) for i, o in enumerate(out)]
        if step == 2:
            break
        image = [(p[i] if i < len(p) else zero) - (p[i - 1] if i else zero) for i in range(len(p) + 1)]
        z = [(z[i] if i < len(z) else zero) - alpha * image[i] for i in range(len(image))]
        new = jnp.maximum(form(z, z, k), 0.0)
        beta = new / rz
        p = [z[i] + beta * (p[i] if i < len(p) else zero) for i in range(len(z))]
        rz = new
    return out


def final_kernel(mom, v0, v1, v2, damage, out):
    sums = jnp.sum(jnp.sum(mom[...], axis=0), axis=1, keepdims=True)
    c0, c1, c2 = cg_coefficients([sums[j : j + 1, :] for j in range(6)])
    step, block = pl.program_id(0), damage.shape[0]
    for at in range(block):
        x, dmg = step * block + at, damage[at]
        out[at] = jnp.maximum(dmg + (c0 * v0[x] + c1 * v1[x] + c2 * v2[x]), dmg)


def swap_or_shift(axis, faces, paired=False):
    count = lax.axis_size(axis)
    if paired:
        out = []
        for start, face in enumerate(faces):
            pairs = [(i, i + 1) for i in range(start, count - 1, 2)]
            out.append(lax.ppermute(face, axis, pairs + [(b, a) for a, b in pairs]))
        return out
    if len(faces) == 1:
        return [lax.ppermute(faces[0], axis, [(0, 1), (1, 0)])]
    forward = [(i, i + 1) for i in range(count - 1)]
    backward = [(b, a) for a, b in forward]
    return [lax.ppermute(faces[1], axis, forward), lax.ppermute(faces[0], axis, backward)]


def exchange(faces, plan):
    xs, rest = faces[:2], faces[2:]
    ys, zs = (rest[:1], rest[1:]) if plan[0] else (rest[:2], rest[2:])
    return [*swap_or_shift("gx", xs, plan[2]), *swap_or_shift("gy", ys), *swap_or_shift("gz", zs)]


STEPS = 4


def spec_of(kind, a):
    if kind == "s":
        return pl.BlockSpec(memory_space=pltpu.SMEM)
    if kind == "v":
        return pl.BlockSpec(memory_space=pltpu.VMEM)
    if kind == "a":
        return pl.BlockSpec(memory_space=pl.ANY)
    lead = len(a.shape) - 3
    block = (*a.shape[:lead], a.shape[lead] // STEPS, *a.shape[lead + 1 :])
    return pl.BlockSpec(block, lambda i: (*(0,) * lead, i, 0, 0))


def call(kernel, kinds, ins, out_kinds, outs, flops, scratch=()):
    moved = sum(4 * a.size for a in (*ins, *outs))
    grid = (STEPS,) if "b" in (*kinds, *out_kinds) else ()
    return pl.pallas_call(
        kernel,
        out_shape=outs,
        grid=grid,
        in_specs=[spec_of(k, a) for k, a in zip(kinds, ins, strict=True)],
        out_specs=[spec_of(k, a) for k, a in zip(out_kinds, outs, strict=True)],
        scratch_shapes=scratch,
        compiler_params=pltpu.CompilerParams(vmem_limit_bytes=VMEM_BYTES),
        cost_estimate=pl.CostEstimate(flops=flops, bytes_accessed=moved, transcendentals=0),
    )(*ins)


def per_device(displacement, velocity, damage, history, contact, notch, labels, table, impact):
    nx, ny, nz = damage.shape
    size = damage.size
    plan = (
        lax.axis_size("gy") == 2,
        lax.axis_size("gz") == 2,
        lax.axis_size("gx") % 2 == 0,
    )
    pos = jnp.stack(
        [lax.axis_index("gy"), lax.axis_index("gz"), lax.axis_index("gx") % 2]
    ).astype(jnp.int32)

    def arr(*shape):
        return jax.ShapeDtypeStruct(shape, F32)

    def face_shapes(fields):
        out = [arr(fields, ny, nz)] * 2
        out += [arr(fields, nx, nz)] * (1 if plan[0] else 2)
        out += [arr(nx, ny, 128)] * (1 if plan[1] else 2)
        return out

    field, small = arr(nx, ny, nz), arr(8, 128)
    faces4, faces1 = face_shapes(4), face_shapes(1)
    n_sides = len(faces4)
    n_flat = 3 if plan[0] else 4
    sides = "v" * n_sides
    sent = call(
        functools.partial(pack_kernel, plan),
        "sbb",
        (pos, displacement, damage),
        "v" * n_flat + "b" * (n_sides - n_flat),
        faces4,
        size,
    )
    got = exchange(sent, plan)
    hist, rd, v0, stress, mom, *sent = call(
        functools.partial(local_kernel, plan, n_sides),
        "ssvvbbb" + sides,
        (pos, table, displacement, damage, history, notch, labels, *got),
        "bvvvv" + sides,
        [field, field, field, arr(6, nx, ny, nz), small, *faces4],
        150 * size,
        [pltpu.VMEM((8, 128), F32)],
    )
    got0 = exchange(sent, plan)
    v1, mom, *sent = call(
        functools.partial(apply_kernel, plan, n_sides, 0),
        "svvv" + sides,
        (pos, v0, rd, mom, *got0),
        "vv" + sides,
        [field, small, *faces1],
        20 * size,
    )
    got1 = exchange(sent, plan)
    new_disp, new_vel, token = call(
        functools.partial(force_kernel, plan, n_sides),
        "sssbbbbv" + sides,
        (pos, table, impact, displacement, velocity, contact, labels, stress, *got0),
        "bbv",
        [arr(3, nx, ny, nz), arr(3, nx, ny, nz), small],
        60 * size,
    )
    v2, mom, *sent = call(
        functools.partial(apply_kernel, plan, n_sides, 1),
        "svvv" + sides + "a",
        (pos, v1, rd, mom, *got1, token),
        "vv" + sides,
        [field, small, *faces1],
        20 * size,
    )
    got2 = exchange(sent, plan)
    axes = ("gx", "gy", "gz")
    peers = lax.axis_size("gx") * lax.axis_size("gy") * lax.axis_size("gz")
    (spread,) = call(
        functools.partial(apply_kernel, plan, n_sides, 2),
        "svvv" + sides,
        (pos, v2, rd, mom, *got2),
        "v",
        [arr(peers, 8, 128)],
        20 * size,
    )
    mom = lax.all_to_all(spread, axes, 0, 0, tiled=True)
    (damage_new,) = call(
        final_kernel, "vvvvb", (mom, v0, v1, v2, damage), "b", [field], 8 * size
    )
    return new_disp, new_vel, hist, damage_new


def solution(mesh):
    placed = (
        P(None, ("case", "gx"), "gy", "gz"),
        P(None, ("case", "gx"), "gy", "gz"),
        P(("case", "gx"), "gy", "gz"),
        P(("case", "gx"), "gy", "gz"),
        P(("case", "gx"), "gy", "gz"),
        P(("case", "gx"), "gy", "gz"),
        P(("case", "gx"), "gy", "gz"),
        P(),
        P("case"),
    )
    return jax.shard_map(
        per_device,
        mesh=mesh,
        in_specs=placed,
        out_specs=(
            P(None, ("case", "gx"), "gy", "gz"),
            P(None, ("case", "gx"), "gy", "gz"),
            P(("case", "gx"), "gy", "gz"),
            P(("case", "gx"), "gy", "gz"),
        ),
        check_vma=False,
    )
```

```python
import functools
import jax
import jax.numpy as jnp
from jax import lax
from jax.experimental import pallas as pl
from jax.experimental.pallas import tpu as pltpu
from jax.sharding import PartitionSpec as P

TIME_STEP = 0.1
KAPPA_COEF = 0.5
NOTCH_LOAD = 20.0
STIFF_FLOOR = 0.001
ALPHA_LOW, ALPHA_HIGH = 0.5, 6.5
VMEM_BYTES = 28 * 1024 * 1024
CHUNKS = 4
F32 = jnp.float32


def iota2(shape, dim):
    return lax.broadcasted_iota(jnp.int32, shape, dim)


def low_high(odd, got):
    if len(got) == 2:
        return jnp.where(odd, got[0], got[1]), jnp.where(odd, got[1], got[0])
    return jnp.where(odd, got[0], 0.0), jnp.where(odd, 0.0, got[0])


def send(odd, refs, index, low, high):
    refs[0][index] = jnp.where(odd, low, high)
    if len(refs) == 2:
        refs[1][index] = jnp.where(odd, high, low)


def send_early(odd, refs, index, plane, is_low):
    def store(ref):
        ref[index] = plane

    at_odd, at_even = (0, 1) if is_low else (1, 0)
    pl.when(odd)(functools.partial(store, refs[at_odd]))
    pl.when(jnp.logical_not(odd))(functools.partial(store, refs[at_even]))


def shift_x(ref, lead, x, at, block, steps, faces):
    count = ref.shape[-3]
    lo, hi = faces
    if at > 0:
        lower = ref[(*lead, x - 1)]
    else:
        lower = jnp.where(x == 0, lo(), ref[(*lead, jnp.maximum(x - 1, 0))])
    if at < block - 1:
        upper = ref[(*lead, x + 1)]
    else:
        upper = jnp.where(x == count - 1, hi(), ref[(*lead, jnp.minimum(x + 1, count - 1))])
    return upper, lower


def shift_y(plane, rows):
    lo, hi = rows
    at = iota2(plane.shape, 0)
    last = plane.shape[0] - 1
    upper = jnp.where(at == last, hi, pltpu.roll(plane, last, 0))
    lower = jnp.where(at == 0, lo, pltpu.roll(plane, 1, 0))
    return upper, lower


def shift_z(plane, column, first_z):
    at = iota2(plane.shape, 1)
    last = plane.shape[1] - 1
    lo = jnp.where(first_z, 0.0, column)
    hi = jnp.where(first_z, column, 0.0)
    upper = jnp.where(at == last, hi, pltpu.roll(plane, last, 1))
    lower = jnp.where(at == 0, lo, pltpu.roll(plane, 1, 1))
    return upper, lower


def send_columns(ref, x, planes, gz):
    depth = planes[0].shape[1]
    lanes = iota2((planes[0].shape[0], 128), 1)
    tile = None
    for field, plane in enumerate(planes):
        part = jnp.where(gz == 0, plane[:, depth - 128 :], plane[:, :128])
        part = pltpu.roll(part, field + 1 - gz, 1)
        tile = part if tile is None else jnp.where(lanes == field, part, tile)
    ref[x] = tile


def folded(values):
    total = None
    for start in range(0, values.shape[1], 128):
        part = values[:, start : start + 128]
        total = part if total is None else total + part
    out = None
    for start in range(0, values.shape[0], 8):
        part = total[start : start + 8]
        out = part if out is None else out + part
    return out


def by_label(labels, scalars):
    picked = scalars[0]
    for region in range(1, len(scalars)):
        picked = jnp.where(labels == region, scalars[region], picked)
    return picked


def unrolled(count, many, body, carry):
    def several(block, carry):
        for at in range(many):
            carry = body(block * many + at, carry)
        return carry

    return lax.fori_loop(0, count // many, several, carry)


def pack_kernel(n_y, pos, disp_hbm, damage_hbm, *refs):
    disp, damage, *rest = refs
    xs, ys, zs, sems = rest[:2], rest[2 : 2 + n_y], rest[2 + n_y], rest[-1]
    odd_x, odd_y, gz = pos[0] == 1, pos[1] == 1, pos[2]
    count = damage.shape[0]
    block = count // CHUNKS
    copies = []
    for chunk in range(CHUNKS):
        part = pl.ds(chunk * block, block)
        for which, (src, dst) in enumerate(
            (
                (disp_hbm.at[:, part], disp.at[:, part]),
                (damage_hbm.at[part], damage.at[part]),
            )
        ):
            copy = pltpu.make_async_copy(src, dst, sems.at[chunk, which])
            copy.start()
            copies.append(copy)
    for chunk in range(CHUNKS):
        copies[2 * chunk].wait()
        copies[2 * chunk + 1].wait()
        for x in range(chunk * block, (chunk + 1) * block):
            planes = [disp[0, x], disp[1, x], disp[2, x], damage[x]]
            for field, plane in enumerate(planes):
                last = plane.shape[0] - 1
                send(
                    odd_y,
                    ys,
                    (field, pl.ds(x, 1), slice(None)),
                    plane[0:1],
                    plane[last : last + 1],
                )
            send_columns(zs, x, planes, gz)
    for field, src in enumerate((disp.at[0], disp.at[1], disp.at[2], damage)):
        send(odd_x, xs, field, src[0], src[count - 1])


def row_tile(v, rd, is_high):
    rows = v.shape[0]
    part = slice(rows - 8, rows) if is_high else slice(0, 8)
    at = iota2((8, v.shape[1]), 0)
    keep = at >= 4 if is_high else at < 4
    return jnp.where(keep, v[part], pltpu.roll(rd[part], 4, 0))


def local_kernel(n_y, pos, table, disp, damage, history, notch, labels, *refs):
    xg, yg, zg = refs[:2], refs[2 : 2 + n_y], refs[2 + n_y]
    refs = refs[3 + n_y :]
    hist_out, rd_out, v_out, stress_out, mom_out = refs[:5]
    refs = refs[5:]
    xs, ys, ds, zs, held = refs[:2], refs[2 : 2 + n_y], refs[2 + n_y : 2 + 3 * n_y], refs[-2], refs[-1]
    odd_x, odd_y, gz = pos[0] == 1, pos[1] == 1, pos[2]
    step, steps = pl.program_id(0), pl.num_programs(0)
    count = damage.shape[0]
    block = hist_out.shape[0]
    tall = count // 8
    regions = table.shape[1]
    lames = [table[0, r] for r in range(regions)]
    shears = [table[1, r] for r in range(regions)]
    fractures = [table[3, r] for r in range(regions)]

    def around(ref, lead, field, plane, x, at):
        faces = (
            lambda: jnp.where(odd_x, xg[0][field], xg[1][field]),
            lambda: jnp.where(odd_x, xg[1][field], xg[0][field]),
        )
        rows = low_high(odd_y, [y[field, pl.ds(x, 1), :] for y in yg])
        column = zg[x][:, field : field + 1]
        return (
            shift_x(ref, lead, x, at, block, steps, faces),
            shift_y(plane, rows),
            shift_z(plane, column, gz == 0),
        )

    total = jnp.where(step == 0, 0.0, held[...])
    for at in range(block):
        x = step * block + at
        g = []
        for c in range(3):
            pairs = around(disp, (c,), c, disp[c, x], x, at)
            g.append([0.5 * (upper - lower) for upper, lower in pairs])
        lab = labels[x]
        lame = by_label(lab, lames)
        shear = by_label(lab, shears)
        fracture = by_label(lab, fractures)
        dmg = damage[x]
        degrade = (1.0 - dmg) * (1.0 - dmg) + STIFF_FLOOR
        trace = g[0][0] + g[1][1] + g[2][2]
        strain = [
            g[0][0],
            g[1][1],
            g[2][2],
            0.5 * (g[0][1] + g[1][0]),
            0.5 * (g[0][2] + g[2][0]),
            0.5 * (g[1][2] + g[2][1]),
        ]
        positive = jnp.maximum(trace, 0.0)
        squares = strain[0] * strain[0] + strain[1] * strain[1] + strain[2] * strain[2]
        squares = squares + 2.0 * (
            strain[3] * strain[3] + strain[4] * strain[4] + strain[5] * strain[5]
        )
        energy = 0.5 * lame * positive * positive + shear * squares
        scale = degrade * (2.0 * shear)
        base = degrade * (lame * trace)
        stress = [base + scale * strain[k] if k < 3 else scale * strain[k] for k in range(6)]
        for k in range(6):
            stress_out[k, x] = stress[k]
        hist = jnp.maximum(
            jnp.maximum(history[x], energy), NOTCH_LOAD * notch[x].astype(F32)
        )
        hist_out[at] = hist
        diagonal = fracture + 2.0 * hist + 6.0 * KAPPA_COEF
        rd = 1.0 / diagonal
        rd_out[x] = rd
        (xu, xl), (yu, yl), (zu, zl) = around(damage, (), 3, dmg, x, at)
        near = ((xu + xl) + (yu + yl)) + (zu + zl)
        residual = 2.0 * hist - (diagonal * dmg - KAPPA_COEF * near)
        v = residual * rd
        v_out[x] = v
        total = total + folded(residual * v)
        send(odd_y, ys, x, row_tile(v, rd, False), row_tile(v, rd, True))
        for c, k in enumerate((3, 1, 5)):
            last = v.shape[0] - 1
            spot = (count + c * tall + lax.div(x, 8), pl.ds(lax.rem(x, 8), 1), slice(None))
            send(odd_y, ys, spot, stress[k][0:1], stress[k][last : last + 1])
        send_columns(zs, x, [stress[4], stress[5], stress[2]], gz)
    held[...] = total

    def x_fields(depth, x):
        out = [(depth - 1, v_out[x])]
        if depth <= 2:
            out.append((2 + depth, rd_out[x]))
        if depth == 1:
            out += [(5, stress_out[0, x]), (6, stress_out[3, x]), (7, stress_out[4, x])]
        return out

    @pl.when(step == 0)
    def _():
        for depth in (1, 2, 3):
            for slot, plane in x_fields(depth, depth - 1):
                send_early(odd_x, xs, slot, plane, True)
        for which in range(n_y):
            for depth in (1, 2):
                tile = ys[which][depth - 1]
                send_early(odd_x, (ds[which], ds[n_y + which]), depth - 1, tile, True)

    @pl.when(step == steps - 1)
    def _():
        for depth in (1, 2, 3):
            for slot, plane in x_fields(depth, count - depth):
                send_early(odd_x, xs, slot, plane, False)
        for which in range(n_y):
            for depth in (1, 2):
                tile = ys[which][count - depth]
                send_early(odd_x, (ds[which], ds[n_y + which]), depth - 1, tile, False)
        mom_out[...] = jnp.zeros((8, 128), F32)
        mom_out[0:1, :] = jnp.sum(total, axis=0, keepdims=True)


class Enlarged:
    def __init__(self, n_y, pos, v, rd, refs):
        self.odd_x, self.odd_y = pos[0] == 1, pos[1] == 1
        self.v, self.rd, self.n_y = v, rd, n_y
        self.xg, self.yg, self.dg = refs[:2], refs[2 : 2 + n_y], refs[2 + n_y : 2 + 3 * n_y]

    def rows(self, tiles):
        at = iota2(tiles[0].shape, 0)
        if self.n_y == 1:
            keep = lax.shift_right_logical(at, 2) == self.odd_y.astype(jnp.int32)
            tile = tiles[0]
            return jnp.where(keep, tile, 0.0), jnp.where(keep, pltpu.roll(tile, 4, 0), 0.0)
        lo, hi = low_high(self.odd_y, tiles)
        tile = jnp.where(at >= 4, lo, hi)
        moved = jnp.where(at >= 4, pltpu.roll(lo, 4, 0), pltpu.roll(hi, 4, 0))
        return tile, moved

    def own(self, x):
        v_rows, rd_rows = self.rows([y[x] for y in self.yg])
        return self.v[x], v_rows, self.rd[x], rd_rows

    def halo(self, is_low, depth):
        first, second = (0, 1) if is_low else (1, 0)

        def of(a, b):
            return jnp.where(self.odd_x, (a, b)[first], (a, b)[second])

        v = of(self.xg[0][depth - 1], self.xg[1][depth - 1])
        nothing = jnp.zeros((8, v.shape[1]), F32)
        if depth > 2:
            return v, nothing, jnp.zeros_like(v), nothing
        rd = of(self.xg[0][2 + depth], self.xg[1][2 + depth])
        tiles = [
            of(self.dg[w][depth - 1], self.dg[self.n_y + w][depth - 1]) for w in range(self.n_y)
        ]
        v_rows, rd_rows = self.rows(tiles)
        return v, v_rows, rd, rd_rows

    def outer(self, count):
        for depth in (1, 2, 3):
            yield -depth, self.halo(True, depth)
            yield count - 1 + depth, self.halo(False, depth)


def join_kernel(n_y, pos, v, rd, *refs):
    big = Enlarged(n_y, pos, v, rd, refs[:-1])
    out = refs[-1]
    first_z = pos[2] == 0
    count, ny, depth = v.shape

    def tile(v_part, rd_part):
        lanes = iota2((v_part.shape[0], 128), 1)
        keep = lax.shift_right_logical(lanes, 6) == 1 - pos[2]
        mine = jnp.where(first_z, v_part[:, depth - 128 :], v_part[:, :128])
        moved = jnp.where(first_z, rd_part[:, depth - 128 :], rd_part[:, :128])
        return jnp.where(keep, mine, pltpu.roll(moved, 64, 1))

    def put(p, parts):
        v_own, v_rows, rd_own, rd_rows = parts
        out[p + 3, 0:ny] = tile(v_own, rd_own)
        out[p + 3, ny : ny + 8] = tile(v_rows, rd_rows)

    for p, parts in big.outer(count):
        put(p, parts)

    def body(x, carry):
        put(x, big.own(x))
        return carry

    unrolled(count, 4, body, 0)


def krylov_kernel(n_y, pos, v, rd, mom, token, z_got, *refs):
    n_got = 2 + 3 * n_y
    big = Enlarged(n_y, pos, v, rd, refs[:n_got])
    v1_out, v2_out, spread, big_v, big_rd, big_v1, big_v2 = refs[n_got:]
    count, ny, nz = v.shape

    def put(p, parts):
        v_own, v_rows, rd_own, rd_rows = parts
        tile = z_got[p + 3]
        keep = lax.shift_right_logical(iota2(tile.shape, 1), 6) == pos[2]
        big_v[p + 3, 0:ny, 0:nz] = v_own
        big_v[p + 3, ny : ny + 8, 0:nz] = v_rows
        big_v[p + 3, :, nz : nz + 128] = jnp.where(keep, tile, 0.0)
        big_rd[p + 3, 0:ny, 0:nz] = rd_own
        big_rd[p + 3, ny : ny + 8, 0:nz] = rd_rows
        big_rd[p + 3, :, nz : nz + 128] = jnp.where(keep, pltpu.roll(tile, 64, 1), 0.0)

    for p, parts in big.outer(count):
        put(p, parts)

    def fill(x, carry):
        put(x, big.own(x))
        return carry

    unrolled(count, 4, fill, 0)

    def image_of(ref, at):
        plane = ref[at]
        rows, lanes = plane.shape
        near = (ref[at - 1] + ref[at + 1]) + (pltpu.roll(plane, 1, 0) + pltpu.roll(plane, rows - 1, 0))
        near = near + (pltpu.roll(plane, 1, 1) + pltpu.roll(plane, lanes - 1, 1))
        return plane, KAPPA_COEF * near

    def inside(values):
        return folded(values[0:ny, 0:nz])

    def first(x, totals):
        plane, image = image_of(big_v, x + 3)
        made = image * big_rd[x + 3]
        big_v1[x + 2] = made
        v1_out[x] = made[0:ny, 0:nz]
        return totals[0] + inside(plane * image), totals[1] + inside(made * image)

    def second(x, totals):
        plane, image = image_of(big_v1, x + 2)
        made = image * big_rd[x + 3]
        big_v2[x + 1] = made
        v2_out[x] = made[0:ny, 0:nz]
        return totals[0] + inside(plane * image), totals[1] + inside(made * image)

    def third(x, total):
        plane, image = image_of(big_v2, x + 1)
        return total + inside(plane * image)

    zero = jnp.zeros((8, 128), F32)
    for p in (-2, -1, count, count + 1):
        big_v1[p + 2] = image_of(big_v, p + 3)[1] * big_rd[p + 3]
    k1, k2 = unrolled(count, 4, first, (zero, zero))
    for p in (-1, count):
        big_v2[p + 1] = image_of(big_v1, p + 2)[1] * big_rd[p + 3]
    k3, k4 = unrolled(count, 4, second, (zero, zero))
    k5 = unrolled(count, 4, third, zero)
    rows = iota2((8, 128), 0)
    result = mom[...]
    for at, total in enumerate((k1, k2, k3, k4, k5)):
        result = jnp.where(rows == at + 1, jnp.sum(total, axis=0, keepdims=True), result)
    for peer in range(spread.shape[0]):
        spread[peer] = result


def force_kernel(n_y, pos, table, impact, disp, vel, contact, labels, stress, *refs):
    xg, yg, zg = refs[:2], refs[2 : 2 + n_y], refs[2 + n_y]
    disp_out, vel_out, token = refs[3 + n_y :]
    token[...] = jnp.zeros((8, 128), F32)
    odd_x, odd_y, gz = pos[0] == 1, pos[1] == 1, pos[2]
    step, steps, block = pl.program_id(0), pl.num_programs(0), contact.shape[0]
    count = stress.shape[1]
    tall = count // 8
    rates = [table[2, r] for r in range(table.shape[1])]
    for at in range(block):
        x = step * block + at
        loaded = contact[at].astype(F32)
        rate = TIME_STEP / by_label(labels[at], rates)
        for c, (kx, ky, kz) in enumerate(((0, 3, 4), (3, 1, 5), (4, 5, 2))):
            faces = (
                lambda: jnp.where(odd_x, xg[0][5 + c], xg[1][5 + c]),
                lambda: jnp.where(odd_x, xg[1][5 + c], xg[0][5 + c]),
            )
            spot = (count + c * tall + lax.div(x, 8), pl.ds(lax.rem(x, 8), 1), slice(None))
            rows = low_high(odd_y, [y[spot] for y in yg])
            xu, xl = shift_x(stress, (kx,), x, at, block, steps, faces)
            yu, yl = shift_y(stress[ky, x], rows)
            zu, zl = shift_z(stress[kz, x], zg[x][:, c : c + 1], gz == 0)
            force = 0.5 * (((xu - xl) + (yu - yl)) + (zu - zl))
            speed = vel[c, at] + rate * (force + loaded * impact[c])
            vel_out[c, at] = speed
            disp_out[c, at] = disp[c, at] + TIME_STEP * speed


def cg_coefficients(k):
    zero, one = jnp.zeros_like(k[0]), jnp.ones_like(k[0])
    z, p, out = [one], [one], [zero, zero, zero]

    def form(a, b, moments):
        total = None
        for i, ai in enumerate(a):
            for j, bj in enumerate(b):
                term = ai * bj * moments[i + j]
                total = term if total is None else total + term
        return total

    energy = [k[j] - k[j + 1] for j in range(5)]
    rz = k[0]
    for step in range(3):
        alpha = jnp.clip(rz / form(p, p, energy), ALPHA_LOW, ALPHA_HIGH)
        out = [o + alpha * (p[i] if i < len(p) else zero) for i, o in enumerate(out)]
        if step == 2:
            break
        image = [(p[i] if i < len(p) else zero) - (p[i - 1] if i else zero) for i in range(len(p) + 1)]
        z = [(z[i] if i < len(z) else zero) - alpha * image[i] for i in range(len(image))]
        new = jnp.maximum(form(z, z, k), 0.0)
        beta = new / rz
        p = [z[i] + beta * (p[i] if i < len(p) else zero) for i in range(len(z))]
        rz = new
    return out


def final_kernel(mom, v0, v1, v2, damage_hbm, out_hbm, damage, out, in_sems, out_sems):
    count = v0.shape[0]
    block = count // CHUNKS
    loads, stores = [], []
    for chunk in range(CHUNKS):
        part = pl.ds(chunk * block, block)
        loads.append(pltpu.make_async_copy(damage_hbm.at[part], damage.at[part], in_sems.at[chunk]))
        stores.append(pltpu.make_async_copy(out.at[part], out_hbm.at[part], out_sems.at[chunk]))
        loads[-1].start()
    sums = jnp.sum(jnp.sum(mom[...], axis=0), axis=1, keepdims=True)
    c0, c1, c2 = cg_coefficients([sums[j : j + 1, :] for j in range(6)])
    for chunk in range(CHUNKS):
        loads[chunk].wait()
        for x in range(chunk * block, (chunk + 1) * block):
            dmg = damage[x]
            out[x] = jnp.maximum(dmg + (c0 * v0[x] + c1 * v1[x] + c2 * v2[x]), dmg)
        stores[chunk].start()
    for store in stores:
        store.wait()


def pairs_of(axis):
    count = lax.axis_size(axis)
    out = [[(i, i + 1) for i in range(start, count - 1, 2)] for start in (0, 1)]
    return [pairs for pairs in out if pairs]


def swap(array, axis, pairs):
    return lax.ppermute(array, axis, pairs + [(b, a) for a, b in pairs])


def swap_along(axis, arrays):
    return [swap(a, axis, pairs) for a, pairs in zip(arrays, pairs_of(axis), strict=True)]


def swap_diagonal(arrays):
    columns = lax.axis_size("gy")
    out = []
    both = [(xp, yp) for xp in pairs_of("gx") for yp in pairs_of("gy")]
    for array, (x_pairs, y_pairs) in zip(arrays, both, strict=True):
        joint = []
        for a, b in x_pairs:
            for c, d in y_pairs:
                joint.append((a * columns + c, b * columns + d))
                joint.append((a * columns + d, b * columns + c))
        out.append(swap(array, ("gx", "gy"), joint))
    return out


def spec_of(kind, a):
    if kind == "s":
        return pl.BlockSpec(memory_space=pltpu.SMEM)
    if kind == "v":
        return pl.BlockSpec(memory_space=pltpu.VMEM)
    if kind == "h":
        return pl.BlockSpec(memory_space=pltpu.HBM)
    if kind == "a":
        return pl.BlockSpec(memory_space=pl.ANY)
    lead = len(a.shape) - 3
    block = (*a.shape[:lead], a.shape[lead] // CHUNKS, *a.shape[lead + 1 :])
    return pl.BlockSpec(block, lambda i: (*(0,) * lead, i, 0, 0))


def call(kernel, kinds, ins, out_kinds, outs, flops, scratch=()):
    moved = sum(4 * a.size for a in (*ins, *outs))
    grid = (CHUNKS,) if "b" in (*kinds, *out_kinds) else ()
    return pl.pallas_call(
        kernel,
        out_shape=outs,
        grid=grid,
        in_specs=[spec_of(k, a) for k, a in zip(kinds, ins, strict=True)],
        out_specs=[spec_of(k, a) for k, a in zip(out_kinds, outs, strict=True)],
        scratch_shapes=scratch,
        compiler_params=pltpu.CompilerParams(vmem_limit_bytes=VMEM_BYTES),
        cost_estimate=pl.CostEstimate(flops=flops, bytes_accessed=moved, transcendentals=0),
    )(*ins)


def per_device(displacement, velocity, damage, history, contact, notch, labels, table, impact):
    nx, ny, nz = damage.shape
    size = damage.size
    n_y = len(pairs_of("gy"))
    pos = jnp.stack(
        [lax.axis_index("gx") % 2, lax.axis_index("gy") % 2, lax.axis_index("gz")]
    ).astype(jnp.int32)

    def arr(*shape):
        return jax.ShapeDtypeStruct(shape, F32)

    field, fields3, small = arr(nx, ny, nz), arr(3, nx, ny, nz), arr(8, 128)
    columns = arr(nx, ny, 128)
    z_pairs = [(0, 1)]

    disp_here, damage_here, *sent = call(
        functools.partial(pack_kernel, n_y),
        "shh",
        (pos, displacement, damage),
        "vv" + "v" * (3 + n_y),
        [fields3, field, *[arr(4, ny, nz)] * 2, *[arr(4, nx, nz)] * n_y, columns],
        size,
        [pltpu.SemaphoreType.DMA((CHUNKS, 2))],
    )
    got = [
        *swap_along("gx", sent[:2]),
        *swap_along("gy", sent[2 : 2 + n_y]),
        swap(sent[-1], "gz", z_pairs),
    ]
    n_sent = 3 + 3 * n_y
    hist, rd, v0, stress, mom, *sent = call(
        functools.partial(local_kernel, n_y),
        "ssvvvvv" + "v" * (3 + n_y),
        (pos, table, disp_here, damage_here, history, notch, labels, *got),
        "bvvvv" + "v" * n_sent,
        [
            field,
            field,
            field,
            arr(6, nx, ny, nz),
            small,
            *[arr(8, ny, nz)] * 2,
            *[arr(nx + 3 * (nx // 8), 8, nz)] * n_y,
            *[arr(2, 8, nz)] * (2 * n_y),
            columns,
        ],
        150 * size,
        [pltpu.VMEM((8, 128), F32)],
    )
    xy = [
        *swap_along("gx", sent[:2]),
        *swap_along("gy", sent[2 : 2 + n_y]),
        *swap_diagonal(sent[2 + n_y : 2 + 3 * n_y]),
    ]
    stress_z = swap(sent[-1], "gz", z_pairs)
    (joined,) = call(
        functools.partial(join_kernel, n_y),
        "svv" + "v" * len(xy),
        (pos, v0, rd, *xy),
        "v",
        [arr(nx + 6, ny + 8, 128)],
        4 * size,
    )
    z_got = swap(joined, "gz", z_pairs)
    new_disp, new_vel, token = call(
        functools.partial(force_kernel, n_y),
        "sssbbbbv" + "v" * (3 + n_y),
        (
            pos,
            table,
            impact,
            displacement,
            velocity,
            contact,
            labels,
            stress,
            *xy[: 2 + n_y],
            stress_z,
        ),
        "bbv",
        [fields3, fields3, small],
        60 * size,
    )
    peers = lax.axis_size("gx") * lax.axis_size("gy") * lax.axis_size("gz")
    v1, v2, spread = call(
        functools.partial(krylov_kernel, n_y),
        "svvvav" + "v" * len(xy),
        (pos, v0, rd, mom, token, z_got, *xy),
        "vvv",
        [field, field, arr(peers, 8, 128)],
        60 * size,
        [
            pltpu.VMEM((nx + 6, ny + 8, nz + 128), F32),
            pltpu.VMEM((nx + 6, ny + 8, nz + 128), F32),
            pltpu.VMEM((nx + 4, ny + 8, nz + 128), F32),
            pltpu.VMEM((nx + 2, ny + 8, nz + 128), F32),
        ],
    )
    mom = lax.all_to_all(spread, ("gx", "gy", "gz"), 0, 0, tiled=True)
    (damage_new,) = call(
        final_kernel,
        "vvvvh",
        (mom, v0, v1, v2, damage),
        "h",
        [field],
        8 * size,
        [
            pltpu.VMEM((nx, ny, nz), F32),
            pltpu.VMEM((nx, ny, nz), F32),
            pltpu.SemaphoreType.DMA((CHUNKS,)),
            pltpu.SemaphoreType.DMA((CHUNKS,)),
        ],
    )
    return new_disp, new_vel, hist, damage_new


def solution(mesh):
    placed = (
        P(None, ("case", "gx"), "gy", "gz"),
        P(None, ("case", "gx"), "gy", "gz"),
        P(("case", "gx"), "gy", "gz"),
        P(("case", "gx"), "gy", "gz"),
        P(("case", "gx"), "gy", "gz"),
        P(("case", "gx"), "gy", "gz"),
        P(("case", "gx"), "gy", "gz"),
        P(),
        P("case"),
    )
    return jax.shard_map(
        per_device,
        mesh=mesh,
        in_specs=placed,
        out_specs=(
            P(None, ("case", "gx"), "gy", "gz"),
            P(None, ("case", "gx"), "gy", "gz"),
            P(("case", "gx"), "gy", "gz"),
            P(("case", "gx"), "gy", "gz"),
        ),
        check_vma=False,
    )
```

```python
import functools
import jax
import jax.numpy as jnp
from jax import lax
from jax.experimental import pallas as pl
from jax.experimental.pallas import tpu as pltpu
from jax.sharding import PartitionSpec as P

TIME_STEP = 0.1
KAPPA_COEF = 0.5
NOTCH_LOAD = 20.0
STIFF_FLOOR = 0.001
ALPHA_LOW, ALPHA_HIGH = 0.5, 6.5
VMEM_BYTES = 28 * 1024 * 1024
MOST_VMEM_BYTES = 60 * 1024 * 1024
CHUNKS = 4
F32 = jnp.float32


def iota2(shape, dim):
    return lax.broadcasted_iota(jnp.int32, shape, dim)


def low_high(odd, got):
    if len(got) == 2:
        return jnp.where(odd, got[0], got[1]), jnp.where(odd, got[1], got[0])
    return jnp.where(odd, got[0], 0.0), jnp.where(odd, 0.0, got[0])


def send(odd, refs, index, low, high):
    refs[0][index] = jnp.where(odd, low, high)
    if len(refs) == 2:
        refs[1][index] = jnp.where(odd, high, low)


def shift_x(ref, lead, x, at, block, faces):
    count = ref.shape[-3]
    lo, hi = faces
    if at > 0:
        lower = ref[(*lead, x - 1)]
    else:
        lower = jnp.where(x == 0, lo(), ref[(*lead, jnp.maximum(x - 1, 0))])
    if at < block - 1:
        upper = ref[(*lead, x + 1)]
    else:
        upper = jnp.where(x == count - 1, hi(), ref[(*lead, jnp.minimum(x + 1, count - 1))])
    return upper, lower


def shift_y(plane, rows):
    lo, hi = rows
    at = iota2(plane.shape, 0)
    last = plane.shape[0] - 1
    upper = jnp.where(at == last, hi, pltpu.roll(plane, last, 0))
    lower = jnp.where(at == 0, lo, pltpu.roll(plane, 1, 0))
    return upper, lower


def shift_z(plane, column, first_z):
    at = iota2(plane.shape, 1)
    last = plane.shape[1] - 1
    lo = jnp.where(first_z, 0.0, column)
    hi = jnp.where(first_z, column, 0.0)
    upper = jnp.where(at == last, hi, pltpu.roll(plane, last, 1))
    lower = jnp.where(at == 0, lo, pltpu.roll(plane, 1, 1))
    return upper, lower


def send_columns(ref, x, planes, gz):
    depth = planes[0].shape[1]
    lanes = iota2((planes[0].shape[0], 128), 1)
    tile = None
    for field, plane in enumerate(planes):
        part = jnp.where(gz == 0, plane[:, depth - 128 :], plane[:, :128])
        part = pltpu.roll(part, field + 1 - gz, 1)
        tile = part if tile is None else jnp.where(lanes == field, part, tile)
    ref[x] = tile


def folded(values):
    total = None
    for start in range(0, values.shape[1], 128):
        part = values[:, start : start + 128]
        total = part if total is None else total + part
    out = None
    for start in range(0, values.shape[0], 8):
        part = total[start : start + 8]
        out = part if out is None else out + part
    return out


def by_label(labels, scalars):
    picked = scalars[0]
    for region in range(1, len(scalars)):
        picked = jnp.where(labels == region, scalars[region], picked)
    return picked


def unrolled(count, many, body, carry):
    def several(block, carry):
        for at in range(many):
            carry = body(block * many + at, carry)
        return carry

    return lax.fori_loop(0, count // many, several, carry)


def pack_kernel(n_y, pos, disp_hbm, damage_hbm, *refs):
    xs, ys, zs = refs[:2], refs[2 : 2 + n_y], refs[2 + n_y]
    disp, damage, sems = refs[3 + n_y :]
    odd_x, odd_y, gz = pos[0] == 1, pos[1] == 1, pos[2]
    count = damage.shape[0]
    block = count // CHUNKS
    copies = []
    for chunk in range(CHUNKS):
        part = pl.ds(chunk * block, block)
        for which, (src, dst) in enumerate(
            (
                (disp_hbm.at[:, part], disp.at[:, part]),
                (damage_hbm.at[part], damage.at[part]),
            )
        ):
            copy = pltpu.make_async_copy(src, dst, sems.at[chunk, which])
            copy.start()
            copies.append(copy)
    for chunk in range(CHUNKS):
        copies[2 * chunk].wait()
        copies[2 * chunk + 1].wait()
        for x in range(chunk * block, (chunk + 1) * block):
            planes = [disp[0, x], disp[1, x], disp[2, x], damage[x]]
            for field, plane in enumerate(planes):
                last = plane.shape[0] - 1
                send(
                    odd_y,
                    ys,
                    (field, pl.ds(x, 1), slice(None)),
                    plane[0:1],
                    plane[last : last + 1],
                )
            send_columns(zs, x, planes, gz)
    for field, src in enumerate((disp.at[0], disp.at[1], disp.at[2], damage)):
        send(odd_x, xs, field, src[0], src[count - 1])


def row_tile(v, rd, is_high):
    rows = v.shape[0]
    part = slice(rows - 8, rows) if is_high else slice(0, 8)
    at = iota2((8, v.shape[1]), 0)
    keep = at >= 4 if is_high else at < 4
    return jnp.where(keep, v[part], pltpu.roll(rd[part], 4, 0))


def local_kernel(n_y, pos, table, disp, damage, history, notch, labels, *refs):
    xg, yg, zg = refs[:2], refs[2 : 2 + n_y], refs[2 + n_y]
    refs = refs[3 + n_y :]
    hist_hbm, rd_out, v_out, stress_out, mom_out = refs[:5]
    refs = refs[5:]
    xs, ys, ds = refs[:2], refs[2 : 2 + n_y], refs[2 + n_y : 2 + 3 * n_y]
    zs, hist_out, sems = refs[2 + 3 * n_y :]
    odd_x, odd_y, gz = pos[0] == 1, pos[1] == 1, pos[2]
    count = damage.shape[0]
    block = count // CHUNKS
    tall = count // 8
    regions = table.shape[1]
    lames = [table[0, r] for r in range(regions)]
    shears = [table[1, r] for r in range(regions)]
    bases = [table[3, r] for r in range(regions)]

    def store(step):
        part = pl.ds(step * block, block)
        return pltpu.make_async_copy(hist_out.at[part], hist_hbm.at[part], sems.at[step])

    def around(ref, lead, field, plane, x, at):
        faces = (
            lambda: jnp.where(odd_x, xg[0][field], xg[1][field]),
            lambda: jnp.where(odd_x, xg[1][field], xg[0][field]),
        )
        rows = low_high(odd_y, [y[field, pl.ds(x, 1), :] for y in yg])
        column = zg[x][:, field : field + 1]
        return (
            shift_x(ref, lead, x, at, block, faces),
            shift_y(plane, rows),
            shift_z(plane, column, gz == 0),
        )

    def body(x, at):
        g = []
        for c in range(3):
            pairs = around(disp, (c,), c, disp[c, x], x, at)
            g.append([upper - lower for upper, lower in pairs])
        lab = labels[x]
        lame = by_label(lab, lames)
        shear = by_label(lab, shears)
        base = by_label(lab, bases)
        dmg = damage[x]
        degrade = 4.0 * ((1.0 - dmg) * (1.0 - dmg) + STIFF_FLOOR)
        trace = g[0][0] + g[1][1] + g[2][2]
        shears3 = [g[0][1] + g[1][0], g[0][2] + g[2][0], g[1][2] + g[2][1]]
        positive = jnp.maximum(trace, 0.0)
        squares = g[0][0] * g[0][0] + g[1][1] * g[1][1] + g[2][2] * g[2][2]
        squares = (squares + squares) + (
            shears3[0] * shears3[0] + shears3[1] * shears3[1] + shears3[2] * shears3[2]
        )
        energy = lame * positive * positive + shear * squares
        half = degrade * shear
        whole = half + half
        level = (degrade * lame) * trace
        stress = [level + whole * g[k][k] for k in range(3)] + [half * e for e in shears3]
        for k in range(6):
            stress_out[k, x] = stress[k]
        hist = jnp.maximum(
            jnp.maximum(history[x], energy), NOTCH_LOAD * notch[x].astype(F32)
        )
        hist_out[x] = hist
        diagonal = base + 2.0 * hist
        rd = 1.0 / diagonal
        rd_out[x] = rd
        (xu, xl), (yu, yl), (zu, zl) = around(damage, (), 3, dmg, x, at)
        near = ((xu + xl) + (yu + yl)) + (zu + zl)
        residual = 2.0 * hist - (diagonal * dmg - KAPPA_COEF * near)
        v = residual * rd
        v_out[x] = v
        send(odd_y, ys, x, row_tile(v, rd, False), row_tile(v, rd, True))
        for c, k in enumerate((3, 1, 5)):
            last = v.shape[0] - 1
            spot = (count + c * tall + lax.div(x, 8), pl.ds(lax.rem(x, 8), 1), slice(None))
            send(odd_y, ys, spot, stress[k][0:1], stress[k][last : last + 1])
        send_columns(zs, x, [stress[4], stress[5], stress[2]], gz)
        return folded(residual * v)

    def several(step, total):
        for at in range(block):
            total = total + body(step * block + at, at)
        store(step).start()
        return total

    total = lax.fori_loop(0, CHUNKS, several, jnp.zeros((8, 128), F32))
    for depth in (1, 2, 3):
        low, high = depth - 1, count - depth
        send(odd_x, xs, depth - 1, v_out[low], v_out[high])
        if depth <= 2:
            send(odd_x, xs, 2 + depth, rd_out[low], rd_out[high])
            for which in range(n_y):
                pair = (ds[which], ds[n_y + which])
                send(odd_x, pair, depth - 1, ys[which][low], ys[which][high])
    for slot, k in ((5, 0), (6, 3), (7, 4)):
        send(odd_x, xs, slot, stress_out[k, 0], stress_out[k, count - 1])
    mom_out[...] = jnp.zeros((8, 128), F32)
    mom_out[0:1, :] = jnp.sum(total, axis=0, keepdims=True)
    for step in range(CHUNKS):
        store(step).wait()


class Enlarged:
    def __init__(self, n_y, pos, v, rd, refs):
        self.odd_x, self.odd_y = pos[0] == 1, pos[1] == 1
        self.v, self.rd, self.n_y = v, rd, n_y
        self.xg, self.yg, self.dg = refs[:2], refs[2 : 2 + n_y], refs[2 + n_y : 2 + 3 * n_y]

    def rows(self, tiles):
        at = iota2(tiles[0].shape, 0)
        if self.n_y == 1:
            keep = lax.shift_right_logical(at, 2) == self.odd_y.astype(jnp.int32)
            tile = tiles[0]
            return jnp.where(keep, tile, 0.0), jnp.where(keep, pltpu.roll(tile, 4, 0), 0.0)
        lo, hi = low_high(self.odd_y, tiles)
        tile = jnp.where(at >= 4, lo, hi)
        moved = jnp.where(at >= 4, pltpu.roll(lo, 4, 0), pltpu.roll(hi, 4, 0))
        return tile, moved

    def own(self, x):
        v_rows, rd_rows = self.rows([y[x] for y in self.yg])
        return self.v[x], v_rows, self.rd[x], rd_rows

    def halo(self, is_low, depth):
        first, second = (0, 1) if is_low else (1, 0)

        def of(a, b):
            return jnp.where(self.odd_x, (a, b)[first], (a, b)[second])

        v = of(self.xg[0][depth - 1], self.xg[1][depth - 1])
        nothing = jnp.zeros((8, v.shape[1]), F32)
        if depth > 2:
            return v, nothing, jnp.zeros_like(v), nothing
        rd = of(self.xg[0][2 + depth], self.xg[1][2 + depth])
        tiles = [
            of(self.dg[w][depth - 1], self.dg[self.n_y + w][depth - 1]) for w in range(self.n_y)
        ]
        v_rows, rd_rows = self.rows(tiles)
        return v, v_rows, rd, rd_rows

    def outer(self, count):
        for depth in (1, 2, 3):
            yield -depth, self.halo(True, depth)
            yield count - 1 + depth, self.halo(False, depth)


def join_kernel(n_y, pos, v, rd, stress_z, *refs):
    big = Enlarged(n_y, pos, v, rd, refs[:-1])
    out = refs[-1]
    first_z = pos[2] == 0
    count, ny, depth = v.shape

    def tile(v_part, rd_part):
        lanes = iota2((v_part.shape[0], 128), 1)
        keep = lax.shift_right_logical(lanes, 6) == 1 - pos[2]
        mine = jnp.where(first_z, v_part[:, depth - 128 :], v_part[:, :128])
        moved = jnp.where(first_z, rd_part[:, depth - 128 :], rd_part[:, :128])
        return jnp.where(keep, mine, pltpu.roll(moved, 64, 1))

    def put(p, parts):
        v_own, v_rows, rd_own, rd_rows = parts
        out[p + 3, 0:ny] = tile(v_own, rd_own)
        out[p + 3, ny : ny + 8] = tile(v_rows, rd_rows)

    for p, parts in big.outer(count):
        put(p, parts)

    def body(x, carry):
        put(x, big.own(x))
        return carry

    unrolled(count, 4, body, 0)


def krylov_kernel(n_y, pos, v, rd, mom, token, z_got, *refs):
    n_got = 2 + 3 * n_y
    big = Enlarged(n_y, pos, v, rd, refs[:n_got])
    v1_out, v2_out, spread, big_v, big_rd, big_v1, big_v2 = refs[n_got:]
    count, ny, nz = v.shape

    def put(p, parts):
        v_own, v_rows, rd_own, rd_rows = parts
        tile = z_got[p + 3]
        keep = lax.shift_right_logical(iota2(tile.shape, 1), 6) == pos[2]
        big_v[p + 3, 0:ny, 0:nz] = v_own
        big_v[p + 3, ny : ny + 8, 0:nz] = v_rows
        big_v[p + 3, :, nz : nz + 128] = jnp.where(keep, tile, 0.0)
        big_rd[p + 3, 0:ny, 0:nz] = rd_own
        big_rd[p + 3, ny : ny + 8, 0:nz] = rd_rows
        big_rd[p + 3, :, nz : nz + 128] = jnp.where(keep, pltpu.roll(tile, 64, 1), 0.0)

    for p, parts in big.outer(count):
        put(p, parts)

    def fill(x, carry):
        put(x, big.own(x))
        return carry

    unrolled(count, 4, fill, 0)

    def image_of(ref, at):
        plane = ref[at]
        rows, lanes = plane.shape
        near = (ref[at - 1] + ref[at + 1]) + (pltpu.roll(plane, 1, 0) + pltpu.roll(plane, rows - 1, 0))
        near = near + (pltpu.roll(plane, 1, 1) + pltpu.roll(plane, lanes - 1, 1))
        return plane, KAPPA_COEF * near

    def inside(values):
        return folded(values[0:ny, 0:nz])

    def first(x, totals):
        plane, image = image_of(big_v, x + 3)
        made = image * big_rd[x + 3]
        big_v1[x + 2] = made
        v1_out[x] = made[0:ny, 0:nz]
        return totals[0] + inside(plane * image), totals[1] + inside(made * image)

    def second(x, totals):
        plane, image = image_of(big_v1, x + 2)
        made = image * big_rd[x + 3]
        big_v2[x + 1] = made
        v2_out[x] = made[0:ny, 0:nz]
        return totals[0] + inside(plane * image), totals[1] + inside(made * image)

    def third(x, total):
        plane, image = image_of(big_v2, x + 1)
        return total + folded(plane[0:ny, 0:nz] * image[0:ny, 0:nz])

    zero = jnp.zeros((8, 128), F32)
    for p in (-2, -1, count, count + 1):
        big_v1[p + 2] = image_of(big_v, p + 3)[1] * big_rd[p + 3]
    k1, k2 = unrolled(count, 4, first, (zero, zero))
    for p in (-1, count):
        big_v2[p + 1] = image_of(big_v1, p + 2)[1] * big_rd[p + 3]
    k3, k4 = unrolled(count, 4, second, (zero, zero))
    k5 = unrolled(count, 4, third, zero)
    rows = iota2((8, 128), 0)
    result = mom[...]
    for at, total in enumerate((k1, k2, k3, k4, k5)):
        result = jnp.where(rows == at + 1, jnp.sum(total, axis=0, keepdims=True), result)
    for peer in range(spread.shape[0]):
        spread[peer] = result


def force_kernel(n_y, pos, table, impact, disp, vel, contact, labels, stress, *refs):
    xg, yg, zg = refs[:2], refs[2 : 2 + n_y], refs[2 + n_y]
    disp_hbm, vel_hbm, token, disp_out, vel_out, sems = refs[3 + n_y :]
    token[...] = jnp.zeros((8, 128), F32)
    odd_x, odd_y, gz = pos[0] == 1, pos[1] == 1, pos[2]
    count = stress.shape[1]
    block = count // CHUNKS
    tall = count // 8
    rates = [table[2, r] for r in range(table.shape[1])]

    def stores(step):
        part = pl.ds(step * block, block)
        return (
            pltpu.make_async_copy(disp_out.at[:, part], disp_hbm.at[:, part], sems.at[step, 0]),
            pltpu.make_async_copy(vel_out.at[:, part], vel_hbm.at[:, part], sems.at[step, 1]),
        )

    def body(x, at):
        loaded = contact[x].astype(F32)
        rate = by_label(labels[x], rates)
        for c, (kx, ky, kz) in enumerate(((0, 3, 4), (3, 1, 5), (4, 5, 2))):
            faces = (
                lambda: jnp.where(odd_x, xg[0][5 + c], xg[1][5 + c]),
                lambda: jnp.where(odd_x, xg[1][5 + c], xg[0][5 + c]),
            )
            spot = (count + c * tall + lax.div(x, 8), pl.ds(lax.rem(x, 8), 1), slice(None))
            rows = low_high(odd_y, [y[spot] for y in yg])
            xu, xl = shift_x(stress, (kx,), x, at, block, faces)
            yu, yl = shift_y(stress[ky, x], rows)
            zu, zl = shift_z(stress[kz, x], zg[x][:, c : c + 1], gz == 0)
            force = 0.5 * (((xu - xl) + (yu - yl)) + (zu - zl))
            speed = vel[c, x] + rate * (force + loaded * impact[c])
            vel_out[c, x] = speed
            disp_out[c, x] = disp[c, x] + TIME_STEP * speed

    def several(step, carry):
        for at in range(block):
            body(step * block + at, at)
        for copy in stores(step):
            copy.start()
        return carry

    lax.fori_loop(0, CHUNKS, several, 0)
    for step in range(CHUNKS):
        for copy in stores(step):
            copy.wait()


def cg_coefficients(k):
    zero, one = jnp.zeros_like(k[0]), jnp.ones_like(k[0])
    z, p, out = [one], [one], [zero, zero, zero]

    def form(a, b, moments):
        total = None
        for i, ai in enumerate(a):
            for j, bj in enumerate(b):
                term = ai * bj * moments[i + j]
                total = term if total is None else total + term
        return total

    energy = [k[j] - k[j + 1] for j in range(5)]
    rz = k[0]
    for step in range(3):
        alpha = jnp.clip(rz / form(p, p, energy), ALPHA_LOW, ALPHA_HIGH)
        out = [o + alpha * (p[i] if i < len(p) else zero) for i, o in enumerate(out)]
        if step == 2:
            break
        image = [(p[i] if i < len(p) else zero) - (p[i - 1] if i else zero) for i in range(len(p) + 1)]
        z = [(z[i] if i < len(z) else zero) - alpha * image[i] for i in range(len(image))]
        new = jnp.maximum(form(z, z, k), 0.0)
        beta = new / rz
        p = [z[i] + beta * (p[i] if i < len(p) else zero) for i in range(len(z))]
        rz = new
    return out


def final_kernel(mom, v0, v1, v2, damage_hbm, out_hbm, damage, out, in_sems, out_sems):
    count = v0.shape[0]
    block = count // CHUNKS
    loads, stores = [], []
    for chunk in range(CHUNKS):
        part = pl.ds(chunk * block, block)
        loads.append(pltpu.make_async_copy(damage_hbm.at[part], damage.at[part], in_sems.at[chunk]))
        stores.append(pltpu.make_async_copy(out.at[part], out_hbm.at[part], out_sems.at[chunk]))
        loads[-1].start()
    sums = jnp.sum(jnp.sum(mom[...], axis=0), axis=1, keepdims=True)
    c0, c1, c2 = cg_coefficients([sums[j : j + 1, :] for j in range(6)])
    for chunk in range(CHUNKS):
        loads[chunk].wait()
        for x in range(chunk * block, (chunk + 1) * block):
            dmg = damage[x]
            out[x] = jnp.maximum(dmg + (c0 * v0[x] + c1 * v1[x] + c2 * v2[x]), dmg)
        stores[chunk].start()
    for store in stores:
        store.wait()


def pairs_of(axis):
    count = lax.axis_size(axis)
    out = [[(i, i + 1) for i in range(start, count - 1, 2)] for start in (0, 1)]
    return [pairs for pairs in out if pairs]


def swap(array, axis, pairs):
    return lax.ppermute(array, axis, pairs + [(b, a) for a, b in pairs])


def swap_along(axis, arrays):
    return [swap(a, axis, pairs) for a, pairs in zip(arrays, pairs_of(axis), strict=True)]


def swap_diagonal(arrays):
    columns = lax.axis_size("gy")
    out = []
    both = [(xp, yp) for xp in pairs_of("gx") for yp in pairs_of("gy")]
    for array, (x_pairs, y_pairs) in zip(arrays, both, strict=True):
        joint = []
        for a, b in x_pairs:
            for c, d in y_pairs:
                joint.append((a * columns + c, b * columns + d))
                joint.append((a * columns + d, b * columns + c))
        out.append(swap(array, ("gx", "gy"), joint))
    return out


def spec_of(kind, a):
    if kind == "s":
        return pl.BlockSpec(memory_space=pltpu.SMEM)
    if kind == "v":
        return pl.BlockSpec(memory_space=pltpu.VMEM)
    if kind == "h":
        return pl.BlockSpec(memory_space=pltpu.HBM)
    if kind == "a":
        return pl.BlockSpec(memory_space=pl.ANY)
    raise ValueError(kind)


def call(kernel, kinds, ins, out_kinds, outs, flops, scratch=(), vmem=VMEM_BYTES):
    moved = sum(4 * a.size for a in (*ins, *outs))
    return pl.pallas_call(
        kernel,
        out_shape=outs,
        in_specs=[spec_of(k, a) for k, a in zip(kinds, ins, strict=True)],
        out_specs=[spec_of(k, a) for k, a in zip(out_kinds, outs, strict=True)],
        scratch_shapes=scratch,
        compiler_params=pltpu.CompilerParams(vmem_limit_bytes=vmem),
        cost_estimate=pl.CostEstimate(flops=flops, bytes_accessed=moved, transcendentals=0),
    )(*ins)


def per_device(displacement, velocity, damage, history, contact, notch, labels, table, impact):
    nx, ny, nz = damage.shape
    size = damage.size
    n_y = len(pairs_of("gy"))
    pos = jnp.stack(
        [lax.axis_index("gx") % 2, lax.axis_index("gy") % 2, lax.axis_index("gz")]
    ).astype(jnp.int32)

    scaled = jnp.stack(
        [table[0] / 8.0, table[1] / 8.0, TIME_STEP / table[2], table[3] + 6.0 * KAPPA_COEF]
    )

    def arr(*shape):
        return jax.ShapeDtypeStruct(shape, F32)

    field, fields3, small = arr(nx, ny, nz), arr(3, nx, ny, nz), arr(8, 128)
    columns = arr(nx, ny, 128)
    z_pairs = [(0, 1)]

    sent = call(
        functools.partial(pack_kernel, n_y),
        "shh",
        (pos, displacement, damage),
        "v" * (3 + n_y),
        [*[arr(4, ny, nz)] * 2, *[arr(4, nx, nz)] * n_y, columns],
        size,
        [
            pltpu.VMEM((3, nx, ny, nz), F32),
            pltpu.VMEM((nx, ny, nz), F32),
            pltpu.SemaphoreType.DMA((CHUNKS, 2)),
        ],
        vmem=MOST_VMEM_BYTES,
    )
    got = [
        *swap_along("gx", sent[:2]),
        *swap_along("gy", sent[2 : 2 + n_y]),
        swap(sent[-1], "gz", z_pairs),
    ]
    n_sent = 3 + 3 * n_y
    hist, rd, v0, stress, mom, *sent = call(
        functools.partial(local_kernel, n_y),
        "ssvvvvv" + "v" * (3 + n_y),
        (pos, scaled, displacement, damage, history, notch, labels, *got),
        "hvvvv" + "v" * n_sent,
        [
            field,
            field,
            field,
            arr(6, nx, ny, nz),
            small,
            *[arr(8, ny, nz)] * 2,
            *[arr(nx + 3 * (nx // 8), 8, nz)] * n_y,
            *[arr(2, 8, nz)] * (2 * n_y),
            columns,
        ],
        150 * size,
        [pltpu.VMEM((nx, ny, nz), F32), pltpu.SemaphoreType.DMA((CHUNKS,))],
    )
    xy = [
        *swap_along("gx", sent[:2]),
        *swap_along("gy", sent[2 : 2 + n_y]),
        *swap_diagonal(sent[2 + n_y : 2 + 3 * n_y]),
    ]
    stress_z = swap(sent[-1], "gz", z_pairs)
    (joined,) = call(
        functools.partial(join_kernel, n_y),
        "svva" + "v" * len(xy),
        (pos, v0, rd, stress_z, *xy),
        "v",
        [arr(nx + 6, ny + 8, 128)],
        4 * size,
    )
    z_got = swap(joined, "gz", z_pairs)
    new_disp, new_vel, token = call(
        functools.partial(force_kernel, n_y),
        "sssvvvvv" + "v" * (3 + n_y),
        (
            pos,
            scaled,
            impact,
            displacement,
            velocity,
            contact,
            labels,
            stress,
            *xy[: 2 + n_y],
            stress_z,
        ),
        "hhv",
        [fields3, fields3, small],
        60 * size,
        [
            pltpu.VMEM((3, nx, ny, nz), F32),
            pltpu.VMEM((3, nx, ny, nz), F32),
            pltpu.SemaphoreType.DMA((CHUNKS, 2)),
        ],
    )
    peers = lax.axis_size("gx") * lax.axis_size("gy") * lax.axis_size("gz")
    v1, v2, spread = call(
        functools.partial(krylov_kernel, n_y),
        "svvvav" + "v" * len(xy),
        (pos, v0, rd, mom, token, z_got, *xy),
        "vvv",
        [field, field, arr(peers, 8, 128)],
        60 * size,
        [
            pltpu.VMEM((nx + 6, ny + 8, nz + 128), F32),
            pltpu.VMEM((nx + 6, ny + 8, nz + 128), F32),
            pltpu.VMEM((nx + 4, ny + 8, nz + 128), F32),
            pltpu.VMEM((nx + 2, ny + 8, nz + 128), F32),
        ],
    )
    mom = lax.all_to_all(spread, ("gx", "gy", "gz"), 0, 0, tiled=True)
    (damage_new,) = call(
        final_kernel,
        "vvvvh",
        (mom, v0, v1, v2, damage),
        "h",
        [field],
        8 * size,
        [
            pltpu.VMEM((nx, ny, nz), F32),
            pltpu.VMEM((nx, ny, nz), F32),
            pltpu.SemaphoreType.DMA((CHUNKS,)),
            pltpu.SemaphoreType.DMA((CHUNKS,)),
        ],
    )
    return new_disp, new_vel, hist, damage_new


def solution(mesh):
    placed = (
        P(None, ("case", "gx"), "gy", "gz"),
        P(None, ("case", "gx"), "gy", "gz"),
        P(("case", "gx"), "gy", "gz"),
        P(("case", "gx"), "gy", "gz"),
        P(("case", "gx"), "gy", "gz"),
        P(("case", "gx"), "gy", "gz"),
        P(("case", "gx"), "gy", "gz"),
        P(),
        P("case"),
    )
    return jax.shard_map(
        per_device,
        mesh=mesh,
        in_specs=placed,
        out_specs=(
            P(None, ("case", "gx"), "gy", "gz"),
            P(None, ("case", "gx"), "gy", "gz"),
            P(("case", "gx"), "gy", "gz"),
            P(("case", "gx"), "gy", "gz"),
        ),
        check_vma=False,
    )
```

```python
import functools
import jax
import jax.numpy as jnp
from jax import lax
from jax.experimental import pallas as pl
from jax.experimental.pallas import tpu as pltpu
from jax.sharding import PartitionSpec as P

TIME_STEP = 0.1
KAPPA_COEF = 0.5
NOTCH_LOAD = 20.0
STIFF_FLOOR = 0.001
ALPHA_LOW, ALPHA_HIGH = 0.5, 6.5
VMEM_BYTES = 28 * 1024 * 1024
STRESS_LANE = 32
CHUNKS = 4
F32 = jnp.float32


def iota2(shape, dim):
    return lax.broadcasted_iota(jnp.int32, shape, dim)


def low_high(odd, got):
    if len(got) == 2:
        return jnp.where(odd, got[0], got[1]), jnp.where(odd, got[1], got[0])
    return jnp.where(odd, got[0], 0.0), jnp.where(odd, 0.0, got[0])


def send(odd, refs, index, low, high):
    refs[0][index] = jnp.where(odd, low, high)
    if len(refs) == 2:
        refs[1][index] = jnp.where(odd, high, low)


def shift_x(ref, lead, x, at, block, faces):
    count = ref.shape[-3]
    lo, hi = faces
    if at > 0:
        lower = ref[(*lead, x - 1)]
    else:
        lower = jnp.where(x == 0, lo(), ref[(*lead, jnp.maximum(x - 1, 0))])
    if at < block - 1:
        upper = ref[(*lead, x + 1)]
    else:
        upper = jnp.where(x == count - 1, hi(), ref[(*lead, jnp.minimum(x + 1, count - 1))])
    return upper, lower


def shift_y(plane, rows):
    lo, hi = rows
    at = iota2(plane.shape, 0)
    last = plane.shape[0] - 1
    upper = jnp.where(at == last, hi, pltpu.roll(plane, last, 0))
    lower = jnp.where(at == 0, lo, pltpu.roll(plane, 1, 0))
    return upper, lower


def shift_z(plane, column, first_z):
    at = iota2(plane.shape, 1)
    last = plane.shape[1] - 1
    lo = jnp.where(first_z, 0.0, column)
    hi = jnp.where(first_z, column, 0.0)
    upper = jnp.where(at == last, hi, pltpu.roll(plane, last, 1))
    lower = jnp.where(at == 0, lo, pltpu.roll(plane, 1, 1))
    return upper, lower


def send_columns(ref, x, planes, gz):
    depth = planes[0].shape[1]
    lanes = iota2((planes[0].shape[0], 128), 1)
    tile = None
    for field, plane in enumerate(planes):
        part = jnp.where(gz == 0, plane[:, depth - 128 :], plane[:, :128])
        part = pltpu.roll(part, field + 1 - gz, 1)
        tile = part if tile is None else jnp.where(lanes == field, part, tile)
    ref[x] = tile


def folded(values):
    total = None
    for start in range(0, values.shape[1], 128):
        part = values[:, start : start + 128]
        total = part if total is None else total + part
    out = None
    for start in range(0, values.shape[0], 8):
        part = total[start : start + 8]
        out = part if out is None else out + part
    return out


def by_label(labels, scalars):
    picked = scalars[0]
    for region in range(1, len(scalars)):
        picked = jnp.where(labels == region, scalars[region], picked)
    return picked


def unrolled(count, many, body, carry):
    def several(block, carry):
        for at in range(many):
            carry = body(block * many + at, carry)
        return carry

    return lax.fori_loop(0, count // many, several, carry)


def pack_kernel(n_y, pos, disp, damage, *refs):
    ys, zs = refs[:n_y], refs[n_y]
    odd_y, gz = pos[1] == 1, pos[2]

    def body(x, carry):
        planes = [disp[0, x], disp[1, x], disp[2, x], damage[x]]
        for field, plane in enumerate(planes):
            last = plane.shape[0] - 1
            spot = (field, pl.ds(x, 1), slice(None))
            send(odd_y, ys, spot, plane[0:1], plane[last : last + 1])
        send_columns(zs, x, planes, gz)
        return carry

    unrolled(damage.shape[0], 8, body, 0)


def row_tile(v, rd, is_high):
    rows = v.shape[0]
    part = slice(rows - 8, rows) if is_high else slice(0, 8)
    at = iota2((8, v.shape[1]), 0)
    keep = at >= 4 if is_high else at < 4
    return jnp.where(keep, v[part], pltpu.roll(rd[part], 4, 0))


def local_kernel(n_y, pos, table, disp, damage, history, notch, labels, *refs):
    xg, yg, zg = refs[:2], refs[2 : 2 + n_y], refs[2 + n_y]
    refs = refs[3 + n_y :]
    hist_hbm, rd_out, v_out, stress_out, mom_out = refs[:5]
    refs = refs[5:]
    xs, ys, ds = refs[:2], refs[2 : 2 + n_y], refs[2 + n_y : 2 + 3 * n_y]
    zs, hist_out, sems = refs[2 + 3 * n_y :]
    odd_x, odd_y, gz = pos[0] == 1, pos[1] == 1, pos[2]
    count = damage.shape[0]
    block = count // CHUNKS
    tall = count // 8
    regions = table.shape[1]
    lames = [table[0, r] for r in range(regions)]
    shears = [table[1, r] for r in range(regions)]
    bases = [table[3, r] for r in range(regions)]

    def store(step):
        part = pl.ds(step * block, block)
        return pltpu.make_async_copy(hist_out.at[part], hist_hbm.at[part], sems.at[step])

    def around(ref, lead, field, plane, x, at):
        faces = (
            lambda: jnp.where(odd_x, xg[0][field], xg[1][field]),
            lambda: jnp.where(odd_x, xg[1][field], xg[0][field]),
        )
        rows = low_high(odd_y, [y[field, pl.ds(x, 1), :] for y in yg])
        column = zg[x][:, field : field + 1]
        return (
            shift_x(ref, lead, x, at, block, faces),
            shift_y(plane, rows),
            shift_z(plane, column, gz == 0),
        )

    def body(x, at):
        g = []
        for c in range(3):
            pairs = around(disp, (c,), c, disp[c, x], x, at)
            g.append([upper - lower for upper, lower in pairs])
        lab = labels[x]
        lame = by_label(lab, lames)
        shear = by_label(lab, shears)
        base = by_label(lab, bases)
        dmg = damage[x]
        degrade = 4.0 * ((1.0 - dmg) * (1.0 - dmg) + STIFF_FLOOR)
        trace = g[0][0] + g[1][1] + g[2][2]
        shears3 = [g[0][1] + g[1][0], g[0][2] + g[2][0], g[1][2] + g[2][1]]
        positive = jnp.maximum(trace, 0.0)
        squares = g[0][0] * g[0][0] + g[1][1] * g[1][1] + g[2][2] * g[2][2]
        squares = (squares + squares) + (
            shears3[0] * shears3[0] + shears3[1] * shears3[1] + shears3[2] * shears3[2]
        )
        energy = lame * positive * positive + shear * squares
        half = degrade * shear
        whole = half + half
        level = (degrade * lame) * trace
        stress = [level + whole * g[k][k] for k in range(3)] + [half * e for e in shears3]
        for k in range(6):
            stress_out[k, x] = stress[k]
        hist = jnp.maximum(
            jnp.maximum(history[x], energy), NOTCH_LOAD * notch[x].astype(F32)
        )
        hist_out[x] = hist
        diagonal = base + 2.0 * hist
        rd = 1.0 / diagonal
        rd_out[x] = rd
        (xu, xl), (yu, yl), (zu, zl) = around(damage, (), 3, dmg, x, at)
        near = ((xu + xl) + (yu + yl)) + (zu + zl)
        residual = 2.0 * hist - (diagonal * dmg - KAPPA_COEF * near)
        v = residual * rd
        v_out[x] = v
        send(odd_y, ys, x, row_tile(v, rd, False), row_tile(v, rd, True))
        for c, k in enumerate((3, 1, 5)):
            last = v.shape[0] - 1
            spot = (count + c * tall + lax.div(x, 8), pl.ds(lax.rem(x, 8), 1), slice(None))
            send(odd_y, ys, spot, stress[k][0:1], stress[k][last : last + 1])
        send_columns(zs, x, [stress[4], stress[5], stress[2]], gz)
        return folded(residual * v)

    def several(step, total):
        for at in range(block):
            total = total + body(step * block + at, at)
        store(step).start()
        return total

    total = lax.fori_loop(0, CHUNKS, several, jnp.zeros((8, 128), F32))
    for depth in (1, 2, 3):
        low, high = depth - 1, count - depth
        send(odd_x, xs, depth - 1, v_out[low], v_out[high])
        if depth <= 2:
            send(odd_x, xs, 2 + depth, rd_out[low], rd_out[high])
            for which in range(n_y):
                pair = (ds[which], ds[n_y + which])
                send(odd_x, pair, depth - 1, ys[which][low], ys[which][high])
    for slot, k in ((5, 0), (6, 3), (7, 4)):
        send(odd_x, xs, slot, stress_out[k, 0], stress_out[k, count - 1])
    mom_out[...] = jnp.zeros((8, 128), F32)
    mom_out[0:1, :] = jnp.sum(total, axis=0, keepdims=True)
    for step in range(CHUNKS):
        store(step).wait()


class Enlarged:
    def __init__(self, n_y, pos, v, rd, refs):
        self.odd_x, self.odd_y = pos[0] == 1, pos[1] == 1
        self.v, self.rd, self.n_y = v, rd, n_y
        self.xg, self.yg, self.dg = refs[:2], refs[2 : 2 + n_y], refs[2 + n_y : 2 + 3 * n_y]

    def rows(self, tiles):
        at = iota2(tiles[0].shape, 0)
        if self.n_y == 1:
            keep = lax.shift_right_logical(at, 2) == self.odd_y.astype(jnp.int32)
            tile = tiles[0]
            return jnp.where(keep, tile, 0.0), jnp.where(keep, pltpu.roll(tile, 4, 0), 0.0)
        lo, hi = low_high(self.odd_y, tiles)
        tile = jnp.where(at >= 4, lo, hi)
        moved = jnp.where(at >= 4, pltpu.roll(lo, 4, 0), pltpu.roll(hi, 4, 0))
        return tile, moved

    def own(self, x):
        v_rows, rd_rows = self.rows([y[x] for y in self.yg])
        return self.v[x], v_rows, self.rd[x], rd_rows

    def halo(self, is_low, depth):
        first, second = (0, 1) if is_low else (1, 0)

        def of(a, b):
            return jnp.where(self.odd_x, (a, b)[first], (a, b)[second])

        v = of(self.xg[0][depth - 1], self.xg[1][depth - 1])
        nothing = jnp.zeros((8, v.shape[1]), F32)
        if depth > 2:
            return v, nothing, jnp.zeros_like(v), nothing
        rd = of(self.xg[0][2 + depth], self.xg[1][2 + depth])
        tiles = [
            of(self.dg[w][depth - 1], self.dg[self.n_y + w][depth - 1]) for w in range(self.n_y)
        ]
        v_rows, rd_rows = self.rows(tiles)
        return v, v_rows, rd, rd_rows

    def outer(self, count):
        for depth in (1, 2, 3):
            yield -depth, self.halo(True, depth)
            yield count - 1 + depth, self.halo(False, depth)


def join_kernel(n_y, pos, v, rd, columns, *refs):
    big = Enlarged(n_y, pos, v, rd, refs[:-1])
    out = refs[-1]
    first_z = pos[2] == 0
    count, ny, depth = v.shape

    def tile(v_part, rd_part):
        lanes = iota2((v_part.shape[0], 128), 1)
        keep = lax.shift_right_logical(lanes, 6) == 1 - pos[2]
        mine = jnp.where(first_z, v_part[:, depth - 128 :], v_part[:, :128])
        moved = jnp.where(first_z, rd_part[:, depth - 128 :], rd_part[:, :128])
        return jnp.where(keep, mine, pltpu.roll(moved, 64, 1))

    def put(p, parts):
        v_own, v_rows, rd_own, rd_rows = parts
        out[p + 3, 0:ny] = tile(v_own, rd_own)
        out[p + 3, ny : ny + 8] = tile(v_rows, rd_rows)

    for p, parts in big.outer(count):
        put(p, parts)

    def body(x, carry):
        put(x, big.own(x))
        lanes = iota2((ny, 128), 1)
        mark = (lanes >= STRESS_LANE) & (lanes < STRESS_LANE + 3)
        moved = pltpu.roll(columns[x], STRESS_LANE, 1)
        out[x + 3, 0:ny] = jnp.where(mark, moved, out[x + 3, 0:ny])
        return carry

    unrolled(count, 4, body, 0)


def fill_kernel(n_y, pos, v, rd, *refs):
    big = Enlarged(n_y, pos, v, rd, refs[:-2])
    big_v, big_rd = refs[-2:]
    count, ny, _ = v.shape

    def put(p, parts):
        v_own, v_rows, rd_own, rd_rows = parts
        big_v[p + 3, 0:ny] = v_own
        big_v[p + 3, ny : ny + 8] = v_rows
        big_rd[p + 3, 0:ny] = rd_own
        big_rd[p + 3, ny : ny + 8] = rd_rows

    for p, parts in big.outer(count):
        put(p, parts)

    def body(x, carry):
        put(x, big.own(x))
        return carry

    unrolled(count, 4, body, 0)


def krylov_kernel(pos, main_v, main_rd, mom, token, z_got, *refs):
    v1_out, v2_out, spread, z_v, z_rd, big_v1, big_v2 = refs
    count, ny, nz = v1_out.shape

    def split(p, carry):
        tile = z_got[p]
        keep = lax.shift_right_logical(iota2(tile.shape, 1), 6) == pos[2]
        z_v[p] = jnp.where(keep, tile, 0.0)
        z_rd[p] = jnp.where(keep, pltpu.roll(tile, 64, 1), 0.0)
        return carry

    unrolled(count + 6, 2, split, 0)

    def v_at(at):
        return jnp.concatenate([main_v[at], z_v[at]], axis=1)

    def rd_at(at):
        return jnp.concatenate([main_rd[at], z_rd[at]], axis=1)

    def image_of(get, at):
        plane = get(at)
        rows, lanes = plane.shape
        near = (get(at - 1) + get(at + 1)) + (pltpu.roll(plane, 1, 0) + pltpu.roll(plane, rows - 1, 0))
        near = near + (pltpu.roll(plane, 1, 1) + pltpu.roll(plane, lanes - 1, 1))
        return plane, KAPPA_COEF * near

    def v1_at(at):
        return big_v1[at]

    def v2_at(at):
        return big_v2[at]

    def inside(values):
        return folded(values[0:ny, 0:nz])

    def first(x, totals):
        plane, image = image_of(v_at, x + 3)
        made = image * rd_at(x + 3)
        big_v1[x + 2] = made
        v1_out[x] = made[0:ny, 0:nz]
        return totals[0] + inside(plane * image), totals[1] + inside(made * image)

    def second(x, totals):
        plane, image = image_of(v1_at, x + 2)
        made = image * rd_at(x + 3)
        big_v2[x + 1] = made
        v2_out[x] = made[0:ny, 0:nz]
        return totals[0] + inside(plane * image), totals[1] + inside(made * image)

    def third(x, total):
        plane, image = image_of(v2_at, x + 1)
        return total + folded(plane[0:ny, 0:nz] * image[0:ny, 0:nz])

    zero = jnp.zeros((8, 128), F32)
    for p in (-2, -1, count, count + 1):
        big_v1[p + 2] = image_of(v_at, p + 3)[1] * rd_at(p + 3)
    k1, k2 = unrolled(count, 4, first, (zero, zero))
    for p in (-1, count):
        big_v2[p + 1] = image_of(v1_at, p + 2)[1] * rd_at(p + 3)
    k3, k4 = unrolled(count, 4, second, (zero, zero))
    k5 = unrolled(count, 4, third, zero)
    rows = iota2((8, 128), 0)
    result = mom[...]
    for at, total in enumerate((k1, k2, k3, k4, k5)):
        result = jnp.where(rows == at + 1, jnp.sum(total, axis=0, keepdims=True), result)
    for peer in range(spread.shape[0]):
        spread[peer] = result


def force_kernel(n_y, pos, table, impact, disp, vel, contact, labels, stress, *refs):
    xg, yg, zg = refs[:2], refs[2 : 2 + n_y], refs[2 + n_y]
    disp_hbm, vel_hbm, token, disp_out, vel_out, sems = refs[3 + n_y :]
    token[...] = jnp.zeros((8, 128), F32)
    odd_x, odd_y, gz = pos[0] == 1, pos[1] == 1, pos[2]
    count = stress.shape[1]
    block = count // CHUNKS
    tall = count // 8
    rates = [table[2, r] for r in range(table.shape[1])]

    def stores(step):
        part = pl.ds(step * block, block)
        return (
            pltpu.make_async_copy(disp_out.at[:, part], disp_hbm.at[:, part], sems.at[step, 0]),
            pltpu.make_async_copy(vel_out.at[:, part], vel_hbm.at[:, part], sems.at[step, 1]),
        )

    def column(x, c):
        lane = STRESS_LANE + c
        return zg[x + 3, 0 : contact.shape[1]][:, lane : lane + 1]

    def body(x, at):
        loaded = contact[x].astype(F32)
        rate = by_label(labels[x], rates)
        for c, (kx, ky, kz) in enumerate(((0, 3, 4), (3, 1, 5), (4, 5, 2))):
            faces = (
                lambda: jnp.where(odd_x, xg[0][5 + c], xg[1][5 + c]),
                lambda: jnp.where(odd_x, xg[1][5 + c], xg[0][5 + c]),
            )
            spot = (count + c * tall + lax.div(x, 8), pl.ds(lax.rem(x, 8), 1), slice(None))
            rows = low_high(odd_y, [y[spot] for y in yg])
            xu, xl = shift_x(stress, (kx,), x, at, block, faces)
            yu, yl = shift_y(stress[ky, x], rows)
            zu, zl = shift_z(stress[kz, x], column(x, c), gz == 0)
            force = 0.5 * (((xu - xl) + (yu - yl)) + (zu - zl))
            speed = vel[c, x] + rate * (force + loaded * impact[c])
            vel_out[c, x] = speed
            disp_out[c, x] = disp[c, x] + TIME_STEP * speed

    def several(step, carry):
        for at in range(block):
            body(step * block + at, at)
        for copy in stores(step):
            copy.start()
        return carry

    lax.fori_loop(0, CHUNKS, several, 0)
    for step in range(CHUNKS):
        for copy in stores(step):
            copy.wait()


def cg_coefficients(k):
    zero, one = jnp.zeros_like(k[0]), jnp.ones_like(k[0])
    z, p, out = [one], [one], [zero, zero, zero]

    def form(a, b, moments):
        total = None
        for i, ai in enumerate(a):
            for j, bj in enumerate(b):
                term = ai * bj * moments[i + j]
                total = term if total is None else total + term
        return total

    energy = [k[j] - k[j + 1] for j in range(5)]
    rz = k[0]
    for step in range(3):
        alpha = jnp.clip(rz / form(p, p, energy), ALPHA_LOW, ALPHA_HIGH)
        out = [o + alpha * (p[i] if i < len(p) else zero) for i, o in enumerate(out)]
        if step == 2:
            break
        image = [(p[i] if i < len(p) else zero) - (p[i - 1] if i else zero) for i in range(len(p) + 1)]
        z = [(z[i] if i < len(z) else zero) - alpha * image[i] for i in range(len(image))]
        new = jnp.maximum(form(z, z, k), 0.0)
        beta = new / rz
        p = [z[i] + beta * (p[i] if i < len(p) else zero) for i in range(len(z))]
        rz = new
    return out


def final_kernel(mom, v0, v1, v2, damage_hbm, out_hbm, damage, out, in_sems, out_sems):
    count = v0.shape[0]
    block = count // CHUNKS
    loads, stores = [], []
    for chunk in range(CHUNKS):
        part = pl.ds(chunk * block, block)
        loads.append(pltpu.make_async_copy(damage_hbm.at[part], damage.at[part], in_sems.at[chunk]))
        stores.append(pltpu.make_async_copy(out.at[part], out_hbm.at[part], out_sems.at[chunk]))
        loads[-1].start()
    sums = jnp.sum(jnp.sum(mom[...], axis=0), axis=1, keepdims=True)
    c0, c1, c2 = cg_coefficients([sums[j : j + 1, :] for j in range(6)])
    for chunk in range(CHUNKS):
        loads[chunk].wait()
        for x in range(chunk * block, (chunk + 1) * block):
            dmg = damage[x]
            out[x] = jnp.maximum(dmg + (c0 * v0[x] + c1 * v1[x] + c2 * v2[x]), dmg)
        stores[chunk].start()
    for store in stores:
        store.wait()


def pairs_of(axis):
    count = lax.axis_size(axis)
    out = [[(i, i + 1) for i in range(start, count - 1, 2)] for start in (0, 1)]
    return [pairs for pairs in out if pairs]


def swap(array, axis, pairs):
    return lax.ppermute(array, axis, pairs + [(b, a) for a, b in pairs])


def swap_along(axis, arrays):
    return [swap(a, axis, pairs) for a, pairs in zip(arrays, pairs_of(axis), strict=True)]


def swap_diagonal(arrays):
    columns = lax.axis_size("gy")
    out = []
    both = [(xp, yp) for xp in pairs_of("gx") for yp in pairs_of("gy")]
    for array, (x_pairs, y_pairs) in zip(arrays, both, strict=True):
        joint = []
        for a, b in x_pairs:
            for c, d in y_pairs:
                joint.append((a * columns + c, b * columns + d))
                joint.append((a * columns + d, b * columns + c))
        out.append(swap(array, ("gx", "gy"), joint))
    return out


def spec_of(kind, a):
    if kind == "s":
        return pl.BlockSpec(memory_space=pltpu.SMEM)
    if kind == "v":
        return pl.BlockSpec(memory_space=pltpu.VMEM)
    if kind == "h":
        return pl.BlockSpec(memory_space=pltpu.HBM)
    if kind == "a":
        return pl.BlockSpec(memory_space=pl.ANY)
    raise ValueError(kind)


def call(kernel, kinds, ins, out_kinds, outs, flops, scratch=()):
    moved = sum(4 * a.size for a in (*ins, *outs))
    return pl.pallas_call(
        kernel,
        out_shape=outs,
        in_specs=[spec_of(k, a) for k, a in zip(kinds, ins, strict=True)],
        out_specs=[spec_of(k, a) for k, a in zip(out_kinds, outs, strict=True)],
        scratch_shapes=scratch,
        compiler_params=pltpu.CompilerParams(vmem_limit_bytes=VMEM_BYTES),
        cost_estimate=pl.CostEstimate(flops=flops, bytes_accessed=moved, transcendentals=0),
    )(*ins)


def per_device(displacement, velocity, damage, history, contact, notch, labels, table, impact):
    nx, ny, nz = damage.shape
    size = damage.size
    n_y = len(pairs_of("gy"))
    pos = jnp.stack(
        [lax.axis_index("gx") % 2, lax.axis_index("gy") % 2, lax.axis_index("gz")]
    ).astype(jnp.int32)

    scaled = jnp.stack(
        [table[0] / 8.0, table[1] / 8.0, TIME_STEP / table[2], table[3] + 6.0 * KAPPA_COEF]
    )

    def arr(*shape):
        return jax.ShapeDtypeStruct(shape, F32)

    field, fields3, small = arr(nx, ny, nz), arr(3, nx, ny, nz), arr(8, 128)
    columns = arr(nx, ny, 128)
    z_pairs = [(0, 1)]

    faces = [
        jnp.concatenate([displacement[:, at], damage[None, at]]) for at in (0, nx - 1)
    ]
    odd = lax.axis_index("gx") % 2 == 1
    got_x = swap_along("gx", [jnp.where(odd, *faces), jnp.where(odd, *faces[::-1])])
    sent = call(
        functools.partial(pack_kernel, n_y),
        "svv",
        (pos, displacement, damage),
        "v" * (1 + n_y),
        [*[arr(4, nx, nz)] * n_y, columns],
        size,
    )
    got = [*got_x, *swap_along("gy", sent[:n_y]), swap(sent[-1], "gz", z_pairs)]
    n_sent = 3 + 3 * n_y
    hist, rd, v0, stress, mom, *sent = call(
        functools.partial(local_kernel, n_y),
        "ssvvvvv" + "v" * (3 + n_y),
        (pos, scaled, displacement, damage, history, notch, labels, *got),
        "hvvvv" + "v" * n_sent,
        [
            field,
            field,
            field,
            arr(6, nx, ny, nz),
            small,
            *[arr(8, ny, nz)] * 2,
            *[arr(nx + 3 * (nx // 8), 8, nz)] * n_y,
            *[arr(2, 8, nz)] * (2 * n_y),
            columns,
        ],
        150 * size,
        [pltpu.VMEM((nx, ny, nz), F32), pltpu.SemaphoreType.DMA((CHUNKS,))],
    )
    xy = [
        *swap_along("gx", sent[:2]),
        *swap_along("gy", sent[2 : 2 + n_y]),
        *swap_diagonal(sent[2 + n_y : 2 + 3 * n_y]),
    ]
    (joined,) = call(
        functools.partial(join_kernel, n_y),
        "svvv" + "v" * len(xy),
        (pos, v0, rd, sent[-1], *xy),
        "v",
        [arr(nx + 6, ny + 8, 128)],
        4 * size,
    )
    z_got = swap(joined, "gz", z_pairs)
    main_v, main_rd = call(
        functools.partial(fill_kernel, n_y),
        "svv" + "v" * len(xy),
        (pos, v0, rd, *xy),
        "vv",
        [arr(nx + 6, ny + 8, nz)] * 2,
        4 * size,
    )
    new_disp, new_vel, token = call(
        functools.partial(force_kernel, n_y),
        "sssvvvvv" + "v" * (3 + n_y),
        (
            pos,
            scaled,
            impact,
            displacement,
            velocity,
            contact,
            labels,
            stress,
            *xy[: 2 + n_y],
            z_got,
        ),
        "hhv",
        [fields3, fields3, small],
        60 * size,
        [
            pltpu.VMEM((3, nx, ny, nz), F32),
            pltpu.VMEM((3, nx, ny, nz), F32),
            pltpu.SemaphoreType.DMA((CHUNKS, 2)),
        ],
    )
    peers = lax.axis_size("gx") * lax.axis_size("gy") * lax.axis_size("gz")
    v1, v2, spread = call(
        krylov_kernel,
        "svvvav",
        (pos, main_v, main_rd, mom, token, z_got),
        "vvv",
        [field, field, arr(peers, 8, 128)],
        60 * size,
        [
            pltpu.VMEM((nx + 6, ny + 8, 128), F32),
            pltpu.VMEM((nx + 6, ny + 8, 128), F32),
            pltpu.VMEM((nx + 4, ny + 8, nz + 128), F32),
            pltpu.VMEM((nx + 2, ny + 8, nz + 128), F32),
        ],
    )
    mom = lax.all_to_all(spread, ("gx", "gy", "gz"), 0, 0, tiled=True)
    (damage_new,) = call(
        final_kernel,
        "vvvvh",
        (mom, v0, v1, v2, damage),
        "h",
        [field],
        8 * size,
        [
            pltpu.VMEM((nx, ny, nz), F32),
            pltpu.VMEM((nx, ny, nz), F32),
            pltpu.SemaphoreType.DMA((CHUNKS,)),
            pltpu.SemaphoreType.DMA((CHUNKS,)),
        ],
    )
    return new_disp, new_vel, hist, damage_new


def solution(mesh):
    placed = (
        P(None, ("case", "gx"), "gy", "gz"),
        P(None, ("case", "gx"), "gy", "gz"),
        P(("case", "gx"), "gy", "gz"),
        P(("case", "gx"), "gy", "gz"),
        P(("case", "gx"), "gy", "gz"),
        P(("case", "gx"), "gy", "gz"),
        P(("case", "gx"), "gy", "gz"),
        P(),
        P("case"),
    )
    return jax.shard_map(
        per_device,
        mesh=mesh,
        in_specs=placed,
        out_specs=(
            P(None, ("case", "gx"), "gy", "gz"),
            P(None, ("case", "gx"), "gy", "gz"),
            P(("case", "gx"), "gy", "gz"),
            P(("case", "gx"), "gy", "gz"),
        ),
        check_vma=False,
    )
```

```python
import functools
import jax
import jax.numpy as jnp
from jax import lax
from jax.experimental import pallas as pl
from jax.experimental.pallas import tpu as pltpu
from jax.sharding import PartitionSpec as P

TIME_STEP = 0.1
KAPPA_COEF = 0.5
NOTCH_LOAD = 20.0
STIFF_FLOOR = 0.001
ALPHA_LOW, ALPHA_HIGH = 0.5, 6.5
VMEM_BYTES = 28 * 1024 * 1024
CHUNKS = 4
F32 = jnp.float32


def iota2(shape, dim):
    return lax.broadcasted_iota(jnp.int32, shape, dim)


def low_high(odd, got):
    if len(got) == 2:
        return jnp.where(odd, got[0], got[1]), jnp.where(odd, got[1], got[0])
    return jnp.where(odd, got[0], 0.0), jnp.where(odd, 0.0, got[0])


def send(odd, refs, index, low, high):
    refs[0][index] = jnp.where(odd, low, high)
    if len(refs) == 2:
        refs[1][index] = jnp.where(odd, high, low)


def shift_y(plane, rows):
    lo, hi = rows
    at = iota2(plane.shape, 0)
    last = plane.shape[0] - 1
    upper = jnp.where(at == last, hi, pltpu.roll(plane, last, 0))
    lower = jnp.where(at == 0, lo, pltpu.roll(plane, 1, 0))
    return upper, lower


def shift_z(plane, column, first_z):
    at = iota2(plane.shape, 1)
    last = plane.shape[1] - 1
    lo = jnp.where(first_z, 0.0, column)
    hi = jnp.where(first_z, column, 0.0)
    upper = jnp.where(at == last, hi, pltpu.roll(plane, last, 1))
    lower = jnp.where(at == 0, lo, pltpu.roll(plane, 1, 1))
    return upper, lower


def send_columns(ref, x, planes, gz):
    depth = planes[0].shape[1]
    lanes = iota2((planes[0].shape[0], 128), 1)
    tile = None
    for field, plane in enumerate(planes):
        part = jnp.where(gz == 0, plane[:, depth - 128 :], plane[:, :128])
        part = pltpu.roll(part, field + 1 - gz, 1)
        tile = part if tile is None else jnp.where(lanes == field, part, tile)
    ref[x] = tile


def folded(values):
    total = None
    for start in range(0, values.shape[1], 128):
        part = values[:, start : start + 128]
        total = part if total is None else total + part
    out = None
    for start in range(0, values.shape[0], 8):
        part = total[start : start + 8]
        out = part if out is None else out + part
    return out


def by_label(labels, scalars):
    picked = scalars[0]
    for region in range(1, len(scalars)):
        picked = jnp.where(labels == region, scalars[region], picked)
    return picked


def unrolled(count, many, body, carry):
    def several(block, carry):
        for at in range(many):
            carry = body(block * many + at, carry)
        return carry

    return lax.fori_loop(0, count // many, several, carry)


def pack_kernel(n_y, pos, disp, damage, *refs):
    ys, zs = refs[:n_y], refs[n_y]
    odd_y, gz = pos[1] == 1, pos[2]

    def body(x, carry):
        planes = [disp[0, x], disp[1, x], disp[2, x], damage[x]]
        for field, plane in enumerate(planes):
            last = plane.shape[0] - 1
            spot = (field, pl.ds(x, 1), slice(None))
            send(odd_y, ys, spot, plane[0:1], plane[last : last + 1])
        send_columns(zs, x, planes, gz)
        return carry

    unrolled(damage.shape[0], 8, body, 0)


def pack_x_kernel(pos, disp, damage, after, *xs):
    odd_x, count = pos[0] == 1, damage.shape[0]
    for field, src in enumerate((disp.at[0], disp.at[1], disp.at[2], damage)):
        send(odd_x, xs, field, src[0], src[count - 1])


def row_tile(v, rd, is_high):
    rows = v.shape[0]
    part = slice(rows - 8, rows) if is_high else slice(0, 8)
    at = iota2((8, v.shape[1]), 0)
    keep = at >= 4 if is_high else at < 4
    return jnp.where(keep, v[part], pltpu.roll(rd[part], 4, 0))


class Local:
    def __init__(self, pos, table, disp, damage, history, notch, labels, yg, zg):
        self.odd_x, self.odd_y, self.gz = pos[0] == 1, pos[1] == 1, pos[2]
        self.disp, self.damage, self.history = disp, damage, history
        self.notch, self.labels, self.yg, self.zg = notch, labels, yg, zg
        regions = range(table.shape[1])
        self.lames = [table[0, r] for r in regions]
        self.shears = [table[1, r] for r in regions]
        self.bases = [table[3, r] for r in regions]

    def around(self, field, plane, x, lower, upper):
        rows = low_high(self.odd_y, [y[field, pl.ds(x, 1), :] for y in self.yg])
        column = self.zg[x][:, field : field + 1]
        return (
            (upper, lower),
            shift_y(plane, rows),
            shift_z(plane, column, self.gz == 0),
        )

    def plane(self, x, lower, upper):
        g = []
        for c in range(3):
            pairs = self.around(c, self.disp[c, x], x, lower(c), upper(c))
            g.append([high - low for high, low in pairs])
        lab = self.labels[x]
        lame = by_label(lab, self.lames)
        shear = by_label(lab, self.shears)
        base = by_label(lab, self.bases)
        dmg = self.damage[x]
        degrade = 4.0 * ((1.0 - dmg) * (1.0 - dmg) + STIFF_FLOOR)
        trace = g[0][0] + g[1][1] + g[2][2]
        shears3 = [g[0][1] + g[1][0], g[0][2] + g[2][0], g[1][2] + g[2][1]]
        positive = jnp.maximum(trace, 0.0)
        squares = g[0][0] * g[0][0] + g[1][1] * g[1][1] + g[2][2] * g[2][2]
        squares = (squares + squares) + (
            shears3[0] * shears3[0] + shears3[1] * shears3[1] + shears3[2] * shears3[2]
        )
        energy = lame * positive * positive + shear * squares
        half = degrade * shear
        whole = half + half
        level = (degrade * lame) * trace
        stress = [level + whole * g[k][k] for k in range(3)] + [half * e for e in shears3]
        hist = jnp.maximum(
            jnp.maximum(self.history[x], energy), NOTCH_LOAD * self.notch[x].astype(F32)
        )
        diagonal = base + 2.0 * hist
        rd = 1.0 / diagonal
        (xu, xl), (yu, yl), (zu, zl) = self.around(3, dmg, x, lower(3), upper(3))
        near = ((xu + xl) + (yu + yl)) + (zu + zl)
        residual = 2.0 * hist - (diagonal * dmg - KAPPA_COEF * near)
        v = residual * rd
        return stress, hist, rd, v, folded(residual * v)

    def send_y(self, ys, x, v, rd, stress):
        count = self.damage.shape[0]
        tall, last = count // 8, v.shape[0] - 1
        send(self.odd_y, ys, x, row_tile(v, rd, False), row_tile(v, rd, True))
        for c, k in enumerate((3, 1, 5)):
            spot = (count + c * tall + lax.div(x, 8), pl.ds(lax.rem(x, 8), 1), slice(None))
            send(self.odd_y, ys, spot, stress[k][0:1], stress[k][last : last + 1])

    def send_z(self, zs, x, stress):
        send_columns(zs, x, [stress[4], stress[5], stress[2]], self.gz)


def inner_steps(count):
    inner = count - 2
    many = max(m for m in range(1, 8) if inner % m == 0)
    return inner // many, many


def inner_kernel(n_y, pos, table, disp, damage, history, notch, labels, *refs):
    local = Local(
        pos, table, disp, damage, history, notch, labels, refs[:n_y], refs[n_y]
    )
    hist_hbm, rd_out, v_out, stress_out, mom_out = refs[n_y + 1 : n_y + 6]
    ys, (zs, hist, sems) = refs[n_y + 6 : 2 * n_y + 6], refs[2 * n_y + 6 :]
    steps, many = inner_steps(damage.shape[0])

    def store(step):
        part = pl.ds(1 + step * many, many)
        return pltpu.make_async_copy(hist.at[part], hist_hbm.at[part], sems.at[step])

    def several(step, total):
        for at in range(many):
            x = 1 + step * many + at

            def lower(c):
                return damage[x - 1] if c == 3 else disp[c, x - 1]

            def upper(c):
                return damage[x + 1] if c == 3 else disp[c, x + 1]

            stress, hist_x, rd, v, part = local.plane(x, lower, upper)
            for k in range(6):
                stress_out[k, x] = stress[k]
            hist[x] = hist_x
            rd_out[x] = rd
            v_out[x] = v
            local.send_y(ys, x, v, rd, stress)
            local.send_z(zs, x, stress)
            total = total + part
        store(step).start()
        return total

    mom_out[...] = lax.fori_loop(0, steps, several, jnp.zeros((8, 128), F32))
    for step in range(steps):
        store(step).wait()


def ends_kernel(n_y, pos, table, disp, damage, history, notch, labels, *refs):
    local = Local(
        pos, table, disp, damage, history, notch, labels, refs[:n_y], refs[n_y]
    )
    refs = refs[n_y + 1 :]
    xg, (_, rd_in, v_in, mom), ys_in, zs_in = (
        refs[:2],
        refs[2:6],
        refs[6 : 6 + n_y],
        refs[6 + n_y],
    )
    refs = refs[7 + n_y :]
    hist_hbm, rd_out, v_out, stress_out, mom_out = refs[:5]
    xs, ys, (zs, hist, sems) = refs[5:7], refs[7 : 7 + n_y], refs[7 + n_y :]
    odd_x, count = local.odd_x, damage.shape[0]
    total = mom[...]
    copies, found = [], []
    for end, x in enumerate((0, count - 1)):

        def outside(c):
            first, second = xg[0][c], xg[1][c]
            if end == 0:
                return jnp.where(odd_x, first, second)
            return jnp.where(odd_x, second, first)

        def beside(c):
            at = 1 if end == 0 else count - 2
            return damage[at] if c == 3 else disp[c, at]

        sides = (outside, beside) if end == 0 else (beside, outside)
        stress, hist_x, rd, v, part = local.plane(x, *sides)
        hist[end] = hist_x
        copies.append(pltpu.make_async_copy(hist.at[end], hist_hbm.at[x], sems.at[end]))
        copies[-1].start()
        for k in range(6):
            stress_out[k, end] = stress[k]
        rd_out[x] = rd
        v_out[x] = v
        total = total + part
        found.append((stress, rd, v))
    tall = count // 8
    for mine, before in zip(ys, ys_in, strict=True):
        for x in [*range(1, count - 1), *range(count, count + 3 * tall)]:
            mine[x] = before[x]
    for x in range(1, count - 1):
        rd_out[x] = rd_in[x]
        v_out[x] = v_in[x]
        zs[x] = zs_in[x]
    for end, x in enumerate((0, count - 1)):
        stress, rd, v = found[end]
        local.send_y(ys, x, v, rd, stress)
        local.send_z(zs, x, stress)
    for depth in (1, 2, 3):
        low, high = depth - 1, count - depth
        send(odd_x, xs, depth - 1, v_out[low], v_out[high])
        if depth <= 2:
            send(odd_x, xs, 2 + depth, rd_out[low], rd_out[high])
    for slot, k in ((5, 0), (6, 3), (7, 4)):
        send(odd_x, xs, slot, stress_out[k, 0], stress_out[k, 1])
    mom_out[...] = jnp.zeros((8, 128), F32)
    mom_out[0:1, :] = jnp.sum(total, axis=0, keepdims=True)
    for copy in copies:
        copy.wait()


def corner_kernel(n_y, pos, after, *refs):
    ys, ds = refs[:n_y], refs[n_y:]
    odd_x, count = pos[0] == 1, after.shape[0]
    for which in range(n_y):
        for depth in (1, 2):
            pair = (ds[which], ds[n_y + which])
            send(odd_x, pair, depth - 1, ys[which][depth - 1], ys[which][count - depth])


class Enlarged:
    def __init__(self, n_y, pos, v, rd, refs):
        self.odd_x, self.odd_y = pos[0] == 1, pos[1] == 1
        self.v, self.rd, self.n_y = v, rd, n_y
        self.xg, self.yg, self.dg = refs[:2], refs[2 : 2 + n_y], refs[2 + n_y : 2 + 3 * n_y]

    def rows(self, tiles):
        at = iota2(tiles[0].shape, 0)
        if self.n_y == 1:
            keep = lax.shift_right_logical(at, 2) == self.odd_y.astype(jnp.int32)
            tile = tiles[0]
            return jnp.where(keep, tile, 0.0), jnp.where(keep, pltpu.roll(tile, 4, 0), 0.0)
        lo, hi = low_high(self.odd_y, tiles)
        tile = jnp.where(at >= 4, lo, hi)
        moved = jnp.where(at >= 4, pltpu.roll(lo, 4, 0), pltpu.roll(hi, 4, 0))
        return tile, moved

    def own(self, x):
        v_rows, rd_rows = self.rows([y[x] for y in self.yg])
        return self.v[x], v_rows, self.rd[x], rd_rows

    def halo(self, is_low, depth):
        first, second = (0, 1) if is_low else (1, 0)

        def of(a, b):
            return jnp.where(self.odd_x, (a, b)[first], (a, b)[second])

        v = of(self.xg[0][depth - 1], self.xg[1][depth - 1])
        nothing = jnp.zeros((8, v.shape[1]), F32)
        if depth > 2:
            return v, nothing, jnp.zeros_like(v), nothing
        rd = of(self.xg[0][2 + depth], self.xg[1][2 + depth])
        tiles = [
            of(self.dg[w][depth - 1], self.dg[self.n_y + w][depth - 1]) for w in range(self.n_y)
        ]
        v_rows, rd_rows = self.rows(tiles)
        return v, v_rows, rd, rd_rows

    def outer(self, count):
        for depth in (1, 2, 3):
            yield -depth, self.halo(True, depth)
            yield count - 1 + depth, self.halo(False, depth)


def join_kernel(n_y, pos, v, rd, *refs):
    big = Enlarged(n_y, pos, v, rd, refs[:-1])
    out = refs[-1]
    first_z = pos[2] == 0
    count, ny, depth = v.shape

    def tile(v_part, rd_part):
        lanes = iota2((v_part.shape[0], 128), 1)
        keep = lax.shift_right_logical(lanes, 6) == 1 - pos[2]
        mine = jnp.where(first_z, v_part[:, depth - 128 :], v_part[:, :128])
        moved = jnp.where(first_z, rd_part[:, depth - 128 :], rd_part[:, :128])
        return jnp.where(keep, mine, pltpu.roll(moved, 64, 1))

    def put(p, parts):
        v_own, v_rows, rd_own, rd_rows = parts
        out[p + 3, 0:ny] = tile(v_own, rd_own)
        out[p + 3, ny : ny + 8] = tile(v_rows, rd_rows)

    for p, parts in big.outer(count):
        put(p, parts)

    def body(x, carry):
        put(x, big.own(x))
        return carry

    unrolled(count, 8, body, 0)


def fill_kernel(n_y, pos, v, rd, *refs):
    big = Enlarged(n_y, pos, v, rd, refs[:-2])
    big_v, big_rd = refs[-2:]
    count, ny, _ = v.shape

    def put(p, parts):
        v_own, v_rows, rd_own, rd_rows = parts
        big_v[p + 3, 0:ny] = v_own
        big_v[p + 3, ny : ny + 8] = v_rows
        big_rd[p + 3, 0:ny] = rd_own
        big_rd[p + 3, ny : ny + 8] = rd_rows

    for p, parts in big.outer(count):
        put(p, parts)

    def body(x, carry):
        put(x, big.own(x))
        return carry

    unrolled(count, 4, body, 0)


def krylov_kernel(pos, main_v, main_rd, mom, token, z_got, *refs):
    v1_out, v2_out, spread, z_v, z_rd, big_v1, big_v2 = refs
    count, ny, nz = v1_out.shape

    def split(p, carry):
        tile = z_got[p]
        keep = lax.shift_right_logical(iota2(tile.shape, 1), 6) == pos[2]
        z_v[p] = jnp.where(keep, tile, 0.0)
        z_rd[p] = jnp.where(keep, pltpu.roll(tile, 64, 1), 0.0)
        return carry

    unrolled(count + 6, 11 if count % 11 == 5 else 1, split, 0)

    def v_at(at):
        return jnp.concatenate([main_v[at], z_v[at]], axis=1)

    def rd_at(at):
        return jnp.concatenate([main_rd[at], z_rd[at]], axis=1)

    def image_of(get, at):
        plane = get(at)
        rows, lanes = plane.shape
        near = (get(at - 1) + get(at + 1)) + (pltpu.roll(plane, 1, 0) + pltpu.roll(plane, rows - 1, 0))
        near = near + (pltpu.roll(plane, 1, 1) + pltpu.roll(plane, lanes - 1, 1))
        return plane, KAPPA_COEF * near

    def v1_at(at):
        return big_v1[at]

    def v2_at(at):
        return big_v2[at]

    def inside(values):
        return folded(values[0:ny, 0:nz])

    def first(x, totals):
        plane, image = image_of(v_at, x + 3)
        made = image * rd_at(x + 3)
        big_v1[x + 2] = made
        v1_out[x] = made[0:ny, 0:nz]
        return totals[0] + inside(plane * image), totals[1] + inside(made * image)

    def second(x, totals):
        plane, image = image_of(v1_at, x + 2)
        made = image * rd_at(x + 3)
        big_v2[x + 1] = made
        v2_out[x] = made[0:ny, 0:nz]
        return totals[0] + inside(plane * image), totals[1] + inside(made * image)

    def third(x, total):
        plane, image = image_of(v2_at, x + 1)
        return total + folded(plane[0:ny, 0:nz] * image[0:ny, 0:nz])

    zero = jnp.zeros((8, 128), F32)
    for p in (-2, -1, count, count + 1):
        big_v1[p + 2] = image_of(v_at, p + 3)[1] * rd_at(p + 3)
    k1, k2 = unrolled(count, 8, first, (zero, zero))
    for p in (-1, count):
        big_v2[p + 1] = image_of(v1_at, p + 2)[1] * rd_at(p + 3)
    k3, k4 = unrolled(count, 8, second, (zero, zero))
    k5 = unrolled(count, 8, third, zero)
    rows = iota2((8, 128), 0)
    result = mom[...]
    for at, total in enumerate((k1, k2, k3, k4, k5)):
        result = jnp.where(rows == at + 1, jnp.sum(total, axis=0, keepdims=True), result)
    for peer in range(spread.shape[0]):
        spread[peer] = result


PARTS = ((0, 3, 4), (3, 1, 5), (4, 5, 2))


class Force:
    def __init__(self, n_y, pos, table, impact, disp, vel, contact, labels, yg, zg):
        self.odd_x, self.odd_y, self.gz = pos[0] == 1, pos[1] == 1, pos[2]
        self.impact, self.disp, self.vel = impact, disp, vel
        self.contact, self.labels, self.yg, self.zg = contact, labels, yg, zg
        self.rates = [table[2, r] for r in range(table.shape[1])]

    def plane(self, x, lower, mine, upper, vel_out, disp_out, at):
        count = self.contact.shape[0]
        tall = count // 8
        loaded = self.contact[x].astype(F32)
        rate = by_label(self.labels[x], self.rates)
        for c, (kx, ky, kz) in enumerate(PARTS):
            spot = (count + c * tall + lax.div(x, 8), pl.ds(lax.rem(x, 8), 1), slice(None))
            rows = low_high(self.odd_y, [y[spot] for y in self.yg])
            column = self.zg[x][:, c : c + 1]
            yu, yl = shift_y(mine(ky), rows)
            zu, zl = shift_z(mine(kz), column, self.gz == 0)
            force = 0.5 * (((upper(c, kx) - lower(c, kx)) + (yu - yl)) + (zu - zl))
            speed = self.vel[c, x] + rate * (force + loaded * self.impact[c])
            vel_out[c, at] = speed
            disp_out[c, at] = self.disp[c, x] + TIME_STEP * speed


def force_inner_kernel(n_y, pos, table, impact, disp, vel, contact, labels, *refs):
    yg, zg, stress, ends = refs[:n_y], refs[n_y], refs[n_y + 1], refs[n_y + 2]
    disp_hbm, vel_hbm, disp_out, vel_out, sems = refs[n_y + 3 :]
    force = Force(n_y, pos, table, impact, disp, vel, contact, labels, yg, zg)
    count = contact.shape[0]
    steps, many = inner_steps(count)

    def stores(step):
        part = pl.ds(1 + step * many, many)
        return (
            pltpu.make_async_copy(disp_out.at[:, part], disp_hbm.at[:, part], sems.at[step, 0]),
            pltpu.make_async_copy(vel_out.at[:, part], vel_hbm.at[:, part], sems.at[step, 1]),
        )

    def several(step, carry):
        for at in range(many):
            x = 1 + step * many + at

            def lower(c, k):
                if at == 0:
                    return jnp.where(step == 0, ends[k, 0], stress[k, x - 1])
                return stress[k, x - 1]

            def upper(c, k):
                if at == many - 1:
                    return jnp.where(step == steps - 1, ends[k, 1], stress[k, x + 1])
                return stress[k, x + 1]

            force.plane(x, lower, lambda k: stress[k, x], upper, vel_out, disp_out, x)
        for copy in stores(step):
            copy.start()
        return carry

    lax.fori_loop(0, steps, several, 0)
    for step in range(steps):
        for copy in stores(step):
            copy.wait()


def force_ends_kernel(n_y, pos, table, impact, disp, vel, contact, labels, *refs):
    yg, zg, stress, ends = refs[:n_y], refs[n_y], refs[n_y + 1], refs[n_y + 2]
    xg = refs[n_y + 3 : n_y + 5]
    disp_hbm, vel_hbm, token, disp_out, vel_out, sems = refs[n_y + 7 :]
    token[...] = jnp.zeros((8, 128), F32)
    force = Force(n_y, pos, table, impact, disp, vel, contact, labels, yg, zg)
    count = contact.shape[0]
    copies = []
    for end, x in enumerate((0, count - 1)):

        def outside(c, k):
            first, second = xg[0][5 + c], xg[1][5 + c]
            if end == 0:
                return jnp.where(force.odd_x, first, second)
            return jnp.where(force.odd_x, second, first)

        def beside(c, k):
            return stress[k, 1 if end == 0 else count - 2]

        lower, upper = (outside, beside) if end == 0 else (beside, outside)
        force.plane(x, lower, lambda k: ends[k, end], upper, vel_out, disp_out, end)
        for which, (src, dst) in enumerate(((disp_out, disp_hbm), (vel_out, vel_hbm))):
            copy = pltpu.make_async_copy(src.at[:, end], dst.at[:, x], sems.at[end, which])
            copy.start()
            copies.append(copy)
    for copy in copies:
        copy.wait()


def cg_coefficients(k):
    zero, one = jnp.zeros_like(k[0]), jnp.ones_like(k[0])
    z, p, out = [one], [one], [zero, zero, zero]

    def form(a, b, moments):
        total = None
        for i, ai in enumerate(a):
            for j, bj in enumerate(b):
                term = ai * bj * moments[i + j]
                total = term if total is None else total + term
        return total

    energy = [k[j] - k[j + 1] for j in range(5)]
    rz = k[0]
    for step in range(3):
        alpha = jnp.clip(rz / form(p, p, energy), ALPHA_LOW, ALPHA_HIGH)
        out = [o + alpha * (p[i] if i < len(p) else zero) for i, o in enumerate(out)]
        if step == 2:
            break
        image = [(p[i] if i < len(p) else zero) - (p[i - 1] if i else zero) for i in range(len(p) + 1)]
        z = [(z[i] if i < len(z) else zero) - alpha * image[i] for i in range(len(image))]
        new = jnp.maximum(form(z, z, k), 0.0)
        beta = new / rz
        p = [z[i] + beta * (p[i] if i < len(p) else zero) for i in range(len(z))]
        rz = new
    return out


def final_kernel(mom, v0, v1, v2, damage_hbm, out_hbm, damage, out, in_sems, out_sems):
    count = v0.shape[0]
    block = count // CHUNKS
    loads, stores = [], []
    for chunk in range(CHUNKS):
        part = pl.ds(chunk * block, block)
        loads.append(pltpu.make_async_copy(damage_hbm.at[part], damage.at[part], in_sems.at[chunk]))
        stores.append(pltpu.make_async_copy(out.at[part], out_hbm.at[part], out_sems.at[chunk]))
        loads[-1].start()
    sums = jnp.sum(jnp.sum(mom[...], axis=0), axis=1, keepdims=True)
    c0, c1, c2 = cg_coefficients([sums[j : j + 1, :] for j in range(6)])
    for chunk in range(CHUNKS):
        loads[chunk].wait()
        for x in range(chunk * block, (chunk + 1) * block):
            dmg = damage[x]
            out[x] = jnp.maximum(dmg + (c0 * v0[x] + c1 * v1[x] + c2 * v2[x]), dmg)
        stores[chunk].start()
    for store in stores:
        store.wait()


def pairs_of(axis):
    count = lax.axis_size(axis)
    out = [[(i, i + 1) for i in range(start, count - 1, 2)] for start in (0, 1)]
    return [pairs for pairs in out if pairs]


def swap(array, axis, pairs):
    return lax.ppermute(array, axis, pairs + [(b, a) for a, b in pairs])


def swap_along(axis, arrays):
    return [swap(a, axis, pairs) for a, pairs in zip(arrays, pairs_of(axis), strict=True)]


def swap_diagonal(arrays):
    columns = lax.axis_size("gy")
    out = []
    both = [(xp, yp) for xp in pairs_of("gx") for yp in pairs_of("gy")]
    for array, (x_pairs, y_pairs) in zip(arrays, both, strict=True):
        joint = []
        for a, b in x_pairs:
            for c, d in y_pairs:
                joint.append((a * columns + c, b * columns + d))
                joint.append((a * columns + d, b * columns + c))
        out.append(swap(array, ("gx", "gy"), joint))
    return out


def spec_of(kind, a):
    if kind == "s":
        return pl.BlockSpec(memory_space=pltpu.SMEM)
    if kind == "v":
        return pl.BlockSpec(memory_space=pltpu.VMEM)
    if kind == "h":
        return pl.BlockSpec(memory_space=pltpu.HBM)
    if kind == "a":
        return pl.BlockSpec(memory_space=pl.ANY)
    raise ValueError(kind)


def call(kernel, kinds, ins, out_kinds, outs, flops, scratch=(), aliases=()):
    moved = sum(4 * a.size for a in (*ins, *outs))
    return pl.pallas_call(
        kernel,
        out_shape=outs,
        in_specs=[spec_of(k, a) for k, a in zip(kinds, ins, strict=True)],
        out_specs=[spec_of(k, a) for k, a in zip(out_kinds, outs, strict=True)],
        scratch_shapes=scratch,
        input_output_aliases=dict(aliases),
        compiler_params=pltpu.CompilerParams(vmem_limit_bytes=VMEM_BYTES),
        cost_estimate=pl.CostEstimate(flops=flops, bytes_accessed=moved, transcendentals=0),
    )(*ins)


def per_device(displacement, velocity, damage, history, contact, notch, labels, table, impact):
    nx, ny, nz = damage.shape
    size = damage.size
    n_y = len(pairs_of("gy"))
    pos = jnp.stack(
        [lax.axis_index("gx") % 2, lax.axis_index("gy") % 2, lax.axis_index("gz")]
    ).astype(jnp.int32)

    scaled = jnp.stack(
        [table[0] / 8.0, table[1] / 8.0, TIME_STEP / table[2], table[3] + 6.0 * KAPPA_COEF]
    )

    def arr(*shape):
        return jax.ShapeDtypeStruct(shape, F32)

    field, fields3, small = arr(nx, ny, nz), arr(3, nx, ny, nz), arr(8, 128)
    columns = arr(nx, ny, 128)
    z_pairs = [(0, 1)]

    sent = call(
        functools.partial(pack_kernel, n_y),
        "svv",
        (pos, displacement, damage),
        "v" * (1 + n_y),
        [*[arr(4, nx, nz)] * n_y, columns],
        size,
    )
    got_yz = [*swap_along("gy", sent[:n_y]), swap(sent[-1], "gz", z_pairs)]
    sent_x = call(
        pack_x_kernel,
        "svva",
        (pos, displacement, damage, sent[-1]),
        "vv",
        [arr(4, ny, nz)] * 2,
        size,
    )
    got_x = swap_along("gx", sent_x)
    rows = [arr(nx + 3 * (nx // 8), 8, nz)] * n_y
    voxels = (pos, scaled, displacement, damage, history, notch, labels, *got_yz)
    hist, rd, v0, stress, mom, *sent = call(
        functools.partial(inner_kernel, n_y),
        "ssvvvvv" + "v" * (1 + n_y),
        voxels,
        "hvvvv" + "v" * (1 + n_y),
        [field, field, field, arr(6, nx, ny, nz), small, *rows, columns],
        140 * size,
        [pltpu.VMEM((nx, ny, nz), F32), pltpu.SemaphoreType.DMA((inner_steps(nx)[0],))],
    )
    more = (*got_x, hist, rd, v0, mom, *sent)
    hist, rd, v0, ends, mom, *sent = call(
        functools.partial(ends_kernel, n_y),
        "ssvvvvv" + "v" * (1 + n_y) + "vvhvvv" + "v" * (1 + n_y),
        (*voxels, *more),
        "hvvvv" + "v" * (3 + n_y),
        [
            field,
            field,
            field,
            arr(6, 2, ny, nz),
            small,
            *[arr(8, ny, nz)] * 2,
            *rows,
            columns,
        ],
        20 * size,
        [pltpu.VMEM((2, ny, nz), F32), pltpu.SemaphoreType.DMA((2,))],
        [(len(voxels) + 2, 0)],
    )
    stress_z = swap(sent[-1], "gz", z_pairs)
    xs = swap_along("gx", sent[:2])
    ys = swap_along("gy", sent[2 : 2 + n_y])
    corners = call(
        functools.partial(corner_kernel, n_y),
        "sa" + "v" * n_y,
        (pos, stress_z, *sent[2 : 2 + n_y]),
        "v" * (2 * n_y),
        [arr(2, 8, nz)] * (2 * n_y),
        1024,
    )
    xy = [*xs, *ys, *swap_diagonal(corners)]
    moving = (
        pos,
        scaled,
        impact,
        displacement,
        velocity,
        contact,
        labels,
        *ys,
        stress_z,
        stress,
        ends,
    )
    new_disp, new_vel = call(
        functools.partial(force_inner_kernel, n_y),
        "sssvvvv" + "v" * (3 + n_y),
        moving,
        "hh",
        [fields3, fields3],
        55 * size,
        [
            pltpu.VMEM((3, nx, ny, nz), F32),
            pltpu.VMEM((3, nx, ny, nz), F32),
            pltpu.SemaphoreType.DMA((inner_steps(nx)[0], 2)),
        ],
    )
    (joined,) = call(
        functools.partial(join_kernel, n_y),
        "svv" + "v" * len(xy),
        (pos, v0, rd, *xy),
        "v",
        [arr(nx + 6, ny + 8, 128)],
        4 * size,
    )
    z_got = swap(joined, "gz", z_pairs)
    main_v, main_rd = call(
        functools.partial(fill_kernel, n_y),
        "svv" + "v" * len(xy),
        (pos, v0, rd, *xy),
        "vv",
        [arr(nx + 6, ny + 8, nz)] * 2,
        4 * size,
    )
    new_disp, new_vel, token = call(
        functools.partial(force_ends_kernel, n_y),
        "sssvvvv" + "v" * (3 + n_y) + "vvhh",
        (*moving, *xs, new_disp, new_vel),
        "hhv",
        [fields3, fields3, small],
        8 * size,
        [
            pltpu.VMEM((3, 2, ny, nz), F32),
            pltpu.VMEM((3, 2, ny, nz), F32),
            pltpu.SemaphoreType.DMA((2, 2)),
        ],
        [(len(moving) + 2, 0), (len(moving) + 3, 1)],
    )
    peers = lax.axis_size("gx") * lax.axis_size("gy") * lax.axis_size("gz")
    v1, v2, spread = call(
        krylov_kernel,
        "svvvav",
        (pos, main_v, main_rd, mom, token, z_got),
        "vvv",
        [field, field, arr(peers, 8, 128)],
        60 * size,
        [
            pltpu.VMEM((nx + 6, ny + 8, 128), F32),
            pltpu.VMEM((nx + 6, ny + 8, 128), F32),
            pltpu.VMEM((nx + 4, ny + 8, nz + 128), F32),
            pltpu.VMEM((nx + 2, ny + 8, nz + 128), F32),
        ],
    )
    mom = lax.all_to_all(spread, ("gx", "gy", "gz"), 0, 0, tiled=True)
    (damage_new,) = call(
        final_kernel,
        "vvvvh",
        (mom, v0, v1, v2, damage),
        "h",
        [field],
        8 * size,
        [
            pltpu.VMEM((nx, ny, nz), F32),
            pltpu.VMEM((nx, ny, nz), F32),
            pltpu.SemaphoreType.DMA((CHUNKS,)),
            pltpu.SemaphoreType.DMA((CHUNKS,)),
        ],
    )
    return new_disp, new_vel, hist, damage_new


def solution(mesh):
    placed = (
        P(None, ("case", "gx"), "gy", "gz"),
        P(None, ("case", "gx"), "gy", "gz"),
        P(("case", "gx"), "gy", "gz"),
        P(("case", "gx"), "gy", "gz"),
        P(("case", "gx"), "gy", "gz"),
        P(("case", "gx"), "gy", "gz"),
        P(("case", "gx"), "gy", "gz"),
        P(),
        P("case"),
    )
    return jax.shard_map(
        per_device,
        mesh=mesh,
        in_specs=placed,
        out_specs=(
            P(None, ("case", "gx"), "gy", "gz"),
            P(None, ("case", "gx"), "gy", "gz"),
            P(("case", "gx"), "gy", "gz"),
            P(("case", "gx"), "gy", "gz"),
        ),
        check_vma=False,
    )
```

```python
import functools
import jax
import jax.numpy as jnp
from jax import lax
from jax.experimental import pallas as pl
from jax.experimental.pallas import tpu as pltpu
from jax.sharding import PartitionSpec as P

TIME_STEP = 0.1
KAPPA_COEF = 0.5
NOTCH_LOAD = 20.0
STIFF_FLOOR = 0.001
ALPHA_LOW, ALPHA_HIGH = 0.5, 6.5
VMEM_BYTES = 28 * 1024 * 1024
CHUNKS = 4
F32 = jnp.float32


def iota2(shape, dim):
    return lax.broadcasted_iota(jnp.int32, shape, dim)


def low_high(odd, got):
    if len(got) == 2:
        return jnp.where(odd, got[0], got[1]), jnp.where(odd, got[1], got[0])
    return jnp.where(odd, got[0], 0.0), jnp.where(odd, 0.0, got[0])


def send(odd, refs, index, low, high):
    refs[0][index] = jnp.where(odd, low, high)
    if len(refs) == 2:
        refs[1][index] = jnp.where(odd, high, low)


def shift_y(plane, rows):
    lo, hi = rows
    at = iota2(plane.shape, 0)
    last = plane.shape[0] - 1
    upper = jnp.where(at == last, hi, pltpu.roll(plane, last, 0))
    lower = jnp.where(at == 0, lo, pltpu.roll(plane, 1, 0))
    return upper, lower


def shift_z(plane, column, first_z):
    at = iota2(plane.shape, 1)
    last = plane.shape[1] - 1
    lo = jnp.where(first_z, 0.0, column)
    hi = jnp.where(first_z, column, 0.0)
    upper = jnp.where(at == last, hi, pltpu.roll(plane, last, 1))
    lower = jnp.where(at == 0, lo, pltpu.roll(plane, 1, 1))
    return upper, lower


def send_columns(ref, x, planes, gz):
    depth = planes[0].shape[1]
    lanes = iota2((planes[0].shape[0], 128), 1)
    tile = None
    for field, plane in enumerate(planes):
        part = jnp.where(gz == 0, plane[:, depth - 128 :], plane[:, :128])
        part = pltpu.roll(part, field + 1 - gz, 1)
        tile = part if tile is None else jnp.where(lanes == field, part, tile)
    ref[x] = tile


def folded(values):
    total = None
    for start in range(0, values.shape[1], 128):
        part = values[:, start : start + 128]
        total = part if total is None else total + part
    out = None
    for start in range(0, values.shape[0], 8):
        part = total[start : start + 8]
        out = part if out is None else out + part
    return out


def by_label(labels, scalars):
    picked = scalars[0]
    for region in range(1, len(scalars)):
        picked = jnp.where(labels == region, scalars[region], picked)
    return picked


def unrolled(count, many, body, carry):
    def several(block, carry):
        for at in range(many):
            carry = body(block * many + at, carry)
        return carry

    return lax.fori_loop(0, count // many, several, carry)


def pack_kernel(n_y, pos, disp, damage, *refs):
    ys, zs = refs[:n_y], refs[n_y]
    odd_y, gz = pos[1] == 1, pos[2]

    def body(x, carry):
        planes = [disp[0, x], disp[1, x], disp[2, x], damage[x]]
        for field, plane in enumerate(planes):
            last = plane.shape[0] - 1
            spot = (field, pl.ds(x, 1), slice(None))
            send(odd_y, ys, spot, plane[0:1], plane[last : last + 1])
        send_columns(zs, x, planes, gz)
        return carry

    unrolled(damage.shape[0], 8, body, 0)


def pack_x_kernel(pos, disp, damage, after, *xs):
    odd_x, count = pos[0] == 1, damage.shape[0]
    for field, src in enumerate((disp.at[0], disp.at[1], disp.at[2], damage)):
        send(odd_x, xs, field, src[0], src[count - 1])


def row_tile(v, rd, is_high):
    rows = v.shape[0]
    part = slice(rows - 8, rows) if is_high else slice(0, 8)
    at = iota2((8, v.shape[1]), 0)
    keep = at >= 4 if is_high else at < 4
    return jnp.where(keep, v[part], pltpu.roll(rd[part], 4, 0))


class Local:
    def __init__(self, pos, table, disp, damage, history, notch, labels, yg, zg):
        self.odd_x, self.odd_y, self.gz = pos[0] == 1, pos[1] == 1, pos[2]
        self.disp, self.damage, self.history = disp, damage, history
        self.notch, self.labels, self.yg, self.zg = notch, labels, yg, zg
        regions = range(table.shape[1])
        self.lames = [table[0, r] for r in regions]
        self.shears = [table[1, r] for r in regions]
        self.bases = [table[3, r] for r in regions]

    def plane(self, x, lower, upper, put):
        lab = self.labels[x]
        shear = by_label(lab, self.shears)
        dmg = self.damage[x]
        degrade = 4.0 * ((1.0 - dmg) * (1.0 - dmg) + STIFF_FLOOR)
        half = degrade * shear
        fields = [self.disp[c, x] for c in range(3)]

        def d(c, j):
            if j == 0:
                return upper(c) - lower(c)
            if j == 1:
                rows = low_high(self.odd_y, [y[c, pl.ds(x, 1), :] for y in self.yg])
                high, low = shift_y(fields[c], rows)
            else:
                column = self.zg[x][:, c : c + 1]
                high, low = shift_z(fields[c], column, self.gz == 0)
            return high - low

        squares = None
        for k, (i, j) in ((3, (0, 1)), (4, (0, 2)), (5, (1, 2))):
            e = d(i, j) + d(j, i)
            put(k, half * e)
            squares = e * e if squares is None else squares + e * e
        straight = [d(c, c) for c in range(3)]
        trace = straight[0] + straight[1] + straight[2]
        lame = by_label(lab, self.lames)
        level = (degrade * lame) * trace
        whole = half + half
        for k in range(3):
            put(k, level + whole * straight[k])
        twice = (
            straight[0] * straight[0] + straight[1] * straight[1] + straight[2] * straight[2]
        )
        squares = squares + (twice + twice)
        positive = jnp.maximum(trace, 0.0)
        energy = lame * positive * positive + shear * squares
        hist = jnp.maximum(
            jnp.maximum(self.history[x], energy), NOTCH_LOAD * self.notch[x].astype(F32)
        )
        diagonal = by_label(lab, self.bases) + 2.0 * hist
        rd = 1.0 / diagonal
        rows = low_high(self.odd_y, [y[3, pl.ds(x, 1), :] for y in self.yg])
        yu, yl = shift_y(dmg, rows)
        zu, zl = shift_z(dmg, self.zg[x][:, 3:4], self.gz == 0)
        near = ((upper(3) + lower(3)) + (yu + yl)) + (zu + zl)
        residual = 2.0 * hist - (diagonal * dmg - KAPPA_COEF * near)
        v = residual * rd
        return hist, rd, v, folded(residual * v)

    def send_y(self, ys, x, v, rd, stress):
        count = self.damage.shape[0]
        tall, last = count // 8, v.shape[0] - 1
        send(self.odd_y, ys, x, row_tile(v, rd, False), row_tile(v, rd, True))
        for c, k in enumerate((3, 1, 5)):
            spot = (count + c * tall + lax.div(x, 8), pl.ds(lax.rem(x, 8), 1), slice(None))
            send(self.odd_y, ys, spot, stress[k][0:1], stress[k][last : last + 1])

    def send_z(self, zs, x, stress):
        send_columns(zs, x, [stress[4], stress[5], stress[2]], self.gz)


def inner_steps(count):
    inner = count - 2
    many = max(m for m in range(1, 8) if inner % m == 0)
    return inner // many, many


def inner_kernel(n_y, pos, table, disp, damage, history, notch, labels, *refs):
    local = Local(
        pos, table, disp, damage, history, notch, labels, refs[:n_y], refs[n_y]
    )
    hist_hbm, rd_out, v_out, stress_out, mom_out = refs[n_y + 1 : n_y + 6]
    ys, (zs, hist, sems) = refs[n_y + 6 : 2 * n_y + 6], refs[2 * n_y + 6 :]
    steps, many = inner_steps(damage.shape[0])

    def store(step):
        part = pl.ds(1 + step * many, many)
        return pltpu.make_async_copy(hist.at[part], hist_hbm.at[part], sems.at[step])

    def several(step, total):
        for at in range(many):
            x = 1 + step * many + at

            def lower(c):
                return damage[x - 1] if c == 3 else disp[c, x - 1]

            def upper(c):
                return damage[x + 1] if c == 3 else disp[c, x + 1]

            stress = {}

            def put(k, plane):
                stress[k] = stress_out[k, x] = plane

            hist_x, rd, v, part = local.plane(x, lower, upper, put)
            hist[x] = hist_x
            rd_out[x] = rd
            v_out[x] = v
            local.send_y(ys, x, v, rd, stress)
            local.send_z(zs, x, stress)
            total = total + part
        store(step).start()
        return total

    mom_out[...] = lax.fori_loop(0, steps, several, jnp.zeros((8, 128), F32))
    for step in range(steps):
        store(step).wait()


def ends_kernel(n_y, pos, table, disp, damage, history, notch, labels, *refs):
    local = Local(
        pos, table, disp, damage, history, notch, labels, refs[:n_y], refs[n_y]
    )
    refs = refs[n_y + 1 :]
    xg, (_, rd_in, v_in, mom), ys_in, zs_in = (
        refs[:2],
        refs[2:6],
        refs[6 : 6 + n_y],
        refs[6 + n_y],
    )
    refs = refs[7 + n_y :]
    hist_hbm, rd_out, v_out, stress_out, mom_out = refs[:5]
    xs, ys, (zs, hist, sems) = refs[5:7], refs[7 : 7 + n_y], refs[7 + n_y :]
    odd_x, count = local.odd_x, damage.shape[0]
    total = mom[...]
    copies, found = [], []
    for end, x in enumerate((0, count - 1)):

        def outside(c):
            first, second = xg[0][c], xg[1][c]
            if end == 0:
                return jnp.where(odd_x, first, second)
            return jnp.where(odd_x, second, first)

        def beside(c):
            at = 1 if end == 0 else count - 2
            return damage[at] if c == 3 else disp[c, at]

        sides = (outside, beside) if end == 0 else (beside, outside)
        stress = {}

        def put(k, plane):
            stress[k] = stress_out[k, end] = plane

        hist_x, rd, v, part = local.plane(x, *sides, put)
        hist[end] = hist_x
        copies.append(pltpu.make_async_copy(hist.at[end], hist_hbm.at[x], sems.at[end]))
        copies[-1].start()
        rd_out[x] = rd
        v_out[x] = v
        total = total + part
        found.append((stress, rd, v))
    tall = count // 8
    for mine, before in zip(ys, ys_in, strict=True):
        for x in [*range(1, count - 1), *range(count, count + 3 * tall)]:
            mine[x] = before[x]
    for x in range(1, count - 1):
        rd_out[x] = rd_in[x]
        v_out[x] = v_in[x]
        zs[x] = zs_in[x]
    for end, x in enumerate((0, count - 1)):
        stress, rd, v = found[end]
        local.send_y(ys, x, v, rd, stress)
        local.send_z(zs, x, stress)
    for depth in (1, 2, 3):
        low, high = depth - 1, count - depth
        send(odd_x, xs, depth - 1, v_out[low], v_out[high])
        if depth <= 2:
            send(odd_x, xs, 2 + depth, rd_out[low], rd_out[high])
    for slot, k in ((5, 0), (6, 3), (7, 4)):
        send(odd_x, xs, slot, stress_out[k, 0], stress_out[k, 1])
    mom_out[...] = jnp.zeros((8, 128), F32)
    mom_out[0:1, :] = jnp.sum(total, axis=0, keepdims=True)
    for copy in copies:
        copy.wait()


def corner_kernel(n_y, pos, after, *refs):
    ys, ds = refs[:n_y], refs[n_y:]
    odd_x, count = pos[0] == 1, after.shape[0]
    for which in range(n_y):
        for depth in (1, 2):
            pair = (ds[which], ds[n_y + which])
            send(odd_x, pair, depth - 1, ys[which][depth - 1], ys[which][count - depth])


class Enlarged:
    def __init__(self, n_y, pos, v, rd, refs):
        self.odd_x, self.odd_y = pos[0] == 1, pos[1] == 1
        self.v, self.rd, self.n_y = v, rd, n_y
        self.xg, self.yg, self.dg = refs[:2], refs[2 : 2 + n_y], refs[2 + n_y : 2 + 3 * n_y]

    def rows(self, tiles):
        at = iota2(tiles[0].shape, 0)
        if self.n_y == 1:
            keep = lax.shift_right_logical(at, 2) == self.odd_y.astype(jnp.int32)
            tile = tiles[0]
            return jnp.where(keep, tile, 0.0), jnp.where(keep, pltpu.roll(tile, 4, 0), 0.0)
        lo, hi = low_high(self.odd_y, tiles)
        tile = jnp.where(at >= 4, lo, hi)
        moved = jnp.where(at >= 4, pltpu.roll(lo, 4, 0), pltpu.roll(hi, 4, 0))
        return tile, moved

    def own(self, x):
        v_rows, rd_rows = self.rows([y[x] for y in self.yg])
        return self.v[x], v_rows, self.rd[x], rd_rows

    def halo(self, is_low, depth):
        first, second = (0, 1) if is_low else (1, 0)

        def of(a, b):
            return jnp.where(self.odd_x, (a, b)[first], (a, b)[second])

        v = of(self.xg[0][depth - 1], self.xg[1][depth - 1])
        nothing = jnp.zeros((8, v.shape[1]), F32)
        if depth > 2:
            return v, nothing, jnp.zeros_like(v), nothing
        rd = of(self.xg[0][2 + depth], self.xg[1][2 + depth])
        tiles = [
            of(self.dg[w][depth - 1], self.dg[self.n_y + w][depth - 1]) for w in range(self.n_y)
        ]
        v_rows, rd_rows = self.rows(tiles)
        return v, v_rows, rd, rd_rows

    def outer(self, count):
        for depth in (1, 2, 3):
            yield -depth, self.halo(True, depth)
            yield count - 1 + depth, self.halo(False, depth)


def join_kernel(n_y, pos, v, rd, token, *refs):
    big = Enlarged(n_y, pos, v, rd, refs[:-1])
    out = refs[-1]
    first_z = pos[2] == 0
    count, ny, depth = v.shape

    def tile(v_part, rd_part):
        lanes = iota2((v_part.shape[0], 128), 1)
        keep = lax.shift_right_logical(lanes, 6) == 1 - pos[2]
        mine = jnp.where(first_z, v_part[:, depth - 128 :], v_part[:, :128])
        moved = jnp.where(first_z, rd_part[:, depth - 128 :], rd_part[:, :128])
        return jnp.where(keep, mine, pltpu.roll(moved, 64, 1))

    def put(p, parts):
        v_own, v_rows, rd_own, rd_rows = parts
        out[p + 3, 0:ny] = tile(v_own, rd_own)
        out[p + 3, ny : ny + 8] = tile(v_rows, rd_rows)

    for p, parts in big.outer(count):
        put(p, parts)

    def body(x, carry):
        put(x, big.own(x))
        return carry

    unrolled(count, 8, body, 0)


def krylov_kernel(pos, main_v, main_rd, mom, z_got, *refs):
    v1_out, v2_out, spread, z_v, z_rd, big_v1, big_v2 = refs
    count, ny, nz = v1_out.shape

    def split(p, carry):
        tile = z_got[p]
        keep = lax.shift_right_logical(iota2(tile.shape, 1), 6) == pos[2]
        z_v[p] = jnp.where(keep, tile, 0.0)
        z_rd[p] = jnp.where(keep, pltpu.roll(tile, 64, 1), 0.0)
        return carry

    unrolled(count + 6, 11 if count % 11 == 5 else 1, split, 0)

    def v_at(at):
        return jnp.concatenate([main_v[at], z_v[at]], axis=1)

    def rd_at(at):
        return jnp.concatenate([main_rd[at], z_rd[at]], axis=1)

    def image_of(get, at):
        plane = get(at)
        rows, lanes = plane.shape
        near = (get(at - 1) + get(at + 1)) + (pltpu.roll(plane, 1, 0) + pltpu.roll(plane, rows - 1, 0))
        near = near + (pltpu.roll(plane, 1, 1) + pltpu.roll(plane, lanes - 1, 1))
        return plane, KAPPA_COEF * near

    def v1_at(at):
        return big_v1[at]

    def v2_at(at):
        return big_v2[at]

    def inside(values):
        return folded(values[0:ny, 0:nz])

    def first(x, totals):
        plane, image = image_of(v_at, x + 3)
        made = image * rd_at(x + 3)
        big_v1[x + 2] = made
        v1_out[x] = made[0:ny, 0:nz]
        return totals[0] + inside(plane * image), totals[1] + inside(made * image)

    def second(x, totals):
        plane, image = image_of(v1_at, x + 2)
        made = image * rd_at(x + 3)
        big_v2[x + 1] = made
        v2_out[x] = made[0:ny, 0:nz]
        return totals[0] + inside(plane * image), totals[1] + inside(made * image)

    def third(x, total):
        plane, image = image_of(v2_at, x + 1)
        return total + folded(plane[0:ny, 0:nz] * image[0:ny, 0:nz])

    zero = jnp.zeros((8, 128), F32)
    for p in (-2, -1, count, count + 1):
        big_v1[p + 2] = image_of(v_at, p + 3)[1] * rd_at(p + 3)
    k1, k2 = unrolled(count, 8, first, (zero, zero))
    for p in (-1, count):
        big_v2[p + 1] = image_of(v1_at, p + 2)[1] * rd_at(p + 3)
    k3, k4 = unrolled(count, 8, second, (zero, zero))
    k5 = unrolled(count, 8, third, zero)
    rows = iota2((8, 128), 0)
    result = mom[...]
    for at, total in enumerate((k1, k2, k3, k4, k5)):
        result = jnp.where(rows == at + 1, jnp.sum(total, axis=0, keepdims=True), result)
    for peer in range(spread.shape[0]):
        spread[peer] = result


PARTS = ((0, 3, 4), (3, 1, 5), (4, 5, 2))


class Force:
    def __init__(self, n_y, pos, table, impact, disp, vel, contact, labels, yg, zg):
        self.odd_x, self.odd_y, self.gz = pos[0] == 1, pos[1] == 1, pos[2]
        self.impact, self.disp, self.vel = impact, disp, vel
        self.contact, self.labels, self.yg, self.zg = contact, labels, yg, zg
        self.rates = [table[2, r] for r in range(table.shape[1])]

    def plane(self, x, lower, mine, upper, vel_out, disp_out, at):
        count = self.contact.shape[0]
        tall = count // 8
        loaded = self.contact[x].astype(F32)
        rate = by_label(self.labels[x], self.rates)
        for c, (kx, ky, kz) in enumerate(PARTS):
            spot = (count + c * tall + lax.div(x, 8), pl.ds(lax.rem(x, 8), 1), slice(None))
            rows = low_high(self.odd_y, [y[spot] for y in self.yg])
            column = self.zg[x][:, c : c + 1]
            yu, yl = shift_y(mine(ky), rows)
            zu, zl = shift_z(mine(kz), column, self.gz == 0)
            force = 0.5 * (((upper(c, kx) - lower(c, kx)) + (yu - yl)) + (zu - zl))
            speed = self.vel[c, x] + rate * (force + loaded * self.impact[c])
            vel_out[c, at] = speed
            disp_out[c, at] = self.disp[c, x] + TIME_STEP * speed


def force_inner_kernel(n_y, pos, table, impact, disp, vel, contact, labels, *refs):
    yg, zg, stress, ends = refs[:n_y], refs[n_y], refs[n_y + 1], refs[n_y + 2]
    disp_hbm, vel_hbm, token, disp_out, vel_out, sems = refs[n_y + 3 :]
    token[...] = jnp.zeros((8, 128), F32)
    force = Force(n_y, pos, table, impact, disp, vel, contact, labels, yg, zg)
    count = contact.shape[0]
    steps, many = inner_steps(count)

    def stores(step):
        part = pl.ds(1 + step * many, many)
        return (
            pltpu.make_async_copy(disp_out.at[:, part], disp_hbm.at[:, part], sems.at[step, 0]),
            pltpu.make_async_copy(vel_out.at[:, part], vel_hbm.at[:, part], sems.at[step, 1]),
        )

    def several(step, carry):
        for at in range(many):
            x = 1 + step * many + at

            def lower(c, k):
                if at == 0:
                    return jnp.where(step == 0, ends[k, 0], stress[k, x - 1])
                return stress[k, x - 1]

            def upper(c, k):
                if at == many - 1:
                    return jnp.where(step == steps - 1, ends[k, 1], stress[k, x + 1])
                return stress[k, x + 1]

            force.plane(x, lower, lambda k: stress[k, x], upper, vel_out, disp_out, x)
        for copy in stores(step):
            copy.start()
        return carry

    lax.fori_loop(0, steps, several, 0)
    for step in range(steps):
        for copy in stores(step):
            copy.wait()


def rest_kernel(n_y, pos, table, impact, disp, vel, contact, labels, *refs):
    yg, zg, stress, ends = refs[:n_y], refs[n_y], refs[n_y + 1], refs[n_y + 2]
    refs = refs[n_y + 3 :]
    v, rd, xy = refs[0], refs[1], refs[2 : 4 + 3 * n_y]
    xg = xy[:2]
    disp_hbm, vel_hbm, big_v, big_rd, disp_out, vel_out, sems = refs[6 + 3 * n_y :]
    force = Force(n_y, pos, table, impact, disp, vel, contact, labels, yg, zg)
    count, ny = contact.shape[0], contact.shape[1]
    copies = []
    for end, x in enumerate((0, count - 1)):

        def outside(c, k):
            first, second = xg[0][5 + c], xg[1][5 + c]
            if end == 0:
                return jnp.where(force.odd_x, first, second)
            return jnp.where(force.odd_x, second, first)

        def beside(c, k):
            return stress[k, 1 if end == 0 else count - 2]

        lower, upper = (outside, beside) if end == 0 else (beside, outside)
        force.plane(x, lower, lambda k: ends[k, end], upper, vel_out, disp_out, end)
        for which, (src, dst) in enumerate(((disp_out, disp_hbm), (vel_out, vel_hbm))):
            copy = pltpu.make_async_copy(src.at[:, end], dst.at[:, x], sems.at[end, which])
            copy.start()
            copies.append(copy)
    big = Enlarged(n_y, pos, v, rd, xy)

    def put(p, parts):
        v_own, v_rows, rd_own, rd_rows = parts
        big_v[p + 3, 0:ny] = v_own
        big_v[p + 3, ny : ny + 8] = v_rows
        big_rd[p + 3, 0:ny] = rd_own
        big_rd[p + 3, ny : ny + 8] = rd_rows

    for p, parts in big.outer(count):
        put(p, parts)

    def body(x, carry):
        put(x, big.own(x))
        return carry

    unrolled(count, 4, body, 0)
    for copy in copies:
        copy.wait()


def cg_coefficients(k):
    zero, one = jnp.zeros_like(k[0]), jnp.ones_like(k[0])
    z, p, out = [one], [one], [zero, zero, zero]

    def form(a, b, moments):
        total = None
        for i, ai in enumerate(a):
            for j, bj in enumerate(b):
                term = ai * bj * moments[i + j]
                total = term if total is None else total + term
        return total

    energy = [k[j] - k[j + 1] for j in range(5)]
    rz = k[0]
    for step in range(3):
        alpha = jnp.clip(rz / form(p, p, energy), ALPHA_LOW, ALPHA_HIGH)
        out = [o + alpha * (p[i] if i < len(p) else zero) for i, o in enumerate(out)]
        if step == 2:
            break
        image = [(p[i] if i < len(p) else zero) - (p[i - 1] if i else zero) for i in range(len(p) + 1)]
        z = [(z[i] if i < len(z) else zero) - alpha * image[i] for i in range(len(image))]
        new = jnp.maximum(form(z, z, k), 0.0)
        beta = new / rz
        p = [z[i] + beta * (p[i] if i < len(p) else zero) for i in range(len(z))]
        rz = new
    return out


def final_kernel(mom, v0, v1, v2, damage_hbm, out_hbm, damage, out, in_sems, out_sems):
    count = v0.shape[0]
    block = count // CHUNKS
    loads, stores = [], []
    for chunk in range(CHUNKS):
        part = pl.ds(chunk * block, block)
        loads.append(pltpu.make_async_copy(damage_hbm.at[part], damage.at[part], in_sems.at[chunk]))
        stores.append(pltpu.make_async_copy(out.at[part], out_hbm.at[part], out_sems.at[chunk]))
        loads[-1].start()
    sums = jnp.sum(jnp.sum(mom[...], axis=0), axis=1, keepdims=True)
    c0, c1, c2 = cg_coefficients([sums[j : j + 1, :] for j in range(6)])
    for chunk in range(CHUNKS):
        loads[chunk].wait()
        for x in range(chunk * block, (chunk + 1) * block):
            dmg = damage[x]
            out[x] = jnp.maximum(dmg + (c0 * v0[x] + c1 * v1[x] + c2 * v2[x]), dmg)
        stores[chunk].start()
    for store in stores:
        store.wait()


def pairs_of(axis):
    count = lax.axis_size(axis)
    out = [[(i, i + 1) for i in range(start, count - 1, 2)] for start in (0, 1)]
    return [pairs for pairs in out if pairs]


def swap(array, axis, pairs):
    return lax.ppermute(array, axis, pairs + [(b, a) for a, b in pairs])


def swap_along(axis, arrays):
    return [swap(a, axis, pairs) for a, pairs in zip(arrays, pairs_of(axis), strict=True)]


def swap_diagonal(arrays):
    columns = lax.axis_size("gy")
    out = []
    both = [(xp, yp) for xp in pairs_of("gx") for yp in pairs_of("gy")]
    for array, (x_pairs, y_pairs) in zip(arrays, both, strict=True):
        joint = []
        for a, b in x_pairs:
            for c, d in y_pairs:
                joint.append((a * columns + c, b * columns + d))
                joint.append((a * columns + d, b * columns + c))
        out.append(swap(array, ("gx", "gy"), joint))
    return out


def spec_of(kind, a):
    if kind == "s":
        return pl.BlockSpec(memory_space=pltpu.SMEM)
    if kind == "v":
        return pl.BlockSpec(memory_space=pltpu.VMEM)
    if kind == "h":
        return pl.BlockSpec(memory_space=pltpu.HBM)
    if kind == "a":
        return pl.BlockSpec(memory_space=pl.ANY)
    raise ValueError(kind)


def call(kernel, kinds, ins, out_kinds, outs, flops, scratch=(), aliases=()):
    moved = sum(4 * a.size for a in (*ins, *outs))
    return pl.pallas_call(
        kernel,
        out_shape=outs,
        in_specs=[spec_of(k, a) for k, a in zip(kinds, ins, strict=True)],
        out_specs=[spec_of(k, a) for k, a in zip(out_kinds, outs, strict=True)],
        scratch_shapes=scratch,
        input_output_aliases=dict(aliases),
        compiler_params=pltpu.CompilerParams(vmem_limit_bytes=VMEM_BYTES),
        cost_estimate=pl.CostEstimate(flops=flops, bytes_accessed=moved, transcendentals=0),
    )(*ins)


def per_device(displacement, velocity, damage, history, contact, notch, labels, table, impact):
    nx, ny, nz = damage.shape
    size = damage.size
    n_y = len(pairs_of("gy"))
    pos = jnp.stack(
        [lax.axis_index("gx") % 2, lax.axis_index("gy") % 2, lax.axis_index("gz")]
    ).astype(jnp.int32)

    scaled = jnp.stack(
        [table[0] / 8.0, table[1] / 8.0, TIME_STEP / table[2], table[3] + 6.0 * KAPPA_COEF]
    )

    def arr(*shape):
        return jax.ShapeDtypeStruct(shape, F32)

    field, fields3, small = arr(nx, ny, nz), arr(3, nx, ny, nz), arr(8, 128)
    columns = arr(nx, ny, 128)
    z_pairs = [(0, 1)]

    sent = call(
        functools.partial(pack_kernel, n_y),
        "svv",
        (pos, displacement, damage),
        "v" * (1 + n_y),
        [*[arr(4, nx, nz)] * n_y, columns],
        size,
    )
    got_yz = [*swap_along("gy", sent[:n_y]), swap(sent[-1], "gz", z_pairs)]
    sent_x = call(
        pack_x_kernel,
        "svva",
        (pos, displacement, damage, sent[-1]),
        "vv",
        [arr(4, ny, nz)] * 2,
        size,
    )
    got_x = swap_along("gx", sent_x)
    rows = [arr(nx + 3 * (nx // 8), 8, nz)] * n_y
    voxels = (pos, scaled, displacement, damage, history, notch, labels, *got_yz)
    hist, rd, v0, stress, mom, *sent = call(
        functools.partial(inner_kernel, n_y),
        "ssvvvvv" + "v" * (1 + n_y),
        voxels,
        "hvvvv" + "v" * (1 + n_y),
        [field, field, field, arr(6, nx, ny, nz), small, *rows, columns],
        140 * size,
        [pltpu.VMEM((nx, ny, nz), F32), pltpu.SemaphoreType.DMA((inner_steps(nx)[0],))],
    )
    more = (*got_x, hist, rd, v0, mom, *sent)
    hist, rd, v0, ends, mom, *sent = call(
        functools.partial(ends_kernel, n_y),
        "ssvvvvv" + "v" * (1 + n_y) + "vvhvvv" + "v" * (1 + n_y),
        (*voxels, *more),
        "hvvvv" + "v" * (3 + n_y),
        [
            field,
            field,
            field,
            arr(6, 2, ny, nz),
            small,
            *[arr(8, ny, nz)] * 2,
            *rows,
            columns,
        ],
        20 * size,
        [pltpu.VMEM((2, ny, nz), F32), pltpu.SemaphoreType.DMA((2,))],
        [(len(voxels) + 2, 0)],
    )
    stress_z = swap(sent[-1], "gz", z_pairs)
    xs = swap_along("gx", sent[:2])
    ys = swap_along("gy", sent[2 : 2 + n_y])
    corners = call(
        functools.partial(corner_kernel, n_y),
        "sa" + "v" * n_y,
        (pos, stress_z, *sent[2 : 2 + n_y]),
        "v" * (2 * n_y),
        [arr(2, 8, nz)] * (2 * n_y),
        1024,
    )
    xy = [*xs, *ys, *swap_diagonal(corners)]
    moving = (
        pos,
        scaled,
        impact,
        displacement,
        velocity,
        contact,
        labels,
        *ys,
        stress_z,
        stress,
        ends,
    )
    new_disp, new_vel, token = call(
        functools.partial(force_inner_kernel, n_y),
        "sssvvvv" + "v" * (3 + n_y),
        moving,
        "hhv",
        [fields3, fields3, small],
        55 * size,
        [
            pltpu.VMEM((3, nx, ny, nz), F32),
            pltpu.VMEM((3, nx, ny, nz), F32),
            pltpu.SemaphoreType.DMA((inner_steps(nx)[0], 2)),
        ],
    )
    (joined,) = call(
        functools.partial(join_kernel, n_y),
        "svva" + "v" * len(xy),
        (pos, v0, rd, token, *xy),
        "v",
        [arr(nx + 6, ny + 8, 128)],
        4 * size,
    )
    z_got = swap(joined, "gz", z_pairs)
    new_disp, new_vel, main_v, main_rd = call(
        functools.partial(rest_kernel, n_y),
        "sssvvvv" + "v" * (3 + n_y) + "vv" + "v" * len(xy) + "hh",
        (*moving, v0, rd, *xy, new_disp, new_vel),
        "hhvv",
        [fields3, fields3, *[arr(nx + 6, ny + 8, nz)] * 2],
        12 * size,
        [
            pltpu.VMEM((3, 2, ny, nz), F32),
            pltpu.VMEM((3, 2, ny, nz), F32),
            pltpu.SemaphoreType.DMA((2, 2)),
        ],
        [(len(moving) + 2 + len(xy), 0), (len(moving) + 3 + len(xy), 1)],
    )
    peers = lax.axis_size("gx") * lax.axis_size("gy") * lax.axis_size("gz")
    v1, v2, spread = call(
        krylov_kernel,
        "svvvv",
        (pos, main_v, main_rd, mom, z_got),
        "vvv",
        [field, field, arr(peers, 8, 128)],
        60 * size,
        [
            pltpu.VMEM((nx + 6, ny + 8, 128), F32),
            pltpu.VMEM((nx + 6, ny + 8, 128), F32),
            pltpu.VMEM((nx + 4, ny + 8, nz + 128), F32),
            pltpu.VMEM((nx + 2, ny + 8, nz + 128), F32),
        ],
    )
    mom = lax.all_to_all(spread, ("gx", "gy", "gz"), 0, 0, tiled=True)
    (damage_new,) = call(
        final_kernel,
        "vvvvh",
        (mom, v0, v1, v2, damage),
        "h",
        [field],
        8 * size,
        [
            pltpu.VMEM((nx, ny, nz), F32),
            pltpu.VMEM((nx, ny, nz), F32),
            pltpu.SemaphoreType.DMA((CHUNKS,)),
            pltpu.SemaphoreType.DMA((CHUNKS,)),
        ],
    )
    return new_disp, new_vel, hist, damage_new


def solution(mesh):
    placed = (
        P(None, ("case", "gx"), "gy", "gz"),
        P(None, ("case", "gx"), "gy", "gz"),
        P(("case", "gx"), "gy", "gz"),
        P(("case", "gx"), "gy", "gz"),
        P(("case", "gx"), "gy", "gz"),
        P(("case", "gx"), "gy", "gz"),
        P(("case", "gx"), "gy", "gz"),
        P(),
        P("case"),
    )
    return jax.shard_map(
        per_device,
        mesh=mesh,
        in_specs=placed,
        out_specs=(
            P(None, ("case", "gx"), "gy", "gz"),
            P(None, ("case", "gx"), "gy", "gz"),
            P(("case", "gx"), "gy", "gz"),
            P(("case", "gx"), "gy", "gz"),
        ),
        check_vma=False,
    )
```

```python
import functools
import jax
import jax.numpy as jnp
from jax import lax
from jax.experimental import pallas as pl
from jax.experimental.pallas import tpu as pltpu
from jax.sharding import PartitionSpec as P

TIME_STEP = 0.1
KAPPA_COEF = 0.5
NOTCH_LOAD = 20.0
STIFF_FLOOR = 0.001
ALPHA_LOW, ALPHA_HIGH = 0.5, 6.5
VMEM_BYTES = 28 * 1024 * 1024
CHUNKS = 4
F32 = jnp.float32


def iota2(shape, dim):
    return lax.broadcasted_iota(jnp.int32, shape, dim)


def low_high(odd, got):
    if len(got) == 2:
        return jnp.where(odd, got[0], got[1]), jnp.where(odd, got[1], got[0])
    return jnp.where(odd, got[0], 0.0), jnp.where(odd, 0.0, got[0])


def send(odd, refs, index, low, high):
    refs[0][index] = jnp.where(odd, low, high)
    if len(refs) == 2:
        refs[1][index] = jnp.where(odd, high, low)


def shift_y(plane, rows):
    lo, hi = rows
    at = iota2(plane.shape, 0)
    last = plane.shape[0] - 1
    upper = jnp.where(at == last, hi, pltpu.roll(plane, last, 0))
    lower = jnp.where(at == 0, lo, pltpu.roll(plane, 1, 0))
    return upper, lower


def shift_z(plane, column, first_z):
    at = iota2(plane.shape, 1)
    last = plane.shape[1] - 1
    lo = jnp.where(first_z, 0.0, column)
    hi = jnp.where(first_z, column, 0.0)
    upper = jnp.where(at == last, hi, pltpu.roll(plane, last, 1))
    lower = jnp.where(at == 0, lo, pltpu.roll(plane, 1, 1))
    return upper, lower


def send_columns(ref, x, planes, gz, tile=None):
    depth = planes[0].shape[1]
    lanes = iota2((planes[0].shape[0], 128), 1)
    for field, plane in enumerate(planes):
        part = jnp.where(gz == 0, plane[:, depth - 128 :], plane[:, :128])
        part = pltpu.roll(part, field + 1 - gz, 1)
        tile = part if tile is None else jnp.where(lanes == field, part, tile)
    ref[x] = tile


def folded(values):
    total = None
    for start in range(0, values.shape[1], 128):
        part = values[:, start : start + 128]
        total = part if total is None else total + part
    out = None
    for start in range(0, values.shape[0], 8):
        part = total[start : start + 8]
        out = part if out is None else out + part
    return out


def by_label(labels, scalars):
    picked = scalars[0]
    for region in range(1, len(scalars)):
        picked = jnp.where(labels == region, scalars[region], picked)
    return picked


def unrolled(count, many, body, carry):
    def several(block, carry):
        for at in range(many):
            carry = body(block * many + at, carry)
        return carry

    return lax.fori_loop(0, count // many, several, carry)


def pack_damage_kernel(n_y, pos, damage, *refs):
    ys, zs = refs[:n_y], refs[n_y]
    odd_y, gz = pos[1] == 1, pos[2]

    def body(x, carry):
        plane = damage[x]
        last = plane.shape[0] - 1
        send(odd_y, ys, (pl.ds(x, 1), slice(None)), plane[0:1], plane[last : last + 1])
        send_columns(zs, x, [plane], gz)
        return carry

    unrolled(damage.shape[0], 8, body, 0)


def pack_kernel(n_y, pos, disp, *refs):
    ys_damage, zs_damage, ys, zs = (
        refs[:n_y],
        refs[n_y],
        refs[n_y + 1 : 2 * n_y + 1],
        refs[2 * n_y + 1],
    )
    odd_y, gz = pos[1] == 1, pos[2]
    for mine, before in zip(ys, ys_damage, strict=True):
        mine[3] = before[...]

    def body(x, carry):
        planes = [disp[0, x], disp[1, x], disp[2, x]]
        for field, plane in enumerate(planes):
            last = plane.shape[0] - 1
            spot = (field, pl.ds(x, 1), slice(None))
            send(odd_y, ys, spot, plane[0:1], plane[last : last + 1])
        send_columns(zs, x, planes, gz, pltpu.roll(zs_damage[x], 3, 1))
        return carry

    unrolled(disp.shape[1], 8, body, 0)


def pack_x_kernel(pos, disp, damage, after, *xs):
    odd_x, count = pos[0] == 1, damage.shape[0]
    for field, src in enumerate((disp.at[0], disp.at[1], disp.at[2], damage)):
        send(odd_x, xs, field, src[0], src[count - 1])


class Local:
    def __init__(self, pos, table, disp, damage, history, notch, labels, yg, zg):
        self.odd_x, self.odd_y, self.gz = pos[0] == 1, pos[1] == 1, pos[2]
        self.disp, self.damage, self.history = disp, damage, history
        self.notch, self.labels, self.yg, self.zg = notch, labels, yg, zg
        regions = range(table.shape[1])
        self.lames = [table[0, r] for r in regions]
        self.shears = [table[1, r] for r in regions]
        self.bases = [table[3, r] for r in regions]

    def plane(self, x, lower, upper, put):
        lab = self.labels[x]
        shear = by_label(lab, self.shears)
        dmg = self.damage[x]
        degrade = 4.0 * ((1.0 - dmg) * (1.0 - dmg) + STIFF_FLOOR)
        half = degrade * shear
        fields = [self.disp[c, x] for c in range(3)]

        def d(c, j):
            if j == 0:
                return upper(c) - lower(c)
            if j == 1:
                rows = low_high(self.odd_y, [y[c, pl.ds(x, 1), :] for y in self.yg])
                high, low = shift_y(fields[c], rows)
            else:
                column = self.zg[x][:, c : c + 1]
                high, low = shift_z(fields[c], column, self.gz == 0)
            return high - low

        squares = None
        for k, (i, j) in ((3, (0, 1)), (4, (0, 2)), (5, (1, 2))):
            e = d(i, j) + d(j, i)
            put(k, half * e)
            squares = e * e if squares is None else squares + e * e
        straight = [d(c, c) for c in range(3)]
        trace = straight[0] + straight[1] + straight[2]
        lame = by_label(lab, self.lames)
        level = (degrade * lame) * trace
        whole = half + half
        for k in range(3):
            put(k, level + whole * straight[k])
        twice = (
            straight[0] * straight[0] + straight[1] * straight[1] + straight[2] * straight[2]
        )
        squares = squares + (twice + twice)
        positive = jnp.maximum(trace, 0.0)
        energy = lame * positive * positive + shear * squares
        hist = jnp.maximum(
            jnp.maximum(self.history[x], energy), NOTCH_LOAD * self.notch[x].astype(F32)
        )
        diagonal = by_label(lab, self.bases) + 2.0 * hist
        rd = 1.0 / diagonal
        rows = low_high(self.odd_y, [y[3, pl.ds(x, 1), :] for y in self.yg])
        yu, yl = shift_y(dmg, rows)
        zu, zl = shift_z(dmg, self.zg[x][:, 3:4], self.gz == 0)
        near = ((upper(3) + lower(3)) + (yu + yl)) + (zu + zl)
        residual = 2.0 * hist - (diagonal * dmg - KAPPA_COEF * near)
        v = residual * rd
        return hist, rd, v, folded(residual * v)

    def send_y(self, ys, x, v, rd, stress):
        rows = v.shape[0]
        sources = [(v, depth) for depth in (1, 2, 3)] + [(rd, depth) for depth in (1, 2)]
        sources += [(stress[k], 1) for k in (3, 1, 5)]
        for slot, (plane, depth) in enumerate(sources):
            low, high = plane[depth - 1 : depth], plane[rows - depth : rows - depth + 1]
            send(self.odd_y, ys, (slot, pl.ds(x, 1), slice(None)), low, high)

    def send_z(self, zs, x, stress):
        send_columns(zs, x, [stress[4], stress[5], stress[2]], self.gz)


def inner_steps(count):
    inner = count - 2
    many = max(m for m in range(1, 8) if inner % m == 0)
    return inner // many, many


def inner_kernel(n_y, pos, table, disp, damage, history, notch, labels, *refs):
    local = Local(
        pos, table, disp, damage, history, notch, labels, refs[:n_y], refs[n_y]
    )
    hist_hbm, rd_out, v_out, stress_out, mom_out = refs[n_y + 1 : n_y + 6]
    ys, (zs, hist, sems) = refs[n_y + 6 : 2 * n_y + 6], refs[2 * n_y + 6 :]
    steps, many = inner_steps(damage.shape[0])

    def store(x):
        return pltpu.make_async_copy(hist.at[x], hist_hbm.at[x], sems.at[x])

    def several(step, total):
        for at in range(many):
            x = 1 + step * many + at

            def lower(c):
                return damage[x - 1] if c == 3 else disp[c, x - 1]

            def upper(c):
                return damage[x + 1] if c == 3 else disp[c, x + 1]

            stress = {}

            def put(k, plane):
                stress[k] = stress_out[k, x] = plane

            hist_x, rd, v, part = local.plane(x, lower, upper, put)
            hist[x] = hist_x
            rd_out[x] = rd
            v_out[x] = v
            local.send_y(ys, x, v, rd, stress)
            local.send_z(zs, x, stress)
            store(x).start()
            total = total + part
        return total

    mom_out[...] = lax.fori_loop(0, steps, several, jnp.zeros((8, 128), F32))
    for x in range(1, damage.shape[0] - 1):
        store(x).wait()


def ends_kernel(n_y, pos, table, disp, damage, history, notch, labels, *refs):
    local = Local(
        pos, table, disp, damage, history, notch, labels, refs[:n_y], refs[n_y]
    )
    refs = refs[n_y + 1 :]
    xg, (_, rd_in, v_in, mom), ys_in, zs_in = (
        refs[:2],
        refs[2:6],
        refs[6 : 6 + n_y],
        refs[6 + n_y],
    )
    refs = refs[7 + n_y :]
    hist_hbm, rd_out, v_out, stress_out, mom_out = refs[:5]
    xs, ys, (zs, hist, sems) = refs[5:7], refs[7 : 7 + n_y], refs[7 + n_y :]
    odd_x, count = local.odd_x, damage.shape[0]
    total = mom[...]
    copies, found = [], []
    for end, x in enumerate((0, count - 1)):

        def outside(c):
            first, second = xg[0][c], xg[1][c]
            if end == 0:
                return jnp.where(odd_x, first, second)
            return jnp.where(odd_x, second, first)

        def beside(c):
            at = 1 if end == 0 else count - 2
            return damage[at] if c == 3 else disp[c, at]

        sides = (outside, beside) if end == 0 else (beside, outside)
        stress = {}

        def put(k, plane):
            stress[k] = stress_out[k, end] = plane

        hist_x, rd, v, part = local.plane(x, *sides, put)
        hist[end] = hist_x
        copies.append(pltpu.make_async_copy(hist.at[end], hist_hbm.at[x], sems.at[end]))
        copies[-1].start()
        rd_out[x] = rd
        v_out[x] = v
        total = total + part
        found.append((stress, rd, v))
    for mine, before in zip(ys, ys_in, strict=True):
        for slot in range(8):
            mine[slot] = before[slot]
    for x in range(1, count - 1):
        rd_out[x] = rd_in[x]
        v_out[x] = v_in[x]
        zs[x] = zs_in[x]
    for end, x in enumerate((0, count - 1)):
        stress, rd, v = found[end]
        local.send_y(ys, x, v, rd, stress)
        local.send_z(zs, x, stress)
    for depth in (1, 2, 3):
        low, high = depth - 1, count - depth
        send(odd_x, xs, depth - 1, v_out[low], v_out[high])
        if depth <= 2:
            send(odd_x, xs, 2 + depth, rd_out[low], rd_out[high])
    for slot, k in ((5, 0), (6, 3), (7, 4)):
        send(odd_x, xs, slot, stress_out[k, 0], stress_out[k, 1])
    mom_out[...] = jnp.zeros((8, 128), F32)
    mom_out[0:1, :] = jnp.sum(total, axis=0, keepdims=True)
    for copy in copies:
        copy.wait()


def corner_kernel(n_y, pos, after, v, rd, *ds):
    odd_x, odd_y = pos[0] == 1, pos[1] == 1
    count, rows = v.shape[0], v.shape[1]
    for depth in (1, 2):
        for slot, (src, deep) in enumerate(((v, 1), (v, 2), (v, 3), (rd, 1), (rd, 2))):
            near, far = pl.ds(deep - 1, 1), pl.ds(rows - deep, 1)
            planes = (depth - 1, count - depth)
            by_y = [(src[x, near, :], src[x, far, :]) for x in planes]
            for which in range(n_y):
                pair = (ds[which], ds[n_y + which])
                picked = [
                    jnp.where(odd_y, *(rows_of if which == 0 else rows_of[::-1]))
                    for rows_of in by_y
                ]
                send(odd_x, pair, (depth - 1, pl.ds(slot, 1), slice(None)), *picked)


class Enlarged:
    def __init__(self, n_y, pos, v, rd, refs):
        self.odd_x, self.odd_y = pos[0] == 1, pos[1] == 1
        self.v, self.rd, self.n_y = v, rd, n_y
        self.xg, self.yg, self.dg = refs[:2], refs[2 : 2 + n_y], refs[2 + n_y : 2 + 3 * n_y]

    def rows(self, found):
        nz = self.v.shape[2]
        at = iota2((8, nz), 0)

        def tile(first, depths):
            out = jnp.zeros((8, nz), F32)
            for depth in range(1, depths + 1):
                got = [found(w, first + depth - 1) for w in range(self.n_y)]
                if self.n_y == 1:
                    spot = jnp.where(self.odd_y, 8 - depth, depth - 1)
                    out = jnp.where(at == spot, got[0], out)
                else:
                    lo, hi = low_high(self.odd_y, got)
                    out = jnp.where(at == depth - 1, hi, out)
                    out = jnp.where(at == 8 - depth, lo, out)
            return out

        return tile(0, 3), tile(3, 2)

    def own(self, x):
        v_rows, rd_rows = self.rows(lambda w, slot: self.yg[w][slot, pl.ds(x, 1), :])
        return self.v[x], v_rows, self.rd[x], rd_rows

    def halo(self, is_low, depth):
        first, second = (0, 1) if is_low else (1, 0)

        def of(a, b):
            return jnp.where(self.odd_x, (a, b)[first], (a, b)[second])

        v = of(self.xg[0][depth - 1], self.xg[1][depth - 1])
        nothing = jnp.zeros((8, v.shape[1]), F32)
        if depth > 2:
            return v, nothing, jnp.zeros_like(v), nothing
        rd = of(self.xg[0][2 + depth], self.xg[1][2 + depth])

        def found(w, slot):
            spot = (depth - 1, pl.ds(slot, 1), slice(None))
            return of(self.dg[w][spot], self.dg[self.n_y + w][spot])

        v_rows, rd_rows = self.rows(found)
        return v, v_rows, rd, rd_rows

    def outer(self, count):
        for depth in (1, 2, 3):
            yield -depth, self.halo(True, depth)
            yield count - 1 + depth, self.halo(False, depth)


def join_kernel(n_y, pos, v, rd, token, *refs):
    big = Enlarged(n_y, pos, v, rd, refs[:-1])
    out = refs[-1]
    first_z = pos[2] == 0
    count, ny, depth = v.shape

    def tile(v_part, rd_part):
        lanes = iota2((v_part.shape[0], 128), 1)
        keep = lax.shift_right_logical(lanes, 6) == 1 - pos[2]
        mine = jnp.where(first_z, v_part[:, depth - 128 :], v_part[:, :128])
        moved = jnp.where(first_z, rd_part[:, depth - 128 :], rd_part[:, :128])
        return jnp.where(keep, mine, pltpu.roll(moved, 64, 1))

    def put(p, parts):
        v_own, v_rows, rd_own, rd_rows = parts
        out[p + 3, 0:ny] = tile(v_own, rd_own)
        out[p + 3, ny : ny + 8] = tile(v_rows, rd_rows)

    for p, parts in big.outer(count):
        put(p, parts)

    def body(x, carry):
        put(x, big.own(x))
        return carry

    unrolled(count, 8, body, 0)


def krylov_kernel(pos, main_v, main_rd, mom, z_got, *refs):
    v1_out, v2_out, spread, z_v, z_rd, big_v1, big_v2 = refs
    count, ny, nz = v1_out.shape

    def split(p, carry):
        tile = z_got[p]
        keep = lax.shift_right_logical(iota2(tile.shape, 1), 6) == pos[2]
        z_v[p] = jnp.where(keep, tile, 0.0)
        z_rd[p] = jnp.where(keep, pltpu.roll(tile, 64, 1), 0.0)
        return carry

    unrolled(count + 6, 11 if count % 11 == 5 else 1, split, 0)

    def v_at(at):
        return jnp.concatenate([main_v[at], z_v[at]], axis=1)

    def rd_at(at):
        return jnp.concatenate([main_rd[at], z_rd[at]], axis=1)

    def image_of(get, at):
        plane = get(at)
        rows, lanes = plane.shape
        near = (get(at - 1) + get(at + 1)) + (pltpu.roll(plane, 1, 0) + pltpu.roll(plane, rows - 1, 0))
        near = near + (pltpu.roll(plane, 1, 1) + pltpu.roll(plane, lanes - 1, 1))
        return plane, KAPPA_COEF * near

    def v1_at(at):
        return big_v1[at]

    def v2_at(at):
        return big_v2[at]

    def inside(values):
        return folded(values[0:ny, 0:nz])

    def first(x, totals):
        plane, image = image_of(v_at, x + 3)
        made = image * rd_at(x + 3)
        big_v1[x + 2] = made
        v1_out[x] = made[0:ny, 0:nz]
        return totals[0] + inside(plane * image), totals[1] + inside(made * image)

    def second(x, totals):
        plane, image = image_of(v1_at, x + 2)
        made = image * rd_at(x + 3)
        big_v2[x + 1] = made
        v2_out[x] = made[0:ny, 0:nz]
        return totals[0] + inside(plane * image), totals[1] + inside(made * image)

    def third(x, total):
        plane, image = image_of(v2_at, x + 1)
        return total + folded(plane[0:ny, 0:nz] * image[0:ny, 0:nz])

    zero = jnp.zeros((8, 128), F32)
    for p in (-2, -1, count, count + 1):
        big_v1[p + 2] = image_of(v_at, p + 3)[1] * rd_at(p + 3)
    k1, k2 = unrolled(count, 8, first, (zero, zero))
    for p in (-1, count):
        big_v2[p + 1] = image_of(v1_at, p + 2)[1] * rd_at(p + 3)
    k3, k4 = unrolled(count, 8, second, (zero, zero))
    k5 = unrolled(count, 8, third, zero)
    rows = iota2((8, 128), 0)
    result = mom[...]
    for at, total in enumerate((k1, k2, k3, k4, k5)):
        result = jnp.where(rows == at + 1, jnp.sum(total, axis=0, keepdims=True), result)
    for peer in range(spread.shape[0]):
        spread[peer] = result


PARTS = ((0, 3, 4), (3, 1, 5), (4, 5, 2))


class Force:
    def __init__(self, n_y, pos, table, impact, disp, vel, contact, labels, yg, zg):
        self.odd_x, self.odd_y, self.gz = pos[0] == 1, pos[1] == 1, pos[2]
        self.impact, self.disp, self.vel = impact, disp, vel
        self.contact, self.labels, self.yg, self.zg = contact, labels, yg, zg
        self.rates = [table[2, r] for r in range(table.shape[1])]

    def plane(self, x, lower, mine, upper, vel_out, disp_out, at):
        loaded = self.contact[x].astype(F32)
        rate = by_label(self.labels[x], self.rates)
        for c, (kx, ky, kz) in enumerate(PARTS):
            rows = low_high(self.odd_y, [y[5 + c, pl.ds(x, 1), :] for y in self.yg])
            column = self.zg[x][:, c : c + 1]
            yu, yl = shift_y(mine(ky), rows)
            zu, zl = shift_z(mine(kz), column, self.gz == 0)
            force = 0.5 * (((upper(c, kx) - lower(c, kx)) + (yu - yl)) + (zu - zl))
            speed = self.vel[c, x] + rate * (force + loaded * self.impact[c])
            vel_out[c, at] = speed
            disp_out[c, at] = self.disp[c, x] + TIME_STEP * speed


def force_inner_kernel(n_y, pos, table, impact, disp, vel, contact, labels, *refs):
    yg, zg, stress, ends = refs[:n_y], refs[n_y], refs[n_y + 1], refs[n_y + 2]
    disp_hbm, vel_hbm, token, disp_out, vel_out, sems = refs[n_y + 3 :]
    token[...] = jnp.zeros((8, 128), F32)
    force = Force(n_y, pos, table, impact, disp, vel, contact, labels, yg, zg)
    count = contact.shape[0]
    steps, many = inner_steps(count)

    def stores(x):
        return (
            pltpu.make_async_copy(disp_out.at[:, x], disp_hbm.at[:, x], sems.at[x, 0]),
            pltpu.make_async_copy(vel_out.at[:, x], vel_hbm.at[:, x], sems.at[x, 1]),
        )

    def several(step, carry):
        for at in range(many):
            x = 1 + step * many + at

            def lower(c, k):
                if at == 0:
                    return jnp.where(step == 0, ends[k, 0], stress[k, x - 1])
                return stress[k, x - 1]

            def upper(c, k):
                if at == many - 1:
                    return jnp.where(step == steps - 1, ends[k, 1], stress[k, x + 1])
                return stress[k, x + 1]

            force.plane(x, lower, lambda k: stress[k, x], upper, vel_out, disp_out, x)
            for copy in stores(x):
                copy.start()
        return carry

    lax.fori_loop(0, steps, several, 0)
    for x in range(1, count - 1):
        for copy in stores(x):
            copy.wait()


def rest_kernel(n_y, pos, table, impact, disp, vel, contact, labels, *refs):
    yg, zg, stress, ends = refs[:n_y], refs[n_y], refs[n_y + 1], refs[n_y + 2]
    refs = refs[n_y + 3 :]
    v, rd, xy = refs[0], refs[1], refs[2 : 4 + 3 * n_y]
    xg = xy[:2]
    disp_hbm, vel_hbm, big_v, big_rd, disp_out, vel_out, sems = refs[6 + 3 * n_y :]
    force = Force(n_y, pos, table, impact, disp, vel, contact, labels, yg, zg)
    count, ny = contact.shape[0], contact.shape[1]
    copies = []
    for end, x in enumerate((0, count - 1)):

        def outside(c, k):
            first, second = xg[0][5 + c], xg[1][5 + c]
            if end == 0:
                return jnp.where(force.odd_x, first, second)
            return jnp.where(force.odd_x, second, first)

        def beside(c, k):
            return stress[k, 1 if end == 0 else count - 2]

        lower, upper = (outside, beside) if end == 0 else (beside, outside)
        force.plane(x, lower, lambda k: ends[k, end], upper, vel_out, disp_out, end)
        for which, (src, dst) in enumerate(((disp_out, disp_hbm), (vel_out, vel_hbm))):
            copy = pltpu.make_async_copy(src.at[:, end], dst.at[:, x], sems.at[end, which])
            copy.start()
            copies.append(copy)
    big = Enlarged(n_y, pos, v, rd, xy)

    def put(p, parts):
        v_own, v_rows, rd_own, rd_rows = parts
        big_v[p + 3, 0:ny] = v_own
        big_v[p + 3, ny : ny + 8] = v_rows
        big_rd[p + 3, 0:ny] = rd_own
        big_rd[p + 3, ny : ny + 8] = rd_rows

    for p, parts in big.outer(count):
        put(p, parts)

    def body(x, carry):
        put(x, big.own(x))
        return carry

    unrolled(count, 4, body, 0)
    for copy in copies:
        copy.wait()


def cg_coefficients(k):
    zero, one = jnp.zeros_like(k[0]), jnp.ones_like(k[0])
    z, p, out = [one], [one], [zero, zero, zero]

    def form(a, b, moments):
        total = None
        for i, ai in enumerate(a):
            for j, bj in enumerate(b):
                term = ai * bj * moments[i + j]
                total = term if total is None else total + term
        return total

    energy = [k[j] - k[j + 1] for j in range(5)]
    rz = k[0]
    for step in range(3):
        alpha = jnp.clip(rz / form(p, p, energy), ALPHA_LOW, ALPHA_HIGH)
        out = [o + alpha * (p[i] if i < len(p) else zero) for i, o in enumerate(out)]
        if step == 2:
            break
        image = [(p[i] if i < len(p) else zero) - (p[i - 1] if i else zero) for i in range(len(p) + 1)]
        z = [(z[i] if i < len(z) else zero) - alpha * image[i] for i in range(len(image))]
        new = jnp.maximum(form(z, z, k), 0.0)
        beta = new / rz
        p = [z[i] + beta * (p[i] if i < len(p) else zero) for i in range(len(z))]
        rz = new
    return out


def final_kernel(mom, v0, v1, v2, damage_hbm, out_hbm, damage, out, in_sems, out_sems):
    count = v0.shape[0]
    block = count // CHUNKS
    loads, stores = [], []
    for chunk in range(CHUNKS):
        part = pl.ds(chunk * block, block)
        loads.append(pltpu.make_async_copy(damage_hbm.at[part], damage.at[part], in_sems.at[chunk]))
        stores.append(pltpu.make_async_copy(out.at[part], out_hbm.at[part], out_sems.at[chunk]))
        loads[-1].start()
    sums = jnp.sum(jnp.sum(mom[...], axis=0), axis=1, keepdims=True)
    c0, c1, c2 = cg_coefficients([sums[j : j + 1, :] for j in range(6)])
    for chunk in range(CHUNKS):
        loads[chunk].wait()
        for x in range(chunk * block, (chunk + 1) * block):
            dmg = damage[x]
            out[x] = jnp.maximum(dmg + (c0 * v0[x] + c1 * v1[x] + c2 * v2[x]), dmg)
        stores[chunk].start()
    for store in stores:
        store.wait()


def pairs_of(axis):
    count = lax.axis_size(axis)
    out = [[(i, i + 1) for i in range(start, count - 1, 2)] for start in (0, 1)]
    return [pairs for pairs in out if pairs]


def swap(array, axis, pairs):
    return lax.ppermute(array, axis, pairs + [(b, a) for a, b in pairs])


def swap_along(axis, arrays):
    return [swap(a, axis, pairs) for a, pairs in zip(arrays, pairs_of(axis), strict=True)]


def swap_diagonal(arrays):
    columns = lax.axis_size("gy")
    out = []
    both = [(xp, yp) for xp in pairs_of("gx") for yp in pairs_of("gy")]
    for array, (x_pairs, y_pairs) in zip(arrays, both, strict=True):
        joint = []
        for a, b in x_pairs:
            for c, d in y_pairs:
                joint.append((a * columns + c, b * columns + d))
                joint.append((a * columns + d, b * columns + c))
        out.append(swap(array, ("gx", "gy"), joint))
    return out


def spec_of(kind, a):
    if kind == "s":
        return pl.BlockSpec(memory_space=pltpu.SMEM)
    if kind == "v":
        return pl.BlockSpec(memory_space=pltpu.VMEM)
    if kind == "h":
        return pl.BlockSpec(memory_space=pltpu.HBM)
    if kind == "a":
        return pl.BlockSpec(memory_space=pl.ANY)
    raise ValueError(kind)


def call(kernel, kinds, ins, out_kinds, outs, flops, scratch=(), aliases=()):
    moved = sum(4 * a.size for a in (*ins, *outs))
    return pl.pallas_call(
        kernel,
        out_shape=outs,
        in_specs=[spec_of(k, a) for k, a in zip(kinds, ins, strict=True)],
        out_specs=[spec_of(k, a) for k, a in zip(out_kinds, outs, strict=True)],
        scratch_shapes=scratch,
        input_output_aliases=dict(aliases),
        compiler_params=pltpu.CompilerParams(vmem_limit_bytes=VMEM_BYTES),
        cost_estimate=pl.CostEstimate(flops=flops, bytes_accessed=moved, transcendentals=0),
    )(*ins)


def per_device(displacement, velocity, damage, history, contact, notch, labels, table, impact):
    nx, ny, nz = damage.shape
    size = damage.size
    n_y = len(pairs_of("gy"))
    pos = jnp.stack(
        [lax.axis_index("gx") % 2, lax.axis_index("gy") % 2, lax.axis_index("gz")]
    ).astype(jnp.int32)

    scaled = jnp.stack(
        [table[0] / 8.0, table[1] / 8.0, TIME_STEP / table[2], table[3] + 6.0 * KAPPA_COEF]
    )

    def arr(*shape):
        return jax.ShapeDtypeStruct(shape, F32)

    field, fields3, small = arr(nx, ny, nz), arr(3, nx, ny, nz), arr(8, 128)
    columns = arr(nx, ny, 128)
    z_pairs = [(0, 1)]

    sent = call(
        functools.partial(pack_damage_kernel, n_y),
        "sv",
        (pos, damage),
        "v" * (1 + n_y),
        [*[arr(nx, nz)] * n_y, columns],
        100 * size,
    )
    sent = call(
        functools.partial(pack_kernel, n_y),
        "sv" + "v" * (1 + n_y),
        (pos, displacement, *sent),
        "v" * (1 + n_y),
        [*[arr(4, nx, nz)] * n_y, columns],
        size,
    )
    got_yz = [*swap_along("gy", sent[:n_y]), swap(sent[-1], "gz", z_pairs)]
    sent_x = call(
        pack_x_kernel,
        "svva",
        (pos, displacement, damage, sent[-1]),
        "vv",
        [arr(4, ny, nz)] * 2,
        size,
    )
    got_x = swap_along("gx", sent_x)
    rows = [arr(8, nx, nz)] * n_y
    voxels = (pos, scaled, displacement, damage, history, notch, labels, *got_yz)
    hist, rd, v0, stress, mom, *sent = call(
        functools.partial(inner_kernel, n_y),
        "ssvvvvv" + "v" * (1 + n_y),
        voxels,
        "hvvvv" + "v" * (1 + n_y),
        [field, field, field, arr(6, nx, ny, nz), small, *rows, columns],
        140 * size,
        [pltpu.VMEM((nx, ny, nz), F32), pltpu.SemaphoreType.DMA((nx,))],
    )
    more = (*got_x, hist, rd, v0, mom, *sent)
    hist, rd, v0, ends, mom, *sent = call(
        functools.partial(ends_kernel, n_y),
        "ssvvvvv" + "v" * (1 + n_y) + "vvhvvv" + "v" * (1 + n_y),
        (*voxels, *more),
        "hvvvv" + "v" * (3 + n_y),
        [
            field,
            field,
            field,
            arr(6, 2, ny, nz),
            small,
            *[arr(8, ny, nz)] * 2,
            *rows,
            columns,
        ],
        20 * size,
        [pltpu.VMEM((2, ny, nz), F32), pltpu.SemaphoreType.DMA((2,))],
        [(len(voxels) + 2, 0)],
    )
    stress_z = swap(sent[-1], "gz", z_pairs)
    xs = swap_along("gx", sent[:2])
    ys = swap_along("gy", sent[2 : 2 + n_y])
    corners = call(
        functools.partial(corner_kernel, n_y),
        "savv",
        (pos, stress_z, v0, rd),
        "v" * (2 * n_y),
        [arr(2, 8, nz)] * (2 * n_y),
        1024,
    )
    xy = [*xs, *ys, *swap_diagonal(corners)]
    moving = (
        pos,
        scaled,
        impact,
        displacement,
        velocity,
        contact,
        labels,
        *ys,
        stress_z,
        stress,
        ends,
    )
    new_disp, new_vel, token = call(
        functools.partial(force_inner_kernel, n_y),
        "sssvvvv" + "v" * (3 + n_y),
        moving,
        "hhv",
        [fields3, fields3, small],
        55 * size,
        [
            pltpu.VMEM((3, nx, ny, nz), F32),
            pltpu.VMEM((3, nx, ny, nz), F32),
            pltpu.SemaphoreType.DMA((nx, 2)),
        ],
    )
    (joined,) = call(
        functools.partial(join_kernel, n_y),
        "svva" + "v" * len(xy),
        (pos, v0, rd, token, *xy),
        "v",
        [arr(nx + 6, ny + 8, 128)],
        4 * size,
    )
    z_got = swap(joined, "gz", z_pairs)
    new_disp, new_vel, main_v, main_rd = call(
        functools.partial(rest_kernel, n_y),
        "sssvvvv" + "v" * (3 + n_y) + "vv" + "v" * len(xy) + "hh",
        (*moving, v0, rd, *xy, new_disp, new_vel),
        "hhvv",
        [fields3, fields3, *[arr(nx + 6, ny + 8, nz)] * 2],
        12 * size,
        [
            pltpu.VMEM((3, 2, ny, nz), F32),
            pltpu.VMEM((3, 2, ny, nz), F32),
            pltpu.SemaphoreType.DMA((2, 2)),
        ],
        [(len(moving) + 2 + len(xy), 0), (len(moving) + 3 + len(xy), 1)],
    )
    peers = lax.axis_size("gx") * lax.axis_size("gy") * lax.axis_size("gz")
    v1, v2, spread = call(
        krylov_kernel,
        "svvvv",
        (pos, main_v, main_rd, mom, z_got),
        "vvv",
        [field, field, arr(peers, 8, 128)],
        60 * size,
        [
            pltpu.VMEM((nx + 6, ny + 8, 128), F32),
            pltpu.VMEM((nx + 6, ny + 8, 128), F32),
            pltpu.VMEM((nx + 4, ny + 8, nz + 128), F32),
            pltpu.VMEM((nx + 2, ny + 8, nz + 128), F32),
        ],
    )
    mom = lax.all_to_all(spread, ("gx", "gy", "gz"), 0, 0, tiled=True)
    (damage_new,) = call(
        final_kernel,
        "vvvvh",
        (mom, v0, v1, v2, damage),
        "h",
        [field],
        8 * size,
        [
            pltpu.VMEM((nx, ny, nz), F32),
            pltpu.VMEM((nx, ny, nz), F32),
            pltpu.SemaphoreType.DMA((CHUNKS,)),
            pltpu.SemaphoreType.DMA((CHUNKS,)),
        ],
    )
    return new_disp, new_vel, hist, damage_new


def solution(mesh):
    placed = (
        P(None, ("case", "gx"), "gy", "gz"),
        P(None, ("case", "gx"), "gy", "gz"),
        P(("case", "gx"), "gy", "gz"),
        P(("case", "gx"), "gy", "gz"),
        P(("case", "gx"), "gy", "gz"),
        P(("case", "gx"), "gy", "gz"),
        P(("case", "gx"), "gy", "gz"),
        P(),
        P("case"),
    )
    return jax.shard_map(
        per_device,
        mesh=mesh,
        in_specs=placed,
        out_specs=(
            P(None, ("case", "gx"), "gy", "gz"),
            P(None, ("case", "gx"), "gy", "gz"),
            P(("case", "gx"), "gy", "gz"),
            P(("case", "gx"), "gy", "gz"),
        ),
        check_vma=False,
    )
```

```python
import functools
import jax
import jax.numpy as jnp
from jax import lax
from jax.experimental import pallas as pl
from jax.experimental.pallas import tpu as pltpu
from jax.sharding import PartitionSpec as P

TIME_STEP = 0.1
KAPPA_COEF = 0.5
NOTCH_LOAD = 20.0
STIFF_FLOOR = 0.001
ALPHA_LOW, ALPHA_HIGH = 0.5, 6.5
VMEM_BYTES = 28 * 1024 * 1024
CHUNKS = 4
F32 = jnp.float32


def iota2(shape, dim):
    return lax.broadcasted_iota(jnp.int32, shape, dim)


def low_high(odd, got):
    if len(got) == 2:
        return jnp.where(odd, got[0], got[1]), jnp.where(odd, got[1], got[0])
    return jnp.where(odd, got[0], 0.0), jnp.where(odd, 0.0, got[0])


def send(odd, refs, index, low, high):
    refs[0][index] = jnp.where(odd, low, high)
    if len(refs) == 2:
        refs[1][index] = jnp.where(odd, high, low)


def shift_y(plane, rows):
    lo, hi = rows
    tiles = [plane[start : start + 8] for start in range(0, plane.shape[0], 8)]
    at = iota2(tiles[0].shape, 0)
    ahead = [pltpu.roll(tile, 7, 0) for tile in tiles]
    behind = [pltpu.roll(tile, 1, 0) for tile in tiles]
    upper = [jnp.where(at == 7, b, a) for a, b in zip(ahead, [*ahead[1:], hi])]
    lower = [jnp.where(at == 0, b, a) for a, b in zip(behind, [lo, *behind[:-1]])]
    return jnp.concatenate(upper, axis=0), jnp.concatenate(lower, axis=0)


def shift_z(plane, column, first_z):
    tiles = [plane[:, start : start + 128] for start in range(0, plane.shape[1], 128)]
    at = iota2(tiles[0].shape, 1)
    wide = jnp.broadcast_to(column, tiles[0].shape)
    lo, hi = jnp.where(first_z, 0.0, wide), jnp.where(first_z, wide, 0.0)
    ahead = [pltpu.roll(tile, 127, 1) for tile in tiles]
    behind = [pltpu.roll(tile, 1, 1) for tile in tiles]
    upper = [jnp.where(at == 127, b, a) for a, b in zip(ahead, [*ahead[1:], hi])]
    lower = [jnp.where(at == 0, b, a) for a, b in zip(behind, [lo, *behind[:-1]])]
    return jnp.concatenate(upper, axis=1), jnp.concatenate(lower, axis=1)


def send_columns(ref, x, planes, gz):
    depth = planes[0].shape[1]
    lanes = iota2((planes[0].shape[0], 128), 1)
    tile = None
    for field, plane in enumerate(planes):
        part = jnp.where(gz == 0, plane[:, depth - 128 :], plane[:, :128])
        part = pltpu.roll(part, field + 1 - gz, 1)
        tile = part if tile is None else jnp.where(lanes == field, part, tile)
    ref[x] = tile


def folded(values):
    total = None
    for start in range(0, values.shape[1], 128):
        part = values[:, start : start + 128]
        total = part if total is None else total + part
    out = None
    for start in range(0, values.shape[0], 8):
        part = total[start : start + 8]
        out = part if out is None else out + part
    return out


def by_label(labels, scalars):
    picked = scalars[0]
    for region in range(1, len(scalars)):
        picked = jnp.where(labels == region, scalars[region], picked)
    return picked


def unrolled(count, many, body, carry):
    def several(block, carry):
        for at in range(many):
            carry = body(block * many + at, carry)
        return carry

    return lax.fori_loop(0, count // many, several, carry)


def pack_kernel(n_y, pos, disp, damage, *refs):
    ys, zs = refs[:n_y], refs[n_y]
    odd_y, gz = pos[1] == 1, pos[2]

    def body(x, carry):
        planes = [disp[0, x], disp[1, x], disp[2, x], damage[x]]
        for field, plane in enumerate(planes):
            last = plane.shape[0] - 1
            spot = (field, pl.ds(x, 1), slice(None))
            send(odd_y, ys, spot, plane[0:1], plane[last : last + 1])
        send_columns(zs, x, planes, gz)
        return carry

    unrolled(damage.shape[0], 8, body, 0)


def pack_x_kernel(pos, disp, damage, after, *xs):
    odd_x, count = pos[0] == 1, damage.shape[0]
    for field, src in enumerate((disp.at[0], disp.at[1], disp.at[2], damage)):
        send(odd_x, xs, field, src[0], src[count - 1])


class Local:
    def __init__(self, pos, table, disp, damage, history, notch, labels, yg, zg):
        self.odd_x, self.odd_y, self.gz = pos[0] == 1, pos[1] == 1, pos[2]
        self.disp, self.damage, self.history = disp, damage, history
        self.notch, self.labels, self.yg, self.zg = notch, labels, yg, zg
        regions = range(table.shape[1])
        self.lames = [table[0, r] for r in regions]
        self.shears = [table[1, r] for r in regions]
        self.bases = [table[3, r] for r in regions]

    def plane(self, x, lower, upper, put):
        lab = self.labels[x]
        shear = by_label(lab, self.shears)
        dmg = self.damage[x]
        degrade = 4.0 * ((1.0 - dmg) * (1.0 - dmg) + STIFF_FLOOR)
        half = degrade * shear
        fields = [self.disp[c, x] for c in range(3)]

        def d(c, j):
            if j == 0:
                return upper(c) - lower(c)
            if j == 1:
                rows = low_high(self.odd_y, [y[c, pl.ds(x, 1), :] for y in self.yg])
                high, low = shift_y(fields[c], rows)
            else:
                column = self.zg[x][:, c : c + 1]
                high, low = shift_z(fields[c], column, self.gz == 0)
            return high - low

        squares = None
        for k, (i, j) in ((3, (0, 1)), (4, (0, 2)), (5, (1, 2))):
            e = d(i, j) + d(j, i)
            put(k, half * e)
            squares = e * e if squares is None else squares + e * e
        straight = [d(c, c) for c in range(3)]
        trace = straight[0] + straight[1] + straight[2]
        lame = by_label(lab, self.lames)
        level = (degrade * lame) * trace
        whole = half + half
        for k in range(3):
            put(k, level + whole * straight[k])
        twice = (
            straight[0] * straight[0] + straight[1] * straight[1] + straight[2] * straight[2]
        )
        squares = squares + (twice + twice)
        positive = jnp.maximum(trace, 0.0)
        energy = lame * positive * positive + shear * squares
        hist = jnp.maximum(
            jnp.maximum(self.history[x], energy), NOTCH_LOAD * self.notch[x].astype(F32)
        )
        diagonal = by_label(lab, self.bases) + 2.0 * hist
        rd = 1.0 / diagonal
        rows = low_high(self.odd_y, [y[3, pl.ds(x, 1), :] for y in self.yg])
        yu, yl = shift_y(dmg, rows)
        zu, zl = shift_z(dmg, self.zg[x][:, 3:4], self.gz == 0)
        near = ((upper(3) + lower(3)) + (yu + yl)) + (zu + zl)
        residual = 2.0 * hist - (diagonal * dmg - KAPPA_COEF * near)
        v = residual * rd
        return hist, rd, v, folded(residual * v)

    def send_y(self, ys, x, v, rd, stress):
        rows = v.shape[0]
        sources = [(v, depth) for depth in (1, 2, 3)] + [(rd, depth) for depth in (1, 2)]
        sources += [(stress[k], 1) for k in (3, 1, 5)]
        for slot, (plane, depth) in enumerate(sources):
            low, high = plane[depth - 1 : depth], plane[rows - depth : rows - depth + 1]
            send(self.odd_y, ys, (slot, pl.ds(x, 1), slice(None)), low, high)

    def send_z(self, zs, x, stress):
        send_columns(zs, x, [stress[4], stress[5], stress[2]], self.gz)


def inner_steps(count):
    inner = count - 2
    many = max(m for m in range(1, 8) if inner % m == 0)
    return inner // many, many


def inner_kernel(n_y, pos, table, disp, damage, history, notch, labels, *refs):
    local = Local(
        pos, table, disp, damage, history, notch, labels, refs[:n_y], refs[n_y]
    )
    hist_hbm, rd_out, v_out, stress_out, mom_out = refs[n_y + 1 : n_y + 6]
    ys, (zs, hist, sems) = refs[n_y + 6 : 2 * n_y + 6], refs[2 * n_y + 6 :]
    steps, many = inner_steps(damage.shape[0])

    def store(step):
        part = pl.ds(1 + step * many, many)
        return pltpu.make_async_copy(hist.at[part], hist_hbm.at[part], sems.at[step])

    def several(step, total):
        for at in range(many):
            x = 1 + step * many + at

            def lower(c):
                return damage[x - 1] if c == 3 else disp[c, x - 1]

            def upper(c):
                return damage[x + 1] if c == 3 else disp[c, x + 1]

            stress = {}

            def put(k, plane):
                stress[k] = stress_out[k, x] = plane

            hist_x, rd, v, part = local.plane(x, lower, upper, put)
            hist[x] = hist_x
            rd_out[x] = rd
            v_out[x] = v
            local.send_y(ys, x, v, rd, stress)
            local.send_z(zs, x, stress)
            total = total + part
        store(step).start()
        return total

    mom_out[...] = lax.fori_loop(0, steps, several, jnp.zeros((8, 128), F32))
    for step in range(steps):
        store(step).wait()


def ends_kernel(n_y, pos, table, disp, damage, history, notch, labels, *refs):
    local = Local(
        pos, table, disp, damage, history, notch, labels, refs[:n_y], refs[n_y]
    )
    refs = refs[n_y + 1 :]
    xg, (_, rd_in, v_in, mom), ys_in, zs_in = (
        refs[:2],
        refs[2:6],
        refs[6 : 6 + n_y],
        refs[6 + n_y],
    )
    refs = refs[7 + n_y :]
    hist_hbm, rd_out, v_out, stress_out, mom_out = refs[:5]
    xs, ys, (zs, hist, sems) = refs[5:7], refs[7 : 7 + n_y], refs[7 + n_y :]
    odd_x, count = local.odd_x, damage.shape[0]
    total = mom[...]
    copies, found = [], []
    for end, x in enumerate((0, count - 1)):

        def outside(c):
            first, second = xg[0][c], xg[1][c]
            if end == 0:
                return jnp.where(odd_x, first, second)
            return jnp.where(odd_x, second, first)

        def beside(c):
            at = 1 if end == 0 else count - 2
            return damage[at] if c == 3 else disp[c, at]

        sides = (outside, beside) if end == 0 else (beside, outside)
        stress = {}

        def put(k, plane):
            stress[k] = stress_out[k, end] = plane

        hist_x, rd, v, part = local.plane(x, *sides, put)
        hist[end] = hist_x
        copies.append(pltpu.make_async_copy(hist.at[end], hist_hbm.at[x], sems.at[end]))
        copies[-1].start()
        rd_out[x] = rd
        v_out[x] = v
        total = total + part
        found.append((stress, rd, v))
    for mine, before in zip(ys, ys_in, strict=True):
        for slot in range(8):
            mine[slot] = before[slot]
    for x in range(1, count - 1):
        rd_out[x] = rd_in[x]
        v_out[x] = v_in[x]
        zs[x] = zs_in[x]
    for end, x in enumerate((0, count - 1)):
        stress, rd, v = found[end]
        local.send_y(ys, x, v, rd, stress)
        local.send_z(zs, x, stress)
    for depth in (1, 2, 3):
        low, high = depth - 1, count - depth
        send(odd_x, xs, depth - 1, v_out[low], v_out[high])
        if depth <= 2:
            send(odd_x, xs, 2 + depth, rd_out[low], rd_out[high])
    for slot, k in ((5, 0), (6, 3), (7, 4)):
        send(odd_x, xs, slot, stress_out[k, 0], stress_out[k, 1])
    mom_out[...] = jnp.zeros((8, 128), F32)
    mom_out[0:1, :] = jnp.sum(total, axis=0, keepdims=True)
    for copy in copies:
        copy.wait()


def corner_kernel(n_y, pos, after, v, rd, *ds):
    odd_x, odd_y = pos[0] == 1, pos[1] == 1
    count, rows = v.shape[0], v.shape[1]
    for depth in (1, 2):
        for slot, (src, deep) in enumerate(((v, 1), (v, 2), (v, 3), (rd, 1), (rd, 2))):
            near, far = pl.ds(deep - 1, 1), pl.ds(rows - deep, 1)
            planes = (depth - 1, count - depth)
            by_y = [(src[x, near, :], src[x, far, :]) for x in planes]
            for which in range(n_y):
                pair = (ds[which], ds[n_y + which])
                picked = [
                    jnp.where(odd_y, *(rows_of if which == 0 else rows_of[::-1]))
                    for rows_of in by_y
                ]
                send(odd_x, pair, (depth - 1, pl.ds(slot, 1), slice(None)), *picked)


class Enlarged:
    def __init__(self, n_y, pos, v, rd, refs):
        self.odd_x, self.odd_y = pos[0] == 1, pos[1] == 1
        self.v, self.rd, self.n_y = v, rd, n_y
        self.xg, self.yg, self.dg = refs[:2], refs[2 : 2 + n_y], refs[2 + n_y : 2 + 3 * n_y]

    def rows(self, found):
        nz = self.v.shape[2]
        at = iota2((8, nz), 0)

        def tile(first, depths):
            out = jnp.zeros((8, nz), F32)
            for depth in range(1, depths + 1):
                got = [found(w, first + depth - 1) for w in range(self.n_y)]
                if self.n_y == 1:
                    spot = jnp.where(self.odd_y, 8 - depth, depth - 1)
                    out = jnp.where(at == spot, got[0], out)
                else:
                    lo, hi = low_high(self.odd_y, got)
                    out = jnp.where(at == depth - 1, hi, out)
                    out = jnp.where(at == 8 - depth, lo, out)
            return out

        return tile(0, 3), tile(3, 2)

    def own(self, x):
        v_rows, rd_rows = self.rows(lambda w, slot: self.yg[w][slot, pl.ds(x, 1), :])
        return self.v[x], v_rows, self.rd[x], rd_rows

    def halo(self, is_low, depth):
        first, second = (0, 1) if is_low else (1, 0)

        def of(a, b):
            return jnp.where(self.odd_x, (a, b)[first], (a, b)[second])

        v = of(self.xg[0][depth - 1], self.xg[1][depth - 1])
        nothing = jnp.zeros((8, v.shape[1]), F32)
        if depth > 2:
            return v, nothing, jnp.zeros_like(v), nothing
        rd = of(self.xg[0][2 + depth], self.xg[1][2 + depth])

        def found(w, slot):
            spot = (depth - 1, pl.ds(slot, 1), slice(None))
            return of(self.dg[w][spot], self.dg[self.n_y + w][spot])

        v_rows, rd_rows = self.rows(found)
        return v, v_rows, rd, rd_rows

    def outer(self, count):
        for depth in (1, 2, 3):
            yield -depth, self.halo(True, depth)
            yield count - 1 + depth, self.halo(False, depth)


def join_kernel(n_y, pos, v, rd, token, *refs):
    big = Enlarged(n_y, pos, v, rd, refs[:-1])
    out = refs[-1]
    first_z = pos[2] == 0
    count, ny, depth = v.shape

    def tile(v_part, rd_part):
        lanes = iota2((v_part.shape[0], 128), 1)
        keep = lax.shift_right_logical(lanes, 6) == 1 - pos[2]
        mine = jnp.where(first_z, v_part[:, depth - 128 :], v_part[:, :128])
        moved = jnp.where(first_z, rd_part[:, depth - 128 :], rd_part[:, :128])
        return jnp.where(keep, mine, pltpu.roll(moved, 64, 1))

    def put(p, parts):
        v_own, v_rows, rd_own, rd_rows = parts
        out[p + 3, 0:ny] = tile(v_own, rd_own)
        out[p + 3, ny : ny + 8] = tile(v_rows, rd_rows)

    for p, parts in big.outer(count):
        put(p, parts)

    def body(x, carry):
        put(x, big.own(x))
        return carry

    unrolled(count, 8, body, 0)


def krylov_kernel(pos, main_v, main_rd, mom, z_got, *refs):
    v1_out, v2_out, spread, z_v, z_rd, big_v1, big_v2 = refs
    count, ny, nz = v1_out.shape

    def split(p, carry):
        tile = z_got[p]
        keep = lax.shift_right_logical(iota2(tile.shape, 1), 6) == pos[2]
        z_v[p] = jnp.where(keep, tile, 0.0)
        z_rd[p] = jnp.where(keep, pltpu.roll(tile, 64, 1), 0.0)
        return carry

    unrolled(count + 6, 11 if count % 11 == 5 else 1, split, 0)

    def v_at(at):
        return jnp.concatenate([main_v[at], z_v[at]], axis=1)

    def rd_at(at):
        return jnp.concatenate([main_rd[at], z_rd[at]], axis=1)

    def image_of(get, at):
        plane = get(at)
        rows, lanes = plane.shape
        near = (get(at - 1) + get(at + 1)) + (pltpu.roll(plane, 1, 0) + pltpu.roll(plane, rows - 1, 0))
        near = near + (pltpu.roll(plane, 1, 1) + pltpu.roll(plane, lanes - 1, 1))
        return plane, KAPPA_COEF * near

    def v1_at(at):
        return big_v1[at]

    def v2_at(at):
        return big_v2[at]

    def inside(values):
        return folded(values[0:ny, 0:nz])

    def first(x, totals):
        plane, image = image_of(v_at, x + 3)
        made = image * rd_at(x + 3)
        big_v1[x + 2] = made
        v1_out[x] = made[0:ny, 0:nz]
        return totals[0] + inside(plane * image), totals[1] + inside(made * image)

    def second(x, totals):
        plane, image = image_of(v1_at, x + 2)
        made = image * rd_at(x + 3)
        big_v2[x + 1] = made
        v2_out[x] = made[0:ny, 0:nz]
        return totals[0] + inside(plane * image), totals[1] + inside(made * image)

    def third(x, total):
        plane, image = image_of(v2_at, x + 1)
        return total + folded(plane[0:ny, 0:nz] * image[0:ny, 0:nz])

    zero = jnp.zeros((8, 128), F32)
    for p in (-2, -1, count, count + 1):
        big_v1[p + 2] = image_of(v_at, p + 3)[1] * rd_at(p + 3)
    k1, k2 = unrolled(count, 8, first, (zero, zero))
    for p in (-1, count):
        big_v2[p + 1] = image_of(v1_at, p + 2)[1] * rd_at(p + 3)
    k3, k4 = unrolled(count, 8, second, (zero, zero))
    k5 = unrolled(count, 8, third, zero)
    rows = iota2((8, 128), 0)
    result = mom[...]
    for at, total in enumerate((k1, k2, k3, k4, k5)):
        result = jnp.where(rows == at + 1, jnp.sum(total, axis=0, keepdims=True), result)
    for peer in range(spread.shape[0]):
        spread[peer] = result


PARTS = ((0, 3, 4), (3, 1, 5), (4, 5, 2))


class Force:
    def __init__(self, n_y, pos, table, impact, disp, vel, contact, labels, yg, zg):
        self.odd_x, self.odd_y, self.gz = pos[0] == 1, pos[1] == 1, pos[2]
        self.impact, self.disp, self.vel = impact, disp, vel
        self.contact, self.labels, self.yg, self.zg = contact, labels, yg, zg
        self.rates = [table[2, r] for r in range(table.shape[1])]

    def plane(self, x, lower, mine, upper, vel_out, disp_out, at):
        loaded = self.contact[x].astype(F32)
        rate = by_label(self.labels[x], self.rates)
        for c, (kx, ky, kz) in enumerate(PARTS):
            rows = low_high(self.odd_y, [y[5 + c, pl.ds(x, 1), :] for y in self.yg])
            column = self.zg[x][:, c : c + 1]
            yu, yl = shift_y(mine(ky), rows)
            zu, zl = shift_z(mine(kz), column, self.gz == 0)
            force = 0.5 * (((upper(c, kx) - lower(c, kx)) + (yu - yl)) + (zu - zl))
            speed = self.vel[c, x] + rate * (force + loaded * self.impact[c])
            vel_out[c, at] = speed
            disp_out[c, at] = self.disp[c, x] + TIME_STEP * speed


def force_inner_kernel(n_y, pos, table, impact, disp, vel, contact, labels, *refs):
    yg, zg, stress, ends = refs[:n_y], refs[n_y], refs[n_y + 1], refs[n_y + 2]
    disp_hbm, vel_hbm, token, disp_out, vel_out, sems = refs[n_y + 3 :]
    token[...] = jnp.zeros((8, 128), F32)
    force = Force(n_y, pos, table, impact, disp, vel, contact, labels, yg, zg)
    count = contact.shape[0]
    steps, many = inner_steps(count)

    def stores(step):
        part = pl.ds(1 + step * many, many)
        return (
            pltpu.make_async_copy(disp_out.at[:, part], disp_hbm.at[:, part], sems.at[step, 0]),
            pltpu.make_async_copy(vel_out.at[:, part], vel_hbm.at[:, part], sems.at[step, 1]),
        )

    def several(step, carry):
        for at in range(many):
            x = 1 + step * many + at

            def lower(c, k):
                if at == 0:
                    return jnp.where(step == 0, ends[k, 0], stress[k, x - 1])
                return stress[k, x - 1]

            def upper(c, k):
                if at == many - 1:
                    return jnp.where(step == steps - 1, ends[k, 1], stress[k, x + 1])
                return stress[k, x + 1]

            force.plane(x, lower, lambda k: stress[k, x], upper, vel_out, disp_out, x)
        for copy in stores(step):
            copy.start()
        return carry

    lax.fori_loop(0, steps, several, 0)
    for step in range(steps):
        for copy in stores(step):
            copy.wait()


def rest_kernel(n_y, pos, table, impact, disp, vel, contact, labels, *refs):
    yg, zg, stress, ends = refs[:n_y], refs[n_y], refs[n_y + 1], refs[n_y + 2]
    refs = refs[n_y + 3 :]
    v, rd, xy = refs[0], refs[1], refs[2 : 4 + 3 * n_y]
    xg = xy[:2]
    disp_hbm, vel_hbm, big_v, big_rd, disp_out, vel_out, sems = refs[6 + 3 * n_y :]
    force = Force(n_y, pos, table, impact, disp, vel, contact, labels, yg, zg)
    count, ny = contact.shape[0], contact.shape[1]
    copies = []
    for end, x in enumerate((0, count - 1)):

        def outside(c, k):
            first, second = xg[0][5 + c], xg[1][5 + c]
            if end == 0:
                return jnp.where(force.odd_x, first, second)
            return jnp.where(force.odd_x, second, first)

        def beside(c, k):
            return stress[k, 1 if end == 0 else count - 2]

        lower, upper = (outside, beside) if end == 0 else (beside, outside)
        force.plane(x, lower, lambda k: ends[k, end], upper, vel_out, disp_out, end)
        for which, (src, dst) in enumerate(((disp_out, disp_hbm), (vel_out, vel_hbm))):
            copy = pltpu.make_async_copy(src.at[:, end], dst.at[:, x], sems.at[end, which])
            copy.start()
            copies.append(copy)
    big = Enlarged(n_y, pos, v, rd, xy)

    def put(p, parts):
        v_own, v_rows, rd_own, rd_rows = parts
        big_v[p + 3, 0:ny] = v_own
        big_v[p + 3, ny : ny + 8] = v_rows
        big_rd[p + 3, 0:ny] = rd_own
        big_rd[p + 3, ny : ny + 8] = rd_rows

    for p, parts in big.outer(count):
        put(p, parts)

    def body(x, carry):
        put(x, big.own(x))
        return carry

    unrolled(count, 4, body, 0)
    for copy in copies:
        copy.wait()


def cg_coefficients(k):
    zero, one = jnp.zeros_like(k[0]), jnp.ones_like(k[0])
    z, p, out = [one], [one], [zero, zero, zero]

    def form(a, b, moments):
        total = None
        for i, ai in enumerate(a):
            for j, bj in enumerate(b):
                term = ai * bj * moments[i + j]
                total = term if total is None else total + term
        return total

    energy = [k[j] - k[j + 1] for j in range(5)]
    rz = k[0]
    for step in range(3):
        alpha = jnp.clip(rz / form(p, p, energy), ALPHA_LOW, ALPHA_HIGH)
        out = [o + alpha * (p[i] if i < len(p) else zero) for i, o in enumerate(out)]
        if step == 2:
            break
        image = [(p[i] if i < len(p) else zero) - (p[i - 1] if i else zero) for i in range(len(p) + 1)]
        z = [(z[i] if i < len(z) else zero) - alpha * image[i] for i in range(len(image))]
        new = jnp.maximum(form(z, z, k), 0.0)
        beta = new / rz
        p = [z[i] + beta * (p[i] if i < len(p) else zero) for i in range(len(z))]
        rz = new
    return out


def final_kernel(mom, v0, v1, v2, damage_hbm, out_hbm, damage, out, in_sems, out_sems):
    count = v0.shape[0]
    block = count // CHUNKS
    loads, stores = [], []
    for chunk in range(CHUNKS):
        part = pl.ds(chunk * block, block)
        loads.append(pltpu.make_async_copy(damage_hbm.at[part], damage.at[part], in_sems.at[chunk]))
        stores.append(pltpu.make_async_copy(out.at[part], out_hbm.at[part], out_sems.at[chunk]))
        loads[-1].start()
    sums = jnp.sum(jnp.sum(mom[...], axis=0), axis=1, keepdims=True)
    c0, c1, c2 = cg_coefficients([sums[j : j + 1, :] for j in range(6)])
    for chunk in range(CHUNKS):
        loads[chunk].wait()
        for x in range(chunk * block, (chunk + 1) * block):
            dmg = damage[x]
            out[x] = jnp.maximum(dmg + (c0 * v0[x] + c1 * v1[x] + c2 * v2[x]), dmg)
        stores[chunk].start()
    for store in stores:
        store.wait()


def pairs_of(axis):
    count = lax.axis_size(axis)
    out = [[(i, i + 1) for i in range(start, count - 1, 2)] for start in (0, 1)]
    return [pairs for pairs in out if pairs]


def swap(array, axis, pairs):
    return lax.ppermute(array, axis, pairs + [(b, a) for a, b in pairs])


def swap_along(axis, arrays):
    return [swap(a, axis, pairs) for a, pairs in zip(arrays, pairs_of(axis), strict=True)]


def swap_diagonal(arrays):
    columns = lax.axis_size("gy")
    out = []
    both = [(xp, yp) for xp in pairs_of("gx") for yp in pairs_of("gy")]
    for array, (x_pairs, y_pairs) in zip(arrays, both, strict=True):
        joint = []
        for a, b in x_pairs:
            for c, d in y_pairs:
                joint.append((a * columns + c, b * columns + d))
                joint.append((a * columns + d, b * columns + c))
        out.append(swap(array, ("gx", "gy"), joint))
    return out


def spec_of(kind, a):
    if kind == "s":
        return pl.BlockSpec(memory_space=pltpu.SMEM)
    if kind == "v":
        return pl.BlockSpec(memory_space=pltpu.VMEM)
    if kind == "h":
        return pl.BlockSpec(memory_space=pltpu.HBM)
    if kind == "a":
        return pl.BlockSpec(memory_space=pl.ANY)
    raise ValueError(kind)


def call(kernel, kinds, ins, out_kinds, outs, flops, scratch=(), aliases=()):
    moved = sum(4 * a.size for a in (*ins, *outs))
    return pl.pallas_call(
        kernel,
        out_shape=outs,
        in_specs=[spec_of(k, a) for k, a in zip(kinds, ins, strict=True)],
        out_specs=[spec_of(k, a) for k, a in zip(out_kinds, outs, strict=True)],
        scratch_shapes=scratch,
        input_output_aliases=dict(aliases),
        compiler_params=pltpu.CompilerParams(vmem_limit_bytes=VMEM_BYTES),
        cost_estimate=pl.CostEstimate(flops=flops, bytes_accessed=moved, transcendentals=0),
    )(*ins)


def per_device(displacement, velocity, damage, history, contact, notch, labels, table, impact):
    nx, ny, nz = damage.shape
    size = damage.size
    n_y = len(pairs_of("gy"))
    pos = jnp.stack(
        [lax.axis_index("gx") % 2, lax.axis_index("gy") % 2, lax.axis_index("gz")]
    ).astype(jnp.int32)

    scaled = jnp.stack(
        [table[0] / 8.0, table[1] / 8.0, TIME_STEP / table[2], table[3] + 6.0 * KAPPA_COEF]
    )

    def arr(*shape):
        return jax.ShapeDtypeStruct(shape, F32)

    field, fields3, small = arr(nx, ny, nz), arr(3, nx, ny, nz), arr(8, 128)
    columns = arr(nx, ny, 128)
    z_pairs = [(0, 1)]

    sent = call(
        functools.partial(pack_kernel, n_y),
        "svv",
        (pos, displacement, damage),
        "v" * (1 + n_y),
        [*[arr(4, nx, nz)] * n_y, columns],
        size,
    )
    got_yz = [*swap_along("gy", sent[:n_y]), swap(sent[-1], "gz", z_pairs)]
    sent_x = call(
        pack_x_kernel,
        "svva",
        (pos, displacement, damage, sent[-1]),
        "vv",
        [arr(4, ny, nz)] * 2,
        size,
    )
    got_x = swap_along("gx", sent_x)
    rows = [arr(8, nx, nz)] * n_y
    voxels = (pos, scaled, displacement, damage, history, notch, labels, *got_yz)
    hist, rd, v0, stress, mom, *sent = call(
        functools.partial(inner_kernel, n_y),
        "ssvvvvv" + "v" * (1 + n_y),
        voxels,
        "hvvvv" + "v" * (1 + n_y),
        [field, field, field, arr(6, nx, ny, nz), small, *rows, columns],
        140 * size,
        [pltpu.VMEM((nx, ny, nz), F32), pltpu.SemaphoreType.DMA((nx,))],
    )
    more = (*got_x, hist, rd, v0, mom, *sent)
    hist, rd, v0, ends, mom, *sent = call(
        functools.partial(ends_kernel, n_y),
        "ssvvvvv" + "v" * (1 + n_y) + "vvhvvv" + "v" * (1 + n_y),
        (*voxels, *more),
        "hvvvv" + "v" * (3 + n_y),
        [
            field,
            field,
            field,
            arr(6, 2, ny, nz),
            small,
            *[arr(8, ny, nz)] * 2,
            *rows,
            columns,
        ],
        20 * size,
        [pltpu.VMEM((2, ny, nz), F32), pltpu.SemaphoreType.DMA((2,))],
        [(len(voxels) + 2, 0)],
    )
    stress_z = swap(sent[-1], "gz", z_pairs)
    xs = swap_along("gx", sent[:2])
    ys = swap_along("gy", sent[2 : 2 + n_y])
    corners = call(
        functools.partial(corner_kernel, n_y),
        "savv",
        (pos, stress_z, v0, rd),
        "v" * (2 * n_y),
        [arr(2, 8, nz)] * (2 * n_y),
        1024,
    )
    xy = [*xs, *ys, *swap_diagonal(corners)]
    moving = (
        pos,
        scaled,
        impact,
        displacement,
        velocity,
        contact,
        labels,
        *ys,
        stress_z,
        stress,
        ends,
    )
    new_disp, new_vel, token = call(
        functools.partial(force_inner_kernel, n_y),
        "sssvvvv" + "v" * (3 + n_y),
        moving,
        "hhv",
        [fields3, fields3, small],
        55 * size,
        [
            pltpu.VMEM((3, nx, ny, nz), F32),
            pltpu.VMEM((3, nx, ny, nz), F32),
            pltpu.SemaphoreType.DMA((nx, 2)),
        ],
    )
    (joined,) = call(
        functools.partial(join_kernel, n_y),
        "svva" + "v" * len(xy),
        (pos, v0, rd, token, *xy),
        "v",
        [arr(nx + 6, ny + 8, 128)],
        4 * size,
    )
    z_got = swap(joined, "gz", z_pairs)
    new_disp, new_vel, main_v, main_rd = call(
        functools.partial(rest_kernel, n_y),
        "sssvvvv" + "v" * (3 + n_y) + "vv" + "v" * len(xy) + "hh",
        (*moving, v0, rd, *xy, new_disp, new_vel),
        "hhvv",
        [fields3, fields3, *[arr(nx + 6, ny + 8, nz)] * 2],
        12 * size,
        [
            pltpu.VMEM((3, 2, ny, nz), F32),
            pltpu.VMEM((3, 2, ny, nz), F32),
            pltpu.SemaphoreType.DMA((2, 2)),
        ],
        [(len(moving) + 2 + len(xy), 0), (len(moving) + 3 + len(xy), 1)],
    )
    peers = lax.axis_size("gx") * lax.axis_size("gy") * lax.axis_size("gz")
    v1, v2, spread = call(
        krylov_kernel,
        "svvvv",
        (pos, main_v, main_rd, mom, z_got),
        "vvv",
        [field, field, arr(peers, 8, 128)],
        60 * size,
        [
            pltpu.VMEM((nx + 6, ny + 8, 128), F32),
            pltpu.VMEM((nx + 6, ny + 8, 128), F32),
            pltpu.VMEM((nx + 4, ny + 8, nz + 128), F32),
            pltpu.VMEM((nx + 2, ny + 8, nz + 128), F32),
        ],
    )
    mom = lax.all_to_all(spread, ("gx", "gy", "gz"), 0, 0, tiled=True)
    (damage_new,) = call(
        final_kernel,
        "vvvvh",
        (mom, v0, v1, v2, damage),
        "h",
        [field],
        8 * size,
        [
            pltpu.VMEM((nx, ny, nz), F32),
            pltpu.VMEM((nx, ny, nz), F32),
            pltpu.SemaphoreType.DMA((CHUNKS,)),
            pltpu.SemaphoreType.DMA((CHUNKS,)),
        ],
    )
    return new_disp, new_vel, hist, damage_new


def solution(mesh):
    placed = (
        P(None, ("case", "gx"), "gy", "gz"),
        P(None, ("case", "gx"), "gy", "gz"),
        P(("case", "gx"), "gy", "gz"),
        P(("case", "gx"), "gy", "gz"),
        P(("case", "gx"), "gy", "gz"),
        P(("case", "gx"), "gy", "gz"),
        P(("case", "gx"), "gy", "gz"),
        P(),
        P("case"),
    )
    return jax.shard_map(
        per_device,
        mesh=mesh,
        in_specs=placed,
        out_specs=(
            P(None, ("case", "gx"), "gy", "gz"),
            P(None, ("case", "gx"), "gy", "gz"),
            P(("case", "gx"), "gy", "gz"),
            P(("case", "gx"), "gy", "gz"),
        ),
        check_vma=False,
    )
```

```python
import functools
import jax
import jax.numpy as jnp
from jax import lax
from jax.experimental import pallas as pl
from jax.experimental.pallas import tpu as pltpu
from jax.sharding import PartitionSpec as P

TIME_STEP = 0.1
KAPPA_COEF = 0.5
NOTCH_LOAD = 20.0
STIFF_FLOOR = 0.001
ALPHA_LOW, ALPHA_HIGH = 0.5, 6.5
VMEM_BYTES = 28 * 1024 * 1024
CHUNKS = 4
F32 = jnp.float32


def iota2(shape, dim):
    return lax.broadcasted_iota(jnp.int32, shape, dim)


def low_high(odd, got):
    if len(got) == 2:
        return jnp.where(odd, got[0], got[1]), jnp.where(odd, got[1], got[0])
    return jnp.where(odd, got[0], 0.0), jnp.where(odd, 0.0, got[0])


def send(odd, refs, index, low, high):
    refs[0][index] = jnp.where(odd, low, high)
    if len(refs) == 2:
        refs[1][index] = jnp.where(odd, high, low)


def shift_y(plane, rows):
    lo, hi = rows
    tiles = [plane[start : start + 8] for start in range(0, plane.shape[0], 8)]
    at = iota2(tiles[0].shape, 0)
    ahead = [pltpu.roll(tile, 7, 0) for tile in tiles]
    behind = [pltpu.roll(tile, 1, 0) for tile in tiles]
    upper = [jnp.where(at == 7, b, a) for a, b in zip(ahead, [*ahead[1:], hi])]
    lower = [jnp.where(at == 0, b, a) for a, b in zip(behind, [lo, *behind[:-1]])]
    return jnp.concatenate(upper, axis=0), jnp.concatenate(lower, axis=0)


def shift_z(plane, column, first_z):
    tiles = [plane[:, start : start + 128] for start in range(0, plane.shape[1], 128)]
    at = iota2(tiles[0].shape, 1)
    wide = jnp.broadcast_to(column, tiles[0].shape)
    lo, hi = jnp.where(first_z, 0.0, wide), jnp.where(first_z, wide, 0.0)
    ahead = [pltpu.roll(tile, 127, 1) for tile in tiles]
    behind = [pltpu.roll(tile, 1, 1) for tile in tiles]
    upper = [jnp.where(at == 127, b, a) for a, b in zip(ahead, [*ahead[1:], hi])]
    lower = [jnp.where(at == 0, b, a) for a, b in zip(behind, [lo, *behind[:-1]])]
    return jnp.concatenate(upper, axis=1), jnp.concatenate(lower, axis=1)


def send_columns(ref, x, planes, gz):
    depth = planes[0].shape[1]
    lanes = iota2((planes[0].shape[0], 128), 1)
    tile = None
    for field, plane in enumerate(planes):
        part = jnp.where(gz == 0, plane[:, depth - 128 :], plane[:, :128])
        part = pltpu.roll(part, field + 1 - gz, 1)
        tile = part if tile is None else jnp.where(lanes == field, part, tile)
    ref[x] = tile


def folded(values):
    total = None
    for start in range(0, values.shape[1], 128):
        part = values[:, start : start + 128]
        total = part if total is None else total + part
    out = None
    for start in range(0, values.shape[0], 8):
        part = total[start : start + 8]
        out = part if out is None else out + part
    return out


def by_label(labels, scalars):
    picked = scalars[0]
    for region in range(1, len(scalars)):
        picked = jnp.where(labels == region, scalars[region], picked)
    return picked


def unrolled(count, many, body, carry):
    def several(block, carry):
        for at in range(many):
            carry = body(block * many + at, carry)
        return carry

    return lax.fori_loop(0, count // many, several, carry)


def pack_kernel(n_y, pos, disp, damage, *refs):
    ys, zs = refs[:n_y], refs[n_y]
    odd_y, gz = pos[1] == 1, pos[2]

    def body(x, carry):
        planes = [disp[0, x], disp[1, x], disp[2, x], damage[x]]
        for field, plane in enumerate(planes):
            last = plane.shape[0] - 1
            spot = (field, pl.ds(x, 1), slice(None))
            send(odd_y, ys, spot, plane[0:1], plane[last : last + 1])
        send_columns(zs, x, planes, gz)
        return carry

    unrolled(damage.shape[0], 8, body, 0)


def pack_x_kernel(pos, disp, damage, after, *xs):
    odd_x, count = pos[0] == 1, damage.shape[0]
    for field, src in enumerate((disp.at[0], disp.at[1], disp.at[2], damage)):
        send(odd_x, xs, field, src[0], src[count - 1])


class Local:
    def __init__(self, pos, table, disp, damage, history, notch, labels, yg, zg):
        self.odd_x, self.odd_y, self.gz = pos[0] == 1, pos[1] == 1, pos[2]
        self.disp, self.damage, self.history = disp, damage, history
        self.notch, self.labels, self.yg, self.zg = notch, labels, yg, zg
        regions = range(table.shape[1])
        self.lames = [table[0, r] for r in regions]
        self.shears = [table[1, r] for r in regions]
        self.bases = [table[3, r] for r in regions]

    def plane(self, x, lower, upper, put):
        lab = self.labels[x]
        shear = by_label(lab, self.shears)
        dmg = self.damage[x]
        degrade = 4.0 * ((1.0 - dmg) * (1.0 - dmg) + STIFF_FLOOR)
        half = degrade * shear
        fields = [self.disp[c, x] for c in range(3)]

        def d(c, j):
            if j == 0:
                return upper(c) - lower(c)
            if j == 1:
                rows = low_high(self.odd_y, [y[c, pl.ds(x, 1), :] for y in self.yg])
                high, low = shift_y(fields[c], rows)
            else:
                column = self.zg[x][:, c : c + 1]
                high, low = shift_z(fields[c], column, self.gz == 0)
            return high - low

        squares = None
        for k, (i, j) in ((3, (0, 1)), (4, (0, 2)), (5, (1, 2))):
            e = d(i, j) + d(j, i)
            put(k, half * e)
            squares = e * e if squares is None else squares + e * e
        straight = [d(c, c) for c in range(3)]
        trace = straight[0] + straight[1] + straight[2]
        lame = by_label(lab, self.lames)
        level = (degrade * lame) * trace
        whole = half + half
        for k in range(3):
            put(k, level + whole * straight[k])
        twice = (
            straight[0] * straight[0] + straight[1] * straight[1] + straight[2] * straight[2]
        )
        squares = squares + (twice + twice)
        positive = jnp.maximum(trace, 0.0)
        energy = lame * positive * positive + shear * squares
        hist = jnp.maximum(
            jnp.maximum(self.history[x], energy), NOTCH_LOAD * self.notch[x].astype(F32)
        )
        diagonal = by_label(lab, self.bases) + 2.0 * hist
        rd = 1.0 / diagonal
        rows = low_high(self.odd_y, [y[3, pl.ds(x, 1), :] for y in self.yg])
        yu, yl = shift_y(dmg, rows)
        zu, zl = shift_z(dmg, self.zg[x][:, 3:4], self.gz == 0)
        near = ((upper(3) + lower(3)) + (yu + yl)) + (zu + zl)
        residual = 2.0 * hist - (diagonal * dmg - KAPPA_COEF * near)
        v = residual * rd
        return hist, rd, v, folded(residual * v)

    def send_y(self, ys, x, v, rd, stress):
        rows = v.shape[0]
        sources = [(v, depth) for depth in (1, 2, 3)] + [(rd, depth) for depth in (1, 2)]
        sources += [(stress[k], 1) for k in (3, 1, 5)]
        for slot, (plane, depth) in enumerate(sources):
            low, high = plane[depth - 1 : depth], plane[rows - depth : rows - depth + 1]
            send(self.odd_y, ys, (slot, pl.ds(x, 1), slice(None)), low, high)

    def send_z(self, zs, x, stress):
        send_columns(zs, x, [stress[4], stress[5], stress[2]], self.gz)


def inner_steps(count):
    inner = count - 2
    many = max(m for m in range(1, 8) if inner % m == 0)
    return inner // many, many


def inner_kernel(n_y, pos, table, disp, damage, history, notch, labels, *refs):
    local = Local(
        pos, table, disp, damage, history, notch, labels, refs[:n_y], refs[n_y]
    )
    hist, rd_out, v_out, stress_out, mom_out = refs[n_y + 1 : n_y + 6]
    ys, zs = refs[n_y + 6 : 2 * n_y + 6], refs[2 * n_y + 6]
    steps, many = inner_steps(damage.shape[0])

    def several(step, total):
        for at in range(many):
            x = 1 + step * many + at

            def lower(c):
                return damage[x - 1] if c == 3 else disp[c, x - 1]

            def upper(c):
                return damage[x + 1] if c == 3 else disp[c, x + 1]

            stress = {}

            def put(k, plane):
                stress[k] = stress_out[k, x] = plane

            hist_x, rd, v, part = local.plane(x, lower, upper, put)
            hist[x] = hist_x
            rd_out[x] = rd
            v_out[x] = v
            local.send_y(ys, x, v, rd, stress)
            local.send_z(zs, x, stress)
            total = total + part
        return total

    mom_out[...] = lax.fori_loop(0, steps, several, jnp.zeros((8, 128), F32))


def ends_kernel(n_y, pos, table, disp, damage, history, notch, labels, *refs):
    local = Local(
        pos, table, disp, damage, history, notch, labels, refs[:n_y], refs[n_y]
    )
    refs = refs[n_y + 1 :]
    xg, (rd_in, v_in, mom), ys_in, zs_in = (
        refs[:2],
        refs[2:5],
        refs[5 : 5 + n_y],
        refs[5 + n_y],
    )
    refs = refs[6 + n_y :]
    hist, rd_out, v_out, stress_out, mom_out = refs[:5]
    xs, ys, zs = refs[5:7], refs[7 : 7 + n_y], refs[7 + n_y]
    odd_x, count = local.odd_x, damage.shape[0]
    total = mom[...]
    found = []
    for end, x in enumerate((0, count - 1)):

        def outside(c):
            first, second = xg[0][c], xg[1][c]
            if end == 0:
                return jnp.where(odd_x, first, second)
            return jnp.where(odd_x, second, first)

        def beside(c):
            at = 1 if end == 0 else count - 2
            return damage[at] if c == 3 else disp[c, at]

        sides = (outside, beside) if end == 0 else (beside, outside)
        stress = {}

        def put(k, plane):
            stress[k] = stress_out[k, end] = plane

        hist_x, rd, v, part = local.plane(x, *sides, put)
        hist[end] = hist_x
        rd_out[x] = rd
        v_out[x] = v
        total = total + part
        found.append((stress, rd, v))
    for mine, before in zip(ys, ys_in, strict=True):
        for slot in range(8):
            mine[slot] = before[slot]
    for x in range(1, count - 1):
        rd_out[x] = rd_in[x]
        v_out[x] = v_in[x]
        zs[x] = zs_in[x]
    for end, x in enumerate((0, count - 1)):
        stress, rd, v = found[end]
        local.send_y(ys, x, v, rd, stress)
        local.send_z(zs, x, stress)
    for depth in (1, 2, 3):
        low, high = depth - 1, count - depth
        send(odd_x, xs, depth - 1, v_out[low], v_out[high])
        if depth <= 2:
            send(odd_x, xs, 2 + depth, rd_out[low], rd_out[high])
    for slot, k in ((5, 0), (6, 3), (7, 4)):
        send(odd_x, xs, slot, stress_out[k, 0], stress_out[k, 1])
    mom_out[...] = jnp.zeros((8, 128), F32)
    mom_out[0:1, :] = jnp.sum(total, axis=0, keepdims=True)


def corner_kernel(n_y, pos, after, v, rd, *ds):
    odd_x, odd_y = pos[0] == 1, pos[1] == 1
    count, rows = v.shape[0], v.shape[1]
    for depth in (1, 2):
        for slot, (src, deep) in enumerate(((v, 1), (v, 2), (v, 3), (rd, 1), (rd, 2))):
            near, far = pl.ds(deep - 1, 1), pl.ds(rows - deep, 1)
            planes = (depth - 1, count - depth)
            by_y = [(src[x, near, :], src[x, far, :]) for x in planes]
            for which in range(n_y):
                pair = (ds[which], ds[n_y + which])
                picked = [
                    jnp.where(odd_y, *(rows_of if which == 0 else rows_of[::-1]))
                    for rows_of in by_y
                ]
                send(odd_x, pair, (depth - 1, pl.ds(slot, 1), slice(None)), *picked)


class Enlarged:
    def __init__(self, n_y, pos, v, rd, refs):
        self.odd_x, self.odd_y = pos[0] == 1, pos[1] == 1
        self.v, self.rd, self.n_y = v, rd, n_y
        self.xg, self.yg, self.dg = refs[:2], refs[2 : 2 + n_y], refs[2 + n_y : 2 + 3 * n_y]

    def rows(self, found):
        nz = self.v.shape[2]
        at = iota2((8, nz), 0)

        def tile(first, depths):
            out = jnp.zeros((8, nz), F32)
            for depth in range(1, depths + 1):
                got = [found(w, first + depth - 1) for w in range(self.n_y)]
                if self.n_y == 1:
                    spot = jnp.where(self.odd_y, 8 - depth, depth - 1)
                    out = jnp.where(at == spot, got[0], out)
                else:
                    lo, hi = low_high(self.odd_y, got)
                    out = jnp.where(at == depth - 1, hi, out)
                    out = jnp.where(at == 8 - depth, lo, out)
            return out

        return tile(0, 3), tile(3, 2)

    def own(self, x):
        v_rows, rd_rows = self.rows(lambda w, slot: self.yg[w][slot, pl.ds(x, 1), :])
        return self.v[x], v_rows, self.rd[x], rd_rows

    def halo(self, is_low, depth):
        first, second = (0, 1) if is_low else (1, 0)

        def of(a, b):
            return jnp.where(self.odd_x, (a, b)[first], (a, b)[second])

        v = of(self.xg[0][depth - 1], self.xg[1][depth - 1])
        nothing = jnp.zeros((8, v.shape[1]), F32)
        if depth > 2:
            return v, nothing, jnp.zeros_like(v), nothing
        rd = of(self.xg[0][2 + depth], self.xg[1][2 + depth])

        def found(w, slot):
            spot = (depth - 1, pl.ds(slot, 1), slice(None))
            return of(self.dg[w][spot], self.dg[self.n_y + w][spot])

        v_rows, rd_rows = self.rows(found)
        return v, v_rows, rd, rd_rows

    def outer(self, count):
        for depth in (1, 2, 3):
            yield -depth, self.halo(True, depth)
            yield count - 1 + depth, self.halo(False, depth)


def join_kernel(n_y, pos, v, rd, token, *refs):
    big = Enlarged(n_y, pos, v, rd, refs[:-1])
    out = refs[-1]
    first_z = pos[2] == 0
    count, ny, depth = v.shape

    def tile(v_part, rd_part):
        lanes = iota2((v_part.shape[0], 128), 1)
        keep = lax.shift_right_logical(lanes, 6) == 1 - pos[2]
        mine = jnp.where(first_z, v_part[:, depth - 128 :], v_part[:, :128])
        moved = jnp.where(first_z, rd_part[:, depth - 128 :], rd_part[:, :128])
        return jnp.where(keep, mine, pltpu.roll(moved, 64, 1))

    def put(p, parts):
        v_own, v_rows, rd_own, rd_rows = parts
        out[p + 3, 0:ny] = tile(v_own, rd_own)
        out[p + 3, ny : ny + 8] = tile(v_rows, rd_rows)

    for p, parts in big.outer(count):
        put(p, parts)

    def body(x, carry):
        put(x, big.own(x))
        return carry

    unrolled(count, 8, body, 0)


def krylov_kernel(pos, main_v, main_rd, mom, z_got, *refs):
    moved, moved_ends, moved_hbm = refs[:2], refs[2:4], refs[4:6]
    v1_out, v2_out, spread, z_v, z_rd, big_v1, big_v2, sems = refs[6:]
    count, ny, nz = v1_out.shape
    inner = pl.ds(1, count - 2)
    copies = []
    for which, (src, ends, dst) in enumerate(zip(moved, moved_ends, moved_hbm)):
        for c in range(3):
            copies.append((src.at[c, inner], dst.at[c, inner], sems.at[which, c]))
        copies.append((ends.at[:, 0], dst.at[:, 0], sems.at[which, 3]))
        copies.append((ends.at[:, 1], dst.at[:, count - 1], sems.at[which, 4]))
    copies = [pltpu.make_async_copy(*copy) for copy in copies]
    for copy in copies:
        copy.start()

    def split(p, carry):
        tile = z_got[p]
        keep = lax.shift_right_logical(iota2(tile.shape, 1), 6) == pos[2]
        z_v[p] = jnp.where(keep, tile, 0.0)
        z_rd[p] = jnp.where(keep, pltpu.roll(tile, 64, 1), 0.0)
        return carry

    unrolled(count + 6, 11 if count % 11 == 5 else 1, split, 0)

    def v_at(at):
        return jnp.concatenate([main_v[at], z_v[at]], axis=1)

    def rd_at(at):
        return jnp.concatenate([main_rd[at], z_rd[at]], axis=1)

    def image_of(get, at):
        plane = get(at)
        rows, lanes = plane.shape
        near = (get(at - 1) + get(at + 1)) + (pltpu.roll(plane, 1, 0) + pltpu.roll(plane, rows - 1, 0))
        near = near + (pltpu.roll(plane, 1, 1) + pltpu.roll(plane, lanes - 1, 1))
        return plane, KAPPA_COEF * near

    def v1_at(at):
        return big_v1[at]

    def v2_at(at):
        return big_v2[at]

    def inside(values):
        return folded(values[0:ny, 0:nz])

    def first(x, totals):
        plane, image = image_of(v_at, x + 3)
        made = image * rd_at(x + 3)
        big_v1[x + 2] = made
        v1_out[x] = made[0:ny, 0:nz]
        return totals[0] + inside(plane * image), totals[1] + inside(made * image)

    def second(x, totals):
        plane, image = image_of(v1_at, x + 2)
        made = image * rd_at(x + 3)
        big_v2[x + 1] = made
        v2_out[x] = made[0:ny, 0:nz]
        return totals[0] + inside(plane * image), totals[1] + inside(made * image)

    def third(x, total):
        plane, image = image_of(v2_at, x + 1)
        return total + folded(plane[0:ny, 0:nz] * image[0:ny, 0:nz])

    zero = jnp.zeros((8, 128), F32)
    for p in (-2, -1, count, count + 1):
        big_v1[p + 2] = image_of(v_at, p + 3)[1] * rd_at(p + 3)
    k1, k2 = unrolled(count, 8, first, (zero, zero))
    for p in (-1, count):
        big_v2[p + 1] = image_of(v1_at, p + 2)[1] * rd_at(p + 3)
    k3, k4 = unrolled(count, 8, second, (zero, zero))
    k5 = unrolled(count, 8, third, zero)
    rows = iota2((8, 128), 0)
    result = mom[...]
    for at, total in enumerate((k1, k2, k3, k4, k5)):
        result = jnp.where(rows == at + 1, jnp.sum(total, axis=0, keepdims=True), result)
    for peer in range(spread.shape[0]):
        spread[peer] = result
    for copy in copies:
        copy.wait()


PARTS = ((0, 3, 4), (3, 1, 5), (4, 5, 2))


class Force:
    def __init__(self, n_y, pos, table, impact, disp, vel, contact, labels, yg, zg):
        self.odd_x, self.odd_y, self.gz = pos[0] == 1, pos[1] == 1, pos[2]
        self.impact, self.disp, self.vel = impact, disp, vel
        self.contact, self.labels, self.yg, self.zg = contact, labels, yg, zg
        self.rates = [table[2, r] for r in range(table.shape[1])]

    def plane(self, x, lower, mine, upper, vel_out, disp_out, at):
        loaded = self.contact[x].astype(F32)
        rate = by_label(self.labels[x], self.rates)
        for c, (kx, ky, kz) in enumerate(PARTS):
            rows = low_high(self.odd_y, [y[5 + c, pl.ds(x, 1), :] for y in self.yg])
            column = self.zg[x][:, c : c + 1]
            yu, yl = shift_y(mine(ky), rows)
            zu, zl = shift_z(mine(kz), column, self.gz == 0)
            force = 0.5 * (((upper(c, kx) - lower(c, kx)) + (yu - yl)) + (zu - zl))
            speed = self.vel[c, x] + rate * (force + loaded * self.impact[c])
            vel_out[c, at] = speed
            disp_out[c, at] = self.disp[c, x] + TIME_STEP * speed


def force_inner_kernel(n_y, pos, table, impact, disp, vel, contact, labels, *refs):
    yg, zg, stress, ends = refs[:n_y], refs[n_y], refs[n_y + 1], refs[n_y + 2]
    hist, hist_ends, hist_hbm, disp_out, vel_out, token, sems = refs[n_y + 3 :]
    token[...] = jnp.zeros((8, 128), F32)
    force = Force(n_y, pos, table, impact, disp, vel, contact, labels, yg, zg)
    count = contact.shape[0]
    steps, many = inner_steps(count)

    inside = pl.ds(1, count - 2)
    copies = [
        pltpu.make_async_copy(hist.at[inside], hist_hbm.at[inside], sems.at[0]),
        pltpu.make_async_copy(hist_ends.at[0], hist_hbm.at[0], sems.at[1]),
        pltpu.make_async_copy(hist_ends.at[1], hist_hbm.at[count - 1], sems.at[2]),
    ]
    for copy in copies:
        copy.start()

    def several(step, carry):
        for at in range(many):
            x = 1 + step * many + at

            def lower(c, k):
                if at == 0:
                    return jnp.where(step == 0, ends[k, 0], stress[k, x - 1])
                return stress[k, x - 1]

            def upper(c, k):
                if at == many - 1:
                    return jnp.where(step == steps - 1, ends[k, 1], stress[k, x + 1])
                return stress[k, x + 1]

            force.plane(x, lower, lambda k: stress[k, x], upper, vel_out, disp_out, x)
        return carry

    lax.fori_loop(0, steps, several, 0)
    for copy in copies:
        copy.wait()


def rest_kernel(n_y, pos, table, impact, disp, vel, contact, labels, *refs):
    yg, zg, stress, ends = refs[:n_y], refs[n_y], refs[n_y + 1], refs[n_y + 2]
    refs = refs[n_y + 3 :]
    v, rd, xy = refs[0], refs[1], refs[2 : 4 + 3 * n_y]
    xg = xy[:2]
    disp_out, vel_out, big_v, big_rd = refs[4 + 3 * n_y :]
    force = Force(n_y, pos, table, impact, disp, vel, contact, labels, yg, zg)
    count, ny = contact.shape[0], contact.shape[1]
    for end, x in enumerate((0, count - 1)):

        def outside(c, k):
            first, second = xg[0][5 + c], xg[1][5 + c]
            if end == 0:
                return jnp.where(force.odd_x, first, second)
            return jnp.where(force.odd_x, second, first)

        def beside(c, k):
            return stress[k, 1 if end == 0 else count - 2]

        lower, upper = (outside, beside) if end == 0 else (beside, outside)
        force.plane(x, lower, lambda k: ends[k, end], upper, vel_out, disp_out, end)
    big = Enlarged(n_y, pos, v, rd, xy)

    def put(p, parts):
        v_own, v_rows, rd_own, rd_rows = parts
        big_v[p + 3, 0:ny] = v_own
        big_v[p + 3, ny : ny + 8] = v_rows
        big_rd[p + 3, 0:ny] = rd_own
        big_rd[p + 3, ny : ny + 8] = rd_rows

    for p, parts in big.outer(count):
        put(p, parts)

    def body(x, carry):
        put(x, big.own(x))
        return carry

    unrolled(count, 4, body, 0)


def cg_coefficients(k):
    zero, one = jnp.zeros_like(k[0]), jnp.ones_like(k[0])
    z, p, out = [one], [one], [zero, zero, zero]

    def form(a, b, moments):
        total = None
        for i, ai in enumerate(a):
            for j, bj in enumerate(b):
                term = ai * bj * moments[i + j]
                total = term if total is None else total + term
        return total

    energy = [k[j] - k[j + 1] for j in range(5)]
    rz = k[0]
    for step in range(3):
        alpha = jnp.clip(rz / form(p, p, energy), ALPHA_LOW, ALPHA_HIGH)
        out = [o + alpha * (p[i] if i < len(p) else zero) for i, o in enumerate(out)]
        if step == 2:
            break
        image = [(p[i] if i < len(p) else zero) - (p[i - 1] if i else zero) for i in range(len(p) + 1)]
        z = [(z[i] if i < len(z) else zero) - alpha * image[i] for i in range(len(image))]
        new = jnp.maximum(form(z, z, k), 0.0)
        beta = new / rz
        p = [z[i] + beta * (p[i] if i < len(p) else zero) for i in range(len(z))]
        rz = new
    return out


def final_kernel(mom, v0, v1, v2, damage, out_hbm, out, sems):
    count = v0.shape[0]
    block = count // CHUNKS
    sums = jnp.sum(jnp.sum(mom[...], axis=0), axis=1, keepdims=True)
    c0, c1, c2 = cg_coefficients([sums[j : j + 1, :] for j in range(6)])
    copies = []
    for chunk in range(CHUNKS):
        for x in range(chunk * block, (chunk + 1) * block):
            dmg = damage[x]
            out[x] = jnp.maximum(dmg + (c0 * v0[x] + c1 * v1[x] + c2 * v2[x]), dmg)
        part = pl.ds(chunk * block, block)
        copies.append(pltpu.make_async_copy(out.at[part], out_hbm.at[part], sems.at[chunk]))
        copies[-1].start()
    for copy in copies:
        copy.wait()


def pairs_of(axis):
    count = lax.axis_size(axis)
    out = [[(i, i + 1) for i in range(start, count - 1, 2)] for start in (0, 1)]
    return [pairs for pairs in out if pairs]


def swap(array, axis, pairs):
    return lax.ppermute(array, axis, pairs + [(b, a) for a, b in pairs])


def swap_along(axis, arrays):
    return [swap(a, axis, pairs) for a, pairs in zip(arrays, pairs_of(axis), strict=True)]


def swap_diagonal(arrays):
    columns = lax.axis_size("gy")
    out = []
    both = [(xp, yp) for xp in pairs_of("gx") for yp in pairs_of("gy")]
    for array, (x_pairs, y_pairs) in zip(arrays, both, strict=True):
        joint = []
        for a, b in x_pairs:
            for c, d in y_pairs:
                joint.append((a * columns + c, b * columns + d))
                joint.append((a * columns + d, b * columns + c))
        out.append(swap(array, ("gx", "gy"), joint))
    return out


def spec_of(kind, a):
    if kind == "s":
        return pl.BlockSpec(memory_space=pltpu.SMEM)
    if kind == "v":
        return pl.BlockSpec(memory_space=pltpu.VMEM)
    if kind == "h":
        return pl.BlockSpec(memory_space=pltpu.HBM)
    if kind == "a":
        return pl.BlockSpec(memory_space=pl.ANY)
    raise ValueError(kind)


def call(kernel, kinds, ins, out_kinds, outs, flops, scratch=(), aliases=()):
    moved = sum(4 * a.size for a in (*ins, *outs))
    return pl.pallas_call(
        kernel,
        out_shape=outs,
        in_specs=[spec_of(k, a) for k, a in zip(kinds, ins, strict=True)],
        out_specs=[spec_of(k, a) for k, a in zip(out_kinds, outs, strict=True)],
        scratch_shapes=scratch,
        input_output_aliases=dict(aliases),
        compiler_params=pltpu.CompilerParams(vmem_limit_bytes=VMEM_BYTES),
        cost_estimate=pl.CostEstimate(flops=flops, bytes_accessed=moved, transcendentals=0),
    )(*ins)


def per_device(displacement, velocity, damage, history, contact, notch, labels, table, impact):
    nx, ny, nz = damage.shape
    size = damage.size
    n_y = len(pairs_of("gy"))
    pos = jnp.stack(
        [lax.axis_index("gx") % 2, lax.axis_index("gy") % 2, lax.axis_index("gz")]
    ).astype(jnp.int32)

    scaled = jnp.stack(
        [table[0] / 8.0, table[1] / 8.0, TIME_STEP / table[2], table[3] + 6.0 * KAPPA_COEF]
    )

    def arr(*shape):
        return jax.ShapeDtypeStruct(shape, F32)

    field, fields3, small = arr(nx, ny, nz), arr(3, nx, ny, nz), arr(8, 128)
    columns = arr(nx, ny, 128)
    z_pairs = [(0, 1)]

    sent = call(
        functools.partial(pack_kernel, n_y),
        "svv",
        (pos, displacement, damage),
        "v" * (1 + n_y),
        [*[arr(4, nx, nz)] * n_y, columns],
        size,
    )
    got_yz = [*swap_along("gy", sent[:n_y]), swap(sent[-1], "gz", z_pairs)]
    sent_x = call(
        pack_x_kernel,
        "svva",
        (pos, displacement, damage, sent[-1]),
        "vv",
        [arr(4, ny, nz)] * 2,
        size,
    )
    got_x = swap_along("gx", sent_x)
    rows = [arr(8, nx, nz)] * n_y
    voxels = (pos, scaled, displacement, damage, history, notch, labels, *got_yz)
    hist, rd, v0, stress, mom, *sent = call(
        functools.partial(inner_kernel, n_y),
        "ssvvvvv" + "v" * (1 + n_y),
        voxels,
        "vvvvv" + "v" * (1 + n_y),
        [field, field, field, arr(6, nx, ny, nz), small, *rows, columns],
        140 * size,
    )
    more = (*got_x, rd, v0, mom, *sent)
    hist_ends, rd, v0, ends, mom, *sent = call(
        functools.partial(ends_kernel, n_y),
        "ssvvvvv" + "v" * (1 + n_y) + "vvvvv" + "v" * (1 + n_y),
        (*voxels, *more),
        "vvvvv" + "v" * (3 + n_y),
        [
            arr(2, ny, nz),
            field,
            field,
            arr(6, 2, ny, nz),
            small,
            *[arr(8, ny, nz)] * 2,
            *rows,
            columns,
        ],
        20 * size,
    )
    stress_z = swap(sent[-1], "gz", z_pairs)
    xs = swap_along("gx", sent[:2])
    ys = swap_along("gy", sent[2 : 2 + n_y])
    corners = call(
        functools.partial(corner_kernel, n_y),
        "savv",
        (pos, stress_z, v0, rd),
        "v" * (2 * n_y),
        [arr(2, 8, nz)] * (2 * n_y),
        1024,
    )
    xy = [*xs, *ys, *swap_diagonal(corners)]
    moving = (
        pos,
        scaled,
        impact,
        displacement,
        velocity,
        contact,
        labels,
        *ys,
        stress_z,
        stress,
        ends,
    )
    hist_new, *moved, token = call(
        functools.partial(force_inner_kernel, n_y),
        "sssvvvv" + "v" * (3 + n_y) + "vv",
        (*moving, hist, hist_ends),
        "hvvv",
        [field, fields3, fields3, small],
        55 * size,
        [pltpu.SemaphoreType.DMA((3,))],
    )
    (joined,) = call(
        functools.partial(join_kernel, n_y),
        "svva" + "v" * len(xy),
        (pos, v0, rd, token, *xy),
        "v",
        [arr(nx + 6, ny + 8, 128)],
        4 * size,
    )
    z_got = swap(joined, "gz", z_pairs)
    *moved_ends, main_v, main_rd = call(
        functools.partial(rest_kernel, n_y),
        "sssvvvv" + "v" * (3 + n_y) + "vv" + "v" * len(xy),
        (*moving, v0, rd, *xy),
        "vvvv",
        [arr(3, 2, ny, nz)] * 2 + [arr(nx + 6, ny + 8, nz)] * 2,
        12 * size,
    )
    peers = lax.axis_size("gx") * lax.axis_size("gy") * lax.axis_size("gz")
    new_disp, new_vel, v1, v2, spread = call(
        krylov_kernel,
        "svvvvvvvv",
        (pos, main_v, main_rd, mom, z_got, *moved, *moved_ends),
        "hhvvv",
        [fields3, fields3, field, field, arr(peers, 8, 128)],
        60 * size,
        [
            pltpu.VMEM((nx + 6, ny + 8, 128), F32),
            pltpu.VMEM((nx + 6, ny + 8, 128), F32),
            pltpu.VMEM((nx + 4, ny + 8, nz + 128), F32),
            pltpu.VMEM((nx + 2, ny + 8, nz + 128), F32),
            pltpu.SemaphoreType.DMA((2, 5)),
        ],
    )
    mom = lax.all_to_all(spread, ("gx", "gy", "gz"), 0, 0, tiled=True)
    (damage_new,) = call(
        final_kernel,
        "vvvvv",
        (mom, v0, v1, v2, damage),
        "h",
        [field],
        8 * size,
        [pltpu.VMEM((nx, ny, nz), F32), pltpu.SemaphoreType.DMA((CHUNKS,))],
    )
    return new_disp, new_vel, hist_new, damage_new


def solution(mesh):
    placed = (
        P(None, ("case", "gx"), "gy", "gz"),
        P(None, ("case", "gx"), "gy", "gz"),
        P(("case", "gx"), "gy", "gz"),
        P(("case", "gx"), "gy", "gz"),
        P(("case", "gx"), "gy", "gz"),
        P(("case", "gx"), "gy", "gz"),
        P(("case", "gx"), "gy", "gz"),
        P(),
        P("case"),
    )
    return jax.shard_map(
        per_device,
        mesh=mesh,
        in_specs=placed,
        out_specs=(
            P(None, ("case", "gx"), "gy", "gz"),
            P(None, ("case", "gx"), "gy", "gz"),
            P(("case", "gx"), "gy", "gz"),
            P(("case", "gx"), "gy", "gz"),
        ),
        check_vma=False,
    )
```

```python
import functools
import jax
import jax.numpy as jnp
from jax import lax
from jax.experimental import pallas as pl
from jax.experimental.pallas import tpu as pltpu
from jax.sharding import PartitionSpec as P

TIME_STEP = 0.1
KAPPA_COEF = 0.5
NOTCH_LOAD = 20.0
STIFF_FLOOR = 0.001
ALPHA_LOW, ALPHA_HIGH = 0.5, 6.5
VMEM_BYTES = 28 * 1024 * 1024
CHUNKS = 4
F32 = jnp.float32


def iota2(shape, dim):
    return lax.broadcasted_iota(jnp.int32, shape, dim)


def low_high(odd, got):
    if len(got) == 2:
        return jnp.where(odd, got[0], got[1]), jnp.where(odd, got[1], got[0])
    return jnp.where(odd, got[0], 0.0), jnp.where(odd, 0.0, got[0])


def send(odd, refs, index, low, high):
    refs[0][index] = jnp.where(odd, low, high)
    if len(refs) == 2:
        refs[1][index] = jnp.where(odd, high, low)


def shift_y(plane, rows):
    lo, hi = rows
    tiles = [plane[start : start + 8] for start in range(0, plane.shape[0], 8)]
    at = iota2(tiles[0].shape, 0)
    ahead = [pltpu.roll(tile, 7, 0) for tile in tiles]
    behind = [pltpu.roll(tile, 1, 0) for tile in tiles]
    upper = [jnp.where(at == 7, b, a) for a, b in zip(ahead, [*ahead[1:], hi])]
    lower = [jnp.where(at == 0, b, a) for a, b in zip(behind, [lo, *behind[:-1]])]
    return jnp.concatenate(upper, axis=0), jnp.concatenate(lower, axis=0)


def shift_z(plane, column, first_z):
    tiles = [plane[:, start : start + 128] for start in range(0, plane.shape[1], 128)]
    at = iota2(tiles[0].shape, 1)
    wide = jnp.broadcast_to(column, tiles[0].shape)
    lo, hi = jnp.where(first_z, 0.0, wide), jnp.where(first_z, wide, 0.0)
    ahead = [pltpu.roll(tile, 127, 1) for tile in tiles]
    behind = [pltpu.roll(tile, 1, 1) for tile in tiles]
    upper = [jnp.where(at == 127, b, a) for a, b in zip(ahead, [*ahead[1:], hi])]
    lower = [jnp.where(at == 0, b, a) for a, b in zip(behind, [lo, *behind[:-1]])]
    return jnp.concatenate(upper, axis=1), jnp.concatenate(lower, axis=1)


def send_columns(ref, x, planes, gz):
    depth = planes[0].shape[1]
    lanes = iota2((planes[0].shape[0], 128), 1)
    tile = None
    for field, plane in enumerate(planes):
        part = jnp.where(gz == 0, plane[:, depth - 128 :], plane[:, :128])
        part = pltpu.roll(part, field + 1 - gz, 1)
        tile = part if tile is None else jnp.where(lanes == field, part, tile)
    ref[x] = tile


def folded(values):
    total = None
    for start in range(0, values.shape[1], 128):
        part = values[:, start : start + 128]
        total = part if total is None else total + part
    out = None
    for start in range(0, values.shape[0], 8):
        part = total[start : start + 8]
        out = part if out is None else out + part
    return out


def by_label(labels, scalars):
    picked = scalars[0]
    for region in range(1, len(scalars)):
        picked = jnp.where(labels == region, scalars[region], picked)
    return picked


def unrolled(count, many, body, carry):
    def several(block, carry):
        for at in range(many):
            carry = body(block * many + at, carry)
        return carry

    return lax.fori_loop(0, count // many, several, carry)


def pack_kernel(n_y, pos, disp, *refs):
    damage = disp.at[3]
    ys, zs = refs[:n_y], refs[n_y]
    odd_y, gz = pos[1] == 1, pos[2]

    def body(x, carry):
        planes = [disp[0, x], disp[1, x], disp[2, x], damage[x]]
        for field, plane in enumerate(planes):
            last = plane.shape[0] - 1
            spot = (field, pl.ds(x, 1), slice(None))
            send(odd_y, ys, spot, plane[0:1], plane[last : last + 1])
        send_columns(zs, x, planes, gz)
        return carry

    unrolled(damage.shape[0], 8, body, 0)


def pack_x_kernel(pos, disp, after, *xs):
    damage = disp.at[3]
    odd_x, count = pos[0] == 1, damage.shape[0]
    for field, src in enumerate((disp.at[0], disp.at[1], disp.at[2], damage)):
        send(odd_x, xs, field, src[0], src[count - 1])


class Local:
    def __init__(self, pos, table, disp, damage, history, notch, labels, yg, zg):
        self.odd_x, self.odd_y, self.gz = pos[0] == 1, pos[1] == 1, pos[2]
        self.disp, self.damage, self.history = disp, damage, history
        self.notch, self.labels, self.yg, self.zg = notch, labels, yg, zg
        regions = range(table.shape[1])
        self.lames = [table[0, r] for r in regions]
        self.shears = [table[1, r] for r in regions]
        self.bases = [table[3, r] for r in regions]

    def plane(self, x, lower, upper, put):
        lab = self.labels[x]
        shear = by_label(lab, self.shears)
        dmg = self.damage[x]
        degrade = 4.0 * ((1.0 - dmg) * (1.0 - dmg) + STIFF_FLOOR)
        half = degrade * shear
        fields = [self.disp[c, x] for c in range(3)]

        def d(c, j):
            if j == 0:
                return upper(c) - lower(c)
            if j == 1:
                rows = low_high(self.odd_y, [y[c, pl.ds(x, 1), :] for y in self.yg])
                high, low = shift_y(fields[c], rows)
            else:
                column = self.zg[x][:, c : c + 1]
                high, low = shift_z(fields[c], column, self.gz == 0)
            return high - low

        squares = None
        for k, (i, j) in ((3, (0, 1)), (4, (0, 2)), (5, (1, 2))):
            e = d(i, j) + d(j, i)
            put(k, half * e)
            squares = e * e if squares is None else squares + e * e
        straight = [d(c, c) for c in range(3)]
        trace = straight[0] + straight[1] + straight[2]
        lame = by_label(lab, self.lames)
        level = (degrade * lame) * trace
        whole = half + half
        for k in range(3):
            put(k, level + whole * straight[k])
        twice = (
            straight[0] * straight[0] + straight[1] * straight[1] + straight[2] * straight[2]
        )
        squares = squares + (twice + twice)
        positive = jnp.maximum(trace, 0.0)
        energy = lame * positive * positive + shear * squares
        hist = jnp.maximum(
            jnp.maximum(self.history[x], energy), NOTCH_LOAD * self.notch[x].astype(F32)
        )
        diagonal = by_label(lab, self.bases) + 2.0 * hist
        rd = 1.0 / diagonal
        rows = low_high(self.odd_y, [y[3, pl.ds(x, 1), :] for y in self.yg])
        yu, yl = shift_y(dmg, rows)
        zu, zl = shift_z(dmg, self.zg[x][:, 3:4], self.gz == 0)
        near = ((upper(3) + lower(3)) + (yu + yl)) + (zu + zl)
        residual = 2.0 * hist - (diagonal * dmg - KAPPA_COEF * near)
        v = residual * rd
        return hist, rd, v, folded(residual * v)

    def send_y(self, ys, x, v, rd, stress):
        rows = v.shape[0]
        sources = [(v, depth) for depth in (1, 2, 3)] + [(rd, depth) for depth in (1, 2)]
        sources += [(stress[k], 1) for k in (3, 1, 5)]
        for slot, (plane, depth) in enumerate(sources):
            low, high = plane[depth - 1 : depth], plane[rows - depth : rows - depth + 1]
            send(self.odd_y, ys, (slot, pl.ds(x, 1), slice(None)), low, high)

    def send_z(self, zs, x, stress):
        send_columns(zs, x, [stress[4], stress[5], stress[2]], self.gz)


def inner_steps(count):
    inner = count - 2
    many = max(m for m in range(1, 8) if inner % m == 0)
    return inner // many, many


def inner_kernel(n_y, pos, table, disp, history, notch, labels, *refs):
    damage = disp.at[3]
    local = Local(
        pos, table, disp, damage, history, notch, labels, refs[:n_y], refs[n_y]
    )
    hist, rd_out, v_out, stress_out, mom_out = refs[n_y + 1 : n_y + 6]
    ys, zs = refs[n_y + 6 : 2 * n_y + 6], refs[2 * n_y + 6]
    steps, many = inner_steps(damage.shape[0])

    def several(step, total):
        for at in range(many):
            x = 1 + step * many + at

            def lower(c):
                return damage[x - 1] if c == 3 else disp[c, x - 1]

            def upper(c):
                return damage[x + 1] if c == 3 else disp[c, x + 1]

            stress = {}

            def put(k, plane):
                stress[k] = stress_out[k, x] = plane

            hist_x, rd, v, part = local.plane(x, lower, upper, put)
            hist[x] = hist_x
            rd_out[x] = rd
            v_out[x] = v
            local.send_y(ys, x, v, rd, stress)
            local.send_z(zs, x, stress)
            total = total + part
        return total

    mom_out[...] = lax.fori_loop(0, steps, several, jnp.zeros((8, 128), F32))


def ends_kernel(n_y, pos, table, disp, history, notch, labels, *refs):
    damage = disp.at[3]
    local = Local(
        pos, table, disp, damage, history, notch, labels, refs[:n_y], refs[n_y]
    )
    refs = refs[n_y + 1 :]
    xg, (rd_in, v_in, mom), ys_in, zs_in = (
        refs[:2],
        refs[2:5],
        refs[5 : 5 + n_y],
        refs[5 + n_y],
    )
    refs = refs[6 + n_y :]
    hist, rd_out, v_out, stress_out, mom_out = refs[:5]
    xs, ys, zs = refs[5:7], refs[7 : 7 + n_y], refs[7 + n_y]
    odd_x, count = local.odd_x, damage.shape[0]
    total = mom[...]
    found = []
    for end, x in enumerate((0, count - 1)):

        def outside(c):
            first, second = xg[0][c], xg[1][c]
            if end == 0:
                return jnp.where(odd_x, first, second)
            return jnp.where(odd_x, second, first)

        def beside(c):
            at = 1 if end == 0 else count - 2
            return damage[at] if c == 3 else disp[c, at]

        sides = (outside, beside) if end == 0 else (beside, outside)
        stress = {}

        def put(k, plane):
            stress[k] = stress_out[k, end] = plane

        hist_x, rd, v, part = local.plane(x, *sides, put)
        hist[end] = hist_x
        rd_out[x] = rd
        v_out[x] = v
        total = total + part
        found.append((stress, rd, v))
    for mine, before in zip(ys, ys_in, strict=True):
        for slot in range(8):
            mine[slot] = before[slot]
    for x in range(1, count - 1):
        rd_out[x] = rd_in[x]
        v_out[x] = v_in[x]
        zs[x] = zs_in[x]
    for end, x in enumerate((0, count - 1)):
        stress, rd, v = found[end]
        local.send_y(ys, x, v, rd, stress)
        local.send_z(zs, x, stress)
    for depth in (1, 2, 3):
        low, high = depth - 1, count - depth
        send(odd_x, xs, depth - 1, v_out[low], v_out[high])
        if depth <= 2:
            send(odd_x, xs, 2 + depth, rd_out[low], rd_out[high])
    for slot, k in ((5, 0), (6, 3), (7, 4)):
        send(odd_x, xs, slot, stress_out[k, 0], stress_out[k, 1])
    mom_out[...] = jnp.zeros((8, 128), F32)
    mom_out[0:1, :] = jnp.sum(total, axis=0, keepdims=True)


def corner_kernel(n_y, pos, after, v, rd, *ds):
    odd_x, odd_y = pos[0] == 1, pos[1] == 1
    count, rows = v.shape[0], v.shape[1]
    for depth in (1, 2):
        for slot, (src, deep) in enumerate(((v, 1), (v, 2), (v, 3), (rd, 1), (rd, 2))):
            near, far = pl.ds(deep - 1, 1), pl.ds(rows - deep, 1)
            planes = (depth - 1, count - depth)
            by_y = [(src[x, near, :], src[x, far, :]) for x in planes]
            for which in range(n_y):
                pair = (ds[which], ds[n_y + which])
                picked = [
                    jnp.where(odd_y, *(rows_of if which == 0 else rows_of[::-1]))
                    for rows_of in by_y
                ]
                send(odd_x, pair, (depth - 1, pl.ds(slot, 1), slice(None)), *picked)


class Enlarged:
    def __init__(self, n_y, pos, v, rd, refs):
        self.odd_x, self.odd_y = pos[0] == 1, pos[1] == 1
        self.v, self.rd, self.n_y = v, rd, n_y
        self.xg, self.yg, self.dg = refs[:2], refs[2 : 2 + n_y], refs[2 + n_y : 2 + 3 * n_y]

    def rows(self, found):
        nz = self.v.shape[2]
        at = iota2((8, nz), 0)

        def tile(first, depths):
            out = jnp.zeros((8, nz), F32)
            for depth in range(1, depths + 1):
                got = [found(w, first + depth - 1) for w in range(self.n_y)]
                if self.n_y == 1:
                    spot = jnp.where(self.odd_y, 8 - depth, depth - 1)
                    out = jnp.where(at == spot, got[0], out)
                else:
                    lo, hi = low_high(self.odd_y, got)
                    out = jnp.where(at == depth - 1, hi, out)
                    out = jnp.where(at == 8 - depth, lo, out)
            return out

        return tile(0, 3), tile(3, 2)

    def own(self, x):
        v_rows, rd_rows = self.rows(lambda w, slot: self.yg[w][slot, pl.ds(x, 1), :])
        return self.v[x], v_rows, self.rd[x], rd_rows

    def halo(self, is_low, depth):
        first, second = (0, 1) if is_low else (1, 0)

        def of(a, b):
            return jnp.where(self.odd_x, (a, b)[first], (a, b)[second])

        v = of(self.xg[0][depth - 1], self.xg[1][depth - 1])
        nothing = jnp.zeros((8, v.shape[1]), F32)
        if depth > 2:
            return v, nothing, jnp.zeros_like(v), nothing
        rd = of(self.xg[0][2 + depth], self.xg[1][2 + depth])

        def found(w, slot):
            spot = (depth - 1, pl.ds(slot, 1), slice(None))
            return of(self.dg[w][spot], self.dg[self.n_y + w][spot])

        v_rows, rd_rows = self.rows(found)
        return v, v_rows, rd, rd_rows

    def outer(self, count):
        for depth in (1, 2, 3):
            yield -depth, self.halo(True, depth)
            yield count - 1 + depth, self.halo(False, depth)


def join_kernel(n_y, pos, v, rd, token, *refs):
    big = Enlarged(n_y, pos, v, rd, refs[:-1])
    out = refs[-1]
    first_z = pos[2] == 0
    count, ny, depth = v.shape

    def tile(v_part, rd_part):
        lanes = iota2((v_part.shape[0], 128), 1)
        keep = lax.shift_right_logical(lanes, 6) == 1 - pos[2]
        mine = jnp.where(first_z, v_part[:, depth - 128 :], v_part[:, :128])
        moved = jnp.where(first_z, rd_part[:, depth - 128 :], rd_part[:, :128])
        return jnp.where(keep, mine, pltpu.roll(moved, 64, 1))

    def put(p, parts):
        v_own, v_rows, rd_own, rd_rows = parts
        out[p + 3, 0:ny] = tile(v_own, rd_own)
        out[p + 3, ny : ny + 8] = tile(v_rows, rd_rows)

    for p, parts in big.outer(count):
        put(p, parts)

    def body(x, carry):
        put(x, big.own(x))
        return carry

    unrolled(count, 8, body, 0)


def krylov_kernel(pos, main_v, main_rd, mom, z_got, *refs):
    moved, moved_ends, moved_hbm = refs[:2], refs[2:4], refs[4:6]
    v1_out, v2_out, spread, z_v, z_rd, big_v1, big_v2, sems = refs[6:]
    count, ny, nz = v1_out.shape
    inner = pl.ds(1, count - 2)
    copies = []
    for which, (src, ends, dst) in enumerate(zip(moved, moved_ends, moved_hbm)):
        for c in range(3):
            copies.append((src.at[c, inner], dst.at[c, inner], sems.at[which, c]))
        copies.append((ends.at[:, 0], dst.at[:, 0], sems.at[which, 3]))
        copies.append((ends.at[:, 1], dst.at[:, count - 1], sems.at[which, 4]))
    copies = [pltpu.make_async_copy(*copy) for copy in copies]
    for copy in copies:
        copy.start()

    def split(p, carry):
        tile = z_got[p]
        keep = lax.shift_right_logical(iota2(tile.shape, 1), 6) == pos[2]
        z_v[p] = jnp.where(keep, tile, 0.0)
        z_rd[p] = jnp.where(keep, pltpu.roll(tile, 64, 1), 0.0)
        return carry

    unrolled(count + 6, 11 if count % 11 == 5 else 1, split, 0)

    def v_at(at):
        return jnp.concatenate([main_v[at], z_v[at]], axis=1)

    def rd_at(at):
        return jnp.concatenate([main_rd[at], z_rd[at]], axis=1)

    def image_of(get, at):
        plane = get(at)
        rows, lanes = plane.shape
        near = (get(at - 1) + get(at + 1)) + (pltpu.roll(plane, 1, 0) + pltpu.roll(plane, rows - 1, 0))
        near = near + (pltpu.roll(plane, 1, 1) + pltpu.roll(plane, lanes - 1, 1))
        return plane, KAPPA_COEF * near

    def v1_at(at):
        return big_v1[at]

    def v2_at(at):
        return big_v2[at]

    def inside(values):
        return folded(values[0:ny, 0:nz])

    def first(x, totals):
        plane, image = image_of(v_at, x + 3)
        made = image * rd_at(x + 3)
        big_v1[x + 2] = made
        v1_out[x] = made[0:ny, 0:nz]
        return totals[0] + inside(plane * image), totals[1] + inside(made * image)

    def second(x, totals):
        plane, image = image_of(v1_at, x + 2)
        made = image * rd_at(x + 3)
        big_v2[x + 1] = made
        v2_out[x] = made[0:ny, 0:nz]
        return totals[0] + inside(plane * image), totals[1] + inside(made * image)

    def third(x, total):
        plane, image = image_of(v2_at, x + 1)
        return total + folded(plane[0:ny, 0:nz] * image[0:ny, 0:nz])

    zero = jnp.zeros((8, 128), F32)
    for p in (-2, -1, count, count + 1):
        big_v1[p + 2] = image_of(v_at, p + 3)[1] * rd_at(p + 3)
    k1, k2 = unrolled(count, 8, first, (zero, zero))
    for p in (-1, count):
        big_v2[p + 1] = image_of(v1_at, p + 2)[1] * rd_at(p + 3)
    k3, k4 = unrolled(count, 8, second, (zero, zero))
    k5 = unrolled(count, 8, third, zero)
    rows = iota2((8, 128), 0)
    result = mom[...]
    for at, total in enumerate((k1, k2, k3, k4, k5)):
        result = jnp.where(rows == at + 1, jnp.sum(total, axis=0, keepdims=True), result)
    mine = rows == iota2((8, 128), 1)
    line = jnp.sum(
        jnp.where(mine, jnp.sum(result, axis=1, keepdims=True), 0.0), axis=0, keepdims=True
    )
    for peer in range(spread.shape[0]):
        spread[peer] = line
    for copy in copies:
        copy.wait()


PARTS = ((0, 3, 4), (3, 1, 5), (4, 5, 2))


class Force:
    def __init__(self, n_y, pos, table, impact, disp, vel, contact, labels, yg, zg):
        self.odd_x, self.odd_y, self.gz = pos[0] == 1, pos[1] == 1, pos[2]
        self.impact, self.disp, self.vel = impact, disp, vel
        self.contact, self.labels, self.yg, self.zg = contact, labels, yg, zg
        self.rates = [table[2, r] for r in range(table.shape[1])]

    def plane(self, x, lower, mine, upper, vel_out, disp_out, at):
        loaded = self.contact[x].astype(F32)
        rate = by_label(self.labels[x], self.rates)
        for c, (kx, ky, kz) in enumerate(PARTS):
            rows = low_high(self.odd_y, [y[5 + c, pl.ds(x, 1), :] for y in self.yg])
            column = self.zg[x][:, c : c + 1]
            yu, yl = shift_y(mine(ky), rows)
            zu, zl = shift_z(mine(kz), column, self.gz == 0)
            force = 0.5 * (((upper(c, kx) - lower(c, kx)) + (yu - yl)) + (zu - zl))
            speed = self.vel[c, x] + rate * (force + loaded * self.impact[c])
            vel_out[c, at] = speed
            disp_out[c, at] = self.disp[c, x] + TIME_STEP * speed


def force_inner_kernel(n_y, pos, table, impact, disp, vel, contact, labels, *refs):
    yg, zg, stress, ends = refs[:n_y], refs[n_y], refs[n_y + 1], refs[n_y + 2]
    hist, hist_ends, hist_hbm, disp_out, vel_out, token, sems = refs[n_y + 3 :]
    token[...] = jnp.zeros((8, 128), F32)
    force = Force(n_y, pos, table, impact, disp, vel, contact, labels, yg, zg)
    count = contact.shape[0]
    steps, many = inner_steps(count)

    inside = pl.ds(1, count - 2)
    copies = [
        pltpu.make_async_copy(hist.at[inside], hist_hbm.at[inside], sems.at[0]),
        pltpu.make_async_copy(hist_ends.at[0], hist_hbm.at[0], sems.at[1]),
        pltpu.make_async_copy(hist_ends.at[1], hist_hbm.at[count - 1], sems.at[2]),
    ]
    for copy in copies:
        copy.start()

    def several(step, carry):
        for at in range(many):
            x = 1 + step * many + at

            def lower(c, k):
                if at == 0:
                    return jnp.where(step == 0, ends[k, 0], stress[k, x - 1])
                return stress[k, x - 1]

            def upper(c, k):
                if at == many - 1:
                    return jnp.where(step == steps - 1, ends[k, 1], stress[k, x + 1])
                return stress[k, x + 1]

            force.plane(x, lower, lambda k: stress[k, x], upper, vel_out, disp_out, x)
        return carry

    lax.fori_loop(0, steps, several, 0)
    for copy in copies:
        copy.wait()


def rest_kernel(n_y, pos, table, impact, disp, vel, contact, labels, *refs):
    yg, zg, stress, ends = refs[:n_y], refs[n_y], refs[n_y + 1], refs[n_y + 2]
    refs = refs[n_y + 3 :]
    v, rd, xy = refs[0], refs[1], refs[2 : 4 + 3 * n_y]
    xg = xy[:2]
    disp_out, vel_out, big_v, big_rd = refs[4 + 3 * n_y :]
    force = Force(n_y, pos, table, impact, disp, vel, contact, labels, yg, zg)
    count, ny = contact.shape[0], contact.shape[1]
    for end, x in enumerate((0, count - 1)):

        def outside(c, k):
            first, second = xg[0][5 + c], xg[1][5 + c]
            if end == 0:
                return jnp.where(force.odd_x, first, second)
            return jnp.where(force.odd_x, second, first)

        def beside(c, k):
            return stress[k, 1 if end == 0 else count - 2]

        lower, upper = (outside, beside) if end == 0 else (beside, outside)
        force.plane(x, lower, lambda k: ends[k, end], upper, vel_out, disp_out, end)
    big = Enlarged(n_y, pos, v, rd, xy)

    def put(p, parts):
        v_own, v_rows, rd_own, rd_rows = parts
        big_v[p + 3, 0:ny] = v_own
        big_v[p + 3, ny : ny + 8] = v_rows
        big_rd[p + 3, 0:ny] = rd_own
        big_rd[p + 3, ny : ny + 8] = rd_rows

    for p, parts in big.outer(count):
        put(p, parts)

    def body(x, carry):
        put(x, big.own(x))
        return carry

    unrolled(count, 4, body, 0)


def cg_coefficients(k):
    zero, one = jnp.zeros_like(k[0]), jnp.ones_like(k[0])
    z, p, out = [one], [one], [zero, zero, zero]

    def form(a, b, moments):
        total = None
        for i, ai in enumerate(a):
            for j, bj in enumerate(b):
                term = ai * bj * moments[i + j]
                total = term if total is None else total + term
        return total

    energy = [k[j] - k[j + 1] for j in range(5)]
    rz = k[0]
    for step in range(3):
        alpha = jnp.clip(rz / form(p, p, energy), ALPHA_LOW, ALPHA_HIGH)
        out = [o + alpha * (p[i] if i < len(p) else zero) for i, o in enumerate(out)]
        if step == 2:
            break
        image = [(p[i] if i < len(p) else zero) - (p[i - 1] if i else zero) for i in range(len(p) + 1)]
        z = [(z[i] if i < len(z) else zero) - alpha * image[i] for i in range(len(image))]
        new = jnp.maximum(form(z, z, k), 0.0)
        beta = new / rz
        p = [z[i] + beta * (p[i] if i < len(p) else zero) for i in range(len(z))]
        rz = new
    return out


def final_kernel(mom, v0, v1, v2, damage, out_hbm, out, sems):
    count = v0.shape[0]
    block = count // CHUNKS
    sums = jnp.sum(mom[...], axis=0)
    c0, c1, c2 = cg_coefficients([sums[:, j : j + 1] for j in range(6)])
    copies = []
    for chunk in range(CHUNKS):
        for x in range(chunk * block, (chunk + 1) * block):
            dmg = damage[x]
            out[x] = jnp.maximum(dmg + (c0 * v0[x] + c1 * v1[x] + c2 * v2[x]), dmg)
        part = pl.ds(chunk * block, block)
        copies.append(pltpu.make_async_copy(out.at[part], out_hbm.at[part], sems.at[chunk]))
        copies[-1].start()
    for copy in copies:
        copy.wait()


def pairs_of(axis):
    count = lax.axis_size(axis)
    out = [[(i, i + 1) for i in range(start, count - 1, 2)] for start in (0, 1)]
    return [pairs for pairs in out if pairs]


def swap(array, axis, pairs):
    return lax.ppermute(array, axis, pairs + [(b, a) for a, b in pairs])


def swap_along(axis, arrays):
    return [swap(a, axis, pairs) for a, pairs in zip(arrays, pairs_of(axis), strict=True)]


def swap_diagonal(arrays):
    columns = lax.axis_size("gy")
    out = []
    both = [(xp, yp) for xp in pairs_of("gx") for yp in pairs_of("gy")]
    for array, (x_pairs, y_pairs) in zip(arrays, both, strict=True):
        joint = []
        for a, b in x_pairs:
            for c, d in y_pairs:
                joint.append((a * columns + c, b * columns + d))
                joint.append((a * columns + d, b * columns + c))
        out.append(swap(array, ("gx", "gy"), joint))
    return out


def spec_of(kind, a):
    if kind == "s":
        return pl.BlockSpec(memory_space=pltpu.SMEM)
    if kind == "v":
        return pl.BlockSpec(memory_space=pltpu.VMEM)
    if kind == "h":
        return pl.BlockSpec(memory_space=pltpu.HBM)
    if kind == "a":
        return pl.BlockSpec(memory_space=pl.ANY)
    raise ValueError(kind)


def call(kernel, kinds, ins, out_kinds, outs, flops, scratch=(), aliases=()):
    moved = sum(4 * a.size for a in (*ins, *outs))
    return pl.pallas_call(
        kernel,
        out_shape=outs,
        in_specs=[spec_of(k, a) for k, a in zip(kinds, ins, strict=True)],
        out_specs=[spec_of(k, a) for k, a in zip(out_kinds, outs, strict=True)],
        scratch_shapes=scratch,
        input_output_aliases=dict(aliases),
        compiler_params=pltpu.CompilerParams(vmem_limit_bytes=VMEM_BYTES),
        cost_estimate=pl.CostEstimate(flops=flops, bytes_accessed=moved, transcendentals=0),
    )(*ins)


def per_device(displacement, velocity, damage, history, contact, notch, labels, table, impact):
    nx, ny, nz = damage.shape
    size = damage.size
    n_y = len(pairs_of("gy"))
    pos = jnp.stack(
        [lax.axis_index("gx") % 2, lax.axis_index("gy") % 2, lax.axis_index("gz")]
    ).astype(jnp.int32)

    scaled = jnp.stack(
        [table[0] / 8.0, table[1] / 8.0, TIME_STEP / table[2], table[3] + 6.0 * KAPPA_COEF]
    )

    def arr(*shape):
        return jax.ShapeDtypeStruct(shape, F32)

    field, fields3, small = arr(nx, ny, nz), arr(3, nx, ny, nz), arr(8, 128)
    columns = arr(nx, ny, 128)
    z_pairs = [(0, 1)]

    both = jnp.concatenate([displacement, damage[None]])
    sent = call(
        functools.partial(pack_kernel, n_y),
        "sv",
        (pos, both),
        "v" * (1 + n_y),
        [*[arr(4, nx, nz)] * n_y, columns],
        size,
    )
    got_yz = [*swap_along("gy", sent[:n_y]), swap(sent[-1], "gz", z_pairs)]
    sent_x = call(
        pack_x_kernel,
        "sva",
        (pos, both, sent[-1]),
        "vv",
        [arr(4, ny, nz)] * 2,
        size,
    )
    got_x = swap_along("gx", sent_x)
    rows = [arr(8, nx, nz)] * n_y
    voxels = (pos, scaled, both, history, notch, labels, *got_yz)
    hist, rd, v0, stress, mom, *sent = call(
        functools.partial(inner_kernel, n_y),
        "ssvvvv" + "v" * (1 + n_y),
        voxels,
        "vvvvv" + "v" * (1 + n_y),
        [field, field, field, arr(6, nx, ny, nz), small, *rows, columns],
        140 * size,
    )
    more = (*got_x, rd, v0, mom, *sent)
    hist_ends, rd, v0, ends, mom, *sent = call(
        functools.partial(ends_kernel, n_y),
        "ssvvvv" + "v" * (1 + n_y) + "vvvvv" + "v" * (1 + n_y),
        (*voxels, *more),
        "vvvvv" + "v" * (3 + n_y),
        [
            arr(2, ny, nz),
            field,
            field,
            arr(6, 2, ny, nz),
            small,
            *[arr(8, ny, nz)] * 2,
            *rows,
            columns,
        ],
        20 * size,
    )
    stress_z = swap(sent[-1], "gz", z_pairs)
    xs = swap_along("gx", sent[:2])
    ys = swap_along("gy", sent[2 : 2 + n_y])
    corners = call(
        functools.partial(corner_kernel, n_y),
        "savv",
        (pos, stress_z, v0, rd),
        "v" * (2 * n_y),
        [arr(2, 8, nz)] * (2 * n_y),
        1024,
    )
    xy = [*xs, *ys, *swap_diagonal(corners)]
    moving = (
        pos,
        scaled,
        impact,
        both,
        velocity,
        contact,
        labels,
        *ys,
        stress_z,
        stress,
        ends,
    )
    hist_new, *moved, token = call(
        functools.partial(force_inner_kernel, n_y),
        "sssvvvv" + "v" * (3 + n_y) + "vv",
        (*moving, hist, hist_ends),
        "hvvv",
        [field, fields3, fields3, small],
        55 * size,
        [pltpu.SemaphoreType.DMA((3,))],
    )
    (joined,) = call(
        functools.partial(join_kernel, n_y),
        "svva" + "v" * len(xy),
        (pos, v0, rd, token, *xy),
        "v",
        [arr(nx + 6, ny + 8, 128)],
        4 * size,
    )
    z_got = swap(joined, "gz", z_pairs)
    *moved_ends, main_v, main_rd = call(
        functools.partial(rest_kernel, n_y),
        "sssvvvv" + "v" * (3 + n_y) + "vv" + "v" * len(xy),
        (*moving, v0, rd, *xy),
        "vvvv",
        [arr(3, 2, ny, nz)] * 2 + [arr(nx + 6, ny + 8, nz)] * 2,
        12 * size,
    )
    peers = lax.axis_size("gx") * lax.axis_size("gy") * lax.axis_size("gz")
    new_disp, new_vel, v1, v2, spread = call(
        krylov_kernel,
        "svvvvvvvv",
        (pos, main_v, main_rd, mom, z_got, *moved, *moved_ends),
        "hhvvv",
        [fields3, fields3, field, field, arr(peers, 1, 128)],
        60 * size,
        [
            pltpu.VMEM((nx + 6, ny + 8, 128), F32),
            pltpu.VMEM((nx + 6, ny + 8, 128), F32),
            pltpu.VMEM((nx + 4, ny + 8, nz + 128), F32),
            pltpu.VMEM((nx + 2, ny + 8, nz + 128), F32),
            pltpu.SemaphoreType.DMA((2, 5)),
        ],
    )
    mom = lax.all_to_all(spread, ("gx", "gy", "gz"), 0, 0, tiled=True)
    (damage_new,) = call(
        final_kernel,
        "vvvvv",
        (mom, v0, v1, v2, damage),
        "h",
        [field],
        8 * size,
        [pltpu.VMEM((nx, ny, nz), F32), pltpu.SemaphoreType.DMA((CHUNKS,))],
    )
    return new_disp, new_vel, hist_new, damage_new


def solution(mesh):
    placed = (
        P(None, ("case", "gx"), "gy", "gz"),
        P(None, ("case", "gx"), "gy", "gz"),
        P(("case", "gx"), "gy", "gz"),
        P(("case", "gx"), "gy", "gz"),
        P(("case", "gx"), "gy", "gz"),
        P(("case", "gx"), "gy", "gz"),
        P(("case", "gx"), "gy", "gz"),
        P(),
        P("case"),
    )
    return jax.shard_map(
        per_device,
        mesh=mesh,
        in_specs=placed,
        out_specs=(
            P(None, ("case", "gx"), "gy", "gz"),
            P(None, ("case", "gx"), "gy", "gz"),
            P(("case", "gx"), "gy", "gz"),
            P(("case", "gx"), "gy", "gz"),
        ),
        check_vma=False,
    )
```

```python
import functools
import jax
import jax.numpy as jnp
from jax import lax
from jax.experimental import pallas as pl
from jax.experimental.pallas import tpu as pltpu
from jax.sharding import PartitionSpec as P

TIME_STEP = 0.1
KAPPA_COEF = 0.5
NOTCH_LOAD = 20.0
STIFF_FLOOR = 0.001
ALPHA_LOW, ALPHA_HIGH = 0.5, 6.5
VMEM_BYTES = 28 * 1024 * 1024
CHUNKS = 4
STRESS_LANE = 32
F32 = jnp.float32


def iota2(shape, dim):
    return lax.broadcasted_iota(jnp.int32, shape, dim)


def low_high(odd, got):
    if len(got) == 2:
        return jnp.where(odd, got[0], got[1]), jnp.where(odd, got[1], got[0])
    return jnp.where(odd, got[0], 0.0), jnp.where(odd, 0.0, got[0])


def send(odd, refs, index, low, high):
    refs[0][index] = jnp.where(odd, low, high)
    if len(refs) == 2:
        refs[1][index] = jnp.where(odd, high, low)


def shift_y(plane, rows):
    lo, hi = rows
    tiles = [plane[start : start + 8] for start in range(0, plane.shape[0], 8)]
    at = iota2(tiles[0].shape, 0)
    ahead = [pltpu.roll(tile, 7, 0) for tile in tiles]
    behind = [pltpu.roll(tile, 1, 0) for tile in tiles]
    upper = [jnp.where(at == 7, b, a) for a, b in zip(ahead, [*ahead[1:], hi])]
    lower = [jnp.where(at == 0, b, a) for a, b in zip(behind, [lo, *behind[:-1]])]
    return jnp.concatenate(upper, axis=0), jnp.concatenate(lower, axis=0)


def shift_z(plane, column, first_z):
    tiles = [plane[:, start : start + 128] for start in range(0, plane.shape[1], 128)]
    at = iota2(tiles[0].shape, 1)
    wide = jnp.broadcast_to(column, tiles[0].shape)
    lo, hi = jnp.where(first_z, 0.0, wide), jnp.where(first_z, wide, 0.0)
    ahead = [pltpu.roll(tile, 127, 1) for tile in tiles]
    behind = [pltpu.roll(tile, 1, 1) for tile in tiles]
    upper = [jnp.where(at == 127, b, a) for a, b in zip(ahead, [*ahead[1:], hi])]
    lower = [jnp.where(at == 0, b, a) for a, b in zip(behind, [lo, *behind[:-1]])]
    return jnp.concatenate(upper, axis=1), jnp.concatenate(lower, axis=1)


def send_columns(ref, x, planes, gz, tile=None, first=0):
    depth = planes[0].shape[1]
    lanes = iota2((planes[0].shape[0], 128), 1)
    for field, plane in enumerate(planes):
        part = jnp.where(gz == 0, plane[:, depth - 128 :], plane[:, :128])
        part = pltpu.roll(part, first + field + 1 - gz, 1)
        tile = part if tile is None else jnp.where(lanes == first + field, part, tile)
    ref[x] = tile


def z_tile(v, rd, gz):
    depth = v.shape[1]
    keep = lax.shift_right_logical(iota2((v.shape[0], 128), 1), 6) == 1 - gz
    mine = jnp.where(gz == 0, v[:, depth - 128 :], v[:, :128])
    moved = jnp.where(gz == 0, rd[:, depth - 128 :], rd[:, :128])
    return jnp.where(keep, mine, pltpu.roll(moved, 64, 1))


def folded(values):
    total = None
    for start in range(0, values.shape[1], 128):
        part = values[:, start : start + 128]
        total = part if total is None else total + part
    out = None
    for start in range(0, values.shape[0], 8):
        part = total[start : start + 8]
        out = part if out is None else out + part
    return out


def by_label(labels, scalars):
    picked = scalars[0]
    for region in range(1, len(scalars)):
        picked = jnp.where(labels == region, scalars[region], picked)
    return picked


def unrolled(count, many, body, carry):
    def several(block, carry):
        for at in range(many):
            carry = body(block * many + at, carry)
        return carry

    if many == count:
        return several(0, carry)
    return lax.fori_loop(0, count // many, several, carry)


def pack_kernel(n_y, pos, disp, *refs):
    damage = disp.at[3]
    ys, zs = refs[:n_y], refs[n_y]
    odd_y, gz = pos[1] == 1, pos[2]

    def body(x, carry):
        planes = [disp[0, x], disp[1, x], disp[2, x], damage[x]]
        for field, plane in enumerate(planes):
            last = plane.shape[0] - 1
            spot = (field, pl.ds(x, 1), slice(None))
            send(odd_y, ys, spot, plane[0:1], plane[last : last + 1])
        send_columns(zs, x, planes, gz)
        return carry

    unrolled(damage.shape[0], damage.shape[0], body, 0)


def pack_x_kernel(pos, disp, after, *xs):
    damage = disp.at[3]
    odd_x, count = pos[0] == 1, damage.shape[0]
    for field, src in enumerate((disp.at[0], disp.at[1], disp.at[2], damage)):
        send(odd_x, xs, field, src[0], src[count - 1])


class Local:
    def __init__(self, pos, table, disp, damage, history, notch, labels, yg, zg):
        self.odd_x, self.odd_y, self.gz = pos[0] == 1, pos[1] == 1, pos[2]
        self.disp, self.damage, self.history = disp, damage, history
        self.notch, self.labels, self.yg, self.zg = notch, labels, yg, zg
        regions = range(table.shape[1])
        self.lames = [table[0, r] for r in regions]
        self.shears = [table[1, r] for r in regions]
        self.bases = [table[3, r] for r in regions]

    def plane(self, x, lower, upper, put):
        lab = self.labels[x]
        shear = by_label(lab, self.shears)
        dmg = self.damage[x]
        degrade = 4.0 * ((1.0 - dmg) * (1.0 - dmg) + STIFF_FLOOR)
        half = degrade * shear
        fields = [self.disp[c, x] for c in range(3)]

        def d(c, j):
            if j == 0:
                return upper(c) - lower(c)
            if j == 1:
                rows = low_high(self.odd_y, [y[c, pl.ds(x, 1), :] for y in self.yg])
                high, low = shift_y(fields[c], rows)
            else:
                column = self.zg[x][:, c : c + 1]
                high, low = shift_z(fields[c], column, self.gz == 0)
            return high - low

        squares = None
        for k, (i, j) in ((3, (0, 1)), (4, (0, 2)), (5, (1, 2))):
            e = d(i, j) + d(j, i)
            put(k, half * e)
            squares = e * e if squares is None else squares + e * e
        straight = [d(c, c) for c in range(3)]
        trace = straight[0] + straight[1] + straight[2]
        lame = by_label(lab, self.lames)
        level = (degrade * lame) * trace
        whole = half + half
        for k in range(3):
            put(k, level + whole * straight[k])
        twice = (
            straight[0] * straight[0] + straight[1] * straight[1] + straight[2] * straight[2]
        )
        squares = squares + (twice + twice)
        positive = jnp.maximum(trace, 0.0)
        energy = lame * positive * positive + shear * squares
        hist = jnp.maximum(
            jnp.maximum(self.history[x], energy), NOTCH_LOAD * self.notch[x].astype(F32)
        )
        diagonal = by_label(lab, self.bases) + 2.0 * hist
        rd = 1.0 / diagonal
        rows = low_high(self.odd_y, [y[3, pl.ds(x, 1), :] for y in self.yg])
        yu, yl = shift_y(dmg, rows)
        zu, zl = shift_z(dmg, self.zg[x][:, 3:4], self.gz == 0)
        near = ((upper(3) + lower(3)) + (yu + yl)) + (zu + zl)
        residual = 2.0 * hist - (diagonal * dmg - KAPPA_COEF * near)
        v = residual * rd
        return hist, rd, v, folded(residual * v)

    def send_y(self, ys, x, v, rd, stress):
        rows = v.shape[0]
        sources = [(v, depth) for depth in (1, 2, 3)] + [(rd, depth) for depth in (1, 2)]
        sources += [(stress[k], 1) for k in (3, 1, 5)]
        for slot, (plane, depth) in enumerate(sources):
            low, high = plane[depth - 1 : depth], plane[rows - depth : rows - depth + 1]
            send(self.odd_y, ys, (slot, pl.ds(x, 1), slice(None)), low, high)

    def send_z(self, zs, x, v, rd, stress):
        base = z_tile(v, rd, self.gz)
        planes = [stress[4], stress[5], stress[2]]
        send_columns(zs, x, planes, self.gz, base, STRESS_LANE)


def inner_steps(count):
    inner = count - 2
    many = max(m for m in range(1, 16) if inner % m == 0)
    return inner // many, many


def inner_kernel(n_y, pos, table, disp, history, notch, labels, *refs):
    damage = disp.at[3]
    local = Local(
        pos, table, disp, damage, history, notch, labels, refs[:n_y], refs[n_y]
    )
    hist, rd_out, v_out, stress_out, mom_out = refs[n_y + 1 : n_y + 6]
    ys, zs = refs[n_y + 6 : 2 * n_y + 6], refs[2 * n_y + 6]
    steps, many = inner_steps(damage.shape[0])

    def several(step, total):
        for at in range(many):
            x = 1 + step * many + at

            def lower(c):
                return damage[x - 1] if c == 3 else disp[c, x - 1]

            def upper(c):
                return damage[x + 1] if c == 3 else disp[c, x + 1]

            stress = {}

            def put(k, plane):
                stress[k] = stress_out[k, x] = plane

            hist_x, rd, v, part = local.plane(x, lower, upper, put)
            hist[x] = hist_x
            rd_out[x] = rd
            v_out[x] = v
            local.send_y(ys, x, v, rd, stress)
            local.send_z(zs, x, v, rd, stress)
            total = total + part
        return total

    mom_out[...] = unrolled(steps, 1, several, jnp.zeros((8, 128), F32))


def ends_kernel(n_y, pos, table, disp, history, notch, labels, *refs):
    damage = disp.at[3]
    local = Local(
        pos, table, disp, damage, history, notch, labels, refs[:n_y], refs[n_y]
    )
    refs = refs[n_y + 1 :]
    xg, (rd_in, v_in, mom), ys_in, zs_in = (
        refs[:2],
        refs[2:5],
        refs[5 : 5 + n_y],
        refs[5 + n_y],
    )
    refs = refs[6 + n_y :]
    hist, rd_out, v_out, stress_out, mom_out = refs[:5]
    xs, ys, zs = refs[5:7], refs[7 : 7 + n_y], refs[7 + n_y]
    odd_x, count = local.odd_x, damage.shape[0]
    total = mom[...]
    found = []
    for end, x in enumerate((0, count - 1)):

        def outside(c):
            first, second = xg[0][c], xg[1][c]
            if end == 0:
                return jnp.where(odd_x, first, second)
            return jnp.where(odd_x, second, first)

        def beside(c):
            at = 1 if end == 0 else count - 2
            return damage[at] if c == 3 else disp[c, at]

        sides = (outside, beside) if end == 0 else (beside, outside)
        stress = {}

        def put(k, plane):
            stress[k] = stress_out[k, end] = plane

        hist_x, rd, v, part = local.plane(x, *sides, put)
        hist[end] = hist_x
        rd_out[x] = rd
        v_out[x] = v
        total = total + part
        found.append((stress, rd, v))
    for mine, before in zip(ys, ys_in, strict=True):
        for slot in range(8):
            mine[slot] = before[slot]
    for x in range(1, count - 1):
        rd_out[x] = rd_in[x]
        v_out[x] = v_in[x]
        zs[x] = zs_in[x]
    for end, x in enumerate((0, count - 1)):
        stress, rd, v = found[end]
        local.send_y(ys, x, v, rd, stress)
        local.send_z(zs, x, v, rd, stress)
    for depth in (1, 2, 3):
        low, high = depth - 1, count - depth
        send(odd_x, xs, depth - 1, v_out[low], v_out[high])
        if depth <= 2:
            send(odd_x, xs, 2 + depth, rd_out[low], rd_out[high])
    for slot, k in ((5, 0), (6, 3), (7, 4)):
        send(odd_x, xs, slot, stress_out[k, 0], stress_out[k, 1])
    mom_out[...] = jnp.zeros((8, 128), F32)
    mom_out[0:1, :] = jnp.sum(total, axis=0, keepdims=True)


def corner_kernel(n_y, pos, after, v, rd, *ds):
    odd_x, odd_y = pos[0] == 1, pos[1] == 1
    count, rows = v.shape[0], v.shape[1]
    for depth in (1, 2):
        for slot, (src, deep) in enumerate(((v, 1), (v, 2), (v, 3), (rd, 1), (rd, 2))):
            near, far = pl.ds(deep - 1, 1), pl.ds(rows - deep, 1)
            planes = (depth - 1, count - depth)
            by_y = [(src[x, near, :], src[x, far, :]) for x in planes]
            for which in range(n_y):
                pair = (ds[which], ds[n_y + which])
                picked = [
                    jnp.where(odd_y, *(rows_of if which == 0 else rows_of[::-1]))
                    for rows_of in by_y
                ]
                send(odd_x, pair, (depth - 1, pl.ds(slot, 1), slice(None)), *picked)


class Enlarged:
    def __init__(self, n_y, pos, v, rd, refs):
        self.odd_x, self.odd_y = pos[0] == 1, pos[1] == 1
        self.v, self.rd, self.n_y = v, rd, n_y
        self.xg, self.yg, self.dg = refs[:2], refs[2 : 2 + n_y], refs[2 + n_y : 2 + 3 * n_y]

    def rows(self, found):
        nz = self.v.shape[2]
        at = iota2((8, nz), 0)

        def tile(first, depths):
            out = jnp.zeros((8, nz), F32)
            for depth in range(1, depths + 1):
                got = [found(w, first + depth - 1) for w in range(self.n_y)]
                if self.n_y == 1:
                    spot = jnp.where(self.odd_y, 8 - depth, depth - 1)
                    out = jnp.where(at == spot, got[0], out)
                else:
                    lo, hi = low_high(self.odd_y, got)
                    out = jnp.where(at == depth - 1, hi, out)
                    out = jnp.where(at == 8 - depth, lo, out)
            return out

        return tile(0, 3), tile(3, 2)

    def own(self, x):
        v_rows, rd_rows = self.rows(lambda w, slot: self.yg[w][slot, pl.ds(x, 1), :])
        return self.v[x], v_rows, self.rd[x], rd_rows

    def halo(self, is_low, depth):
        first, second = (0, 1) if is_low else (1, 0)

        def of(a, b):
            return jnp.where(self.odd_x, (a, b)[first], (a, b)[second])

        v = of(self.xg[0][depth - 1], self.xg[1][depth - 1])
        nothing = jnp.zeros((8, v.shape[1]), F32)
        if depth > 2:
            return v, nothing, jnp.zeros_like(v), nothing
        rd = of(self.xg[0][2 + depth], self.xg[1][2 + depth])

        def found(w, slot):
            spot = (depth - 1, pl.ds(slot, 1), slice(None))
            return of(self.dg[w][spot], self.dg[self.n_y + w][spot])

        v_rows, rd_rows = self.rows(found)
        return v, v_rows, rd, rd_rows

    def outer(self, count):
        for depth in (1, 2, 3):
            yield -depth, self.halo(True, depth)
            yield count - 1 + depth, self.halo(False, depth)


def outer_index(p, count):
    return -p - 1 if p < 0 else 3 + p - count


def join_kernel(n_y, pos, v, rd, token, *refs):
    big = Enlarged(n_y, pos, v, rd, refs[:-1])
    out, gz = refs[-1], pos[2]
    count, ny, _ = v.shape
    tall = ny // 8
    for p, (v_own, v_rows, rd_own, rd_rows) in big.outer(count):
        out[p + 3] = z_tile(v_rows, rd_rows, gz)
        start = count + 6 + tall * outer_index(p, count)
        out[start : start + tall] = z_tile(v_own, rd_own, gz).reshape(tall, 8, 128)

    def body(x, carry):
        _, v_rows, _, rd_rows = big.own(x)
        out[x + 3] = z_tile(v_rows, rd_rows, gz)
        return carry

    unrolled(count, count, body, 0)


def krylov_kernel(pos, main_v, main_rd, mom, z_own, z_got, *refs):
    moved, moved_ends, moved_hbm = refs[:2], refs[2:4], refs[4:6]
    v1_out, v2_out, spread, z_v, z_rd, big_v1, big_v2, sems = refs[6:]
    count, ny, nz = v1_out.shape
    inner = pl.ds(1, count - 2)
    copies = []
    for which, (src, ends, dst) in enumerate(zip(moved, moved_ends, moved_hbm)):
        for c in range(3):
            copies.append((src.at[c, inner], dst.at[c, inner], sems.at[which, c]))
        copies.append((ends.at[:, 0], dst.at[:, 0], sems.at[which, 3]))
        copies.append((ends.at[:, 1], dst.at[:, count - 1], sems.at[which, 4]))
    copies = [pltpu.make_async_copy(*copy) for copy in copies]
    for copy in copies:
        copy.start()

    tall = ny // 8

    def split(at, rows, tile):
        keep = lax.shift_right_logical(iota2(tile.shape, 1), 6) == pos[2]
        z_v[at, rows] = jnp.where(keep, tile, 0.0)
        z_rd[at, rows] = jnp.where(keep, pltpu.roll(tile, 64, 1), 0.0)

    for p in (-3, -2, -1, count, count + 1, count + 2):
        start = count + 6 + tall * outer_index(p, count)
        split(p + 3, slice(0, ny), z_got[start : start + tall].reshape(ny, 128))
        split(p + 3, slice(ny, ny + 8), z_got[p + 3])
    for x in range(count):
        split(x + 3, slice(0, ny), z_own[x])
        split(x + 3, slice(ny, ny + 8), z_got[x + 3])

    def v_at(at):
        return jnp.concatenate([main_v[at], z_v[at]], axis=1)

    def rd_at(at):
        return jnp.concatenate([main_rd[at], z_rd[at]], axis=1)

    def image_of(get, at):
        plane = get(at)
        rows, lanes = plane.shape
        near = (get(at - 1) + get(at + 1)) + (pltpu.roll(plane, 1, 0) + pltpu.roll(plane, rows - 1, 0))
        near = near + (pltpu.roll(plane, 1, 1) + pltpu.roll(plane, lanes - 1, 1))
        return plane, KAPPA_COEF * near

    def v1_at(at):
        return big_v1[at]

    def v2_at(at):
        return big_v2[at]

    def inside(values):
        return folded(values[0:ny, 0:nz])

    def first(x, totals):
        plane, image = image_of(v_at, x + 3)
        made = image * rd_at(x + 3)
        big_v1[x + 2] = made
        v1_out[x] = made[0:ny, 0:nz]
        return totals[0] + inside(plane * image), totals[1] + inside(made * image)

    def second(x, totals):
        plane, image = image_of(v1_at, x + 2)
        made = image * rd_at(x + 3)
        big_v2[x + 1] = made
        v2_out[x] = made[0:ny, 0:nz]
        return totals[0] + inside(plane * image), totals[1] + inside(made * image)

    def third(x, total):
        plane, image = image_of(v2_at, x + 1)
        return total + folded(plane[0:ny, 0:nz] * image[0:ny, 0:nz])

    zero = jnp.zeros((8, 128), F32)
    for p in (-2, -1, count, count + 1):
        big_v1[p + 2] = image_of(v_at, p + 3)[1] * rd_at(p + 3)
    k1, k2 = unrolled(count, count, first, (zero, zero))
    for p in (-1, count):
        big_v2[p + 1] = image_of(v1_at, p + 2)[1] * rd_at(p + 3)
    k3, k4 = unrolled(count, count, second, (zero, zero))
    k5 = unrolled(count, count, third, zero)
    rows = iota2((8, 128), 0)
    result = mom[...]
    for at, total in enumerate((k1, k2, k3, k4, k5)):
        result = jnp.where(rows == at + 1, jnp.sum(total, axis=0, keepdims=True), result)
    mine = rows == iota2((8, 128), 1)
    line = jnp.sum(
        jnp.where(mine, jnp.sum(result, axis=1, keepdims=True), 0.0), axis=0, keepdims=True
    )
    for peer in range(spread.shape[0]):
        spread[peer] = line
    for copy in copies:
        copy.wait()


PARTS = ((0, 3, 4), (3, 1, 5), (4, 5, 2))


class Force:
    def __init__(self, n_y, pos, table, impact, disp, vel, contact, labels, yg, zg):
        self.odd_x, self.odd_y, self.gz = pos[0] == 1, pos[1] == 1, pos[2]
        self.impact, self.disp, self.vel = impact, disp, vel
        self.contact, self.labels, self.yg, self.zg = contact, labels, yg, zg
        self.rates = [table[2, r] for r in range(table.shape[1])]

    def plane(self, x, lower, mine, upper, vel_out, disp_out, at):
        loaded = self.contact[x].astype(F32)
        rate = by_label(self.labels[x], self.rates)
        for c, (kx, ky, kz) in enumerate(PARTS):
            rows = low_high(self.odd_y, [y[5 + c, pl.ds(x, 1), :] for y in self.yg])
            lane = STRESS_LANE + c
            column = self.zg[x][:, lane : lane + 1]
            yu, yl = shift_y(mine(ky), rows)
            zu, zl = shift_z(mine(kz), column, self.gz == 0)
            force = 0.5 * (((upper(c, kx) - lower(c, kx)) + (yu - yl)) + (zu - zl))
            speed = self.vel[c, x] + rate * (force + loaded * self.impact[c])
            vel_out[c, at] = speed
            disp_out[c, at] = self.disp[c, x] + TIME_STEP * speed


def force_inner_kernel(n_y, pos, table, impact, disp, vel, contact, labels, *refs):
    yg, zg, stress, ends = refs[:n_y], refs[n_y], refs[n_y + 1], refs[n_y + 2]
    hist, hist_ends, hist_hbm, disp_out, vel_out, token, sems = refs[n_y + 3 :]
    token[...] = jnp.zeros((8, 128), F32)
    force = Force(n_y, pos, table, impact, disp, vel, contact, labels, yg, zg)
    count = contact.shape[0]
    steps, many = inner_steps(count)

    inside = pl.ds(1, count - 2)
    copies = [
        pltpu.make_async_copy(hist.at[inside], hist_hbm.at[inside], sems.at[0]),
        pltpu.make_async_copy(hist_ends.at[0], hist_hbm.at[0], sems.at[1]),
        pltpu.make_async_copy(hist_ends.at[1], hist_hbm.at[count - 1], sems.at[2]),
    ]
    for copy in copies:
        copy.start()

    def several(step, carry):
        for at in range(many):
            x = 1 + step * many + at

            def lower(c, k):
                if at == 0:
                    return jnp.where(step == 0, ends[k, 0], stress[k, x - 1])
                return stress[k, x - 1]

            def upper(c, k):
                if at == many - 1:
                    return jnp.where(step == steps - 1, ends[k, 1], stress[k, x + 1])
                return stress[k, x + 1]

            force.plane(x, lower, lambda k: stress[k, x], upper, vel_out, disp_out, x)
        return carry

    unrolled(steps, 1, several, 0)
    for copy in copies:
        copy.wait()


def rest_kernel(n_y, pos, table, impact, disp, vel, contact, labels, *refs):
    yg, zg, stress, ends = refs[:n_y], refs[n_y], refs[n_y + 1], refs[n_y + 2]
    refs = refs[n_y + 3 :]
    v, rd, xy = refs[0], refs[1], refs[2 : 4 + 3 * n_y]
    xg = xy[:2]
    disp_out, vel_out, big_v, big_rd = refs[4 + 3 * n_y :]
    force = Force(n_y, pos, table, impact, disp, vel, contact, labels, yg, zg)
    count, ny = contact.shape[0], contact.shape[1]
    for end, x in enumerate((0, count - 1)):

        def outside(c, k):
            first, second = xg[0][5 + c], xg[1][5 + c]
            if end == 0:
                return jnp.where(force.odd_x, first, second)
            return jnp.where(force.odd_x, second, first)

        def beside(c, k):
            return stress[k, 1 if end == 0 else count - 2]

        lower, upper = (outside, beside) if end == 0 else (beside, outside)
        force.plane(x, lower, lambda k: ends[k, end], upper, vel_out, disp_out, end)
    big = Enlarged(n_y, pos, v, rd, xy)

    def put(p, parts):
        v_own, v_rows, rd_own, rd_rows = parts
        big_v[p + 3, 0:ny] = v_own
        big_v[p + 3, ny : ny + 8] = v_rows
        big_rd[p + 3, 0:ny] = rd_own
        big_rd[p + 3, ny : ny + 8] = rd_rows

    for p, parts in big.outer(count):
        put(p, parts)

    def body(x, carry):
        put(x, big.own(x))
        return carry

    unrolled(count, 4, body, 0)


def cg_coefficients(k):
    zero, one = jnp.zeros_like(k[0]), jnp.ones_like(k[0])
    z, p, out = [one], [one], [zero, zero, zero]

    def form(a, b, moments):
        total = None
        for i, ai in enumerate(a):
            for j, bj in enumerate(b):
                term = ai * bj * moments[i + j]
                total = term if total is None else total + term
        return total

    energy = [k[j] - k[j + 1] for j in range(5)]
    rz = k[0]
    for step in range(3):
        alpha = jnp.clip(rz / form(p, p, energy), ALPHA_LOW, ALPHA_HIGH)
        out = [o + alpha * (p[i] if i < len(p) else zero) for i, o in enumerate(out)]
        if step == 2:
            break
        image = [(p[i] if i < len(p) else zero) - (p[i - 1] if i else zero) for i in range(len(p) + 1)]
        z = [(z[i] if i < len(z) else zero) - alpha * image[i] for i in range(len(image))]
        new = jnp.maximum(form(z, z, k), 0.0)
        beta = new / rz
        p = [z[i] + beta * (p[i] if i < len(p) else zero) for i in range(len(z))]
        rz = new
    return out


def final_kernel(mom, v0, v1, v2, damage, out_hbm, out, sems):
    count = v0.shape[0]
    block = count // CHUNKS
    sums = jnp.sum(mom[...], axis=0)
    c0, c1, c2 = cg_coefficients([sums[:, j : j + 1] for j in range(6)])
    copies = []
    for chunk in range(CHUNKS):
        for x in range(chunk * block, (chunk + 1) * block):
            dmg = damage[x]
            out[x] = jnp.maximum(dmg + (c0 * v0[x] + c1 * v1[x] + c2 * v2[x]), dmg)
        part = pl.ds(chunk * block, block)
        copies.append(pltpu.make_async_copy(out.at[part], out_hbm.at[part], sems.at[chunk]))
        copies[-1].start()
    for copy in copies:
        copy.wait()


def pairs_of(axis):
    count = lax.axis_size(axis)
    out = [[(i, i + 1) for i in range(start, count - 1, 2)] for start in (0, 1)]
    return [pairs for pairs in out if pairs]


def swap(array, axis, pairs):
    return lax.ppermute(array, axis, pairs + [(b, a) for a, b in pairs])


def swap_along(axis, arrays):
    return [swap(a, axis, pairs) for a, pairs in zip(arrays, pairs_of(axis), strict=True)]


def swap_diagonal(arrays):
    columns = lax.axis_size("gy")
    out = []
    both = [(xp, yp) for xp in pairs_of("gx") for yp in pairs_of("gy")]
    for array, (x_pairs, y_pairs) in zip(arrays, both, strict=True):
        joint = []
        for a, b in x_pairs:
            for c, d in y_pairs:
                joint.append((a * columns + c, b * columns + d))
                joint.append((a * columns + d, b * columns + c))
        out.append(swap(array, ("gx", "gy"), joint))
    return out


def spec_of(kind, a):
    if kind == "s":
        return pl.BlockSpec(memory_space=pltpu.SMEM)
    if kind == "v":
        return pl.BlockSpec(memory_space=pltpu.VMEM)
    if kind == "h":
        return pl.BlockSpec(memory_space=pltpu.HBM)
    if kind == "a":
        return pl.BlockSpec(memory_space=pl.ANY)
    raise ValueError(kind)


def call(kernel, kinds, ins, out_kinds, outs, flops, scratch=(), aliases=()):
    moved = sum(4 * a.size for a in (*ins, *outs))
    return pl.pallas_call(
        kernel,
        out_shape=outs,
        in_specs=[spec_of(k, a) for k, a in zip(kinds, ins, strict=True)],
        out_specs=[spec_of(k, a) for k, a in zip(out_kinds, outs, strict=True)],
        scratch_shapes=scratch,
        input_output_aliases=dict(aliases),
        compiler_params=pltpu.CompilerParams(vmem_limit_bytes=VMEM_BYTES),
        cost_estimate=pl.CostEstimate(flops=flops, bytes_accessed=moved, transcendentals=0),
    )(*ins)


def per_device(displacement, velocity, damage, history, contact, notch, labels, table, impact):
    nx, ny, nz = damage.shape
    size = damage.size
    n_y = len(pairs_of("gy"))
    pos = jnp.stack(
        [lax.axis_index("gx") % 2, lax.axis_index("gy") % 2, lax.axis_index("gz")]
    ).astype(jnp.int32)

    scaled = jnp.stack(
        [table[0] / 8.0, table[1] / 8.0, TIME_STEP / table[2], table[3] + 6.0 * KAPPA_COEF]
    )

    def arr(*shape):
        return jax.ShapeDtypeStruct(shape, F32)

    field, fields3, small = arr(nx, ny, nz), arr(3, nx, ny, nz), arr(8, 128)
    columns = arr(nx, ny, 128)
    z_pairs = [(0, 1)]

    both = jnp.concatenate([displacement, damage[None]])
    sent = call(
        functools.partial(pack_kernel, n_y),
        "sv",
        (pos, both),
        "v" * (1 + n_y),
        [*[arr(4, nx, nz)] * n_y, columns],
        size,
    )
    got_yz = [*swap_along("gy", sent[:n_y]), swap(sent[-1], "gz", z_pairs)]
    sent_x = call(
        pack_x_kernel,
        "sva",
        (pos, both, sent[-1]),
        "vv",
        [arr(4, ny, nz)] * 2,
        size,
    )
    got_x = swap_along("gx", sent_x)
    rows = [arr(8, nx, nz)] * n_y
    voxels = (pos, scaled, both, history, notch, labels, *got_yz)
    hist, rd, v0, stress, mom, *sent = call(
        functools.partial(inner_kernel, n_y),
        "ssvvvv" + "v" * (1 + n_y),
        voxels,
        "vvvvv" + "v" * (1 + n_y),
        [field, field, field, arr(6, nx, ny, nz), small, *rows, columns],
        140 * size,
    )
    more = (*got_x, rd, v0, mom, *sent)
    hist_ends, rd, v0, ends, mom, *sent = call(
        functools.partial(ends_kernel, n_y),
        "ssvvvv" + "v" * (1 + n_y) + "vvvvv" + "v" * (1 + n_y),
        (*voxels, *more),
        "vvvvv" + "v" * (3 + n_y),
        [
            arr(2, ny, nz),
            field,
            field,
            arr(6, 2, ny, nz),
            small,
            *[arr(8, ny, nz)] * 2,
            *rows,
            columns,
        ],
        20 * size,
    )
    stress_z = swap(sent[-1], "gz", z_pairs)
    xs = swap_along("gx", sent[:2])
    ys = swap_along("gy", sent[2 : 2 + n_y])
    corners = call(
        functools.partial(corner_kernel, n_y),
        "savv",
        (pos, stress_z, v0, rd),
        "v" * (2 * n_y),
        [arr(2, 8, nz)] * (2 * n_y),
        1024,
    )
    xy = [*xs, *ys, *swap_diagonal(corners)]
    moving = (
        pos,
        scaled,
        impact,
        both,
        velocity,
        contact,
        labels,
        *ys,
        stress_z,
        stress,
        ends,
    )
    hist_new, *moved, token = call(
        functools.partial(force_inner_kernel, n_y),
        "sssvvvv" + "v" * (3 + n_y) + "vv",
        (*moving, hist, hist_ends),
        "hvvv",
        [field, fields3, fields3, small],
        55 * size,
        [pltpu.SemaphoreType.DMA((3,))],
    )
    (joined,) = call(
        functools.partial(join_kernel, n_y),
        "svva" + "v" * len(xy),
        (pos, v0, rd, token, *xy),
        "v",
        [arr(nx + 6 + 6 * (ny // 8), 8, 128)],
        4 * size,
    )
    z_got = swap(joined, "gz", z_pairs)
    *moved_ends, main_v, main_rd = call(
        functools.partial(rest_kernel, n_y),
        "sssvvvv" + "v" * (3 + n_y) + "vv" + "v" * len(xy),
        (*moving, v0, rd, *xy),
        "vvvv",
        [arr(3, 2, ny, nz)] * 2 + [arr(nx + 6, ny + 8, nz)] * 2,
        12 * size,
    )
    peers = lax.axis_size("gx") * lax.axis_size("gy") * lax.axis_size("gz")
    new_disp, new_vel, v1, v2, spread = call(
        krylov_kernel,
        "svvvvvvvvv",
        (pos, main_v, main_rd, mom, stress_z, z_got, *moved, *moved_ends),
        "hhvvv",
        [fields3, fields3, field, field, arr(peers, 1, 128)],
        60 * size,
        [
            pltpu.VMEM((nx + 6, ny + 8, 128), F32),
            pltpu.VMEM((nx + 6, ny + 8, 128), F32),
            pltpu.VMEM((nx + 4, ny + 8, nz + 128), F32),
            pltpu.VMEM((nx + 2, ny + 8, nz + 128), F32),
            pltpu.SemaphoreType.DMA((2, 5)),
        ],
    )
    mom = lax.all_to_all(spread, ("gx", "gy", "gz"), 0, 0, tiled=True)
    (damage_new,) = call(
        final_kernel,
        "vvvvv",
        (mom, v0, v1, v2, damage),
        "h",
        [field],
        8 * size,
        [pltpu.VMEM((nx, ny, nz), F32), pltpu.SemaphoreType.DMA((CHUNKS,))],
    )
    return new_disp, new_vel, hist_new, damage_new


def solution(mesh):
    placed = (
        P(None, ("case", "gx"), "gy", "gz"),
        P(None, ("case", "gx"), "gy", "gz"),
        P(("case", "gx"), "gy", "gz"),
        P(("case", "gx"), "gy", "gz"),
        P(("case", "gx"), "gy", "gz"),
        P(("case", "gx"), "gy", "gz"),
        P(("case", "gx"), "gy", "gz"),
        P(),
        P("case"),
    )
    return jax.shard_map(
        per_device,
        mesh=mesh,
        in_specs=placed,
        out_specs=(
            P(None, ("case", "gx"), "gy", "gz"),
            P(None, ("case", "gx"), "gy", "gz"),
            P(("case", "gx"), "gy", "gz"),
            P(("case", "gx"), "gy", "gz"),
        ),
        check_vma=False,
    )
```

```python
import functools
import jax
import jax.numpy as jnp
from jax import lax
from jax.experimental import pallas as pl
from jax.experimental.pallas import tpu as pltpu
from jax.sharding import PartitionSpec as P

TIME_STEP = 0.1
KAPPA_COEF = 0.5
NOTCH_LOAD = 20.0
STIFF_FLOOR = 0.001
ALPHA_LOW, ALPHA_HIGH = 0.5, 6.5
VMEM_BYTES = 28 * 1024 * 1024
CHUNKS = 4
STRESS_LANE = 32
F32 = jnp.float32


def iota2(shape, dim):
    return lax.broadcasted_iota(jnp.int32, shape, dim)


def low_high(odd, got):
    if len(got) == 2:
        return jnp.where(odd, got[0], got[1]), jnp.where(odd, got[1], got[0])
    return jnp.where(odd, got[0], 0.0), jnp.where(odd, 0.0, got[0])


def send(odd, refs, index, low, high):
    refs[0][index] = jnp.where(odd, low, high)
    if len(refs) == 2:
        refs[1][index] = jnp.where(odd, high, low)


def shift_y(plane, rows):
    lo, hi = rows
    tiles = [plane[start : start + 8] for start in range(0, plane.shape[0], 8)]
    at = iota2(tiles[0].shape, 0)
    ahead = [pltpu.roll(tile, 7, 0) for tile in tiles]
    behind = [pltpu.roll(tile, 1, 0) for tile in tiles]
    upper = [jnp.where(at == 7, b, a) for a, b in zip(ahead, [*ahead[1:], hi])]
    lower = [jnp.where(at == 0, b, a) for a, b in zip(behind, [lo, *behind[:-1]])]
    return jnp.concatenate(upper, axis=0), jnp.concatenate(lower, axis=0)


def shift_z(plane, column, first_z):
    tiles = [plane[:, start : start + 128] for start in range(0, plane.shape[1], 128)]
    at = iota2(tiles[0].shape, 1)
    wide = jnp.broadcast_to(column, tiles[0].shape)
    lo, hi = jnp.where(first_z, 0.0, wide), jnp.where(first_z, wide, 0.0)
    ahead = [pltpu.roll(tile, 127, 1) for tile in tiles]
    behind = [pltpu.roll(tile, 1, 1) for tile in tiles]
    upper = [jnp.where(at == 127, b, a) for a, b in zip(ahead, [*ahead[1:], hi])]
    lower = [jnp.where(at == 0, b, a) for a, b in zip(behind, [lo, *behind[:-1]])]
    return jnp.concatenate(upper, axis=1), jnp.concatenate(lower, axis=1)


def send_columns(ref, x, planes, gz, tile=None, first=0):
    depth = planes[0].shape[1]
    lanes = iota2((planes[0].shape[0], 128), 1)
    for field, plane in enumerate(planes):
        part = jnp.where(gz == 0, plane[:, depth - 128 :], plane[:, :128])
        part = pltpu.roll(part, first + field + 1 - gz, 1)
        tile = part if tile is None else jnp.where(lanes == first + field, part, tile)
    ref[x] = tile


def z_tile(v, rd, gz):
    depth = v.shape[1]
    keep = lax.shift_right_logical(iota2((v.shape[0], 128), 1), 6) == 1 - gz
    mine = jnp.where(gz == 0, v[:, depth - 128 :], v[:, :128])
    moved = jnp.where(gz == 0, rd[:, depth - 128 :], rd[:, :128])
    return jnp.where(keep, mine, pltpu.roll(moved, 64, 1))


def folded(values):
    total = None
    for start in range(0, values.shape[1], 128):
        part = values[:, start : start + 128]
        total = part if total is None else total + part
    out = None
    for start in range(0, values.shape[0], 8):
        part = total[start : start + 8]
        out = part if out is None else out + part
    return out


def by_label(labels, scalars):
    picked = scalars[0]
    for region in range(1, len(scalars)):
        picked = jnp.where(labels == region, scalars[region], picked)
    return picked


def unrolled(count, many, body, carry):
    def several(block, carry):
        for at in range(many):
            carry = body(block * many + at, carry)
        return carry

    if many == count:
        return several(0, carry)
    return lax.fori_loop(0, count // many, several, carry)


def pack_kernel(n_y, pos, disp, *refs):
    damage = disp.at[3]
    ys, zs = refs[:n_y], refs[n_y]
    odd_y, gz = pos[1] == 1, pos[2]

    def body(x, carry):
        planes = [disp[0, x], disp[1, x], disp[2, x], damage[x]]
        for field, plane in enumerate(planes):
            last = plane.shape[0] - 1
            spot = (field, pl.ds(x, 1), slice(None))
            send(odd_y, ys, spot, plane[0:1], plane[last : last + 1])
        send_columns(zs, x, planes, gz)
        return carry

    unrolled(damage.shape[0], damage.shape[0], body, 0)


def pack_x_kernel(pos, disp, after, *xs):
    damage = disp.at[3]
    odd_x, count = pos[0] == 1, damage.shape[0]
    for field, src in enumerate((disp.at[0], disp.at[1], disp.at[2], damage)):
        send(odd_x, xs, field, src[0], src[count - 1])


class Local:
    def __init__(self, pos, table, disp, damage, history, notch, labels, yg, zg):
        self.odd_x, self.odd_y, self.gz = pos[0] == 1, pos[1] == 1, pos[2]
        self.disp, self.damage, self.history = disp, damage, history
        self.notch, self.labels, self.yg, self.zg = notch, labels, yg, zg
        regions = range(table.shape[1])
        self.lames = [table[0, r] for r in regions]
        self.shears = [table[1, r] for r in regions]
        self.bases = [table[3, r] for r in regions]

    def plane(self, x, lower, upper, put):
        lab = self.labels[x]
        shear = by_label(lab, self.shears)
        dmg = self.damage[x]
        degrade = 4.0 * ((1.0 - dmg) * (1.0 - dmg) + STIFF_FLOOR)
        half = degrade * shear
        fields = [self.disp[c, x] for c in range(3)]

        def d(c, j):
            if j == 0:
                return upper(c) - lower(c)
            if j == 1:
                rows = low_high(self.odd_y, [y[c, pl.ds(x, 1), :] for y in self.yg])
                high, low = shift_y(fields[c], rows)
            else:
                column = self.zg[x][:, c : c + 1]
                high, low = shift_z(fields[c], column, self.gz == 0)
            return high - low

        squares = None
        for k, (i, j) in ((3, (0, 1)), (4, (0, 2)), (5, (1, 2))):
            e = d(i, j) + d(j, i)
            put(k, half * e)
            squares = e * e if squares is None else squares + e * e
        straight = [d(c, c) for c in range(3)]
        trace = straight[0] + straight[1] + straight[2]
        lame = by_label(lab, self.lames)
        level = (degrade * lame) * trace
        whole = half + half
        for k in range(3):
            put(k, level + whole * straight[k])
        twice = (
            straight[0] * straight[0] + straight[1] * straight[1] + straight[2] * straight[2]
        )
        squares = squares + (twice + twice)
        positive = jnp.maximum(trace, 0.0)
        energy = lame * positive * positive + shear * squares
        hist = jnp.maximum(
            jnp.maximum(self.history[x], energy), NOTCH_LOAD * self.notch[x].astype(F32)
        )
        diagonal = by_label(lab, self.bases) + 2.0 * hist
        rd = 1.0 / diagonal
        rows = low_high(self.odd_y, [y[3, pl.ds(x, 1), :] for y in self.yg])
        yu, yl = shift_y(dmg, rows)
        zu, zl = shift_z(dmg, self.zg[x][:, 3:4], self.gz == 0)
        near = ((upper(3) + lower(3)) + (yu + yl)) + (zu + zl)
        residual = 2.0 * hist - (diagonal * dmg - KAPPA_COEF * near)
        v = residual * rd
        return hist, rd, v, folded(residual * v)

    def send_y(self, ys, x, v, rd, stress):
        rows = v.shape[0]
        sources = [(v, depth) for depth in (1, 2, 3)] + [(rd, depth) for depth in (1, 2)]
        sources += [(stress[k], 1) for k in (3, 1, 5)]
        for slot, (plane, depth) in enumerate(sources):
            low, high = plane[depth - 1 : depth], plane[rows - depth : rows - depth + 1]
            send(self.odd_y, ys, (slot, pl.ds(x, 1), slice(None)), low, high)

    def send_z(self, zs, x, v, rd, stress):
        base = z_tile(v, rd, self.gz)
        planes = [stress[4], stress[5], stress[2]]
        send_columns(zs, x, planes, self.gz, base, STRESS_LANE)


def inner_steps(count, most):
    inner = count - 2
    many = max(m for m in range(1, most + 1) if inner % m == 0)
    return inner // many, many


def inner_kernel(n_y, pos, table, disp, history, notch, labels, *refs):
    damage = disp.at[3]
    local = Local(
        pos, table, disp, damage, history, notch, labels, refs[:n_y], refs[n_y]
    )
    hist, rd_out, v_out, stress_out, mom_out = refs[n_y + 1 : n_y + 6]
    ys, zs = refs[n_y + 6 : 2 * n_y + 6], refs[2 * n_y + 6]
    steps, many = inner_steps(damage.shape[0], 2)

    def several(step, total):
        for at in range(many):
            x = 1 + step * many + at

            def lower(c):
                return damage[x - 1] if c == 3 else disp[c, x - 1]

            def upper(c):
                return damage[x + 1] if c == 3 else disp[c, x + 1]

            stress = {}

            def put(k, plane):
                stress[k] = stress_out[k, x] = plane

            hist_x, rd, v, part = local.plane(x, lower, upper, put)
            hist[x] = hist_x
            rd_out[x] = rd
            v_out[x] = v
            local.send_y(ys, x, v, rd, stress)
            local.send_z(zs, x, v, rd, stress)
            total = total + part
        return total

    mom_out[...] = unrolled(steps, 1, several, jnp.zeros((8, 128), F32))


def ends_kernel(n_y, pos, table, disp, history, notch, labels, *refs):
    damage = disp.at[3]
    local = Local(
        pos, table, disp, damage, history, notch, labels, refs[:n_y], refs[n_y]
    )
    refs = refs[n_y + 1 :]
    xg, (rd_in, v_in, mom), ys_in, zs_in = (
        refs[:2],
        refs[2:5],
        refs[5 : 5 + n_y],
        refs[5 + n_y],
    )
    refs = refs[6 + n_y :]
    hist, rd_out, v_out, stress_out, mom_out = refs[:5]
    xs, ys, zs = refs[5:7], refs[7 : 7 + n_y], refs[7 + n_y]
    odd_x, count = local.odd_x, damage.shape[0]
    total = mom[...]
    found = []
    for end, x in enumerate((0, count - 1)):

        def outside(c):
            first, second = xg[0][c], xg[1][c]
            if end == 0:
                return jnp.where(odd_x, first, second)
            return jnp.where(odd_x, second, first)

        def beside(c):
            at = 1 if end == 0 else count - 2
            return damage[at] if c == 3 else disp[c, at]

        sides = (outside, beside) if end == 0 else (beside, outside)
        stress = {}

        def put(k, plane):
            stress[k] = stress_out[k, end] = plane

        hist_x, rd, v, part = local.plane(x, *sides, put)
        hist[end] = hist_x
        rd_out[x] = rd
        v_out[x] = v
        total = total + part
        found.append((stress, rd, v))
    for mine, before in zip(ys, ys_in, strict=True):
        for slot in range(8):
            mine[slot] = before[slot]
    for x in range(1, count - 1):
        rd_out[x] = rd_in[x]
        v_out[x] = v_in[x]
        zs[x] = zs_in[x]
    for end, x in enumerate((0, count - 1)):
        stress, rd, v = found[end]
        local.send_y(ys, x, v, rd, stress)
        local.send_z(zs, x, v, rd, stress)
    for depth in (1, 2, 3):
        low, high = depth - 1, count - depth
        send(odd_x, xs, depth - 1, v_out[low], v_out[high])
        if depth <= 2:
            send(odd_x, xs, 2 + depth, rd_out[low], rd_out[high])
    for slot, k in ((5, 0), (6, 3), (7, 4)):
        send(odd_x, xs, slot, stress_out[k, 0], stress_out[k, 1])
    mom_out[...] = jnp.zeros((8, 128), F32)
    mom_out[0:1, :] = jnp.sum(total, axis=0, keepdims=True)


def corner_kernel(n_y, pos, after, v, rd, *ds):
    odd_x, odd_y = pos[0] == 1, pos[1] == 1
    count, rows = v.shape[0], v.shape[1]
    for depth in (1, 2):
        for slot, (src, deep) in enumerate(((v, 1), (v, 2), (v, 3), (rd, 1), (rd, 2))):
            near, far = pl.ds(deep - 1, 1), pl.ds(rows - deep, 1)
            planes = (depth - 1, count - depth)
            by_y = [(src[x, near, :], src[x, far, :]) for x in planes]
            for which in range(n_y):
                pair = (ds[which], ds[n_y + which])
                picked = [
                    jnp.where(odd_y, *(rows_of if which == 0 else rows_of[::-1]))
                    for rows_of in by_y
                ]
                send(odd_x, pair, (depth - 1, pl.ds(slot, 1), slice(None)), *picked)


class Enlarged:
    def __init__(self, n_y, pos, v, rd, refs):
        self.odd_x, self.odd_y = pos[0] == 1, pos[1] == 1
        self.v, self.rd, self.n_y = v, rd, n_y
        self.xg, self.yg, self.dg = refs[:2], refs[2 : 2 + n_y], refs[2 + n_y : 2 + 3 * n_y]

    def rows(self, found):
        nz = self.v.shape[2]
        at = iota2((8, nz), 0)

        def tile(first, depths):
            out = jnp.zeros((8, nz), F32)
            for depth in range(1, depths + 1):
                got = [found(w, first + depth - 1) for w in range(self.n_y)]
                if self.n_y == 1:
                    spot = jnp.where(self.odd_y, 8 - depth, depth - 1)
                    out = jnp.where(at == spot, got[0], out)
                else:
                    lo, hi = low_high(self.odd_y, got)
                    out = jnp.where(at == depth - 1, hi, out)
                    out = jnp.where(at == 8 - depth, lo, out)
            return out

        return tile(0, 3), tile(3, 2)

    def own(self, x):
        v_rows, rd_rows = self.rows(lambda w, slot: self.yg[w][slot, pl.ds(x, 1), :])
        return self.v[x], v_rows, self.rd[x], rd_rows

    def halo(self, is_low, depth):
        first, second = (0, 1) if is_low else (1, 0)

        def of(a, b):
            return jnp.where(self.odd_x, (a, b)[first], (a, b)[second])

        v = of(self.xg[0][depth - 1], self.xg[1][depth - 1])
        nothing = jnp.zeros((8, v.shape[1]), F32)
        if depth > 2:
            return v, nothing, jnp.zeros_like(v), nothing
        rd = of(self.xg[0][2 + depth], self.xg[1][2 + depth])

        def found(w, slot):
            spot = (depth - 1, pl.ds(slot, 1), slice(None))
            return of(self.dg[w][spot], self.dg[self.n_y + w][spot])

        v_rows, rd_rows = self.rows(found)
        return v, v_rows, rd, rd_rows

    def outer(self, count):
        for depth in (1, 2, 3):
            yield -depth, self.halo(True, depth)
            yield count - 1 + depth, self.halo(False, depth)


def outer_index(p, count):
    return -p - 1 if p < 0 else 3 + p - count


def join_kernel(n_y, pos, v, rd, token, *refs):
    big = Enlarged(n_y, pos, v, rd, refs[:-1])
    out, gz = refs[-1], pos[2]
    count, ny, _ = v.shape
    tall = ny // 8
    for p, (v_own, v_rows, rd_own, rd_rows) in big.outer(count):
        out[p + 3] = z_tile(v_rows, rd_rows, gz)
        start = count + 6 + tall * outer_index(p, count)
        out[start : start + tall] = z_tile(v_own, rd_own, gz).reshape(tall, 8, 128)

    def body(x, carry):
        _, v_rows, _, rd_rows = big.own(x)
        out[x + 3] = z_tile(v_rows, rd_rows, gz)
        return carry

    unrolled(count, count, body, 0)


def krylov_kernel(pos, main_v, main_rd, mom, z_own, z_got, *refs):
    moved, moved_ends, moved_hbm = refs[:2], refs[2:4], refs[4:6]
    v1_out, v2_out, spread, z_v, z_rd, big_v1, big_v2, sems = refs[6:]
    count, ny, nz = v1_out.shape
    inner = pl.ds(1, count - 2)
    copies = []
    for which, (src, ends, dst) in enumerate(zip(moved, moved_ends, moved_hbm)):
        for c in range(3):
            copies.append((src.at[c, inner], dst.at[c, inner], sems.at[which, c]))
        copies.append((ends.at[:, 0], dst.at[:, 0], sems.at[which, 3]))
        copies.append((ends.at[:, 1], dst.at[:, count - 1], sems.at[which, 4]))
    copies = [pltpu.make_async_copy(*copy) for copy in copies]
    for copy in copies:
        copy.start()

    tall = ny // 8

    def split(at, rows, tile):
        keep = lax.shift_right_logical(iota2(tile.shape, 1), 6) == pos[2]
        z_v[at, rows] = jnp.where(keep, tile, 0.0)
        z_rd[at, rows] = jnp.where(keep, pltpu.roll(tile, 64, 1), 0.0)

    for p in (-3, -2, -1, count, count + 1, count + 2):
        start = count + 6 + tall * outer_index(p, count)
        split(p + 3, slice(0, ny), z_got[start : start + tall].reshape(ny, 128))
        split(p + 3, slice(ny, ny + 8), z_got[p + 3])

    def split_own(x, carry):
        split(x + 3, slice(0, ny), z_own[x])
        split(x + 3, slice(ny, ny + 8), z_got[x + 3])
        return carry

    unrolled(count, 8, split_own, 0)

    def v_at(at):
        return jnp.concatenate([main_v[at], z_v[at]], axis=1)

    def rd_at(at):
        return jnp.concatenate([main_rd[at], z_rd[at]], axis=1)

    def image_of(get, at):
        plane = get(at)
        rows, lanes = plane.shape
        near = (get(at - 1) + get(at + 1)) + (pltpu.roll(plane, 1, 0) + pltpu.roll(plane, rows - 1, 0))
        near = near + (pltpu.roll(plane, 1, 1) + pltpu.roll(plane, lanes - 1, 1))
        return plane, KAPPA_COEF * near

    def v1_at(at):
        return big_v1[at]

    def v2_at(at):
        return big_v2[at]

    def inside(values):
        return folded(values[0:ny, 0:nz])

    def first(x, totals):
        plane, image = image_of(v_at, x + 3)
        made = image * rd_at(x + 3)
        big_v1[x + 2] = made
        v1_out[x] = made[0:ny, 0:nz]
        return totals[0] + inside(plane * image), totals[1] + inside(made * image)

    def second(x, totals):
        plane, image = image_of(v1_at, x + 2)
        made = image * rd_at(x + 3)
        big_v2[x + 1] = made
        v2_out[x] = made[0:ny, 0:nz]
        return totals[0] + inside(plane * image), totals[1] + inside(made * image)

    def third(x, total):
        plane, image = image_of(v2_at, x + 1)
        return total + folded(plane[0:ny, 0:nz] * image[0:ny, 0:nz])

    zero = jnp.zeros((8, 128), F32)
    for p in (-2, -1, count, count + 1):
        big_v1[p + 2] = image_of(v_at, p + 3)[1] * rd_at(p + 3)
    k1, k2 = unrolled(count, 8, first, (zero, zero))
    for p in (-1, count):
        big_v2[p + 1] = image_of(v1_at, p + 2)[1] * rd_at(p + 3)
    k3, k4 = unrolled(count, 8, second, (zero, zero))
    k5 = unrolled(count, 8, third, zero)
    rows = iota2((8, 128), 0)
    result = mom[...]
    for at, total in enumerate((k1, k2, k3, k4, k5)):
        result = jnp.where(rows == at + 1, jnp.sum(total, axis=0, keepdims=True), result)
    mine = rows == iota2((8, 128), 1)
    line = jnp.sum(
        jnp.where(mine, jnp.sum(result, axis=1, keepdims=True), 0.0), axis=0, keepdims=True
    )
    for peer in range(spread.shape[0]):
        spread[peer] = line
    for copy in copies:
        copy.wait()


PARTS = ((0, 3, 4), (3, 1, 5), (4, 5, 2))


class Force:
    def __init__(self, n_y, pos, table, impact, disp, vel, contact, labels, yg, zg):
        self.odd_x, self.odd_y, self.gz = pos[0] == 1, pos[1] == 1, pos[2]
        self.impact, self.disp, self.vel = impact, disp, vel
        self.contact, self.labels, self.yg, self.zg = contact, labels, yg, zg
        self.rates = [table[2, r] for r in range(table.shape[1])]

    def plane(self, x, lower, mine, upper, vel_out, disp_out, at):
        loaded = self.contact[x].astype(F32)
        rate = by_label(self.labels[x], self.rates)
        for c, (kx, ky, kz) in enumerate(PARTS):
            rows = low_high(self.odd_y, [y[5 + c, pl.ds(x, 1), :] for y in self.yg])
            lane = STRESS_LANE + c
            column = self.zg[x][:, lane : lane + 1]
            yu, yl = shift_y(mine(ky), rows)
            zu, zl = shift_z(mine(kz), column, self.gz == 0)
            force = 0.5 * (((upper(c, kx) - lower(c, kx)) + (yu - yl)) + (zu - zl))
            speed = self.vel[c, x] + rate * (force + loaded * self.impact[c])
            vel_out[c, at] = speed
            disp_out[c, at] = self.disp[c, x] + TIME_STEP * speed


def force_inner_kernel(n_y, pos, table, impact, disp, vel, contact, labels, *refs):
    yg, zg, stress, ends = refs[:n_y], refs[n_y], refs[n_y + 1], refs[n_y + 2]
    hist, hist_ends, hist_hbm, disp_out, vel_out, token, sems = refs[n_y + 3 :]
    token[...] = jnp.zeros((8, 128), F32)
    force = Force(n_y, pos, table, impact, disp, vel, contact, labels, yg, zg)
    count = contact.shape[0]
    steps, many = inner_steps(count, 7)

    inside = pl.ds(1, count - 2)
    copies = [
        pltpu.make_async_copy(hist.at[inside], hist_hbm.at[inside], sems.at[0]),
        pltpu.make_async_copy(hist_ends.at[0], hist_hbm.at[0], sems.at[1]),
        pltpu.make_async_copy(hist_ends.at[1], hist_hbm.at[count - 1], sems.at[2]),
    ]
    for copy in copies:
        copy.start()

    def several(step, carry):
        for at in range(many):
            x = 1 + step * many + at

            def lower(c, k):
                if at == 0:
                    return jnp.where(step == 0, ends[k, 0], stress[k, x - 1])
                return stress[k, x - 1]

            def upper(c, k):
                if at == many - 1:
                    return jnp.where(step == steps - 1, ends[k, 1], stress[k, x + 1])
                return stress[k, x + 1]

            force.plane(x, lower, lambda k: stress[k, x], upper, vel_out, disp_out, x)
        return carry

    unrolled(steps, 1, several, 0)
    for copy in copies:
        copy.wait()


def rest_kernel(n_y, pos, table, impact, disp, vel, contact, labels, *refs):
    yg, zg, stress, ends = refs[:n_y], refs[n_y], refs[n_y + 1], refs[n_y + 2]
    refs = refs[n_y + 3 :]
    v, rd, xy = refs[0], refs[1], refs[2 : 4 + 3 * n_y]
    xg = xy[:2]
    disp_out, vel_out, big_v, big_rd = refs[4 + 3 * n_y :]
    force = Force(n_y, pos, table, impact, disp, vel, contact, labels, yg, zg)
    count, ny = contact.shape[0], contact.shape[1]
    for end, x in enumerate((0, count - 1)):

        def outside(c, k):
            first, second = xg[0][5 + c], xg[1][5 + c]
            if end == 0:
                return jnp.where(force.odd_x, first, second)
            return jnp.where(force.odd_x, second, first)

        def beside(c, k):
            return stress[k, 1 if end == 0 else count - 2]

        lower, upper = (outside, beside) if end == 0 else (beside, outside)
        force.plane(x, lower, lambda k: ends[k, end], upper, vel_out, disp_out, end)
    big = Enlarged(n_y, pos, v, rd, xy)

    def put(p, parts):
        v_own, v_rows, rd_own, rd_rows = parts
        big_v[p + 3, 0:ny] = v_own
        big_v[p + 3, ny : ny + 8] = v_rows
        big_rd[p + 3, 0:ny] = rd_own
        big_rd[p + 3, ny : ny + 8] = rd_rows

    for p, parts in big.outer(count):
        put(p, parts)

    def body(x, carry):
        put(x, big.own(x))
        return carry

    unrolled(count, 4, body, 0)


def cg_coefficients(k):
    zero, one = jnp.zeros_like(k[0]), jnp.ones_like(k[0])
    z, p, out = [one], [one], [zero, zero, zero]

    def form(a, b, moments):
        total = None
        for i, ai in enumerate(a):
            for j, bj in enumerate(b):
                term = ai * bj * moments[i + j]
                total = term if total is None else total + term
        return total

    energy = [k[j] - k[j + 1] for j in range(5)]
    rz = k[0]
    for step in range(3):
        alpha = jnp.clip(rz / form(p, p, energy), ALPHA_LOW, ALPHA_HIGH)
        out = [o + alpha * (p[i] if i < len(p) else zero) for i, o in enumerate(out)]
        if step == 2:
            break
        image = [(p[i] if i < len(p) else zero) - (p[i - 1] if i else zero) for i in range(len(p) + 1)]
        z = [(z[i] if i < len(z) else zero) - alpha * image[i] for i in range(len(image))]
        new = jnp.maximum(form(z, z, k), 0.0)
        beta = new / rz
        p = [z[i] + beta * (p[i] if i < len(p) else zero) for i in range(len(z))]
        rz = new
    return out


def final_kernel(mom, v0, v1, v2, damage, out_hbm, out, sems):
    count = v0.shape[0]
    block = count // CHUNKS
    sums = jnp.sum(mom[...], axis=0)
    c0, c1, c2 = cg_coefficients([sums[:, j : j + 1] for j in range(6)])
    copies = []
    for chunk in range(CHUNKS):
        for x in range(chunk * block, (chunk + 1) * block):
            dmg = damage[x]
            out[x] = jnp.maximum(dmg + (c0 * v0[x] + c1 * v1[x] + c2 * v2[x]), dmg)
        part = pl.ds(chunk * block, block)
        copies.append(pltpu.make_async_copy(out.at[part], out_hbm.at[part], sems.at[chunk]))
        copies[-1].start()
    for copy in copies:
        copy.wait()


def pairs_of(axis):
    count = lax.axis_size(axis)
    out = [[(i, i + 1) for i in range(start, count - 1, 2)] for start in (0, 1)]
    return [pairs for pairs in out if pairs]


def swap(array, axis, pairs):
    return lax.ppermute(array, axis, pairs + [(b, a) for a, b in pairs])


def swap_along(axis, arrays):
    return [swap(a, axis, pairs) for a, pairs in zip(arrays, pairs_of(axis), strict=True)]


def swap_diagonal(arrays):
    columns = lax.axis_size("gy")
    out = []
    both = [(xp, yp) for xp in pairs_of("gx") for yp in pairs_of("gy")]
    for array, (x_pairs, y_pairs) in zip(arrays, both, strict=True):
        joint = []
        for a, b in x_pairs:
            for c, d in y_pairs:
                joint.append((a * columns + c, b * columns + d))
                joint.append((a * columns + d, b * columns + c))
        out.append(swap(array, ("gx", "gy"), joint))
    return out


def spec_of(kind, a):
    if kind == "s":
        return pl.BlockSpec(memory_space=pltpu.SMEM)
    if kind == "v":
        return pl.BlockSpec(memory_space=pltpu.VMEM)
    if kind == "h":
        return pl.BlockSpec(memory_space=pltpu.HBM)
    if kind == "a":
        return pl.BlockSpec(memory_space=pl.ANY)
    raise ValueError(kind)


def call(kernel, kinds, ins, out_kinds, outs, flops, scratch=(), aliases=()):
    moved = sum(4 * a.size for a in (*ins, *outs))
    return pl.pallas_call(
        kernel,
        out_shape=outs,
        in_specs=[spec_of(k, a) for k, a in zip(kinds, ins, strict=True)],
        out_specs=[spec_of(k, a) for k, a in zip(out_kinds, outs, strict=True)],
        scratch_shapes=scratch,
        input_output_aliases=dict(aliases),
        compiler_params=pltpu.CompilerParams(vmem_limit_bytes=VMEM_BYTES),
        cost_estimate=pl.CostEstimate(flops=flops, bytes_accessed=moved, transcendentals=0),
    )(*ins)


def per_device(displacement, velocity, damage, history, contact, notch, labels, table, impact):
    nx, ny, nz = damage.shape
    size = damage.size
    n_y = len(pairs_of("gy"))
    pos = jnp.stack(
        [lax.axis_index("gx") % 2, lax.axis_index("gy") % 2, lax.axis_index("gz")]
    ).astype(jnp.int32)

    scaled = jnp.stack(
        [table[0] / 8.0, table[1] / 8.0, TIME_STEP / table[2], table[3] + 6.0 * KAPPA_COEF]
    )

    def arr(*shape):
        return jax.ShapeDtypeStruct(shape, F32)

    field, fields3, small = arr(nx, ny, nz), arr(3, nx, ny, nz), arr(8, 128)
    columns = arr(nx, ny, 128)
    z_pairs = [(0, 1)]

    both = jnp.concatenate([displacement, damage[None]])
    sent = call(
        functools.partial(pack_kernel, n_y),
        "sv",
        (pos, both),
        "v" * (1 + n_y),
        [*[arr(4, nx, nz)] * n_y, columns],
        size,
    )
    got_yz = [*swap_along("gy", sent[:n_y]), swap(sent[-1], "gz", z_pairs)]
    sent_x = call(
        pack_x_kernel,
        "sva",
        (pos, both, sent[-1]),
        "vv",
        [arr(4, ny, nz)] * 2,
        size,
    )
    got_x = swap_along("gx", sent_x)
    rows = [arr(8, nx, nz)] * n_y
    voxels = (pos, scaled, both, history, notch, labels, *got_yz)
    hist, rd, v0, stress, mom, *sent = call(
        functools.partial(inner_kernel, n_y),
        "ssvvvv" + "v" * (1 + n_y),
        voxels,
        "vvvvv" + "v" * (1 + n_y),
        [field, field, field, arr(6, nx, ny, nz), small, *rows, columns],
        140 * size,
    )
    more = (*got_x, rd, v0, mom, *sent)
    hist_ends, rd, v0, ends, mom, *sent = call(
        functools.partial(ends_kernel, n_y),
        "ssvvvv" + "v" * (1 + n_y) + "vvvvv" + "v" * (1 + n_y),
        (*voxels, *more),
        "vvvvv" + "v" * (3 + n_y),
        [
            arr(2, ny, nz),
            field,
            field,
            arr(6, 2, ny, nz),
            small,
            *[arr(8, ny, nz)] * 2,
            *rows,
            columns,
        ],
        20 * size,
    )
    stress_z = swap(sent[-1], "gz", z_pairs)
    xs = swap_along("gx", sent[:2])
    ys = swap_along("gy", sent[2 : 2 + n_y])
    corners = call(
        functools.partial(corner_kernel, n_y),
        "savv",
        (pos, stress_z, v0, rd),
        "v" * (2 * n_y),
        [arr(2, 8, nz)] * (2 * n_y),
        1024,
    )
    xy = [*xs, *ys, *swap_diagonal(corners)]
    moving = (
        pos,
        scaled,
        impact,
        both,
        velocity,
        contact,
        labels,
        *ys,
        stress_z,
        stress,
        ends,
    )
    hist_new, *moved, token = call(
        functools.partial(force_inner_kernel, n_y),
        "sssvvvv" + "v" * (3 + n_y) + "vv",
        (*moving, hist, hist_ends),
        "hvvv",
        [field, fields3, fields3, small],
        55 * size,
        [pltpu.SemaphoreType.DMA((3,))],
    )
    (joined,) = call(
        functools.partial(join_kernel, n_y),
        "svva" + "v" * len(xy),
        (pos, v0, rd, token, *xy),
        "v",
        [arr(nx + 6 + 6 * (ny // 8), 8, 128)],
        4 * size,
    )
    z_got = swap(joined, "gz", z_pairs)
    *moved_ends, main_v, main_rd = call(
        functools.partial(rest_kernel, n_y),
        "sssvvvv" + "v" * (3 + n_y) + "vv" + "v" * len(xy),
        (*moving, v0, rd, *xy),
        "vvvv",
        [arr(3, 2, ny, nz)] * 2 + [arr(nx + 6, ny + 8, nz)] * 2,
        12 * size,
    )
    peers = lax.axis_size("gx") * lax.axis_size("gy") * lax.axis_size("gz")
    new_disp, new_vel, v1, v2, spread = call(
        krylov_kernel,
        "svvvvvvvvv",
        (pos, main_v, main_rd, mom, stress_z, z_got, *moved, *moved_ends),
        "hhvvv",
        [fields3, fields3, field, field, arr(peers, 1, 128)],
        60 * size,
        [
            pltpu.VMEM((nx + 6, ny + 8, 128), F32),
            pltpu.VMEM((nx + 6, ny + 8, 128), F32),
            pltpu.VMEM((nx + 4, ny + 8, nz + 128), F32),
            pltpu.VMEM((nx + 2, ny + 8, nz + 128), F32),
            pltpu.SemaphoreType.DMA((2, 5)),
        ],
    )
    mom = lax.all_to_all(spread, ("gx", "gy", "gz"), 0, 0, tiled=True)
    (damage_new,) = call(
        final_kernel,
        "vvvvv",
        (mom, v0, v1, v2, damage),
        "h",
        [field],
        8 * size,
        [pltpu.VMEM((nx, ny, nz), F32), pltpu.SemaphoreType.DMA((CHUNKS,))],
    )
    return new_disp, new_vel, hist_new, damage_new


def solution(mesh):
    placed = (
        P(None, ("case", "gx"), "gy", "gz"),
        P(None, ("case", "gx"), "gy", "gz"),
        P(("case", "gx"), "gy", "gz"),
        P(("case", "gx"), "gy", "gz"),
        P(("case", "gx"), "gy", "gz"),
        P(("case", "gx"), "gy", "gz"),
        P(("case", "gx"), "gy", "gz"),
        P(),
        P("case"),
    )
    return jax.shard_map(
        per_device,
        mesh=mesh,
        in_specs=placed,
        out_specs=(
            P(None, ("case", "gx"), "gy", "gz"),
            P(None, ("case", "gx"), "gy", "gz"),
            P(("case", "gx"), "gy", "gz"),
            P(("case", "gx"), "gy", "gz"),
        ),
        check_vma=False,
    )
```

```python
import functools
import jax
import jax.numpy as jnp
from jax import lax
from jax.experimental import pallas as pl
from jax.experimental.pallas import tpu as pltpu
from jax.sharding import PartitionSpec as P

TIME_STEP = 0.1
KAPPA_COEF = 0.5
NOTCH_LOAD = 20.0
STIFF_FLOOR = 0.001
ALPHA_LOW, ALPHA_HIGH = 0.5, 6.5
VMEM_BYTES = 28 * 1024 * 1024
CHUNKS = 4
STRESS_LANE = 32
F32 = jnp.float32


def iota2(shape, dim):
    return lax.broadcasted_iota(jnp.int32, shape, dim)


def low_high(odd, got):
    if len(got) == 2:
        return jnp.where(odd, got[0], got[1]), jnp.where(odd, got[1], got[0])
    return jnp.where(odd, got[0], 0.0), jnp.where(odd, 0.0, got[0])


def send(odd, refs, index, low, high):
    refs[0][index] = jnp.where(odd, low, high)
    if len(refs) == 2:
        refs[1][index] = jnp.where(odd, high, low)


def shift_y(plane, rows):
    lo, hi = rows
    tiles = [plane[start : start + 8] for start in range(0, plane.shape[0], 8)]
    at = iota2(tiles[0].shape, 0)
    ahead = [pltpu.roll(tile, 7, 0) for tile in tiles]
    behind = [pltpu.roll(tile, 1, 0) for tile in tiles]
    upper = [jnp.where(at == 7, b, a) for a, b in zip(ahead, [*ahead[1:], hi])]
    lower = [jnp.where(at == 0, b, a) for a, b in zip(behind, [lo, *behind[:-1]])]
    return jnp.concatenate(upper, axis=0), jnp.concatenate(lower, axis=0)


def shift_z(plane, column, first_z):
    tiles = [plane[:, start : start + 128] for start in range(0, plane.shape[1], 128)]
    at = iota2(tiles[0].shape, 1)
    wide = jnp.broadcast_to(column, tiles[0].shape)
    lo, hi = jnp.where(first_z, 0.0, wide), jnp.where(first_z, wide, 0.0)
    ahead = [pltpu.roll(tile, 127, 1) for tile in tiles]
    behind = [pltpu.roll(tile, 1, 1) for tile in tiles]
    upper = [jnp.where(at == 127, b, a) for a, b in zip(ahead, [*ahead[1:], hi])]
    lower = [jnp.where(at == 0, b, a) for a, b in zip(behind, [lo, *behind[:-1]])]
    return jnp.concatenate(upper, axis=1), jnp.concatenate(lower, axis=1)


def send_columns(ref, x, planes, gz, tile=None, first=0):
    depth = planes[0].shape[1]
    lanes = iota2((planes[0].shape[0], 128), 1)
    for field, plane in enumerate(planes):
        part = jnp.where(gz == 0, plane[:, depth - 128 :], plane[:, :128])
        part = pltpu.roll(part, first + field + 1 - gz, 1)
        tile = part if tile is None else jnp.where(lanes == first + field, part, tile)
    ref[x] = tile


def z_tile(v, rd, gz):
    depth = v.shape[1]
    keep = lax.shift_right_logical(iota2((v.shape[0], 128), 1), 6) == 1 - gz
    mine = jnp.where(gz == 0, v[:, depth - 128 :], v[:, :128])
    moved = jnp.where(gz == 0, rd[:, depth - 128 :], rd[:, :128])
    return jnp.where(keep, mine, pltpu.roll(moved, 64, 1))


def folded(values):
    total = None
    for start in range(0, values.shape[1], 128):
        part = values[:, start : start + 128]
        total = part if total is None else total + part
    out = None
    for start in range(0, values.shape[0], 8):
        part = total[start : start + 8]
        out = part if out is None else out + part
    return out


def by_label(labels, scalars):
    picked = scalars[0]
    for region in range(1, len(scalars)):
        picked = jnp.where(labels == region, scalars[region], picked)
    return picked


def unrolled(count, many, body, carry):
    def several(block, carry):
        for at in range(many):
            carry = body(block * many + at, carry)
        return carry

    if many == count:
        return several(0, carry)
    return lax.fori_loop(0, count // many, several, carry)


def pack_kernel(n_y, pos, disp, *refs):
    damage = disp.at[3]
    ys, zs = refs[:n_y], refs[n_y]
    odd_y, gz = pos[1] == 1, pos[2]

    def body(x, carry):
        planes = [disp[0, x], disp[1, x], disp[2, x], damage[x]]
        for field, plane in enumerate(planes):
            last = plane.shape[0] - 1
            spot = (field, pl.ds(x, 1), slice(None))
            send(odd_y, ys, spot, plane[0:1], plane[last : last + 1])
        send_columns(zs, x, planes, gz)
        return carry

    unrolled(damage.shape[0], damage.shape[0], body, 0)


def pack_x_kernel(pos, disp, after, *xs):
    damage = disp.at[3]
    odd_x, count = pos[0] == 1, damage.shape[0]
    for field, src in enumerate((disp.at[0], disp.at[1], disp.at[2], damage)):
        send(odd_x, xs, field, src[0], src[count - 1])


class Local:
    def __init__(self, pos, table, disp, damage, history, notch, labels, yg, zg):
        self.odd_x, self.odd_y, self.gz = pos[0] == 1, pos[1] == 1, pos[2]
        self.disp, self.damage, self.history = disp, damage, history
        self.notch, self.labels, self.yg, self.zg = notch, labels, yg, zg
        regions = range(table.shape[1])
        self.lames = [table[0, r] for r in regions]
        self.shears = [table[1, r] for r in regions]
        self.bases = [table[3, r] for r in regions]

    def plane(self, x, lower, upper, put):
        lab = self.labels[x]
        shear = by_label(lab, self.shears)
        dmg = self.damage[x]
        degrade = 4.0 * ((1.0 - dmg) * (1.0 - dmg) + STIFF_FLOOR)
        half = degrade * shear
        fields = [self.disp[c, x] for c in range(3)]

        def d(c, j):
            if j == 0:
                return upper(c) - lower(c)
            if j == 1:
                rows = low_high(self.odd_y, [y[c, pl.ds(x, 1), :] for y in self.yg])
                high, low = shift_y(fields[c], rows)
            else:
                column = self.zg[x][:, c : c + 1]
                high, low = shift_z(fields[c], column, self.gz == 0)
            return high - low

        squares = None
        for k, (i, j) in ((3, (0, 1)), (4, (0, 2)), (5, (1, 2))):
            e = d(i, j) + d(j, i)
            put(k, half * e)
            squares = e * e if squares is None else squares + e * e
        straight = [d(c, c) for c in range(3)]
        trace = straight[0] + straight[1] + straight[2]
        lame = by_label(lab, self.lames)
        level = (degrade * lame) * trace
        whole = half + half
        for k in range(3):
            put(k, level + whole * straight[k])
        twice = (
            straight[0] * straight[0] + straight[1] * straight[1] + straight[2] * straight[2]
        )
        squares = squares + (twice + twice)
        positive = jnp.maximum(trace, 0.0)
        energy = lame * positive * positive + shear * squares
        hist = jnp.maximum(
            jnp.maximum(self.history[x], energy), NOTCH_LOAD * self.notch[x].astype(F32)
        )
        diagonal = by_label(lab, self.bases) + 2.0 * hist
        rd = 1.0 / diagonal
        rows = low_high(self.odd_y, [y[3, pl.ds(x, 1), :] for y in self.yg])
        yu, yl = shift_y(dmg, rows)
        zu, zl = shift_z(dmg, self.zg[x][:, 3:4], self.gz == 0)
        near = ((upper(3) + lower(3)) + (yu + yl)) + (zu + zl)
        residual = 2.0 * hist - (diagonal * dmg - KAPPA_COEF * near)
        v = residual * rd
        return hist, rd, v, folded(residual * v)

    def send_y(self, ys, x, v, rd, stress):
        rows = v.shape[0]
        sources = [(v, depth) for depth in (1, 2, 3)] + [(rd, depth) for depth in (1, 2)]
        sources += [(stress[k], 1) for k in (3, 1, 5)]
        for slot, (plane, depth) in enumerate(sources):
            low, high = plane[depth - 1 : depth], plane[rows - depth : rows - depth + 1]
            send(self.odd_y, ys, (slot, pl.ds(x, 1), slice(None)), low, high)

    def send_z(self, zs, x, v, rd, stress):
        base = z_tile(v, rd, self.gz)
        planes = [stress[4], stress[5], stress[2]]
        send_columns(zs, x, planes, self.gz, base, STRESS_LANE)


def inner_steps(count, most):
    inner = count - 2
    many = max(m for m in range(1, most + 1) if inner % m == 0)
    return inner // many, many


def inner_kernel(n_y, pos, table, disp, history, notch, labels, *refs):
    damage = disp.at[3]
    local = Local(
        pos, table, disp, damage, history, notch, labels, refs[:n_y], refs[n_y]
    )
    hist, rd_out, v_out, stress_out, mom_out = refs[n_y + 1 : n_y + 6]
    ys, zs = refs[n_y + 6 : 2 * n_y + 6], refs[2 * n_y + 6]
    steps, many = inner_steps(damage.shape[0], 7)

    def several(step, total):
        for at in range(many):
            x = 1 + step * many + at

            def lower(c):
                return damage[x - 1] if c == 3 else disp[c, x - 1]

            def upper(c):
                return damage[x + 1] if c == 3 else disp[c, x + 1]

            stress = {}

            def put(k, plane):
                stress[k] = stress_out[k, x] = plane

            hist_x, rd, v, part = local.plane(x, lower, upper, put)
            hist[x] = hist_x
            rd_out[x] = rd
            v_out[x] = v
            local.send_y(ys, x, v, rd, stress)
            local.send_z(zs, x, v, rd, stress)
            total = total + part
        return total

    mom_out[...] = unrolled(steps, 1, several, jnp.zeros((8, 128), F32))


def ends_kernel(n_y, pos, table, disp, history, notch, labels, *refs):
    damage = disp.at[3]
    local = Local(
        pos, table, disp, damage, history, notch, labels, refs[:n_y], refs[n_y]
    )
    refs = refs[n_y + 1 :]
    xg, (rd_in, v_in, mom), ys_in, zs_in = (
        refs[:2],
        refs[2:5],
        refs[5 : 5 + n_y],
        refs[5 + n_y],
    )
    refs = refs[6 + n_y :]
    hist, rd_out, v_out, stress_out, mom_out = refs[:5]
    xs, ys, zs = refs[5:7], refs[7 : 7 + n_y], refs[7 + n_y]
    odd_x, count = local.odd_x, damage.shape[0]
    total = mom[...]
    found = []
    for end, x in enumerate((0, count - 1)):

        def outside(c):
            first, second = xg[0][c], xg[1][c]
            if end == 0:
                return jnp.where(odd_x, first, second)
            return jnp.where(odd_x, second, first)

        def beside(c):
            at = 1 if end == 0 else count - 2
            return damage[at] if c == 3 else disp[c, at]

        sides = (outside, beside) if end == 0 else (beside, outside)
        stress = {}

        def put(k, plane):
            stress[k] = stress_out[k, end] = plane

        hist_x, rd, v, part = local.plane(x, *sides, put)
        hist[end] = hist_x
        rd_out[x] = rd
        v_out[x] = v
        total = total + part
        found.append((stress, rd, v))
    for mine, before in zip(ys, ys_in, strict=True):
        for slot in range(8):
            mine[slot] = before[slot]
    for x in range(1, count - 1):
        rd_out[x] = rd_in[x]
        v_out[x] = v_in[x]
        zs[x] = zs_in[x]
    for end, x in enumerate((0, count - 1)):
        stress, rd, v = found[end]
        local.send_y(ys, x, v, rd, stress)
        local.send_z(zs, x, v, rd, stress)
    for depth in (1, 2, 3):
        low, high = depth - 1, count - depth
        send(odd_x, xs, depth - 1, v_out[low], v_out[high])
        if depth <= 2:
            send(odd_x, xs, 2 + depth, rd_out[low], rd_out[high])
    for slot, k in ((5, 0), (6, 3), (7, 4)):
        send(odd_x, xs, slot, stress_out[k, 0], stress_out[k, 1])
    mom_out[...] = jnp.zeros((8, 128), F32)
    mom_out[0:1, :] = jnp.sum(total, axis=0, keepdims=True)


def corner_kernel(n_y, pos, after, v, rd, *ds):
    odd_x, odd_y = pos[0] == 1, pos[1] == 1
    count, rows = v.shape[0], v.shape[1]
    for depth in (1, 2):
        for slot, (src, deep) in enumerate(((v, 1), (v, 2), (v, 3), (rd, 1), (rd, 2))):
            near, far = pl.ds(deep - 1, 1), pl.ds(rows - deep, 1)
            planes = (depth - 1, count - depth)
            by_y = [(src[x, near, :], src[x, far, :]) for x in planes]
            for which in range(n_y):
                pair = (ds[which], ds[n_y + which])
                picked = [
                    jnp.where(odd_y, *(rows_of if which == 0 else rows_of[::-1]))
                    for rows_of in by_y
                ]
                send(odd_x, pair, (depth - 1, pl.ds(slot, 1), slice(None)), *picked)


class Enlarged:
    def __init__(self, n_y, pos, v, rd, refs):
        self.odd_x, self.odd_y = pos[0] == 1, pos[1] == 1
        self.v, self.rd, self.n_y = v, rd, n_y
        self.xg, self.yg, self.dg = refs[:2], refs[2 : 2 + n_y], refs[2 + n_y : 2 + 3 * n_y]

    def rows(self, found):
        nz = self.v.shape[2]
        at = iota2((8, nz), 0)

        def tile(first, depths):
            out = jnp.zeros((8, nz), F32)
            for depth in range(1, depths + 1):
                got = [found(w, first + depth - 1) for w in range(self.n_y)]
                if self.n_y == 1:
                    spot = jnp.where(self.odd_y, 8 - depth, depth - 1)
                    out = jnp.where(at == spot, got[0], out)
                else:
                    lo, hi = low_high(self.odd_y, got)
                    out = jnp.where(at == depth - 1, hi, out)
                    out = jnp.where(at == 8 - depth, lo, out)
            return out

        return tile(0, 3), tile(3, 2)

    def own(self, x):
        v_rows, rd_rows = self.rows(lambda w, slot: self.yg[w][slot, pl.ds(x, 1), :])
        return self.v[x], v_rows, self.rd[x], rd_rows

    def halo(self, is_low, depth):
        first, second = (0, 1) if is_low else (1, 0)

        def of(a, b):
            return jnp.where(self.odd_x, (a, b)[first], (a, b)[second])

        v = of(self.xg[0][depth - 1], self.xg[1][depth - 1])
        nothing = jnp.zeros((8, v.shape[1]), F32)
        if depth > 2:
            return v, nothing, jnp.zeros_like(v), nothing
        rd = of(self.xg[0][2 + depth], self.xg[1][2 + depth])

        def found(w, slot):
            spot = (depth - 1, pl.ds(slot, 1), slice(None))
            return of(self.dg[w][spot], self.dg[self.n_y + w][spot])

        v_rows, rd_rows = self.rows(found)
        return v, v_rows, rd, rd_rows

    def outer(self, count):
        for depth in (1, 2, 3):
            yield -depth, self.halo(True, depth)
            yield count - 1 + depth, self.halo(False, depth)


def outer_index(p, count):
    return -p - 1 if p < 0 else 3 + p - count


def join_kernel(n_y, pos, v, rd, token, *refs):
    big = Enlarged(n_y, pos, v, rd, refs[:-1])
    out, gz = refs[-1], pos[2]
    count, ny, _ = v.shape
    tall = ny // 8
    for p, (v_own, v_rows, rd_own, rd_rows) in big.outer(count):
        out[p + 3] = z_tile(v_rows, rd_rows, gz)
        start = count + 6 + tall * outer_index(p, count)
        out[start : start + tall] = z_tile(v_own, rd_own, gz).reshape(tall, 8, 128)

    def body(x, carry):
        _, v_rows, _, rd_rows = big.own(x)
        out[x + 3] = z_tile(v_rows, rd_rows, gz)
        return carry

    unrolled(count, count, body, 0)


def krylov_kernel(pos, main_v, main_rd, mom, z_own, z_got, *refs):
    moved, moved_ends, moved_hbm = refs[:2], refs[2:4], refs[4:6]
    v1_out, v2_out, spread, z_v, z_rd, big_v1, big_v2, sems = refs[6:]
    count, ny, nz = v1_out.shape
    inner = pl.ds(1, count - 2)
    copies = []
    for which, (src, ends, dst) in enumerate(zip(moved, moved_ends, moved_hbm)):
        for c in range(3):
            copies.append((src.at[c, inner], dst.at[c, inner], sems.at[which, c]))
        copies.append((ends.at[:, 0], dst.at[:, 0], sems.at[which, 3]))
        copies.append((ends.at[:, 1], dst.at[:, count - 1], sems.at[which, 4]))
    copies = [pltpu.make_async_copy(*copy) for copy in copies]
    for copy in copies:
        copy.start()

    tall = ny // 8

    def split(at, rows, tile):
        keep = lax.shift_right_logical(iota2(tile.shape, 1), 6) == pos[2]
        z_v[at, rows] = jnp.where(keep, tile, 0.0)
        z_rd[at, rows] = jnp.where(keep, pltpu.roll(tile, 64, 1), 0.0)

    for p in (-3, -2, -1, count, count + 1, count + 2):
        start = count + 6 + tall * outer_index(p, count)
        split(p + 3, slice(0, ny), z_got[start : start + tall].reshape(ny, 128))
        split(p + 3, slice(ny, ny + 8), z_got[p + 3])

    def split_own(x, carry):
        split(x + 3, slice(0, ny), z_own[x])
        split(x + 3, slice(ny, ny + 8), z_got[x + 3])
        return carry

    unrolled(count, 8, split_own, 0)

    def v_at(at):
        return jnp.concatenate([main_v[at], z_v[at]], axis=1)

    def rd_at(at):
        return jnp.concatenate([main_rd[at], z_rd[at]], axis=1)

    def image_of(get, at):
        plane = get(at)
        rows, lanes = plane.shape
        near = (get(at - 1) + get(at + 1)) + (pltpu.roll(plane, 1, 0) + pltpu.roll(plane, rows - 1, 0))
        near = near + (pltpu.roll(plane, 1, 1) + pltpu.roll(plane, lanes - 1, 1))
        return plane, KAPPA_COEF * near

    def v1_at(at):
        return big_v1[at]

    def v2_at(at):
        return big_v2[at]

    def inside(values):
        return folded(values[0:ny, 0:nz])

    def first(x, totals):
        plane, image = image_of(v_at, x + 3)
        made = image * rd_at(x + 3)
        big_v1[x + 2] = made
        v1_out[x] = made[0:ny, 0:nz]
        return totals[0] + inside(plane * image), totals[1] + inside(made * image)

    def second(x, totals):
        plane, image = image_of(v1_at, x + 2)
        made = image * rd_at(x + 3)
        big_v2[x + 1] = made
        v2_out[x] = made[0:ny, 0:nz]
        return totals[0] + inside(plane * image), totals[1] + inside(made * image)

    def third(x, total):
        plane, image = image_of(v2_at, x + 1)
        return total + folded(plane[0:ny, 0:nz] * image[0:ny, 0:nz])

    zero = jnp.zeros((8, 128), F32)
    for p in (-2, -1, count, count + 1):
        big_v1[p + 2] = image_of(v_at, p + 3)[1] * rd_at(p + 3)
    k1, k2 = unrolled(count, 8, first, (zero, zero))
    for p in (-1, count):
        big_v2[p + 1] = image_of(v1_at, p + 2)[1] * rd_at(p + 3)
    k3, k4 = unrolled(count, 8, second, (zero, zero))
    k5 = unrolled(count, 8, third, zero)
    rows = iota2((8, 128), 0)
    result = mom[...]
    for at, total in enumerate((k1, k2, k3, k4, k5)):
        result = jnp.where(rows == at + 1, jnp.sum(total, axis=0, keepdims=True), result)
    mine = rows == iota2((8, 128), 1)
    line = jnp.sum(
        jnp.where(mine, jnp.sum(result, axis=1, keepdims=True), 0.0), axis=0, keepdims=True
    )
    for peer in range(spread.shape[0]):
        spread[peer] = line
    for copy in copies:
        copy.wait()


PARTS = ((0, 3, 4), (3, 1, 5), (4, 5, 2))


class Force:
    def __init__(self, n_y, pos, table, impact, disp, vel, contact, labels, yg, zg):
        self.odd_x, self.odd_y, self.gz = pos[0] == 1, pos[1] == 1, pos[2]
        self.impact, self.disp, self.vel = impact, disp, vel
        self.contact, self.labels, self.yg, self.zg = contact, labels, yg, zg
        self.rates = [table[2, r] for r in range(table.shape[1])]

    def plane(self, x, lower, mine, upper, vel_out, disp_out, at):
        loaded = self.contact[x].astype(F32)
        rate = by_label(self.labels[x], self.rates)
        for c, (kx, ky, kz) in enumerate(PARTS):
            rows = low_high(self.odd_y, [y[5 + c, pl.ds(x, 1), :] for y in self.yg])
            lane = STRESS_LANE + c
            column = self.zg[x][:, lane : lane + 1]
            yu, yl = shift_y(mine(ky), rows)
            zu, zl = shift_z(mine(kz), column, self.gz == 0)
            force = 0.5 * (((upper(c, kx) - lower(c, kx)) + (yu - yl)) + (zu - zl))
            speed = self.vel[c, x] + rate * (force + loaded * self.impact[c])
            vel_out[c, at] = speed
            disp_out[c, at] = self.disp[c, x] + TIME_STEP * speed


def force_inner_kernel(n_y, pos, table, impact, disp, vel, contact, labels, *refs):
    yg, zg, stress, ends = refs[:n_y], refs[n_y], refs[n_y + 1], refs[n_y + 2]
    hist, hist_ends, hist_hbm, disp_out, vel_out, token, sems = refs[n_y + 3 :]
    token[...] = jnp.zeros((8, 128), F32)
    force = Force(n_y, pos, table, impact, disp, vel, contact, labels, yg, zg)
    count = contact.shape[0]
    steps, many = inner_steps(count, 7)

    inside = pl.ds(1, count - 2)
    copies = [
        pltpu.make_async_copy(hist.at[inside], hist_hbm.at[inside], sems.at[0]),
        pltpu.make_async_copy(hist_ends.at[0], hist_hbm.at[0], sems.at[1]),
        pltpu.make_async_copy(hist_ends.at[1], hist_hbm.at[count - 1], sems.at[2]),
    ]
    for copy in copies:
        copy.start()

    def several(step, carry):
        for at in range(many):
            x = 1 + step * many + at

            def lower(c, k):
                if at == 0:
                    return jnp.where(step == 0, ends[k, 0], stress[k, x - 1])
                return stress[k, x - 1]

            def upper(c, k):
                if at == many - 1:
                    return jnp.where(step == steps - 1, ends[k, 1], stress[k, x + 1])
                return stress[k, x + 1]

            force.plane(x, lower, lambda k: stress[k, x], upper, vel_out, disp_out, x)
        return carry

    unrolled(steps, 1, several, 0)
    for copy in copies:
        copy.wait()


def rest_kernel(n_y, pos, table, impact, disp, vel, contact, labels, *refs):
    yg, zg, stress, ends = refs[:n_y], refs[n_y], refs[n_y + 1], refs[n_y + 2]
    refs = refs[n_y + 3 :]
    v, rd, xy = refs[0], refs[1], refs[2 : 4 + 3 * n_y]
    xg = xy[:2]
    disp_out, vel_out, big_v, big_rd = refs[4 + 3 * n_y :]
    force = Force(n_y, pos, table, impact, disp, vel, contact, labels, yg, zg)
    count, ny = contact.shape[0], contact.shape[1]
    for end, x in enumerate((0, count - 1)):

        def outside(c, k):
            first, second = xg[0][5 + c], xg[1][5 + c]
            if end == 0:
                return jnp.where(force.odd_x, first, second)
            return jnp.where(force.odd_x, second, first)

        def beside(c, k):
            return stress[k, 1 if end == 0 else count - 2]

        lower, upper = (outside, beside) if end == 0 else (beside, outside)
        force.plane(x, lower, lambda k: ends[k, end], upper, vel_out, disp_out, end)
    big = Enlarged(n_y, pos, v, rd, xy)

    def put(p, parts):
        v_own, v_rows, rd_own, rd_rows = parts
        big_v[p + 3, 0:ny] = v_own
        big_v[p + 3, ny : ny + 8] = v_rows
        big_rd[p + 3, 0:ny] = rd_own
        big_rd[p + 3, ny : ny + 8] = rd_rows

    for p, parts in big.outer(count):
        put(p, parts)

    def body(x, carry):
        put(x, big.own(x))
        return carry

    unrolled(count, 4, body, 0)


def cg_coefficients(k):
    zero, one = jnp.zeros_like(k[0]), jnp.ones_like(k[0])
    z, p, out = [one], [one], [zero, zero, zero]

    def form(a, b, moments):
        total = None
        for i, ai in enumerate(a):
            for j, bj in enumerate(b):
                term = ai * bj * moments[i + j]
                total = term if total is None else total + term
        return total

    energy = [k[j] - k[j + 1] for j in range(5)]
    rz = k[0]
    for step in range(3):
        alpha = jnp.clip(rz / form(p, p, energy), ALPHA_LOW, ALPHA_HIGH)
        out = [o + alpha * (p[i] if i < len(p) else zero) for i, o in enumerate(out)]
        if step == 2:
            break
        image = [(p[i] if i < len(p) else zero) - (p[i - 1] if i else zero) for i in range(len(p) + 1)]
        z = [(z[i] if i < len(z) else zero) - alpha * image[i] for i in range(len(image))]
        new = jnp.maximum(form(z, z, k), 0.0)
        beta = new / rz
        p = [z[i] + beta * (p[i] if i < len(p) else zero) for i in range(len(z))]
        rz = new
    return out


def final_kernel(mom, v0, v1, v2, damage, out_hbm, out, sems):
    count = v0.shape[0]
    block = count // CHUNKS
    sums = jnp.sum(mom[...], axis=0)
    c0, c1, c2 = cg_coefficients([sums[:, j : j + 1] for j in range(6)])
    copies = []
    for chunk in range(CHUNKS):
        for x in range(chunk * block, (chunk + 1) * block):
            dmg = damage[x]
            out[x] = jnp.maximum(dmg + (c0 * v0[x] + c1 * v1[x] + c2 * v2[x]), dmg)
        part = pl.ds(chunk * block, block)
        copies.append(pltpu.make_async_copy(out.at[part], out_hbm.at[part], sems.at[chunk]))
        copies[-1].start()
    for copy in copies:
        copy.wait()


def pairs_of(axis):
    count = lax.axis_size(axis)
    out = [[(i, i + 1) for i in range(start, count - 1, 2)] for start in (0, 1)]
    return [pairs for pairs in out if pairs]


def swap(array, axis, pairs):
    return lax.ppermute(array, axis, pairs + [(b, a) for a, b in pairs])


def swap_along(axis, arrays):
    return [swap(a, axis, pairs) for a, pairs in zip(arrays, pairs_of(axis), strict=True)]


def swap_diagonal(arrays):
    columns = lax.axis_size("gy")
    out = []
    both = [(xp, yp) for xp in pairs_of("gx") for yp in pairs_of("gy")]
    for array, (x_pairs, y_pairs) in zip(arrays, both, strict=True):
        joint = []
        for a, b in x_pairs:
            for c, d in y_pairs:
                joint.append((a * columns + c, b * columns + d))
                joint.append((a * columns + d, b * columns + c))
        out.append(swap(array, ("gx", "gy"), joint))
    return out


def spec_of(kind, a):
    if kind == "s":
        return pl.BlockSpec(memory_space=pltpu.SMEM)
    if kind == "v":
        return pl.BlockSpec(memory_space=pltpu.VMEM)
    if kind == "h":
        return pl.BlockSpec(memory_space=pltpu.HBM)
    if kind == "a":
        return pl.BlockSpec(memory_space=pl.ANY)
    raise ValueError(kind)


def call(kernel, kinds, ins, out_kinds, outs, flops, scratch=(), aliases=()):
    moved = sum(4 * a.size for a in (*ins, *outs))
    return pl.pallas_call(
        kernel,
        out_shape=outs,
        in_specs=[spec_of(k, a) for k, a in zip(kinds, ins, strict=True)],
        out_specs=[spec_of(k, a) for k, a in zip(out_kinds, outs, strict=True)],
        scratch_shapes=scratch,
        input_output_aliases=dict(aliases),
        compiler_params=pltpu.CompilerParams(vmem_limit_bytes=VMEM_BYTES),
        cost_estimate=pl.CostEstimate(flops=flops, bytes_accessed=moved, transcendentals=0),
    )(*ins)


def per_device(displacement, velocity, damage, history, contact, notch, labels, table, impact):
    nx, ny, nz = damage.shape
    size = damage.size
    n_y = len(pairs_of("gy"))
    pos = jnp.stack(
        [lax.axis_index("gx") % 2, lax.axis_index("gy") % 2, lax.axis_index("gz")]
    ).astype(jnp.int32)

    scaled = jnp.stack(
        [table[0] / 8.0, table[1] / 8.0, TIME_STEP / table[2], table[3] + 6.0 * KAPPA_COEF]
    )

    def arr(*shape):
        return jax.ShapeDtypeStruct(shape, F32)

    field, fields3, small = arr(nx, ny, nz), arr(3, nx, ny, nz), arr(8, 128)
    columns = arr(nx, ny, 128)
    z_pairs = [(0, 1)]

    both = jnp.concatenate([displacement, damage[None]])
    sent = call(
        functools.partial(pack_kernel, n_y),
        "sv",
        (pos, both),
        "v" * (1 + n_y),
        [*[arr(4, nx, nz)] * n_y, columns],
        size,
    )
    got_yz = [*swap_along("gy", sent[:n_y]), swap(sent[-1], "gz", z_pairs)]
    sent_x = call(
        pack_x_kernel,
        "sva",
        (pos, both, sent[-1]),
        "vv",
        [arr(4, ny, nz)] * 2,
        size,
    )
    got_x = swap_along("gx", sent_x)
    rows = [arr(8, nx, nz)] * n_y
    voxels = (pos, scaled, both, history, notch, labels, *got_yz)
    hist, rd, v0, stress, mom, *sent = call(
        functools.partial(inner_kernel, n_y),
        "ssvvvv" + "v" * (1 + n_y),
        voxels,
        "vvvvv" + "v" * (1 + n_y),
        [field, field, field, arr(6, nx, ny, nz), small, *rows, columns],
        140 * size,
    )
    more = (*got_x, rd, v0, mom, *sent)
    hist_ends, rd, v0, ends, mom, *sent = call(
        functools.partial(ends_kernel, n_y),
        "ssvvvv" + "v" * (1 + n_y) + "vvvvv" + "v" * (1 + n_y),
        (*voxels, *more),
        "vvvvv" + "v" * (3 + n_y),
        [
            arr(2, ny, nz),
            field,
            field,
            arr(6, 2, ny, nz),
            small,
            *[arr(8, ny, nz)] * 2,
            *rows,
            columns,
        ],
        20 * size,
    )
    stress_z = swap(sent[-1], "gz", z_pairs)
    xs = swap_along("gx", sent[:2])
    ys = swap_along("gy", sent[2 : 2 + n_y])
    corners = call(
        functools.partial(corner_kernel, n_y),
        "savv",
        (pos, stress_z, v0, rd),
        "v" * (2 * n_y),
        [arr(2, 8, nz)] * (2 * n_y),
        1024,
    )
    xy = [*xs, *ys, *swap_diagonal(corners)]
    moving = (
        pos,
        scaled,
        impact,
        both,
        velocity,
        contact,
        labels,
        *ys,
        stress_z,
        stress,
        ends,
    )
    hist_new, *moved, token = call(
        functools.partial(force_inner_kernel, n_y),
        "sssvvvv" + "v" * (3 + n_y) + "vv",
        (*moving, hist, hist_ends),
        "hvvv",
        [field, fields3, fields3, small],
        55 * size,
        [pltpu.SemaphoreType.DMA((3,))],
    )
    (joined,) = call(
        functools.partial(join_kernel, n_y),
        "svva" + "v" * len(xy),
        (pos, v0, rd, token, *xy),
        "v",
        [arr(nx + 6 + 6 * (ny // 8), 8, 128)],
        4 * size,
    )
    z_got = swap(joined, "gz", z_pairs)
    *moved_ends, main_v, main_rd = call(
        functools.partial(rest_kernel, n_y),
        "sssvvvv" + "v" * (3 + n_y) + "vv" + "v" * len(xy),
        (*moving, v0, rd, *xy),
        "vvvv",
        [arr(3, 2, ny, nz)] * 2 + [arr(nx + 6, ny + 8, nz)] * 2,
        12 * size,
    )
    peers = lax.axis_size("gx") * lax.axis_size("gy") * lax.axis_size("gz")
    new_disp, new_vel, v1, v2, spread = call(
        krylov_kernel,
        "svvvvvvvvv",
        (pos, main_v, main_rd, mom, stress_z, z_got, *moved, *moved_ends),
        "hhvvv",
        [fields3, fields3, field, field, arr(peers, 1, 128)],
        60 * size,
        [
            pltpu.VMEM((nx + 6, ny + 8, 128), F32),
            pltpu.VMEM((nx + 6, ny + 8, 128), F32),
            pltpu.VMEM((nx + 4, ny + 8, nz + 128), F32),
            pltpu.VMEM((nx + 2, ny + 8, nz + 128), F32),
            pltpu.SemaphoreType.DMA((2, 5)),
        ],
    )
    mom = lax.all_to_all(spread, ("gx", "gy", "gz"), 0, 0, tiled=True)
    (damage_new,) = call(
        final_kernel,
        "vvvvv",
        (mom, v0, v1, v2, damage),
        "h",
        [field],
        8 * size,
        [pltpu.VMEM((nx, ny, nz), F32), pltpu.SemaphoreType.DMA((CHUNKS,))],
    )
    return new_disp, new_vel, hist_new, damage_new


def solution(mesh):
    placed = (
        P(None, ("case", "gx"), "gy", "gz"),
        P(None, ("case", "gx"), "gy", "gz"),
        P(("case", "gx"), "gy", "gz"),
        P(("case", "gx"), "gy", "gz"),
        P(("case", "gx"), "gy", "gz"),
        P(("case", "gx"), "gy", "gz"),
        P(("case", "gx"), "gy", "gz"),
        P(),
        P("case"),
    )
    return jax.shard_map(
        per_device,
        mesh=mesh,
        in_specs=placed,
        out_specs=(
            P(None, ("case", "gx"), "gy", "gz"),
            P(None, ("case", "gx"), "gy", "gz"),
            P(("case", "gx"), "gy", "gz"),
            P(("case", "gx"), "gy", "gz"),
        ),
        check_vma=False,
    )
```
